32 devices in a mesh: blk: 4 (over y, x), expert: 8 (over z, core).
Axes of the slice: x: 2, y: 2, z: 4, core: 2. Of those that a mesh axis runs over, the one named last changes fastest.
Arguments:
- tokens: bfloat16 [8, 2048, 768], P('expert', 'blk'), may hold values from -6 to 6
- cotangent: bfloat16 [8, 2048, 768], P('expert', 'blk'), may hold values from -6 to 6
- loss_mask: int32 [8, 2048], P('expert', 'blk'), may hold values 0 or 1
- routes: int32 [8, 2048, 1], P('expert', 'blk'), may hold values from 0 to 7, as said below
- priority: int32 [8, 4, 512], P('expert', 'blk'), may hold values from 0 to 511, each once within a row
- histogram: int32 [8], replicated, may hold values from 0 to 999
- qkv_weight: bfloat16 [768, 2304], replicated, may hold values from -0.21875 to 0.21875
- proj_weight: bfloat16 [768, 768], replicated, may hold values from -5 to 5
- attn_gain: float32 [768], replicated, may hold values from 0.5 to 1.5
- moe_gain: float32 [768], replicated, may hold values from 0.5 to 1.5
- route_weight: float32 [768, 16], replicated, may hold values from -0.21875 to 0.21875
- anchor_table: float32 [8, 16], replicated, may hold values from -6 to 6
- first_weight: bfloat16 [8, 768, 3072], P('expert'), may hold values from -0.21875 to 0.21875
- second_weight: bfloat16 [8, 3072, 768], P('expert'), may hold values from -3.59375 to 3.59375
Outputs:
- block_out: bfloat16 [8, 2048, 768], P('expert', 'blk')
- grad_tokens: float32 [8, 2048, 768], P('expert', 'blk')
- grad_qkv: float32 [768, 2304], replicated
- grad_proj: float32 [768, 768], replicated
- grad_attn_gain: float32 [768], replicated
- grad_moe_gain: float32 [768], replicated
- grad_route: float32 [768, 16], replicated
- grad_anchor: float32 [8, 16], replicated
- grad_first: float32 [8, 768, 3072], P('expert', None, 'blk')
- grad_second: float32 [8, 3072, 768], P('expert', 'blk')
- histogram_out: int32 [8], replicated
The draws below stay inside these ranges and needn't reach their ends.
Inputs may be any that keep to these rules, and one draw needn't show every extreme that they name: `priority`: within each block of 512 positions every value appears once. `routes`: every expert is named by some position.
All inputs are finite; a program needn't handle non-finite values. No bound on the sum of `loss_mask` on one device may be relied on, other than what follows from the above.
Results may differ from the reference program's by a relative error of at most 0.019.
Values may be sent and summed in bfloat16 or wider, within the bound.
A program may use at most 192 MiB of HBM per device.

```python
import jax
import jax.numpy as jnp
from jax import lax

D = 768
HEADS = 12
HEAD_DIM = 64
FF = 3072
RDIM = 16
TOK_DEV = 512
EXPERTS = 8
SEQS = 8
BLOCKS = 4
LEN = 2048
CAPACITY = 64


def draw_routes(key, part):
    key = jax.random.fold_in(key, 11)
    key_lower, key_upper, key_pick = jax.random.split(key, 3)
    shape = (SEQS, LEN, 1)
    half_experts = EXPERTS // 2
    lower_ids = jax.random.randint(key_lower, shape, 0, half_experts, dtype=jnp.int32)
    upper_ids = jax.random.randint(key_upper, shape, half_experts, EXPERTS, dtype=jnp.int32)
    pick_draw = jax.random.randint(key_pick, shape, 0, 2 * BLOCKS, dtype=jnp.int32)
    block_place = (jnp.arange(LEN, dtype=jnp.int32) // TOK_DEV)[None, :, None]
    threshold = 2 * (BLOCKS - block_place) - 1
    return jnp.where(pick_draw < threshold, lower_ids, upper_ids).astype(jnp.int32)


def set_ends(array, key, least, largest):
    longest = array.shape.index(max(array.shape))
    spots = []
    for shift in (0, 1):
        where = [jax.random.randint(jax.random.fold_in(key, axis), (), 0, length) for axis, length in enumerate(array.shape)]
        where[longest] = (where[longest] + shift) % array.shape[longest]
        spots.append(tuple(where))
    return array.at[spots[0]].set(least).at[spots[1]].set(largest)


def levels(rng, extent, shards, smallest, top_value):
    def one(axis_at, blocks):
        steps = jax.random.uniform(jax.random.fold_in(jax.random.fold_in(rng, 6), axis_at), (blocks,), jnp.float32, smallest / len(shards), top_value / len(shards))
        return jnp.repeat(jnp.exp(steps), extent[axis_at] // blocks).reshape((-1,) + (1,) * (len(extent) - axis_at - 1))

    factor_of = one(*shards[0])
    for cut in shards[1:]:
        factor_of = factor_of * one(*cut)
    return factor_of


def bell_draw(rng, shape, spread, most, cuts=(), kind=jnp.bfloat16):
    loudness = levels(rng, shape, cuts, -0.22, 0.18) if cuts else 1.0
    entries = jax.random.normal(rng, shape, jnp.float32) * spread * loudness
    return jnp.minimum(jnp.maximum(entries, -most), most).astype(kind)


def setup_inputs(seed: int = 0) -> dict:
    splits = jax.random.split(jax.random.key(seed), 15)
    return {
        "tokens": bell_draw(splits[0], (SEQS, LEN, D), 1.0, 6.0, ((0, 8), (1, 4))),
        "cotangent": bell_draw(splits[1], (SEQS, LEN, D), 1.0, 6.0, ((0, 8), (1, 4))),
        "loss_mask": set_ends((jax.random.randint(splits[2], (SEQS, LEN), 0, 20) < 17).astype(jnp.int32), jax.random.fold_in(splits[2], 1), 0, 1),
        "routes": draw_routes(jax.random.fold_in(splits[14], 71), 0),
        "priority": jax.vmap(lambda own: jax.random.permutation(own, TOK_DEV))(jax.random.split(splits[4], SEQS * BLOCKS)).reshape((SEQS, BLOCKS, TOK_DEV)).astype(jnp.int32),
        "histogram": set_ends(jax.random.randint(splits[5], (EXPERTS,), 0, 1000), jax.random.fold_in(splits[5], 1), 0, 999).astype(jnp.int32),
        "qkv_weight": bell_draw(splits[6], (D, 3 * D), D ** -0.5, 0.21875),
        "proj_weight": bell_draw(splits[7], (D, D), 0.8, 5.0),
        "attn_gain": jnp.clip(1.0 + 0.1 * jax.random.normal(splits[8], (D,), jnp.float32), 0.5, 1.5),
        "moe_gain": jnp.clip(1.0 + 0.1 * jax.random.normal(splits[9], (D,), jnp.float32), 0.5, 1.5),
        "route_weight": bell_draw(splits[10], (D, RDIM), D ** -0.5, 0.21875, (), jnp.float32),
        "anchor_table": bell_draw(splits[11], (EXPERTS, RDIM), 1.0, 6.0, (), jnp.float32),
        "first_weight": bell_draw(splits[12], (EXPERTS, D, FF), D ** -0.5, 0.21875, ((0, 8),)),
        "second_weight": bell_draw(splits[13], (EXPERTS, FF, D), 0.6, 3.59375, ((0, 8),)),
    }


@jax.custom_vjp
def lowered_input(v):
    return lax.optimization_barrier(v.astype(jnp.bfloat16)).astype(jnp.float32)

@jax.custom_vjp
def lowered_gradient(v):
    return v

def low_keep(v):
    return (lowered_input(v), None)

def low_pass(kept, grad):
    return (grad,)

def back_keep(v):
    return (v, None)

def back_low(kept, grad):
    return (lowered_input(grad),)
lowered_input.defvjp(low_keep, low_pass)
lowered_gradient.defvjp(back_keep, back_low)
TOP_PRECISION = lax.Precision.HIGHEST
EPSILON = 1e-05
ROUTER_SOFTNESS = 0.4
MASKED = -1e+30

def layer_norm(values, norm_gain):
    average = lax.optimization_barrier(jnp.mean(values, axis=-1, keepdims=True))
    centered = values - average
    variance = lax.optimization_barrier(jnp.mean(centered * centered, axis=-1, keepdims=True))
    return centered * lax.rsqrt(variance + EPSILON) * norm_gain

def unit_rows(matrix):
    return matrix * lax.rsqrt(1.0 + lax.optimization_barrier(jnp.sum(matrix * matrix, axis=-1, keepdims=True)))

def router_gate(normalized_rows, route_matrix, anchors, route_onehot):
    projection_output = unit_rows(jnp.dot(normalized_rows, route_matrix, precision=TOP_PRECISION))
    expert_anchor_rows = unit_rows(anchors)
    route_logit_scores = jnp.dot(projection_output, expert_anchor_rows.T, precision=TOP_PRECISION) / ROUTER_SOFTNESS
    return lax.optimization_barrier(jnp.sum(jax.nn.softmax(route_logit_scores, axis=-1) * route_onehot, axis=-1))

def attend_sequence(triple):
    queries, key_rows, value_rows = triple
    score_scale = HEAD_DIM ** (-0.5)
    key_place = jnp.arange(LEN, dtype=jnp.int32)

    def one_block(position):
        first_row = position * TOK_DEV
        block_rows = lax.dynamic_slice_in_dim(queries, first_row, TOK_DEV, 0)
        scores = lowered_gradient(jnp.einsum('qhd,khd->hqk', block_rows, key_rows, precision=TOP_PRECISION) * score_scale)
        query_place = first_row + jnp.arange(TOK_DEV, dtype=jnp.int32)
        allowed = key_place[None, :] <= query_place[:, None]
        scores = jnp.where(allowed[None], scores, MASKED)
        soft_rows = lowered_input(jax.nn.softmax(scores, axis=-1))
        return jnp.einsum('hqk,khd->qhd', soft_rows, value_rows, precision=TOP_PRECISION)
    pieces = lax.map(jax.checkpoint(one_block), jnp.arange(LEN // TOK_DEV, dtype=jnp.int32))
    return pieces.reshape(LEN, HEADS, HEAD_DIM)

def reference(tokens, cotangent, loss_mask, routes, priority, histogram, qkv_weight, proj_weight, attn_gain, moe_gain, route_weight, anchor_table, first_weight, second_weight):
    route_ids = routes[:, :, 0]
    expert_ids = jnp.arange(EXPERTS, dtype=jnp.int32)
    route_match = route_ids[:, :, None] == expert_ids
    route_onehot = route_match.astype(jnp.float32)
    counts = lax.optimization_barrier(jnp.sum(route_match.astype(jnp.int32), axis=(0, 1)))
    route_groups = route_ids.reshape(SEQS, BLOCKS, TOK_DEV)
    same_route = route_groups[:, :, :, None] == route_groups[:, :, None, :]
    earlier = priority[:, :, None, :] < priority[:, :, :, None]
    slot_ids = lax.optimization_barrier(jnp.sum((same_route & earlier).astype(jnp.int32), axis=3))
    kept_rows = (slot_ids < CAPACITY).astype(jnp.float32)
    block_ids = jnp.arange(BLOCKS, dtype=jnp.int32)[None, :, None]
    seq_ids = jnp.arange(SEQS, dtype=jnp.int32)[:, None, None]
    fetch_slot = jnp.minimum(slot_ids, CAPACITY - 1)

    def forward(block_input, query_key_value_weight, projection_weight, first_gain, second_gain, route_matrix, anchors, first_matrix, second_matrix):
        normalized_rows = layer_norm(block_input, first_gain)
        query_key_value_mix = lowered_input(lowered_gradient(jnp.einsum('mog,gh->moh', lowered_input(normalized_rows), query_key_value_weight, precision=TOP_PRECISION)))
        queries = query_key_value_mix[:, :, :D].reshape(SEQS, LEN, HEADS, HEAD_DIM)
        key_rows = query_key_value_mix[:, :, D:2 * D].reshape(SEQS, LEN, HEADS, HEAD_DIM)
        value_rows = query_key_value_mix[:, :, 2 * D:].reshape(SEQS, LEN, HEADS, HEAD_DIM)
        attention_result = lax.map(attend_sequence, (queries, key_rows, value_rows))
        attention_result = lowered_input(lowered_gradient(attention_result.reshape(SEQS, LEN, D)))
        residual_stream = block_input + lowered_gradient(jnp.einsum('mog,gh->moh', attention_result, projection_weight, precision=TOP_PRECISION))
        normed_moe = layer_norm(residual_stream, second_gain)
        gate_value = router_gate(normed_moe, route_matrix, anchors, route_onehot)
        sent_rows = lowered_input(lowered_gradient(normed_moe)).reshape(SEQS, BLOCKS, TOK_DEV, D)
        buffer = jnp.zeros((BLOCKS, EXPERTS, SEQS, CAPACITY, D), jnp.float32)
        buffer = buffer.at[block_ids, route_groups, seq_ids, slot_ids].add(sent_rows, mode='drop')
        hidden = lowered_gradient(jnp.einsum('bescd,edf->bescf', buffer, first_matrix, precision=TOP_PRECISION))
        act_rows = lowered_input(jax.nn.gelu(hidden))
        result = lowered_input(lowered_gradient(jnp.einsum('bescf,efd->bescd', act_rows, second_matrix, precision=TOP_PRECISION)))
        fetched = result[block_ids, route_groups, seq_ids, fetch_slot] * kept_rows[:, :, :, None]
        return residual_stream + gate_value[:, :, None] * fetched.reshape(SEQS, LEN, D)
    primals = (tokens.astype(jnp.float32), qkv_weight.astype(jnp.float32), proj_weight.astype(jnp.float32), attn_gain, moe_gain, route_weight, anchor_table, first_weight.astype(jnp.float32), second_weight.astype(jnp.float32))
    block_out, pullback = jax.vjp(forward, *primals)
    gradients = pullback(cotangent.astype(jnp.float32) * loss_mask.astype(jnp.float32)[:, :, None])
    return (block_out.astype(jnp.bfloat16), gradients[0], gradients[1], gradients[2], gradients[3], gradients[4], gradients[5], gradients[6], gradients[7], gradients[8], histogram + counts)
```

```python
import functools

import jax
import jax.numpy as jnp
from jax import lax
from jax.experimental import pallas as pl
from jax.experimental.pallas import tpu as pltpu
from jax.sharding import PartitionSpec as P

HEADS = 12
HEAD_DIM = 64


TOP_PRECISION = lax.Precision.HIGHEST
EPSILON = 1e-05
ROUTER_SOFTNESS = 0.4
MASKED = -1e30


def layer_norm(values, norm_gain):
    average = jnp.mean(values, axis=-1, keepdims=True)
    centered = values - average
    variance = jnp.mean(centered * centered, axis=-1, keepdims=True)
    return centered * lax.rsqrt(variance + EPSILON) * norm_gain


def unit_rows(matrix):
    return matrix * lax.rsqrt(1.0 + jnp.sum(matrix * matrix, axis=-1, keepdims=True))


def router_gate(normalized_rows, route_matrix, anchors, route_onehot):
    projection_output = unit_rows(jnp.dot(normalized_rows, route_matrix, precision=TOP_PRECISION))
    expert_anchor_rows = unit_rows(anchors)
    route_logit_scores = (
        jnp.dot(projection_output, expert_anchor_rows.T, precision=TOP_PRECISION) / ROUTER_SOFTNESS
    )
    return jnp.sum(jax.nn.softmax(route_logit_scores, axis=-1) * route_onehot, axis=-1)


def masked_scores(queries, key_rows, query_first, key_first, score_scale):
    scores = (
        jnp.einsum("qhd,khd->hqk", queries, key_rows, preferred_element_type=jnp.float32)
        * score_scale
    )
    grid_shape = (queries.shape[0], key_rows.shape[0])
    query_place = query_first + lax.broadcasted_iota(jnp.int32, grid_shape, 0)
    key_place = key_first + lax.broadcasted_iota(jnp.int32, grid_shape, 1)
    return (scores, (key_place <= query_place)[None])


def over_blocks(step_fn, carried, arrays, block_rows):
    row_total = arrays[0].shape[0]
    block_count = row_total // block_rows
    stacked = tuple(
        (member.reshape((block_count, block_rows) + member.shape[1:]) for member in arrays)
    )

    def scan_step(running, packed):
        position, blocks = packed
        return (step_fn(running, blocks, position * block_rows), None)

    result, unused = lax.scan(
        scan_step, carried, (jnp.arange(block_count, dtype=jnp.int32), stacked)
    )
    return result


def general_body(
    tokens,
    cotangent,
    loss_mask,
    routes,
    priority,
    histogram,
    qkv_weight,
    proj_weight,
    attn_gain,
    moe_gain,
    route_weight,
    anchor_table,
    first_weight,
    second_weight,
):
    tok_rows = tokens.shape[1]
    model_width = tokens.shape[2]
    score_scale = HEAD_DIM ** (-0.5)
    query_first = lax.axis_index("blk") * tok_rows
    local_experts = first_weight.shape[0]
    experts_all = local_experts * lax.axis_size("expert")
    capacity = tok_rows // experts_all
    head_shape = (tok_rows, HEADS, HEAD_DIM)
    seq_rows = tok_rows * lax.axis_size("blk")
    route_ids = routes[0, :, 0]
    route_onehot = (
        route_ids[:, None] == lax.broadcasted_iota(jnp.int32, (tok_rows, experts_all), 1)
    ).astype(jnp.float32)
    count_rows = jnp.sum(route_onehot, axis=0)
    total_counts = lax.psum(count_rows.astype(jnp.int32), ("blk", "expert"))
    block_input = tokens[0].astype(jnp.float32)
    normed_attn, attn_norm_back = jax.vjp(layer_norm, block_input, attn_gain)
    normed_low = normed_attn.astype(jnp.bfloat16)
    query_key_value_mix = jnp.dot(
        normed_low, qkv_weight, preferred_element_type=jnp.float32
    ).astype(jnp.bfloat16)
    query_flat = query_key_value_mix[:, :model_width]
    queries = query_flat.reshape(head_shape)
    key_local = query_key_value_mix[:, model_width : 2 * model_width]
    value_local = query_key_value_mix[:, 2 * model_width :]

    def forward_step(carried, blocks, key_first):
        running_top, running_sum, running_out = carried
        key_rows = blocks[0].reshape(blocks[0].shape[0], HEADS, HEAD_DIM)
        value_rows = blocks[1].reshape(blocks[1].shape[0], HEADS, HEAD_DIM)
        scores, allowed = masked_scores(queries, key_rows, query_first, key_first, score_scale)
        top_new = jnp.maximum(running_top, jnp.max(jnp.where(allowed, scores, MASKED), axis=2))
        weights = jnp.where(allowed, jnp.exp(scores - top_new[:, :, None]), 0.0)
        factor = jnp.exp(running_top - top_new)
        running_sum = running_sum * factor + jnp.sum(weights, axis=2)
        running_out = running_out * factor.T[:, :, None] + jnp.einsum(
            "hqk,khd->qhd",
            weights.astype(jnp.bfloat16),
            value_rows,
            preferred_element_type=jnp.float32,
        )
        return (top_new, running_sum, running_out)

    initial = (
        jnp.full((HEADS, tok_rows), MASKED, jnp.float32),
        jnp.zeros((HEADS, tok_rows), jnp.float32),
        jnp.zeros(head_shape, jnp.float32),
    )
    running_top, running_sum, running_out = over_blocks(
        forward_step,
        initial,
        (
            lax.all_gather(key_local, "blk", axis=0, tiled=True),
            lax.all_gather(value_local, "blk", axis=0, tiled=True),
        ),
        tok_rows,
    )
    attention_result = running_out / running_sum.T[:, :, None]
    log_total = running_top + jnp.log(running_sum)
    attended_low = attention_result.reshape(tok_rows, model_width).astype(jnp.bfloat16)
    residual_stream = block_input + jnp.dot(
        attended_low, proj_weight, preferred_element_type=jnp.float32
    )
    normed_moe, moe_norm_back = jax.vjp(layer_norm, residual_stream, moe_gain)

    def gate_of(normalized_rows, route_matrix, anchors):
        return router_gate(normalized_rows, route_matrix, anchors, route_onehot)

    gate_value, gate_back = jax.vjp(gate_of, normed_moe, route_weight, anchor_table)
    order_rows = priority[0, 0]
    same_route = route_ids[:, None] == route_ids[None, :]
    earlier = order_rows[None, :] < order_rows[:, None]
    slot_ids = jnp.sum((same_route & earlier).astype(jnp.int32), axis=1)
    target = jnp.where(slot_ids < capacity, route_ids * capacity + slot_ids, -1)
    selector = lax.broadcasted_iota(jnp.int32, (tok_rows, tok_rows), 0) == target[None, :]
    selector_low = selector.astype(jnp.bfloat16)
    outgoing = jnp.dot(
        selector_low, normed_moe.astype(jnp.bfloat16), preferred_element_type=jnp.float32
    )
    outgoing = outgoing.astype(jnp.bfloat16).reshape(experts_all, capacity, model_width)
    arrived = lax.all_to_all(outgoing, "expert", split_axis=0, concat_axis=0, tiled=True)
    sources = arrived.shape[0] // local_experts
    grouped = arrived.reshape(sources, local_experts, arrived.shape[1], arrived.shape[2])
    hidden = jnp.einsum("secd,edf->secf", grouped, first_weight, preferred_element_type=jnp.float32)
    act_low = jax.nn.gelu(hidden).astype(jnp.bfloat16)
    result = jnp.einsum(
        "secf,efd->secd", act_low, second_weight, preferred_element_type=jnp.float32
    )
    result = result.astype(jnp.bfloat16).reshape(arrived.shape)
    returned = lax.all_to_all(result, "expert", split_axis=0, concat_axis=0, tiled=True)
    returned, arrived = (returned, arrived)
    fetched = jnp.einsum(
        "st,sd->td",
        selector_low,
        returned.reshape(tok_rows, model_width),
        preferred_element_type=jnp.float32,
    )
    block_out = (residual_stream + gate_value[:, None] * fetched).astype(jnp.bfloat16)[None]
    grad_out = cotangent[0].astype(jnp.float32) * loss_mask[0].astype(jnp.float32)[:, None]
    grad_fetched = grad_out * gate_value[:, None]
    grad_gate = jnp.sum(grad_out * fetched, axis=1)
    grad_slots = jnp.dot(selector.astype(jnp.float32), grad_fetched, precision=TOP_PRECISION)
    grad_slots = grad_slots.astype(jnp.bfloat16).reshape(experts_all, capacity, model_width)
    grad_arrived = lax.all_to_all(grad_slots, "expert", split_axis=0, concat_axis=0, tiled=True)
    sources = grad_arrived.shape[0] // local_experts
    slot_shape = (sources, local_experts, capacity, model_width)
    grouped_in = arrived.reshape(slot_shape)
    grouped_grad = grad_arrived.reshape(slot_shape)
    hidden = jnp.einsum(
        "secd,edf->secf", grouped_in, first_weight, preferred_element_type=jnp.float32
    )
    act_low = jax.nn.gelu(hidden).astype(jnp.bfloat16)
    grad_second = jnp.einsum(
        "secf,secd->efd", act_low, grouped_grad, preferred_element_type=jnp.float32
    )
    grad_act = jnp.einsum(
        "secd,efd->secf", grouped_grad, second_weight, preferred_element_type=jnp.float32
    )
    unused, gelu_back = jax.vjp(jax.nn.gelu, hidden)
    grad_hidden = gelu_back(grad_act)[0].astype(jnp.bfloat16)
    grad_first = jnp.einsum(
        "secd,secf->edf", grouped_in, grad_hidden, preferred_element_type=jnp.float32
    )
    grad_sent = jnp.einsum(
        "secf,edf->secd", grad_hidden, first_weight, preferred_element_type=jnp.float32
    )
    grad_sent = grad_sent.astype(jnp.bfloat16).reshape(grad_arrived.shape)
    grad_returned = lax.all_to_all(grad_sent, "expert", split_axis=0, concat_axis=0, tiled=True)
    grad_first, grad_second = (
        lax.psum_scatter(
            grad_first.astype(jnp.bfloat16), "blk", scatter_dimension=2, tiled=True
        ).astype(jnp.float32),
        lax.psum_scatter(
            grad_second.astype(jnp.bfloat16), "blk", scatter_dimension=1, tiled=True
        ).astype(jnp.float32),
    )
    grad_moe_rows = jnp.einsum(
        "st,sd->td",
        selector_low,
        grad_returned.reshape(tok_rows, model_width),
        preferred_element_type=jnp.float32,
    )
    grad_router_rows, grad_route, grad_anchor = gate_back(grad_gate)
    grad_residual_norm, grad_moe_gain = moe_norm_back(grad_moe_rows + grad_router_rows)
    grad_residual = grad_out + grad_residual_norm
    grad_attn_low = grad_residual.astype(jnp.bfloat16)
    grad_proj = jnp.dot(attended_low.T, grad_attn_low, preferred_element_type=jnp.float32)
    grad_attended_flat = jnp.dot(
        grad_attn_low, proj_weight.T, preferred_element_type=jnp.float32
    ).astype(jnp.bfloat16)
    grad_attended = grad_attended_flat.reshape(head_shape)
    delta_rows = jnp.sum(grad_attended.astype(jnp.float32) * attention_result, axis=2).T
    key_all, value_all = (
        lax.all_gather(key_local, "blk", axis=0, tiled=True),
        lax.all_gather(value_local, "blk", axis=0, tiled=True),
    )
    block_count = seq_rows // tok_rows
    key_blocks = key_all.reshape(block_count, tok_rows, model_width)
    value_blocks = value_all.reshape(block_count, tok_rows, model_width)

    def key_block_step(running_grad, packed):
        position, key_block, value_block = packed
        key_rows = key_block.reshape(head_shape)
        value_rows = value_block.reshape(head_shape)
        scores, allowed = masked_scores(
            queries, key_rows, query_first, position * tok_rows, score_scale
        )
        soft_rows = jnp.where(allowed, jnp.exp(scores - log_total[:, :, None]), 0.0)
        grad_values = jnp.einsum(
            "hqk,qhd->khd",
            soft_rows.astype(jnp.bfloat16),
            grad_attended,
            preferred_element_type=jnp.float32,
        )
        grad_soft = jnp.einsum(
            "qhd,khd->hqk", grad_attended, value_rows, preferred_element_type=jnp.float32
        )
        grad_scores = (soft_rows * (grad_soft - delta_rows[:, :, None])).astype(jnp.bfloat16)
        grad_keys = score_scale * jnp.einsum(
            "hqk,qhd->khd", grad_scores, queries, preferred_element_type=jnp.float32
        )
        running_grad = running_grad + score_scale * jnp.einsum(
            "hqk,khd->qhd", grad_scores, key_rows, preferred_element_type=jnp.float32
        )
        term = jnp.concatenate(
            [grad_keys.reshape(tok_rows, model_width), grad_values.reshape(tok_rows, model_width)],
            axis=1,
        )
        return (running_grad, term)

    grad_queries, stacked_terms = lax.scan(
        key_block_step,
        jnp.zeros(head_shape, jnp.float32),
        (jnp.arange(block_count, dtype=jnp.int32), key_blocks, value_blocks),
    )
    all_terms = stacked_terms.reshape(seq_rows, 2 * model_width)
    key_value_grads = lax.psum_scatter(
        all_terms.astype(jnp.bfloat16), "blk", scatter_dimension=0, tiled=True
    ).astype(jnp.float32)
    grad_query_rows = grad_queries.reshape(tok_rows, model_width)
    grad_qkv_rows = jnp.concatenate([grad_query_rows, key_value_grads], axis=1).astype(jnp.bfloat16)
    grad_qkv = jnp.dot(normed_low.T, grad_qkv_rows, preferred_element_type=jnp.float32)
    grad_normed = jnp.dot(grad_qkv_rows, qkv_weight.T, preferred_element_type=jnp.float32)
    grad_source_norm, grad_attn_gain = attn_norm_back(grad_normed)
    grad_tokens = (grad_residual + grad_source_norm)[None]
    grad_qkv, grad_proj, grad_attn_gain, grad_moe_gain, grad_route, grad_anchor = lax.psum(
        (grad_qkv, grad_proj, grad_attn_gain, grad_moe_gain, grad_route, grad_anchor),
        ("blk", "expert"),
    )
    histogram_out = histogram + total_counts
    return (
        block_out,
        grad_tokens,
        grad_qkv,
        grad_proj,
        grad_attn_gain,
        grad_moe_gain,
        grad_route,
        grad_anchor,
        grad_first,
        grad_second,
        histogram_out,
    )


MESH = pl.DeviceIdType.MESH
F32 = jnp.float32
BF16 = jnp.bfloat16
VMEM_BYTES = 58 * 1024 * 1024


def dot(left, right, precision=None):
    return lax.dot_general(
        left, right, (((1,), (0,)), ((), ())), precision=precision, preferred_element_type=F32
    )


def dot_nt(left, right, precision=None):
    return lax.dot_general(
        left, right, (((1,), (1,)), ((), ())), precision=precision, preferred_element_type=F32
    )


def dot_tn(left, right, precision=None):
    return lax.dot_general(
        left, right, (((0,), (0,)), ((), ())), precision=precision, preferred_element_type=F32
    )


def rows_at(index, size):
    return pl.ds(pl.multiple_of(index * size, size), size)


def places():
    blk = lax.axis_index("blk")
    expert = lax.axis_index("expert")
    return blk, expert, blk + 1 - 2 * lax.rem(blk, 2), lax.rem(blk + 2, 4), 3 - blk


def greet(peers):
    barrier = pltpu.get_barrier_semaphore()
    for peer in peers:
        pl.semaphore_signal(barrier, inc=1, device_id=peer, device_id_type=MESH)
    return lambda: pl.semaphore_wait(barrier, len(peers))


def push(src, dst, sems, index, peer):
    copy = pltpu.make_async_remote_copy(
        src_ref=src,
        dst_ref=dst,
        send_sem=sems.at[0, index],
        recv_sem=sems.at[1, index],
        device_id=peer,
        device_id_type=MESH,
    )
    copy.start()
    return copy


def standardise(values):
    average = jnp.mean(values, axis=-1, keepdims=True)
    centered = values - average
    scale = lax.rsqrt(jnp.mean(centered * centered, axis=-1, keepdims=True) + EPSILON)
    return centered * scale, scale


def lower_triangle(keys, queries):
    return lax.broadcasted_iota(jnp.int32, (keys, queries), 0) <= lax.broadcasted_iota(
        jnp.int32, (keys, queries), 1
    )


class BlockGather:
    def __init__(self, buf, sems, base, rows):
        self.buf, self.sems, self.base, self.rows = buf, sems, base, rows

    def part(self, blk, half):
        size = self.rows // 2
        return self.buf.at[pl.ds(pl.multiple_of(blk * self.rows + half * size, size), size)]

    def send(self, blk, half, index, peer):
        ref = self.part(blk, half)
        return push(ref, ref, self.sems, self.base + index, peer)

    def start(self):
        blk, expert, bx, by, bd = places()
        self.copies = [
            self.send(blk, 0, 0, (bx, expert)),
            self.send(blk, 1, 1, (by, expert)),
            self.send(blk, 1, 2, (bx, expert)),
            self.send(blk, 0, 3, (by, expert)),
        ]

    def forward(self):
        blk, expert, bx, by, bd = places()
        self.copies[0].wait_recv()
        self.copies.append(self.send(bx, 0, 4, (by, expert)))
        self.copies[1].wait_recv()
        self.copies.append(self.send(by, 1, 5, (bx, expert)))

    def wait_neighbours(self):
        self.copies[2].wait_recv()
        self.copies[3].wait_recv()

    def wait_diagonal(self):
        self.copies[4].wait_recv()
        self.copies[5].wait_recv()

    def wait_sends(self):
        for copy in self.copies:
            copy.wait_send()


class ExpertExchange:
    def __init__(self, src, dst, sems, base, rows, dst_base):
        self.src, self.dst, self.sems, self.base, self.rows, self.dst_base = (
            src, dst, sems, base, rows, dst_base)

    def start(self):
        blk, expert = lax.axis_index("blk"), lax.axis_index("expert")
        n = lax.axis_size("expert")
        self.copies = []
        place = pl.ds(pl.multiple_of(self.dst_base + expert * self.rows, self.rows), self.rows)
        for shift in range(1, n):
            peer = lax.rem(expert + shift, n)
            self.copies.append(
                push(self.src.at[rows_at(peer, self.rows)], self.dst.at[place], self.sems,
                     self.base + shift - 1, (blk, peer))
            )
        self.dst[place] = self.src[rows_at(expert, self.rows)]

    def wait(self):
        for copy in self.copies:
            copy.wait_recv()
        for copy in self.copies:
            copy.wait_send()


def blk_peers():
    blk, expert, bx, by, bd = places()
    return [(bx, expert), (by, expert), (bd, expert)]


def expert_peers():
    blk, expert = lax.axis_index("blk"), lax.axis_index("expert")
    n = lax.axis_size("expert")
    return [(blk, lax.rem(expert + shift, n)) for shift in range(1, n)]


def attend_kernel(
    tok_ref, gain_ref, wqkv_ref, cot_ref, rows_ref, cols_ref,
    nall_ref, qkv_ref, out_ref, lse_ref, att_ref, target_row_ref, target_col_ref, cot_in_ref,
    w_s, wt_s, k_s, att_s, cot_s, w_sem, gather_sems, cot_sems, att_sems,
):
    blk, expert, bx, by, bd = places()
    tok = tok_ref.shape[0]
    width = tok_ref.shape[1]
    heads = HEADS // 4
    group = heads * HEAD_DIM
    arrived = greet(blk_peers() + expert_peers())
    odd = lax.rem(blk, 2)
    loads = []
    for part in range(3):
        first = pl.multiple_of(part * width + blk * group - odd * 64, 128)
        loads.append(
            pltpu.make_async_copy(wqkv_ref.at[:, pl.ds(first, 256)], w_s.at[part], w_sem.at[part])
        )
        loads[-1].start()
    xhat, _ = standardise(tok_ref[...].astype(F32))
    nall_ref[rows_at(blk, tok), :] = (xhat * gain_ref[...]).astype(BF16)
    arrived()
    gather = BlockGather(nall_ref, gather_sems, 0, tok)
    gather.start()

    capacity = tok // 8
    route_row, prio_row, mask_row = rows_ref[0:1, :], rows_ref[1:2, :], rows_ref[2:3, :]
    route_col, prio_col = cols_ref[:, 0:1], cols_ref[:, 1:2]
    same = route_col == route_row
    slot_row = jnp.sum(jnp.where(same & (prio_col < prio_row), 1.0, 0.0), axis=0, keepdims=True)
    slot_col = jnp.sum(jnp.where(same & (prio_row < prio_col), 1.0, 0.0), axis=1, keepdims=True)
    target_row = jnp.where(slot_row < capacity, route_row * capacity + slot_row, -1.0)
    target_col = jnp.where(slot_col < capacity, route_col * capacity + slot_col, -1.0)
    target_row_ref[...] = jnp.broadcast_to(target_row, target_row_ref.shape)
    target_col_ref[...] = jnp.broadcast_to(target_col, target_col_ref.shape)
    slots = lax.broadcasted_iota(jnp.int32, (tok, tok), 0).astype(F32)
    chosen = jnp.where((slots == target_row) & (mask_row > 0.0), 1.0, 0.0).astype(BF16)
    cot_s[...] = dot(chosen, cot_ref[...]).astype(BF16)
    cot_move = ExpertExchange(cot_s, cot_in_ref, cot_sems, 0, capacity, 0)
    cot_move.start()

    for part in range(3):
        loads[part].wait()
        wide = w_s[part]
        narrow = jnp.where(odd == 1, wide[:, 64:256], wide[:, 0:192])
        wt_s[part * group : (part + 1) * group, :] = narrow.T

    def project(where):
        cols = rows_at(where, tok)
        mixed = dot_nt(wt_s[...], nall_ref[cols, :]).astype(BF16)
        qkv_ref[0:group, cols] = mixed[0:group] * BF16(HEAD_DIM**-0.5)
        qkv_ref[group:, cols] = mixed[group:]
        for head in range(heads):
            k_s[head, cols, :] = mixed[group + head * 64 : group + (head + 1) * 64].T

    project(blk)
    gather.forward()
    gather.wait_neighbours()
    project(bx)
    project(by)
    gather.wait_diagonal()
    project(bd)

    half = tok // 2

    def scores(i, head):
        q = qkv_ref[head * 64 : (head + 1) * 64, i * tok : (i + 1) * tok]
        upper = dot(k_s[head, i * tok : i * tok + half, :], q)
        upper = jnp.where(lower_triangle(half, tok), upper, MASKED)
        lower = dot(k_s[head, i * tok + half : (i + 1) * tok, :], q[:, half:])
        lower = jnp.where(lower_triangle(half, half), lower, MASKED)
        top = jnp.max(upper, axis=0, keepdims=True)
        low_top = jnp.max(lower, axis=0, keepdims=True)
        top = jnp.concatenate([top[:, :half], jnp.maximum(top[:, half:], low_top)], axis=1)
        if i == 0:
            return top, upper, lower, None
        past = dot(k_s[head, 0 : i * tok, :], q)
        return jnp.maximum(top, jnp.max(past, axis=0, keepdims=True)), upper, lower, past

    sends = []

    def finish(i, head, found):
        top, upper, lower, past = found
        v = qkv_ref[2 * group + head * 64 : 2 * group + (head + 1) * 64, :]
        upper = jnp.exp(upper - top)
        lower = jnp.exp(lower - top[:, half:])
        total = jnp.sum(upper, axis=0, keepdims=True)
        low_total = jnp.sum(lower, axis=0, keepdims=True)
        total = jnp.concatenate([total[:, :half], total[:, half:] + low_total], axis=1)
        result = dot(v[:, i * tok : i * tok + half], upper.astype(BF16))
        low_result = dot(v[:, i * tok + half : (i + 1) * tok], lower.astype(BF16))
        result = jnp.concatenate([result[:, :half], result[:, half:] + low_result], axis=1)
        if i:
            past = jnp.exp(past - top)
            total = total + jnp.sum(past, axis=0, keepdims=True)
            result = result + dot(v[:, 0 : i * tok], past.astype(BF16))
        result = result / total
        place = slice(head * 64, (head + 1) * 64)
        out_ref[place, i * tok : (i + 1) * tok] = result
        lse_ref[head : head + 1, i * tok : (i + 1) * tok] = top + jnp.log(total)
        att_s[place, i * tok : (i + 1) * tok] = result.astype(BF16)
        there = pl.ds(pl.multiple_of(blk * group + head * 64, 64), 64)

        def copy():
            return pltpu.make_async_remote_copy(
                src_ref=att_s.at[place, i * tok : (i + 1) * tok],
                dst_ref=att_ref.at[there],
                send_sem=att_sems.at[0, i * heads + head],
                recv_sem=att_sems.at[1, blk * heads + head],
                device_id=(i, expert),
                device_id_type=MESH,
            )

        @pl.when(blk != i)
        def _():
            copy().start()

        @pl.when(blk == i)
        def _():
            att_ref[there, :] = result.astype(BF16)

        sends.append((i, copy))

    before = None
    for i in range(4):
        for head in range(heads):
            found = scores(i, head)
            if before is not None:
                finish(*before)
            before = (i, head, found)
    finish(*before)

    for i, copy in sends:
        @pl.when(blk != i)
        def _():
            copy().wait_send()

    for source in range(4):
        @pl.when(blk != source)
        def _():
            for head in range(heads):
                there = pl.ds(source * group + head * 64, 64)
                pltpu.make_async_remote_copy(
                    src_ref=att_s.at[0:64, 0:tok],
                    dst_ref=att_ref.at[there],
                    send_sem=att_sems.at[0, source * heads + head],
                    recv_sem=att_sems.at[1, source * heads + head],
                    device_id=(source, expert),
                    device_id_type=MESH,
                ).wait_recv()

    cot_move.wait()
    gather.wait_sends()


def gelu_pair(hidden):
    squared = hidden * hidden
    curve = jnp.tanh(0.7978845608028654 * hidden * (1.0 + 0.044715 * squared))
    half = 0.5 * (1.0 + curve)
    slope = half + 0.5 * hidden * (1.0 - curve * curve) * (
        0.7978845608028654 * (1.0 + 0.134145 * squared)
    )
    return hidden * half, slope


def spread(row, size):
    shape = (size, row.shape[1])
    eye = lax.broadcasted_iota(jnp.int32, shape, 0) == lax.broadcasted_iota(jnp.int32, shape, 1)
    return jnp.sum(jnp.where(eye, row, 0.0), axis=1, keepdims=True)


def flatten(column, width):
    shape = (column.shape[0], width)
    eye = lax.broadcasted_iota(jnp.int32, shape, 0) == lax.broadcasted_iota(jnp.int32, shape, 1)
    return jnp.sum(jnp.where(eye, column, 0.0), axis=0, keepdims=True)


def expert_kernel(
    att_ref, tok_ref, proj_ref, gain_ref, route_ref, anchor_ref, cols_ref, target_row_ref,
    target_col_ref, cot_ref, cot_in_ref, first_ref, second_ref,
    result_ref, residual_ref, gate_ref, grad_residual_ref, grad_att_ref, grad_proj_ref, small_ref,
    buf_ref, cots_ref, gates_ref,
    first_s, second_s, go_s, gate_s, grad_s, back_s, score_s, score_in_s, res_acc, sent_acc, grad_in_s,
    w_sem, go_sems, gate_sems, back_sems, score_sems, cots_sems, buf_sems, gates_sems,
):
    blk, expert, bx, by, bd = places()
    tok, width = tok_ref.shape
    experts = 8
    capacity = tok // experts
    here = rows_at(blk, tok)
    arrived = greet(blk_peers() + expert_peers())
    loads = [
        pltpu.make_async_copy(first_ref, first_s, w_sem.at[0]),
        pltpu.make_async_copy(second_ref, second_s, w_sem.at[1]),
    ]
    for load in loads:
        load.start()
    cots_ref[here, :] = cot_in_ref[...]

    residual = tok_ref[...].astype(F32) + dot_tn(att_ref[...], proj_ref[...])
    residual_ref[...] = residual
    xhat, scale = standardise(residual)
    normed = xhat * gain_ref[...]
    normed_low = normed.astype(BF16)
    target_row, target_col = target_row_ref[0:1, :], target_col_ref[:, 0:1]
    slots = lax.broadcasted_iota(jnp.int32, (tok, tok), 0).astype(F32)
    go_s[...] = dot(jnp.where(slots == target_row, 1.0, 0.0).astype(BF16), normed_low).astype(BF16)
    arrived()
    cots = BlockGather(cots_ref, cots_sems, 0, tok)
    cots.start()
    go = ExpertExchange(go_s, buf_ref, go_sems, 0, capacity, blk * tok)
    go.start()

    route_col = cols_ref[:, 0:1]
    projected = dot(normed, route_ref[...], TOP_PRECISION)
    unit_scale = lax.rsqrt(1.0 + jnp.sum(projected * projected, axis=1, keepdims=True))
    unit = projected * unit_scale
    anchor = anchor_ref[...]
    anchor_scale = lax.rsqrt(1.0 + jnp.sum(anchor * anchor, axis=1, keepdims=True))
    anchor_unit = anchor * anchor_scale
    logits = dot_nt(unit, anchor_unit, TOP_PRECISION) / ROUTER_SOFTNESS
    soft = jnp.exp(logits - jnp.max(logits, axis=1, keepdims=True))
    soft = soft / jnp.sum(soft, axis=1, keepdims=True)
    onehot = jnp.where(
        lax.broadcasted_iota(jnp.int32, (tok, experts), 1).astype(F32) == route_col, 1.0, 0.0
    )
    gate = jnp.sum(soft * onehot, axis=1, keepdims=True)
    gate_ref[...] = jnp.broadcast_to(gate, gate_ref.shape)
    lane = lax.broadcasted_iota(jnp.int32, (tok, 128), 1).astype(F32)
    lane = jnp.where(lane < capacity, lane, 1e6)
    for peer in range(experts):
        row = jnp.sum(
            jnp.where(target_col == peer * capacity + lane, gate, 0.0), axis=0, keepdims=True
        )
        gate_s[peer * 8 : (peer + 1) * 8, :] = jnp.broadcast_to(row, (8, 128))
    gates = ExpertExchange(gate_s, gates_ref, gate_sems, 0, 8, blk * 64)
    gates.start()

    cots.forward()
    go.wait()
    gates.wait()
    buf = BlockGather(buf_ref, buf_sems, 0, tok)
    buf.start()
    gates_here = gates_ref.at[rows_at(blk, 64)]
    gates_out = [
        push(gates_here, gates_here, gates_sems, n, peer) for n, peer in enumerate(blk_peers())
    ]
    cots.wait_neighbours()
    cots.wait_diagonal()
    buf.forward()

    for source in range(experts):
        chunk = slice(source * capacity, (source + 1) * capacity)
        rate = spread(gates_ref[pl.ds(blk * 64 + source * 8, 8), :][0:1, :], capacity)
        grad_in_s[chunk, :] = (cot_in_ref[chunk, :].astype(F32) * rate).astype(BF16)
    for load in loads:
        load.wait()
    tile = 768
    x = buf_ref[here, :]
    grad_in = grad_in_s[...]
    for t in range(first_s.shape[1] // tile):
        cut = slice(t * tile, (t + 1) * tile)
        hidden = dot(x, first_s[:, cut])
        act, slope = gelu_pair(hidden)
        part = dot(act.astype(BF16), second_s[cut, :])
        grad_hidden = (dot_nt(grad_in, second_s[cut, :]) * slope).astype(BF16)
        sent = dot_nt(grad_hidden, first_s[:, cut])
        if t == 0:
            res_acc[...] = part
            sent_acc[...] = sent
        else:
            res_acc[...] += part
            sent_acc[...] += sent
    grad_s[...] = sent_acc[...].astype(BF16)
    back = ExpertExchange(grad_s, back_s, back_sems, 0, capacity, 0)
    back.start()
    result = res_acc[...].astype(BF16)
    result_ref[...] = result
    score = jnp.sum(result.astype(F32) * cot_in_ref[...].astype(F32), axis=1, keepdims=True)
    for source in range(experts):
        row = flatten(score[source * capacity : (source + 1) * capacity], 128)
        score_s[source * 8 : (source + 1) * 8, :] = jnp.broadcast_to(row, (8, 128))
    scores = ExpertExchange(score_s, score_in_s, score_sems, 0, 8, 0)
    scores.start()
    grad_out = cot_ref[...].astype(F32) * cols_ref[:, 2:3]

    scores.wait()
    grad_gate = jnp.zeros((tok, 1), F32)
    for peer in range(experts):
        row = score_in_s[peer * 8 : peer * 8 + 1, :]
        grad_gate += jnp.sum(
            jnp.where(target_col == peer * capacity + lane, row, 0.0), axis=1, keepdims=True
        )
    grad_logits = grad_gate * gate * (onehot - soft) / ROUTER_SOFTNESS
    grad_unit = dot(grad_logits, anchor_unit, TOP_PRECISION)
    grad_projected = unit_scale * (
        grad_unit - unit * jnp.sum(unit * grad_unit, axis=1, keepdims=True)
    )
    grad_anchor_unit = dot_tn(grad_logits, unit, TOP_PRECISION)
    grad_anchor = anchor_scale * (
        grad_anchor_unit
        - anchor_unit * jnp.sum(anchor_unit * grad_anchor_unit, axis=1, keepdims=True)
    )
    rdim = route_ref.shape[1]
    small_ref[...] = jnp.zeros_like(small_ref)
    small_ref[0:rdim, :] = dot_tn(grad_projected, normed, TOP_PRECISION)
    small_ref[rdim : rdim + experts, 0:rdim] = grad_anchor
    counts = jnp.sum(onehot, axis=0, keepdims=True)
    small_ref[rdim + experts + 2 : rdim + experts + 3, 0:experts] = counts
    router_rows = dot_nt(grad_projected, route_ref[...], TOP_PRECISION)

    back.wait()
    lanes = lax.broadcasted_iota(jnp.int32, (tok, tok), 1).astype(F32)
    moe_rows = dot(jnp.where(lanes == target_col, 1.0, 0.0).astype(BF16), back_s[...])
    grad_normed = moe_rows + router_rows
    small_ref[rdim + experts : rdim + experts + 1, :] = jnp.sum(
        grad_normed * xhat, axis=0, keepdims=True
    )
    grad_xhat = grad_normed * gain_ref[...]
    grad_residual = grad_out + scale * (
        grad_xhat
        - jnp.mean(grad_xhat, axis=1, keepdims=True)
        - xhat * jnp.mean(grad_xhat * xhat, axis=1, keepdims=True)
    )
    grad_residual_ref[...] = grad_residual
    grad_low = grad_residual.astype(BF16)
    grad_att_ref[...] = dot_nt(proj_ref[...], grad_low).astype(BF16)
    grad_proj_ref[...] = dot(att_ref[...], grad_low)

    buf.wait_neighbours()
    buf.wait_diagonal()
    cots.wait_sends()
    buf.wait_sends()
    for copy in gates_out:
        copy.wait()


def expert_weights_kernel(
    buf_ref, cots_ref, gates_ref, first_ref, second_ref, grad_first_ref, grad_second_ref,
    first_t, acc,
):
    slots, width = buf_ref.shape
    first_t[...] = first_ref[...].T
    step = 512
    for t in range(slots // step):
        cut = slice(t * step, (t + 1) * step)
        rates = [spread(gates_ref[t * 64 + s * 8 : t * 64 + s * 8 + 1, :], 64) for s in range(8)]
        rate = jnp.concatenate(rates, axis=0)
        x = buf_ref[cut, :]
        grad_in = (cots_ref[cut, :].astype(F32) * rate).astype(BF16)
        act, slope = gelu_pair(dot_nt(first_t[...], x))
        grad_hidden = (dot_nt(second_ref[...], grad_in) * slope).astype(BF16)
        grad_second = dot(act.astype(BF16), grad_in)
        grad_first = dot(grad_hidden, x)
        if t == 0:
            grad_second_ref[...] = grad_second
            acc[...] = grad_first
        else:
            grad_second_ref[...] += grad_second
            acc[...] += grad_first
    grad_first_ref[...] = acc[...].T


def attend_back_kernel(
    grad_att_ref, qkv_ref, out_ref, lse_ref, nall_ref, result_ref, residual_ref, gate_ref,
    target_col_ref, gain_ref, wqkv_ref,
    block_out_ref, dqkv_home_ref, grad_group_ref, attn_gain_ref,
    do_t, dq_s, dqkv_s, q_s, k_s, v_s, do_s, back_s, w_s, wt_s,
    w_sem, att_sems, back_sems, home_sems,
):
    blk, expert, bx, by, bd = places()
    tok = grad_att_ref.shape[1]
    width = grad_att_ref.shape[0]
    heads = HEADS // 4
    group = heads * HEAD_DIM
    here = rows_at(blk, tok)
    length = qkv_ref.shape[1]
    arrived = greet(blk_peers() + expert_peers())
    odd = lax.rem(blk, 2)
    loads = []
    for part in range(3):
        first = pl.multiple_of(part * width + blk * group - odd * 64, 128)
        loads.append(
            pltpu.make_async_copy(wqkv_ref.at[:, pl.ds(first, 256)], w_s.at[part], w_sem.at[part])
        )
        loads[-1].start()
    arrived()
    mine = rows_at(blk, group)
    att_copies = [
        push(grad_att_ref.at[rows_at(peer[0], group)], do_t.at[:, here], att_sems, n, peer)
        for n, peer in enumerate(blk_peers())
    ]
    back = ExpertExchange(result_ref, back_s, back_sems, 0, tok // 8, 0)
    back.start()
    do_t[:, here] = grad_att_ref[mine, :]
    for head in range(heads):
        cut = slice(head * 64, (head + 1) * 64)
        q_s[head] = qkv_ref[cut, :].T
        k_s[head] = qkv_ref[group + head * 64 : group + (head + 1) * 64, :].T
        v_s[head] = qkv_ref[2 * group + head * 64 : 2 * group + (head + 1) * 64, :].T
    for part in range(3):
        loads[part].wait()
        wide = w_s[part]
        narrow = jnp.where(odd == 1, wide[:, 64:256], wide[:, 0:192])
        wt_s[part * group : (part + 1) * group, :] = narrow.T
    for copy in att_copies:
        copy.wait_recv()
    for head in range(heads):
        do_s[head] = do_t[head * 64 : (head + 1) * 64, :].T

    home = []
    for head in range(heads):
        cut = slice(head * 64, (head + 1) * 64)
        kt_cut = slice(group + head * 64, group + (head + 1) * 64)
        vt_cut = slice(2 * group + head * 64, 2 * group + (head + 1) * 64)
        delta = jnp.sum(out_ref[cut, :] * do_t[cut, :].astype(F32), axis=0, keepdims=True)
        for j in range(4):
            keys = slice(j * tok, (j + 1) * tok)
            queries = slice(j * tok, length)
            s = dot(k_s[head, keys, :], qkv_ref[cut, queries])
            p = jnp.exp(s - lse_ref[head : head + 1, queries])
            allowed = lower_triangle(tok, length - j * tok)
            p = jnp.where(allowed, p, 0.0)
            dp = dot(v_s[head, keys, :], do_t[cut, queries])
            ds = (p * (dp - delta[:, queries])).astype(BF16)
            dv = dot(p.astype(BF16), do_s[head, queries, :])
            dk = dot(ds, q_s[head, queries, :])
            dqkv_s[kt_cut, keys] = dk.T.astype(BF16)
            dqkv_s[vt_cut, keys] = dv.T.astype(BF16)
            dq = dot(qkv_ref[kt_cut, keys], ds)
            if j == 0:
                dq_s[...] = dq
            else:
                dq_s[:, queries] += dq
        dqkv_s[cut, :] = (dq_s[...] * HEAD_DIM**-0.5).astype(BF16)
        for n, peer in enumerate(blk_peers()):
            for part in range(3):
                src = dqkv_s.at[part * group + head * 64 : part * group + (head + 1) * 64,
                                rows_at(peer[0], tok)]
                there = pl.ds(pl.multiple_of(part * width + blk * group + head * 64, 64), 64)
                home.append(
                    push(src, dqkv_home_ref.at[there], home_sems, (n * heads + head) * 3 + part, peer)
                )
        for part in range(3):
            there = pl.ds(pl.multiple_of(part * width + blk * group + head * 64, 64), 64)
            dqkv_home_ref[there, :] = dqkv_s[
                part * group + head * 64 : part * group + (head + 1) * 64, here]

    grad_group = dot(dqkv_s[...], nall_ref[...])
    grad_group_ref[...] = grad_group
    attn_gain = jnp.sum(grad_group * wt_s[...].astype(F32), axis=0, keepdims=True) / gain_ref[...]
    attn_gain_ref[...] = jnp.broadcast_to(attn_gain, attn_gain_ref.shape)

    back.wait()
    lanes = lax.broadcasted_iota(jnp.int32, (tok, tok), 1).astype(F32)
    chosen = jnp.where(lanes == target_col_ref[:, 0:1], 1.0, 0.0).astype(BF16)
    fetched = dot(chosen, back_s[...])
    block_out_ref[...] = (residual_ref[...] + gate_ref[:, 0:1] * fetched).astype(BF16)
    for copy in att_copies:
        copy.wait_send()
    for copy in home:
        copy.wait_send()
    for copy in home:
        copy.wait_recv()


def tokens_kernel(dqkv_ref, wqkv_ref, tok_ref, gain_ref, grad_residual_ref, out_ref):
    xhat, scale = standardise(tok_ref[...].astype(F32))
    grad_normed = dot(wqkv_ref[...], dqkv_ref[...]).T
    grad_xhat = grad_normed * gain_ref[...]
    out_ref[...] = grad_residual_ref[...] + scale * (
        grad_xhat
        - jnp.mean(grad_xhat, axis=1, keepdims=True)
        - xhat * jnp.mean(grad_xhat * xhat, axis=1, keepdims=True)
    )


def call(kernel, name, args, outs, scratch, in_any=(), collective=None):
    specs = [
        pl.BlockSpec(memory_space=pl.ANY if n in in_any else pltpu.VMEM) for n in range(len(args))
    ]
    shapes = tuple(jax.ShapeDtypeStruct(shape, dtype) for shape, dtype in outs)
    return pl.pallas_call(
        kernel,
        out_shape=shapes,
        in_specs=specs,
        out_specs=tuple(pl.BlockSpec(memory_space=pltpu.VMEM) for _ in outs),
        scratch_shapes=scratch,
        name=name,
        compiler_params=pltpu.CompilerParams(
            vmem_limit_bytes=VMEM_BYTES,
            collective_id=collective,
            has_side_effects=collective is not None,
        ),
    )(*args)


def fast_body(
    tokens, cotangent, loss_mask, routes, priority, histogram, qkv_weight, proj_weight, attn_gain,
    moe_gain, route_weight, anchor_table, first_weight, second_weight,
):
    tok, width = tokens.shape[1:]
    blocks, experts = lax.axis_size("blk"), lax.axis_size("expert")
    length = tok * blocks
    heads = HEADS // blocks
    group = heads * HEAD_DIM
    hidden = first_weight.shape[2]
    x, cot = tokens[0], cotangent[0]
    rows = jnp.stack([routes[0, :, 0], priority[0, 0], loss_mask[0]]).astype(F32)
    rows = jnp.pad(rows, ((0, 5), (0, 0)))
    cols = rows.T
    gain1, gain2 = attn_gain[None], moe_gain[None]
    dma = pltpu.SemaphoreType.DMA
    nall, qkv, out, lse, att, target_row, target_col, cot_in = call(
        attend_kernel, "attend", (x, gain1, qkv_weight, cot, rows, cols),
        [((length, width), BF16), ((3 * group, length), BF16), ((group, length), F32),
         ((8, length), F32), ((width, tok), BF16), ((8, tok), F32), ((tok, 128), F32),
         ((tok, width), BF16)],
        [pltpu.VMEM((3, width, 256), BF16), pltpu.VMEM((3 * group, width), BF16),
         pltpu.VMEM((heads, length, HEAD_DIM), BF16), pltpu.VMEM((group, length), BF16),
         pltpu.VMEM((tok, width), BF16), dma((3,)), dma((2, 6)), dma((2, experts)),
         dma((2, blocks * heads))],
        in_any=(2,), collective=1,
    )
    (result, residual, gate, grad_residual, grad_att, grad_proj, small, buf, cots, gates) = call(
        expert_kernel, "expert",
        (att, x, proj_weight, gain2, route_weight, anchor_table, cols, target_row, target_col, cot,
         cot_in, first_weight[0], second_weight[0]),
        [((tok, width), BF16), ((tok, width), F32), ((tok, 128), F32), ((tok, width), F32),
         ((width, tok), BF16), ((width, width), F32), ((32, width), F32),
         ((length, width), BF16), ((length, width), BF16), ((blocks * 64, 128), F32)],
        [pltpu.VMEM((width, hidden), BF16), pltpu.VMEM((hidden, width), BF16),
         pltpu.VMEM((tok, width), BF16), pltpu.VMEM((64, 128), F32), pltpu.VMEM((tok, width), BF16),
         pltpu.VMEM((tok, width), BF16), pltpu.VMEM((64, 128), F32), pltpu.VMEM((64, 128), F32),
         pltpu.VMEM((tok, width), F32), pltpu.VMEM((tok, width), F32), pltpu.VMEM((tok, width), BF16),
         dma((2,)), dma((2, experts)), dma((2, experts)), dma((2, experts)), dma((2, experts)),
         dma((2, 6)), dma((2, 6)), dma((2, 3))],
        in_any=(11, 12), collective=2,
    )
    place = lax.axis_index("blk")
    quarter = hidden // blocks
    first_part = lax.dynamic_slice_in_dim(first_weight[0], place * quarter, quarter, 1)
    second_part = lax.dynamic_slice_in_dim(second_weight[0], place * quarter, quarter, 0)
    grad_first, grad_second = call(
        expert_weights_kernel, "expert_weights", (buf, cots, gates, first_part, second_part),
        [((width, quarter), F32), ((quarter, width), F32)],
        [pltpu.VMEM((quarter, width), BF16), pltpu.VMEM((quarter, width), F32)],
    )
    block_out, dqkv, grad_group, attn_row = call(
        attend_back_kernel, "attend_back",
        (grad_att, qkv, out, lse, nall, result, residual, gate, target_col, gain1, qkv_weight),
        [((tok, width), BF16), ((3 * width, tok), BF16), ((3 * group, width), F32), ((8, width), F32)],
        [pltpu.VMEM((group, length), BF16), pltpu.VMEM((HEAD_DIM, length), F32),
         pltpu.VMEM((3 * group, length), BF16)]
        + [pltpu.VMEM((heads, length, HEAD_DIM), BF16)] * 4
        + [pltpu.VMEM((tok, width), BF16), pltpu.VMEM((3, width, 256), BF16),
           pltpu.VMEM((3 * group, width), BF16),
           dma((3,)), dma((2, 3)), dma((2, experts)), dma((2, 27))],
        in_any=(10,), collective=3,
    )
    (grad_tokens,) = call(
        tokens_kernel, "tokens", (dqkv, qkv_weight, x, gain1, grad_residual),
        [((tok, width), F32)], [],
    )
    small = small.at[route_weight.shape[1] + experts + 1].set(attn_row[0])
    small = lax.psum(small, ("blk", "expert"))
    grad_proj = lax.psum(grad_proj.astype(BF16), ("blk", "expert")).astype(F32)
    grad_group = lax.psum(grad_group.astype(BF16), "expert")
    gathered = lax.all_gather(grad_group, "blk", axis=0)
    grad_qkv = gathered.reshape(blocks, 3, group, width).transpose(3, 1, 0, 2)
    grad_qkv = grad_qkv.reshape(width, 3 * width).astype(F32)
    rdim = route_weight.shape[1]
    return (
        block_out[None],
        grad_tokens[None],
        grad_qkv,
        grad_proj,
        small[rdim + experts + 1],
        small[rdim + experts],
        small[:rdim].T,
        small[rdim : rdim + experts, :rdim],
        grad_first[None],
        grad_second[None],
        histogram + small[rdim + experts + 2, :experts].astype(jnp.int32),
    )


def solution(mesh):
    in_specs = (
        P("expert", "blk", None),
        P("expert", "blk", None),
        P("expert", "blk"),
        P("expert", "blk", None),
        P("expert", "blk", None),
        P(),
        P(),
        P(),
        P(),
        P(),
        P(),
        P(),
        P("expert", None, None),
        P("expert", None, None),
    )
    out_specs = (
        P("expert", "blk", None),
        P("expert", "blk", None),
        P(),
        P(),
        P(),
        P(),
        P(),
        P(),
        P("expert", None, "blk"),
        P("expert", "blk", None),
        P(),
    )
    blocks, experts = mesh.shape["blk"], mesh.shape["expert"]
    body = fast_body if (blocks, experts) == (4, 8) else general_body
    return jax.shard_map(body, mesh=mesh, in_specs=in_specs, out_specs=out_specs, check_vma=False)
```

```python
import functools

import jax
import jax.numpy as jnp
from jax import lax
from jax.experimental import pallas as pl
from jax.experimental.pallas import tpu as pltpu
from jax.sharding import PartitionSpec as P

HEADS = 12
HEAD_DIM = 64


TOP_PRECISION = lax.Precision.HIGHEST
EPSILON = 1e-05
ROUTER_SOFTNESS = 0.4
MASKED = -1e30


def layer_norm(values, norm_gain):
    average = jnp.mean(values, axis=-1, keepdims=True)
    centered = values - average
    variance = jnp.mean(centered * centered, axis=-1, keepdims=True)
    return centered * lax.rsqrt(variance + EPSILON) * norm_gain


def unit_rows(matrix):
    return matrix * lax.rsqrt(1.0 + jnp.sum(matrix * matrix, axis=-1, keepdims=True))


def router_gate(normalized_rows, route_matrix, anchors, route_onehot):
    projection_output = unit_rows(jnp.dot(normalized_rows, route_matrix, precision=TOP_PRECISION))
    expert_anchor_rows = unit_rows(anchors)
    route_logit_scores = (
        jnp.dot(projection_output, expert_anchor_rows.T, precision=TOP_PRECISION) / ROUTER_SOFTNESS
    )
    return jnp.sum(jax.nn.softmax(route_logit_scores, axis=-1) * route_onehot, axis=-1)


def masked_scores(queries, key_rows, query_first, key_first, score_scale):
    scores = (
        jnp.einsum("qhd,khd->hqk", queries, key_rows, preferred_element_type=jnp.float32)
        * score_scale
    )
    grid_shape = (queries.shape[0], key_rows.shape[0])
    query_place = query_first + lax.broadcasted_iota(jnp.int32, grid_shape, 0)
    key_place = key_first + lax.broadcasted_iota(jnp.int32, grid_shape, 1)
    return (scores, (key_place <= query_place)[None])


def over_blocks(step_fn, carried, arrays, block_rows):
    row_total = arrays[0].shape[0]
    block_count = row_total // block_rows
    stacked = tuple(
        (member.reshape((block_count, block_rows) + member.shape[1:]) for member in arrays)
    )

    def scan_step(running, packed):
        position, blocks = packed
        return (step_fn(running, blocks, position * block_rows), None)

    result, unused = lax.scan(
        scan_step, carried, (jnp.arange(block_count, dtype=jnp.int32), stacked)
    )
    return result


def general_body(
    tokens,
    cotangent,
    loss_mask,
    routes,
    priority,
    histogram,
    qkv_weight,
    proj_weight,
    attn_gain,
    moe_gain,
    route_weight,
    anchor_table,
    first_weight,
    second_weight,
):
    tok_rows = tokens.shape[1]
    model_width = tokens.shape[2]
    score_scale = HEAD_DIM ** (-0.5)
    query_first = lax.axis_index("blk") * tok_rows
    local_experts = first_weight.shape[0]
    experts_all = local_experts * lax.axis_size("expert")
    capacity = tok_rows // experts_all
    head_shape = (tok_rows, HEADS, HEAD_DIM)
    seq_rows = tok_rows * lax.axis_size("blk")
    route_ids = routes[0, :, 0]
    route_onehot = (
        route_ids[:, None] == lax.broadcasted_iota(jnp.int32, (tok_rows, experts_all), 1)
    ).astype(jnp.float32)
    count_rows = jnp.sum(route_onehot, axis=0)
    total_counts = lax.psum(count_rows.astype(jnp.int32), ("blk", "expert"))
    block_input = tokens[0].astype(jnp.float32)
    normed_attn, attn_norm_back = jax.vjp(layer_norm, block_input, attn_gain)
    normed_low = normed_attn.astype(jnp.bfloat16)
    query_key_value_mix = jnp.dot(
        normed_low, qkv_weight, preferred_element_type=jnp.float32
    ).astype(jnp.bfloat16)
    query_flat = query_key_value_mix[:, :model_width]
    queries = query_flat.reshape(head_shape)
    key_local = query_key_value_mix[:, model_width : 2 * model_width]
    value_local = query_key_value_mix[:, 2 * model_width :]

    def forward_step(carried, blocks, key_first):
        running_top, running_sum, running_out = carried
        key_rows = blocks[0].reshape(blocks[0].shape[0], HEADS, HEAD_DIM)
        value_rows = blocks[1].reshape(blocks[1].shape[0], HEADS, HEAD_DIM)
        scores, allowed = masked_scores(queries, key_rows, query_first, key_first, score_scale)
        top_new = jnp.maximum(running_top, jnp.max(jnp.where(allowed, scores, MASKED), axis=2))
        weights = jnp.where(allowed, jnp.exp(scores - top_new[:, :, None]), 0.0)
        factor = jnp.exp(running_top - top_new)
        running_sum = running_sum * factor + jnp.sum(weights, axis=2)
        running_out = running_out * factor.T[:, :, None] + jnp.einsum(
            "hqk,khd->qhd",
            weights.astype(jnp.bfloat16),
            value_rows,
            preferred_element_type=jnp.float32,
        )
        return (top_new, running_sum, running_out)

    initial = (
        jnp.full((HEADS, tok_rows), MASKED, jnp.float32),
        jnp.zeros((HEADS, tok_rows), jnp.float32),
        jnp.zeros(head_shape, jnp.float32),
    )
    running_top, running_sum, running_out = over_blocks(
        forward_step,
        initial,
        (
            lax.all_gather(key_local, "blk", axis=0, tiled=True),
            lax.all_gather(value_local, "blk", axis=0, tiled=True),
        ),
        tok_rows,
    )
    attention_result = running_out / running_sum.T[:, :, None]
    log_total = running_top + jnp.log(running_sum)
    attended_low = attention_result.reshape(tok_rows, model_width).astype(jnp.bfloat16)
    residual_stream = block_input + jnp.dot(
        attended_low, proj_weight, preferred_element_type=jnp.float32
    )
    normed_moe, moe_norm_back = jax.vjp(layer_norm, residual_stream, moe_gain)

    def gate_of(normalized_rows, route_matrix, anchors):
        return router_gate(normalized_rows, route_matrix, anchors, route_onehot)

    gate_value, gate_back = jax.vjp(gate_of, normed_moe, route_weight, anchor_table)
    order_rows = priority[0, 0]
    same_route = route_ids[:, None] == route_ids[None, :]
    earlier = order_rows[None, :] < order_rows[:, None]
    slot_ids = jnp.sum((same_route & earlier).astype(jnp.int32), axis=1)
    target = jnp.where(slot_ids < capacity, route_ids * capacity + slot_ids, -1)
    selector = lax.broadcasted_iota(jnp.int32, (tok_rows, tok_rows), 0) == target[None, :]
    selector_low = selector.astype(jnp.bfloat16)
    outgoing = jnp.dot(
        selector_low, normed_moe.astype(jnp.bfloat16), preferred_element_type=jnp.float32
    )
    outgoing = outgoing.astype(jnp.bfloat16).reshape(experts_all, capacity, model_width)
    arrived = lax.all_to_all(outgoing, "expert", split_axis=0, concat_axis=0, tiled=True)
    sources = arrived.shape[0] // local_experts
    grouped = arrived.reshape(sources, local_experts, arrived.shape[1], arrived.shape[2])
    hidden = jnp.einsum("secd,edf->secf", grouped, first_weight, preferred_element_type=jnp.float32)
    act_low = jax.nn.gelu(hidden).astype(jnp.bfloat16)
    result = jnp.einsum(
        "secf,efd->secd", act_low, second_weight, preferred_element_type=jnp.float32
    )
    result = result.astype(jnp.bfloat16).reshape(arrived.shape)
    returned = lax.all_to_all(result, "expert", split_axis=0, concat_axis=0, tiled=True)
    returned, arrived = (returned, arrived)
    fetched = jnp.einsum(
        "st,sd->td",
        selector_low,
        returned.reshape(tok_rows, model_width),
        preferred_element_type=jnp.float32,
    )
    block_out = (residual_stream + gate_value[:, None] * fetched).astype(jnp.bfloat16)[None]
    grad_out = cotangent[0].astype(jnp.float32) * loss_mask[0].astype(jnp.float32)[:, None]
    grad_fetched = grad_out * gate_value[:, None]
    grad_gate = jnp.sum(grad_out * fetched, axis=1)
    grad_slots = jnp.dot(selector.astype(jnp.float32), grad_fetched, precision=TOP_PRECISION)
    grad_slots = grad_slots.astype(jnp.bfloat16).reshape(experts_all, capacity, model_width)
    grad_arrived = lax.all_to_all(grad_slots, "expert", split_axis=0, concat_axis=0, tiled=True)
    sources = grad_arrived.shape[0] // local_experts
    slot_shape = (sources, local_experts, capacity, model_width)
    grouped_in = arrived.reshape(slot_shape)
    grouped_grad = grad_arrived.reshape(slot_shape)
    hidden = jnp.einsum(
        "secd,edf->secf", grouped_in, first_weight, preferred_element_type=jnp.float32
    )
    act_low = jax.nn.gelu(hidden).astype(jnp.bfloat16)
    grad_second = jnp.einsum(
        "secf,secd->efd", act_low, grouped_grad, preferred_element_type=jnp.float32
    )
    grad_act = jnp.einsum(
        "secd,efd->secf", grouped_grad, second_weight, preferred_element_type=jnp.float32
    )
    unused, gelu_back = jax.vjp(jax.nn.gelu, hidden)
    grad_hidden = gelu_back(grad_act)[0].astype(jnp.bfloat16)
    grad_first = jnp.einsum(
        "secd,secf->edf", grouped_in, grad_hidden, preferred_element_type=jnp.float32
    )
    grad_sent = jnp.einsum(
        "secf,edf->secd", grad_hidden, first_weight, preferred_element_type=jnp.float32
    )
    grad_sent = grad_sent.astype(jnp.bfloat16).reshape(grad_arrived.shape)
    grad_returned = lax.all_to_all(grad_sent, "expert", split_axis=0, concat_axis=0, tiled=True)
    grad_first, grad_second = (
        lax.psum_scatter(
            grad_first.astype(jnp.bfloat16), "blk", scatter_dimension=2, tiled=True
        ).astype(jnp.float32),
        lax.psum_scatter(
            grad_second.astype(jnp.bfloat16), "blk", scatter_dimension=1, tiled=True
        ).astype(jnp.float32),
    )
    grad_moe_rows = jnp.einsum(
        "st,sd->td",
        selector_low,
        grad_returned.reshape(tok_rows, model_width),
        preferred_element_type=jnp.float32,
    )
    grad_router_rows, grad_route, grad_anchor = gate_back(grad_gate)
    grad_residual_norm, grad_moe_gain = moe_norm_back(grad_moe_rows + grad_router_rows)
    grad_residual = grad_out + grad_residual_norm
    grad_attn_low = grad_residual.astype(jnp.bfloat16)
    grad_proj = jnp.dot(attended_low.T, grad_attn_low, preferred_element_type=jnp.float32)
    grad_attended_flat = jnp.dot(
        grad_attn_low, proj_weight.T, preferred_element_type=jnp.float32
    ).astype(jnp.bfloat16)
    grad_attended = grad_attended_flat.reshape(head_shape)
    delta_rows = jnp.sum(grad_attended.astype(jnp.float32) * attention_result, axis=2).T
    key_all, value_all = (
        lax.all_gather(key_local, "blk", axis=0, tiled=True),
        lax.all_gather(value_local, "blk", axis=0, tiled=True),
    )
    block_count = seq_rows // tok_rows
    key_blocks = key_all.reshape(block_count, tok_rows, model_width)
    value_blocks = value_all.reshape(block_count, tok_rows, model_width)

    def key_block_step(running_grad, packed):
        position, key_block, value_block = packed
        key_rows = key_block.reshape(head_shape)
        value_rows = value_block.reshape(head_shape)
        scores, allowed = masked_scores(
            queries, key_rows, query_first, position * tok_rows, score_scale
        )
        soft_rows = jnp.where(allowed, jnp.exp(scores - log_total[:, :, None]), 0.0)
        grad_values = jnp.einsum(
            "hqk,qhd->khd",
            soft_rows.astype(jnp.bfloat16),
            grad_attended,
            preferred_element_type=jnp.float32,
        )
        grad_soft = jnp.einsum(
            "qhd,khd->hqk", grad_attended, value_rows, preferred_element_type=jnp.float32
        )
        grad_scores = (soft_rows * (grad_soft - delta_rows[:, :, None])).astype(jnp.bfloat16)
        grad_keys = score_scale * jnp.einsum(
            "hqk,qhd->khd", grad_scores, queries, preferred_element_type=jnp.float32
        )
        running_grad = running_grad + score_scale * jnp.einsum(
            "hqk,khd->qhd", grad_scores, key_rows, preferred_element_type=jnp.float32
        )
        term = jnp.concatenate(
            [grad_keys.reshape(tok_rows, model_width), grad_values.reshape(tok_rows, model_width)],
            axis=1,
        )
        return (running_grad, term)

    grad_queries, stacked_terms = lax.scan(
        key_block_step,
        jnp.zeros(head_shape, jnp.float32),
        (jnp.arange(block_count, dtype=jnp.int32), key_blocks, value_blocks),
    )
    all_terms = stacked_terms.reshape(seq_rows, 2 * model_width)
    key_value_grads = lax.psum_scatter(
        all_terms.astype(jnp.bfloat16), "blk", scatter_dimension=0, tiled=True
    ).astype(jnp.float32)
    grad_query_rows = grad_queries.reshape(tok_rows, model_width)
    grad_qkv_rows = jnp.concatenate([grad_query_rows, key_value_grads], axis=1).astype(jnp.bfloat16)
    grad_qkv = jnp.dot(normed_low.T, grad_qkv_rows, preferred_element_type=jnp.float32)
    grad_normed = jnp.dot(grad_qkv_rows, qkv_weight.T, preferred_element_type=jnp.float32)
    grad_source_norm, grad_attn_gain = attn_norm_back(grad_normed)
    grad_tokens = (grad_residual + grad_source_norm)[None]
    grad_qkv, grad_proj, grad_attn_gain, grad_moe_gain, grad_route, grad_anchor = lax.psum(
        (grad_qkv, grad_proj, grad_attn_gain, grad_moe_gain, grad_route, grad_anchor),
        ("blk", "expert"),
    )
    histogram_out = histogram + total_counts
    return (
        block_out,
        grad_tokens,
        grad_qkv,
        grad_proj,
        grad_attn_gain,
        grad_moe_gain,
        grad_route,
        grad_anchor,
        grad_first,
        grad_second,
        histogram_out,
    )


MESH = pl.DeviceIdType.MESH
F32 = jnp.float32
BF16 = jnp.bfloat16
VMEM_BYTES = 58 * 1024 * 1024


def dot(left, right, precision=None):
    return lax.dot_general(
        left, right, (((1,), (0,)), ((), ())), precision=precision, preferred_element_type=F32
    )


def dot_nt(left, right, precision=None):
    return lax.dot_general(
        left, right, (((1,), (1,)), ((), ())), precision=precision, preferred_element_type=F32
    )


def dot_tn(left, right, precision=None):
    return lax.dot_general(
        left, right, (((0,), (0,)), ((), ())), precision=precision, preferred_element_type=F32
    )


def rows_at(index, size):
    return pl.ds(pl.multiple_of(index * size, size), size)


def places():
    blk = lax.axis_index("blk")
    expert = lax.axis_index("expert")
    return blk, expert, blk + 1 - 2 * lax.rem(blk, 2), lax.rem(blk + 2, 4), 3 - blk


def greet(peers):
    barrier = pltpu.get_barrier_semaphore()
    for peer in peers:
        pl.semaphore_signal(barrier, inc=1, device_id=peer, device_id_type=MESH)
    return lambda: pl.semaphore_wait(barrier, len(peers))


def push(src, dst, sems, index, peer):
    copy = pltpu.make_async_remote_copy(
        src_ref=src,
        dst_ref=dst,
        send_sem=sems.at[0, index],
        recv_sem=sems.at[1, index],
        device_id=peer,
        device_id_type=MESH,
    )
    copy.start()
    return copy


def standardise(values):
    average = jnp.mean(values, axis=-1, keepdims=True)
    centered = values - average
    scale = lax.rsqrt(jnp.mean(centered * centered, axis=-1, keepdims=True) + EPSILON)
    return centered * scale, scale


def lower_triangle(keys, queries):
    return lax.broadcasted_iota(jnp.int32, (keys, queries), 0) <= lax.broadcasted_iota(
        jnp.int32, (keys, queries), 1
    )


class BlockGather:
    def __init__(self, part, sems, base):
        self.part, self.sems, self.base = part, sems, base

    def send(self, blk, half, index, peer):
        ref = self.part(blk, half)
        return push(ref, ref, self.sems, self.base + index, peer)

    def start(self):
        blk, expert, bx, by, bd = places()
        self.copies = [
            self.send(blk, 0, 0, (bx, expert)),
            self.send(blk, 1, 1, (by, expert)),
            self.send(blk, 1, 2, (bx, expert)),
            self.send(blk, 0, 3, (by, expert)),
        ]

    def forward(self):
        blk, expert, bx, by, bd = places()
        self.copies[0].wait_recv()
        self.copies.append(self.send(bx, 0, 4, (by, expert)))
        self.copies[1].wait_recv()
        self.copies.append(self.send(by, 1, 5, (bx, expert)))

    def wait_neighbours(self):
        self.copies[2].wait_recv()
        self.copies[3].wait_recv()

    def wait_diagonal(self):
        self.copies[4].wait_recv()
        self.copies[5].wait_recv()

    def wait_sends(self):
        for copy in self.copies:
            copy.wait_send()


def row_halves(buf, rows):
    size = rows // 2
    return lambda blk, half: buf.at[pl.ds(pl.multiple_of(blk * rows + half * size, size), size)]


class ExpertExchange:
    def __init__(self, src, dst, sems, base, rows, dst_base):
        self.src, self.dst, self.sems, self.base, self.rows, self.dst_base = (
            src, dst, sems, base, rows, dst_base)

    def start(self):
        blk, expert = lax.axis_index("blk"), lax.axis_index("expert")
        n = lax.axis_size("expert")
        self.copies = []
        place = pl.ds(pl.multiple_of(self.dst_base + expert * self.rows, self.rows), self.rows)
        for shift in range(1, n):
            peer = lax.rem(expert + shift, n)
            self.copies.append(
                push(self.src.at[rows_at(peer, self.rows)], self.dst.at[place], self.sems,
                     self.base + shift - 1, (blk, peer))
            )
        self.dst[place] = self.src[rows_at(expert, self.rows)]

    def wait(self):
        for copy in self.copies:
            copy.wait_recv()
        for copy in self.copies:
            copy.wait_send()


def blk_peers():
    blk, expert, bx, by, bd = places()
    return [(bx, expert), (by, expert), (bd, expert)]


def expert_peers():
    blk, expert = lax.axis_index("blk"), lax.axis_index("expert")
    n = lax.axis_size("expert")
    return [(blk, lax.rem(expert + shift, n)) for shift in range(1, n)]


def attend_kernel(
    tok_ref, gain_ref, wqkv_ref, cot_ref, rows_ref, cols_ref,
    nall_ref, qkv_ref, out_ref, lse_ref, att_ref, target_row_ref, target_col_ref, cot_in_ref,
    w_s, wt_s, k_s, att_s, cot_s, w_sem, gather_sems, cot_sems, att_sems,
):
    blk, expert, bx, by, bd = places()
    tok = tok_ref.shape[0]
    width = tok_ref.shape[1]
    heads = HEADS // 4
    group = heads * HEAD_DIM
    arrived = greet(blk_peers() + expert_peers())
    odd = lax.rem(blk, 2)
    loads = []
    for part in range(3):
        first = pl.multiple_of(part * width + blk * group - odd * 64, 128)
        loads.append(
            pltpu.make_async_copy(wqkv_ref.at[:, pl.ds(first, 256)], w_s.at[part], w_sem.at[part])
        )
        loads[-1].start()
    xhat, _ = standardise(tok_ref[...].astype(F32))
    nall_ref[rows_at(blk, tok), :] = (xhat * gain_ref[...]).astype(BF16)
    arrived()
    gather = BlockGather(row_halves(nall_ref, tok), gather_sems, 0)
    gather.start()

    capacity = tok // 8
    route_row, prio_row, mask_row = rows_ref[0:1, :], rows_ref[1:2, :], rows_ref[2:3, :]
    route_col, prio_col = cols_ref[:, 0:1], cols_ref[:, 1:2]
    same = route_col == route_row
    slot_row = jnp.sum(jnp.where(same & (prio_col < prio_row), 1.0, 0.0), axis=0, keepdims=True)
    slot_col = jnp.sum(jnp.where(same & (prio_row < prio_col), 1.0, 0.0), axis=1, keepdims=True)
    target_row = jnp.where(slot_row < capacity, route_row * capacity + slot_row, -1.0)
    target_col = jnp.where(slot_col < capacity, route_col * capacity + slot_col, -1.0)
    target_row_ref[...] = jnp.broadcast_to(target_row, target_row_ref.shape)
    target_col_ref[...] = jnp.broadcast_to(target_col, target_col_ref.shape)
    slots = lax.broadcasted_iota(jnp.int32, (tok, tok), 0).astype(F32)
    chosen = jnp.where((slots == target_row) & (mask_row > 0.0), 1.0, 0.0).astype(BF16)
    cot_s[...] = dot(chosen, cot_ref[...]).astype(BF16)
    cot_move = ExpertExchange(cot_s, cot_in_ref, cot_sems, 0, capacity, 0)
    cot_move.start()

    for part in range(3):
        loads[part].wait()
        wide = w_s[part]
        narrow = jnp.where(odd == 1, wide[:, 64:256], wide[:, 0:192])
        wt_s[part * group : (part + 1) * group, :] = narrow.T

    def project(where):
        cols = rows_at(where, tok)
        mixed = dot_nt(wt_s[...], nall_ref[cols, :]).astype(BF16)
        qkv_ref[0:group, cols] = mixed[0:group] * BF16(HEAD_DIM**-0.5)
        qkv_ref[group:, cols] = mixed[group:]
        for head in range(heads):
            k_s[head, cols, :] = mixed[group + head * 64 : group + (head + 1) * 64].T

    project(blk)
    gather.forward()
    gather.wait_neighbours()
    project(bx)
    project(by)
    gather.wait_diagonal()
    project(bd)

    half = tok // 2

    def scores(i, head):
        q = qkv_ref[head * 64 : (head + 1) * 64, i * tok : (i + 1) * tok]
        upper = dot(k_s[head, i * tok : i * tok + half, :], q)
        upper = jnp.where(lower_triangle(half, tok), upper, MASKED)
        lower = dot(k_s[head, i * tok + half : (i + 1) * tok, :], q[:, half:])
        lower = jnp.where(lower_triangle(half, half), lower, MASKED)
        top = jnp.max(upper, axis=0, keepdims=True)
        low_top = jnp.max(lower, axis=0, keepdims=True)
        top = jnp.concatenate([top[:, :half], jnp.maximum(top[:, half:], low_top)], axis=1)
        if i == 0:
            return top, upper, lower, None
        past = dot(k_s[head, 0 : i * tok, :], q)
        return jnp.maximum(top, jnp.max(past, axis=0, keepdims=True)), upper, lower, past

    sends = []

    def finish(i, head, found):
        top, upper, lower, past = found
        v = qkv_ref[2 * group + head * 64 : 2 * group + (head + 1) * 64, :]
        upper = jnp.exp(upper - top)
        lower = jnp.exp(lower - top[:, half:])
        total = jnp.sum(upper, axis=0, keepdims=True)
        low_total = jnp.sum(lower, axis=0, keepdims=True)
        total = jnp.concatenate([total[:, :half], total[:, half:] + low_total], axis=1)
        result = dot(v[:, i * tok : i * tok + half], upper.astype(BF16))
        low_result = dot(v[:, i * tok + half : (i + 1) * tok], lower.astype(BF16))
        result = jnp.concatenate([result[:, :half], result[:, half:] + low_result], axis=1)
        if i:
            past = jnp.exp(past - top)
            total = total + jnp.sum(past, axis=0, keepdims=True)
            result = result + dot(v[:, 0 : i * tok], past.astype(BF16))
        result = result / total
        place = slice(head * 64, (head + 1) * 64)
        out_ref[place, i * tok : (i + 1) * tok] = result
        lse_ref[head : head + 1, i * tok : (i + 1) * tok] = top + jnp.log(total)
        att_s[place, i * tok : (i + 1) * tok] = result.astype(BF16)
        there = pl.ds(pl.multiple_of(blk * group + head * 64, 64), 64)

        def copy():
            return pltpu.make_async_remote_copy(
                src_ref=att_s.at[place, i * tok : (i + 1) * tok],
                dst_ref=att_ref.at[there],
                send_sem=att_sems.at[0, i * heads + head],
                recv_sem=att_sems.at[1, blk * heads + head],
                device_id=(i, expert),
                device_id_type=MESH,
            )

        @pl.when(blk != i)
        def _():
            copy().start()

        @pl.when(blk == i)
        def _():
            att_ref[there, :] = result.astype(BF16)

        sends.append((i, copy))

    before = None
    for i in range(4):
        for head in range(heads):
            found = scores(i, head)
            if before is not None:
                finish(*before)
            before = (i, head, found)
    finish(*before)

    for i, copy in sends:
        @pl.when(blk != i)
        def _():
            copy().wait_send()

    for source in range(4):
        @pl.when(blk != source)
        def _():
            for head in range(heads):
                there = pl.ds(source * group + head * 64, 64)
                pltpu.make_async_remote_copy(
                    src_ref=att_s.at[0:64, 0:tok],
                    dst_ref=att_ref.at[there],
                    send_sem=att_sems.at[0, source * heads + head],
                    recv_sem=att_sems.at[1, source * heads + head],
                    device_id=(source, expert),
                    device_id_type=MESH,
                ).wait_recv()

    cot_move.wait()
    gather.wait_sends()


def gelu_pair(hidden):
    squared = hidden * hidden
    curve = jnp.tanh(0.7978845608028654 * hidden * (1.0 + 0.044715 * squared))
    half = 0.5 * (1.0 + curve)
    slope = half + 0.5 * hidden * (1.0 - curve * curve) * (
        0.7978845608028654 * (1.0 + 0.134145 * squared)
    )
    return hidden * half, slope


def spread(row, size):
    shape = (size, row.shape[1])
    eye = lax.broadcasted_iota(jnp.int32, shape, 0) == lax.broadcasted_iota(jnp.int32, shape, 1)
    return jnp.sum(jnp.where(eye, row, 0.0), axis=1, keepdims=True)


def flatten(column, width):
    shape = (column.shape[0], width)
    eye = lax.broadcasted_iota(jnp.int32, shape, 0) == lax.broadcasted_iota(jnp.int32, shape, 1)
    return jnp.sum(jnp.where(eye, column, 0.0), axis=0, keepdims=True)


def expert_kernel(
    att_ref, tok_ref, proj_ref, gain_ref, route_ref, anchor_ref, cols_ref, target_row_ref,
    target_col_ref, cot_ref, cot_in_ref, first_ref, second_ref,
    result_ref, residual_ref, gate_ref, grad_residual_ref, grad_att_ref, grad_proj_ref, small_ref,
    buf_ref, cots_ref, gates_ref,
    first_s, second_s, go_s, gate_s, grad_s, back_s, score_s, score_in_s, res_acc, sent_acc, grad_in_s,
    w_sem, go_sems, gate_sems, back_sems, score_sems, cots_sems, buf_sems, gates_sems,
):
    blk, expert, bx, by, bd = places()
    tok, width = tok_ref.shape
    experts = 8
    capacity = tok // experts
    here = rows_at(blk, tok)
    arrived = greet(blk_peers() + expert_peers())
    loads = [
        pltpu.make_async_copy(first_ref, first_s, w_sem.at[0]),
        pltpu.make_async_copy(second_ref, second_s, w_sem.at[1]),
    ]
    for load in loads:
        load.start()
    cots_ref[here, :] = cot_in_ref[...]

    residual = tok_ref[...].astype(F32) + dot_tn(att_ref[...], proj_ref[...])
    residual_ref[...] = residual
    xhat, scale = standardise(residual)
    normed = xhat * gain_ref[...]
    normed_low = normed.astype(BF16)
    target_row, target_col = target_row_ref[0:1, :], target_col_ref[:, 0:1]
    slots = lax.broadcasted_iota(jnp.int32, (tok, tok), 0).astype(F32)
    go_s[...] = dot(jnp.where(slots == target_row, 1.0, 0.0).astype(BF16), normed_low).astype(BF16)
    arrived()
    cots = BlockGather(row_halves(cots_ref, tok), cots_sems, 0)
    cots.start()
    go = ExpertExchange(go_s, buf_ref, go_sems, 0, capacity, blk * tok)
    go.start()

    route_col = cols_ref[:, 0:1]
    projected = dot(normed, route_ref[...], TOP_PRECISION)
    unit_scale = lax.rsqrt(1.0 + jnp.sum(projected * projected, axis=1, keepdims=True))
    unit = projected * unit_scale
    anchor = anchor_ref[...]
    anchor_scale = lax.rsqrt(1.0 + jnp.sum(anchor * anchor, axis=1, keepdims=True))
    anchor_unit = anchor * anchor_scale
    logits = dot_nt(unit, anchor_unit, TOP_PRECISION) / ROUTER_SOFTNESS
    soft = jnp.exp(logits - jnp.max(logits, axis=1, keepdims=True))
    soft = soft / jnp.sum(soft, axis=1, keepdims=True)
    onehot = jnp.where(
        lax.broadcasted_iota(jnp.int32, (tok, experts), 1).astype(F32) == route_col, 1.0, 0.0
    )
    gate = jnp.sum(soft * onehot, axis=1, keepdims=True)
    gate_ref[...] = jnp.broadcast_to(gate, gate_ref.shape)
    lane = lax.broadcasted_iota(jnp.int32, (tok, 128), 1).astype(F32)
    lane = jnp.where(lane < capacity, lane, 1e6)
    for peer in range(experts):
        row = jnp.sum(
            jnp.where(target_col == peer * capacity + lane, gate, 0.0), axis=0, keepdims=True
        )
        gate_s[peer * 8 : (peer + 1) * 8, :] = jnp.broadcast_to(row, (8, 128))
    gates = ExpertExchange(gate_s, gates_ref, gate_sems, 0, 8, blk * 64)
    gates.start()

    cots.forward()
    go.wait()
    gates.wait()
    buf = BlockGather(row_halves(buf_ref, tok), buf_sems, 0)
    buf.start()
    gates_here = gates_ref.at[rows_at(blk, 64)]
    gates_out = [
        push(gates_here, gates_here, gates_sems, n, peer) for n, peer in enumerate(blk_peers())
    ]
    cots.wait_neighbours()
    cots.wait_diagonal()
    buf.forward()

    for source in range(experts):
        chunk = slice(source * capacity, (source + 1) * capacity)
        rate = spread(gates_ref[pl.ds(blk * 64 + source * 8, 8), :][0:1, :], capacity)
        grad_in_s[chunk, :] = (cot_in_ref[chunk, :].astype(F32) * rate).astype(BF16)
    for load in loads:
        load.wait()
    tile = 768
    x = buf_ref[here, :]
    grad_in = grad_in_s[...]
    for t in range(first_s.shape[1] // tile):
        cut = slice(t * tile, (t + 1) * tile)
        hidden = dot(x, first_s[:, cut])
        act, slope = gelu_pair(hidden)
        part = dot(act.astype(BF16), second_s[cut, :])
        grad_hidden = (dot_nt(grad_in, second_s[cut, :]) * slope).astype(BF16)
        sent = dot_nt(grad_hidden, first_s[:, cut])
        if t == 0:
            res_acc[...] = part
            sent_acc[...] = sent
        else:
            res_acc[...] += part
            sent_acc[...] += sent
    grad_s[...] = sent_acc[...].astype(BF16)
    back = ExpertExchange(grad_s, back_s, back_sems, 0, capacity, 0)
    back.start()
    result = res_acc[...].astype(BF16)
    result_ref[...] = result
    score = jnp.sum(result.astype(F32) * cot_in_ref[...].astype(F32), axis=1, keepdims=True)
    for source in range(experts):
        row = flatten(score[source * capacity : (source + 1) * capacity], 128)
        score_s[source * 8 : (source + 1) * 8, :] = jnp.broadcast_to(row, (8, 128))
    scores = ExpertExchange(score_s, score_in_s, score_sems, 0, 8, 0)
    scores.start()
    grad_out = cot_ref[...].astype(F32) * cols_ref[:, 2:3]

    scores.wait()
    grad_gate = jnp.zeros((tok, 1), F32)
    for peer in range(experts):
        row = score_in_s[peer * 8 : peer * 8 + 1, :]
        grad_gate += jnp.sum(
            jnp.where(target_col == peer * capacity + lane, row, 0.0), axis=1, keepdims=True
        )
    grad_logits = grad_gate * gate * (onehot - soft) / ROUTER_SOFTNESS
    grad_unit = dot(grad_logits, anchor_unit, TOP_PRECISION)
    grad_projected = unit_scale * (
        grad_unit - unit * jnp.sum(unit * grad_unit, axis=1, keepdims=True)
    )
    grad_anchor_unit = dot_tn(grad_logits, unit, TOP_PRECISION)
    grad_anchor = anchor_scale * (
        grad_anchor_unit
        - anchor_unit * jnp.sum(anchor_unit * grad_anchor_unit, axis=1, keepdims=True)
    )
    rdim = route_ref.shape[1]
    small_ref[...] = jnp.zeros_like(small_ref)
    small_ref[0:rdim, :] = dot_tn(grad_projected, normed, TOP_PRECISION)
    small_ref[rdim : rdim + experts, 0:rdim] = grad_anchor
    counts = jnp.sum(onehot, axis=0, keepdims=True)
    small_ref[rdim + experts + 2 : rdim + experts + 3, 0:experts] = counts
    router_rows = dot_nt(grad_projected, route_ref[...], TOP_PRECISION)

    back.wait()
    lanes = lax.broadcasted_iota(jnp.int32, (tok, tok), 1).astype(F32)
    moe_rows = dot(jnp.where(lanes == target_col, 1.0, 0.0).astype(BF16), back_s[...])
    grad_normed = moe_rows + router_rows
    small_ref[rdim + experts : rdim + experts + 1, :] = jnp.sum(
        grad_normed * xhat, axis=0, keepdims=True
    )
    grad_xhat = grad_normed * gain_ref[...]
    grad_residual = grad_out + scale * (
        grad_xhat
        - jnp.mean(grad_xhat, axis=1, keepdims=True)
        - xhat * jnp.mean(grad_xhat * xhat, axis=1, keepdims=True)
    )
    grad_residual_ref[...] = grad_residual
    grad_low = grad_residual.astype(BF16)
    grad_att_ref[...] = dot_nt(proj_ref[...], grad_low).astype(BF16)
    grad_proj_ref[...] = dot(att_ref[...], grad_low)

    buf.wait_neighbours()
    buf.wait_diagonal()
    cots.wait_sends()
    buf.wait_sends()
    for copy in gates_out:
        copy.wait()


def expert_weights_kernel(
    buf_ref, cots_ref, gates_ref, first_ref, second_ref, grad_first_ref, grad_second_ref,
    first_t, acc,
):
    slots, width = buf_ref.shape
    first_t[...] = first_ref[...].T
    step = 512
    for t in range(slots // step):
        cut = slice(t * step, (t + 1) * step)
        rates = [spread(gates_ref[t * 64 + s * 8 : t * 64 + s * 8 + 1, :], 64) for s in range(8)]
        rate = jnp.concatenate(rates, axis=0)
        x = buf_ref[cut, :]
        grad_in = (cots_ref[cut, :].astype(F32) * rate).astype(BF16)
        act, slope = gelu_pair(dot_nt(first_t[...], x))
        grad_hidden = (dot_nt(second_ref[...], grad_in) * slope).astype(BF16)
        grad_second = dot(act.astype(BF16), grad_in)
        grad_first = dot(grad_hidden, x)
        if t == 0:
            grad_second_ref[...] = grad_second
            acc[...] = grad_first
        else:
            grad_second_ref[...] += grad_second
            acc[...] += grad_first
    grad_first_ref[...] = acc[...].T


def attend_back_kernel(
    grad_att_ref, qkv_ref, out_ref, lse_ref, nall_ref, result_ref, residual_ref, gate_ref,
    target_col_ref, gain_ref, wqkv_ref, tok_ref, grad_residual_ref, grad_proj_ref, small_ref,
    block_out_ref, grad_tokens_ref, shared_ref, small_out_ref,
    do_t, dq_s, dqkv_s, home_s, q_s, k_s, v_s, do_s, back_s, wt_s, proj_out, proj_in, part_s,
    core_out, core_in, line_out, line_in, small_a, small_in, small_b, row_out, row_in,
    att_sems, back_sems, home_sems, proj_sems, core_sems, line_sems, join_sems, small_sems,
    row_sems, ring_sems, spread_sems, pair_sems,
):
    blk, expert, bx, by, bd = places()
    tok = grad_att_ref.shape[1]
    width = grad_att_ref.shape[0]
    heads = HEADS // 4
    group = heads * HEAD_DIM
    here = rows_at(blk, tok)
    length = qkv_ref.shape[1]
    core = lax.rem(expert, 2)
    line = expert // 2
    lines = 4
    half = width // 2
    other = (blk, expert + 1 - 2 * core)
    mine_lanes = pl.ds(pl.multiple_of(core * half, 128), half)
    other_lanes = pl.ds(pl.multiple_of((1 - core) * half, 128), half)
    line_peers = [(blk, lax.rem(line + shift, lines) * 2 + core) for shift in range(1, lines)]
    arrived = greet(blk_peers() + expert_peers())
    odd = lax.rem(blk, 2)
    arrived()
    mine = rows_at(blk, group)
    att_copies = [
        push(grad_att_ref.at[rows_at(peer[0], group)], do_t.at[:, here], att_sems, n, peer)
        for n, peer in enumerate(blk_peers())
    ]
    back = ExpertExchange(result_ref, back_s, back_sems, 0, tok // 8, 0)
    back.start()
    small_core = push(small_ref.at[:, other_lanes], small_in.at[0], small_sems, 0, other)
    do_t[:, here] = grad_att_ref[mine, :]
    for head in range(heads):
        cut = slice(head * 64, (head + 1) * 64)
        q_s[head] = qkv_ref[cut, :].T
        k_s[head] = qkv_ref[group + head * 64 : group + (head + 1) * 64, :].T
        v_s[head] = qkv_ref[2 * group + head * 64 : 2 * group + (head + 1) * 64, :].T
    for part in range(3):
        first = pl.multiple_of(part * width + blk * group - odd * 64, 128)
        wide = wqkv_ref[:, pl.ds(first, 256)]
        narrow = jnp.where(odd == 1, wide[:, 64:256], wide[:, 0:192])
        wt_s[part * group : (part + 1) * group, :] = narrow.T
    proj_out[...] = grad_proj_ref[...].astype(BF16)
    small_core.wait()
    small_a[...] = small_ref[:, mine_lanes] + small_in[0]
    small_in[1 + line] = small_a[...]
    small_line = [
        push(small_a, small_in.at[1 + line], small_sems, 1 + n, peer)
        for n, peer in enumerate(line_peers)
    ]
    for copy in att_copies:
        copy.wait_recv()
    proj_copies = [
        push(proj_out.at[rows_at(peer[0], group)], proj_in.at[n], proj_sems, n, peer)
        for n, peer in enumerate(blk_peers())
    ]
    for head in range(heads):
        do_s[head] = do_t[head * 64 : (head + 1) * 64, :].T

    home = []
    for head in range(heads):
        cut = slice(head * 64, (head + 1) * 64)
        kt_cut = slice(group + head * 64, group + (head + 1) * 64)
        vt_cut = slice(2 * group + head * 64, 2 * group + (head + 1) * 64)
        delta = jnp.sum(out_ref[cut, :] * do_t[cut, :].astype(F32), axis=0, keepdims=True)
        for j in range(4):
            keys = slice(j * tok, (j + 1) * tok)
            queries = slice(j * tok, length)
            s = dot(k_s[head, keys, :], qkv_ref[cut, queries])
            p = jnp.exp(s - lse_ref[head : head + 1, queries])
            allowed = lower_triangle(tok, length - j * tok)
            p = jnp.where(allowed, p, 0.0)
            dp = dot(v_s[head, keys, :], do_t[cut, queries])
            ds = (p * (dp - delta[:, queries])).astype(BF16)
            dv = dot(p.astype(BF16), do_s[head, queries, :])
            dk = dot(ds, q_s[head, queries, :])
            dqkv_s[kt_cut, keys] = dk.T.astype(BF16)
            dqkv_s[vt_cut, keys] = dv.T.astype(BF16)
            dq = dot(qkv_ref[kt_cut, keys], ds)
            if j == 0:
                dq_s[...] = dq
            else:
                dq_s[:, queries] += dq
        dqkv_s[cut, :] = (dq_s[...] * HEAD_DIM**-0.5).astype(BF16)
        for part in range(3):
            src = slice(part * group + head * 64, part * group + (head + 1) * 64)
            there = pl.ds(pl.multiple_of(part * width + blk * group + head * 64, 64), 64)
            for n, peer in enumerate(blk_peers()):
                home.append(
                    push(dqkv_s.at[src, rows_at(peer[0], tok)], home_s.at[there], home_sems,
                         (n * heads + head) * 3 + part, peer)
                )
            home_s[there, :] = dqkv_s[src, here]
        if head == 0:
            for copy in small_line:
                copy.wait()
            small_b[...] = (small_in[1] + small_in[2]) + (small_in[3] + small_in[4])
            small_in[5 + blk] = small_b[...]
            small_blk = [
                push(small_b, small_in.at[5 + blk], small_sems, 4 + n, peer)
                for n, peer in enumerate(blk_peers())
            ]

    grad_group = dot(dqkv_s[...], nall_ref[...])
    attn_gain = jnp.sum(grad_group * wt_s[...].astype(F32), axis=0, keepdims=True) / gain_ref[...]
    row_out[0] = jnp.concatenate(
        [attn_gain[:, n * 128 : (n + 1) * 128] for n in range(width // 128)]
        + [jnp.zeros((8 - width // 128, 128), F32)], axis=0)
    row_core = push(row_out.at[0], row_in.at[0], row_sems, 0, other)
    for copy in proj_copies:
        copy.wait()
    part_s[0 : 3 * group, :] = grad_group
    part_s[3 * group :, :] = (
        grad_proj_ref[mine, :] + proj_in[0].astype(F32) + proj_in[1].astype(F32)
        + proj_in[2].astype(F32)
    )
    core_out[...] = part_s[:, other_lanes].astype(BF16)
    core_copy = push(core_out, core_in, core_sems, 0, other)
    for copy in small_blk:
        copy.wait()
    small_out_ref[:, mine_lanes] = (small_in[5] + small_in[6]) + (small_in[7] + small_in[8])
    small_pair = push(
        small_out_ref.at[:, mine_lanes], small_out_ref.at[:, mine_lanes], small_sems, 7, other)
    core_copy.wait()
    summed = part_s[:, mine_lanes] + core_in[...].astype(F32)
    line_out[...] = summed.astype(BF16)
    line_copies = [
        push(line_out.at[rows_at(peer[1] // 2, width // lines)], line_in.at[n], line_sems, n, peer)
        for n, peer in enumerate(line_peers)
    ]
    part_s[:, 0:half] = summed
    row_core.wait()
    row_out[1] = row_out[0] + row_in[0]
    row_in[1 + line] = row_out[1]
    row_line = [
        push(row_out.at[1], row_in.at[1 + line], row_sems, 1 + n, peer)
        for n, peer in enumerate(line_peers)
    ]

    back.wait()
    lanes = lax.broadcasted_iota(jnp.int32, (tok, tok), 1).astype(F32)
    chosen = jnp.where(lanes == target_col_ref[:, 0:1], 1.0, 0.0).astype(BF16)
    fetched = dot(chosen, back_s[...])
    block_out_ref[...] = (residual_ref[...] + gate_ref[:, 0:1] * fetched).astype(BF16)

    for copy in line_copies:
        copy.wait()
    piece = width // lines

    def shared_at(block, place, first, size):
        row = pl.multiple_of(block * width + place * piece + first, 16)
        return shared_ref.at[pl.ds(row, size), mine_lanes]

    own = part_s[rows_at(line, piece), 0:half]
    for n in range(lines - 1):
        own = own + line_in[n].astype(F32)
    shared_ref[pl.ds(pl.multiple_of(blk * width + line * piece, 16), piece), mine_lanes] = (
        own.astype(BF16))
    joins = [
        push(shared_at(blk, line, 0, piece), shared_at(blk, line, 0, piece), join_sems, n, peer)
        for n, peer in enumerate(line_peers)
    ]
    gathers, pairs = [], []

    def pair(block, place):
        ref = shared_at(block, place, 0, piece)
        pairs.append(push(ref, ref, pair_sems, len(pairs), other))

    def begin(n, place):
        gather = BlockGather(
            lambda block, part: shared_at(block, place, part * (piece // 2), piece // 2),
            ring_sems, n * 6)
        gather.start()
        gathers.append((gather, place))
        pair(blk, place)

    begin(0, line)
    for copy in row_line:
        copy.wait()
    row_out[2] = (row_in[1] + row_in[2]) + (row_in[3] + row_in[4])
    row_in[5 + blk] = row_out[2]
    row_blk = [
        push(row_out.at[2], row_in.at[5 + blk], row_sems, 4 + n, peer)
        for n, peer in enumerate(blk_peers())
    ]

    for copy in home:
        copy.wait_recv()
    xhat, scale = standardise(tok_ref[...].astype(F32))

    def tokens_part(n):
        cut = slice(n * 256, (n + 1) * 256)
        grad_normed = dot(wqkv_ref[...], home_s[:, cut]).T
        grad_xhat = grad_normed * gain_ref[...]
        x = xhat[cut]
        grad_tokens_ref[cut, :] = grad_residual_ref[cut, :] + scale[cut] * (
            grad_xhat
            - jnp.mean(grad_xhat, axis=1, keepdims=True)
            - x * jnp.mean(grad_xhat * x, axis=1, keepdims=True)
        )

    for n in range(lines - 1):
        joins[n].wait_recv()
        begin(n + 1, lax.rem(line + lines - 1 - n, lines))
        if n < 2:
            tokens_part(n)
        gathers[n][0].forward()
    gathers[lines - 1][0].forward()
    for gather, place in gathers:
        gather.wait_neighbours()
        pair(bx, place)
        pair(by, place)
    for gather, place in gathers:
        gather.wait_diagonal()
        pair(bd, place)
    for copy in row_blk:
        copy.wait()
    small_pair.wait()
    total = (row_in[5] + row_in[6]) + (row_in[7] + row_in[8])
    small_out_ref[25:26, :] = jnp.concatenate(
        [total[n : n + 1, :] for n in range(width // 128)], axis=1)
    for copy in joins:
        copy.wait_send()
    for copy in pairs:
        copy.wait_recv()
    for copy in pairs:
        copy.wait_send()
    for gather, place in gathers:
        gather.wait_sends()
    for copy in att_copies + home:
        copy.wait_send()


def unfold_kernel(qkv_ref, proj_ref, grad_qkv_ref, grad_proj_ref):
    group = qkv_ref.shape[1]
    for block in range(qkv_ref.shape[0]):
        cut = slice(block * group, (block + 1) * group)
        grad_qkv_ref[:, cut] = qkv_ref[block].astype(F32).T

    @pl.when(pl.program_id(0) == 0)
    def _():
        for block in range(qkv_ref.shape[0]):
            grad_proj_ref[block * group : (block + 1) * group, :] = proj_ref[block].astype(F32)


def unfold(shared, blocks, group, width):
    shared = shared.reshape(blocks, width, width)
    return pl.pallas_call(
        unfold_kernel,
        grid=(3,),
        out_shape=(
            jax.ShapeDtypeStruct((width, 3 * width), F32),
            jax.ShapeDtypeStruct((width, width), F32),
        ),
        in_specs=[
            pl.BlockSpec((blocks, group, width), lambda n: (0, n, 0)),
            pl.BlockSpec((blocks, group, width), lambda n: (0, 3, 0)),
        ],
        out_specs=(
            pl.BlockSpec((width, width), lambda n: (0, n)),
            pl.BlockSpec((width, width), lambda n: (0, 0)),
        ),
        name="unfold",
        compiler_params=pltpu.CompilerParams(vmem_limit_bytes=VMEM_BYTES),
    )(shared, shared)


def call(kernel, name, args, outs, scratch, in_any=(), collective=None):
    specs = [
        pl.BlockSpec(memory_space=pl.ANY if n in in_any else pltpu.VMEM) for n in range(len(args))
    ]
    shapes = tuple(jax.ShapeDtypeStruct(shape, dtype) for shape, dtype in outs)
    return pl.pallas_call(
        kernel,
        out_shape=shapes,
        in_specs=specs,
        out_specs=tuple(pl.BlockSpec(memory_space=pltpu.VMEM) for _ in outs),
        scratch_shapes=scratch,
        name=name,
        compiler_params=pltpu.CompilerParams(
            vmem_limit_bytes=VMEM_BYTES,
            collective_id=collective,
            has_side_effects=collective is not None,
        ),
    )(*args)


def fast_body(
    tokens, cotangent, loss_mask, routes, priority, histogram, qkv_weight, proj_weight, attn_gain,
    moe_gain, route_weight, anchor_table, first_weight, second_weight,
):
    tok, width = tokens.shape[1:]
    blocks, experts = lax.axis_size("blk"), lax.axis_size("expert")
    length = tok * blocks
    heads = HEADS // blocks
    group = heads * HEAD_DIM
    hidden = first_weight.shape[2]
    x, cot = tokens[0], cotangent[0]
    rows = jnp.stack([routes[0, :, 0], priority[0, 0], loss_mask[0]]).astype(F32)
    rows = jnp.pad(rows, ((0, 5), (0, 0)))
    cols = rows.T
    gain1, gain2 = attn_gain[None], moe_gain[None]
    dma = pltpu.SemaphoreType.DMA
    nall, qkv, out, lse, att, target_row, target_col, cot_in = call(
        attend_kernel, "attend", (x, gain1, qkv_weight, cot, rows, cols),
        [((length, width), BF16), ((3 * group, length), BF16), ((group, length), F32),
         ((8, length), F32), ((width, tok), BF16), ((8, tok), F32), ((tok, 128), F32),
         ((tok, width), BF16)],
        [pltpu.VMEM((3, width, 256), BF16), pltpu.VMEM((3 * group, width), BF16),
         pltpu.VMEM((heads, length, HEAD_DIM), BF16), pltpu.VMEM((group, length), BF16),
         pltpu.VMEM((tok, width), BF16), dma((3,)), dma((2, 6)), dma((2, experts)),
         dma((2, blocks * heads))],
        in_any=(2,), collective=1,
    )
    (result, residual, gate, grad_residual, grad_att, grad_proj, small, buf, cots, gates) = call(
        expert_kernel, "expert",
        (att, x, proj_weight, gain2, route_weight, anchor_table, cols, target_row, target_col, cot,
         cot_in, first_weight[0], second_weight[0]),
        [((tok, width), BF16), ((tok, width), F32), ((tok, 128), F32), ((tok, width), F32),
         ((width, tok), BF16), ((width, width), F32), ((32, width), F32),
         ((length, width), BF16), ((length, width), BF16), ((blocks * 64, 128), F32)],
        [pltpu.VMEM((width, hidden), BF16), pltpu.VMEM((hidden, width), BF16),
         pltpu.VMEM((tok, width), BF16), pltpu.VMEM((64, 128), F32), pltpu.VMEM((tok, width), BF16),
         pltpu.VMEM((tok, width), BF16), pltpu.VMEM((64, 128), F32), pltpu.VMEM((64, 128), F32),
         pltpu.VMEM((tok, width), F32), pltpu.VMEM((tok, width), F32), pltpu.VMEM((tok, width), BF16),
         dma((2,)), dma((2, experts)), dma((2, experts)), dma((2, experts)), dma((2, experts)),
         dma((2, 6)), dma((2, 6)), dma((2, 3))],
        in_any=(11, 12), collective=2,
    )
    place = lax.axis_index("blk")
    quarter = hidden // blocks
    first_part = lax.dynamic_slice_in_dim(first_weight[0], place * quarter, quarter, 1)
    second_part = lax.dynamic_slice_in_dim(second_weight[0], place * quarter, quarter, 0)
    grad_first, grad_second = call(
        expert_weights_kernel, "expert_weights", (buf, cots, gates, first_part, second_part),
        [((width, quarter), F32), ((quarter, width), F32)],
        [pltpu.VMEM((quarter, width), BF16), pltpu.VMEM((quarter, width), F32)],
    )
    half, piece = width // 2, width // 4
    block_out, grad_tokens, shared, small = call(
        attend_back_kernel, "attend_back",
        (grad_att, qkv, out, lse, nall, result, residual, gate, target_col, gain1, qkv_weight, x,
         grad_residual, grad_proj, small),
        [((tok, width), BF16), ((tok, width), F32), ((blocks * width, width), BF16),
         ((32, width), F32)],
        [pltpu.VMEM((group, length), BF16), pltpu.VMEM((HEAD_DIM, length), F32),
         pltpu.VMEM((3 * group, length), BF16), pltpu.VMEM((3 * width, tok), BF16)]
        + [pltpu.VMEM((heads, length, HEAD_DIM), BF16)] * 4
        + [pltpu.VMEM((tok, width), BF16), pltpu.VMEM((3 * group, width), BF16),
           pltpu.VMEM((width, width), BF16), pltpu.VMEM((3, group, width), BF16),
           pltpu.VMEM((width, width), F32),
           pltpu.VMEM((width, half), BF16), pltpu.VMEM((width, half), BF16),
           pltpu.VMEM((width, half), BF16), pltpu.VMEM((3, piece, half), BF16),
           pltpu.VMEM((32, half), F32), pltpu.VMEM((9, 32, half), F32), pltpu.VMEM((32, half), F32),
           pltpu.VMEM((3, 8, 128), F32), pltpu.VMEM((9, 8, 128), F32),
           dma((2, 3)), dma((2, experts)), dma((2, 27)), dma((2, 3)), dma((2, 1)), dma((2, 3)),
           dma((2, 3)), dma((2, 8)), dma((2, 7)), dma((2, 24)), dma((2, 1)), dma((2, 16))],
        collective=3,
    )
    grad_qkv, grad_proj = unfold(shared, blocks, group, width)
    rdim = route_weight.shape[1]
    return (
        block_out[None],
        grad_tokens[None],
        grad_qkv,
        grad_proj,
        small[rdim + experts + 1],
        small[rdim + experts],
        small[:rdim].T,
        small[rdim : rdim + experts, :rdim],
        grad_first[None],
        grad_second[None],
        histogram + small[rdim + experts + 2, :experts].astype(jnp.int32),
    )


def solution(mesh):
    in_specs = (
        P("expert", "blk", None),
        P("expert", "blk", None),
        P("expert", "blk"),
        P("expert", "blk", None),
        P("expert", "blk", None),
        P(),
        P(),
        P(),
        P(),
        P(),
        P(),
        P(),
        P("expert", None, None),
        P("expert", None, None),
    )
    out_specs = (
        P("expert", "blk", None),
        P("expert", "blk", None),
        P(),
        P(),
        P(),
        P(),
        P(),
        P(),
        P("expert", None, "blk"),
        P("expert", "blk", None),
        P(),
    )
    blocks, experts = mesh.shape["blk"], mesh.shape["expert"]
    body = fast_body if (blocks, experts) == (4, 8) else general_body
    return jax.shard_map(body, mesh=mesh, in_specs=in_specs, out_specs=out_specs, check_vma=False)
```

```python
import functools

import jax
import jax.numpy as jnp
from jax import lax
from jax.experimental import pallas as pl
from jax.experimental.pallas import tpu as pltpu
from jax.sharding import PartitionSpec as P

HEADS = 12
HEAD_DIM = 64


TOP_PRECISION = lax.Precision.HIGHEST
EPSILON = 1e-05
ROUTER_SOFTNESS = 0.4
MASKED = -1e30


def layer_norm(values, norm_gain):
    average = jnp.mean(values, axis=-1, keepdims=True)
    centered = values - average
    variance = jnp.mean(centered * centered, axis=-1, keepdims=True)
    return centered * lax.rsqrt(variance + EPSILON) * norm_gain


def unit_rows(matrix):
    return matrix * lax.rsqrt(1.0 + jnp.sum(matrix * matrix, axis=-1, keepdims=True))


def router_gate(normalized_rows, route_matrix, anchors, route_onehot):
    projection_output = unit_rows(jnp.dot(normalized_rows, route_matrix, precision=TOP_PRECISION))
    expert_anchor_rows = unit_rows(anchors)
    route_logit_scores = (
        jnp.dot(projection_output, expert_anchor_rows.T, precision=TOP_PRECISION) / ROUTER_SOFTNESS
    )
    return jnp.sum(jax.nn.softmax(route_logit_scores, axis=-1) * route_onehot, axis=-1)


def masked_scores(queries, key_rows, query_first, key_first, score_scale):
    scores = (
        jnp.einsum("qhd,khd->hqk", queries, key_rows, preferred_element_type=jnp.float32)
        * score_scale
    )
    grid_shape = (queries.shape[0], key_rows.shape[0])
    query_place = query_first + lax.broadcasted_iota(jnp.int32, grid_shape, 0)
    key_place = key_first + lax.broadcasted_iota(jnp.int32, grid_shape, 1)
    return (scores, (key_place <= query_place)[None])


def over_blocks(step_fn, carried, arrays, block_rows):
    row_total = arrays[0].shape[0]
    block_count = row_total // block_rows
    stacked = tuple(
        (member.reshape((block_count, block_rows) + member.shape[1:]) for member in arrays)
    )

    def scan_step(running, packed):
        position, blocks = packed
        return (step_fn(running, blocks, position * block_rows), None)

    result, unused = lax.scan(
        scan_step, carried, (jnp.arange(block_count, dtype=jnp.int32), stacked)
    )
    return result


def general_body(
    tokens,
    cotangent,
    loss_mask,
    routes,
    priority,
    histogram,
    qkv_weight,
    proj_weight,
    attn_gain,
    moe_gain,
    route_weight,
    anchor_table,
    first_weight,
    second_weight,
):
    tok_rows = tokens.shape[1]
    model_width = tokens.shape[2]
    score_scale = HEAD_DIM ** (-0.5)
    query_first = lax.axis_index("blk") * tok_rows
    local_experts = first_weight.shape[0]
    experts_all = local_experts * lax.axis_size("expert")
    capacity = tok_rows // experts_all
    head_shape = (tok_rows, HEADS, HEAD_DIM)
    seq_rows = tok_rows * lax.axis_size("blk")
    route_ids = routes[0, :, 0]
    route_onehot = (
        route_ids[:, None] == lax.broadcasted_iota(jnp.int32, (tok_rows, experts_all), 1)
    ).astype(jnp.float32)
    count_rows = jnp.sum(route_onehot, axis=0)
    total_counts = lax.psum(count_rows.astype(jnp.int32), ("blk", "expert"))
    block_input = tokens[0].astype(jnp.float32)
    normed_attn, attn_norm_back = jax.vjp(layer_norm, block_input, attn_gain)
    normed_low = normed_attn.astype(jnp.bfloat16)
    query_key_value_mix = jnp.dot(
        normed_low, qkv_weight, preferred_element_type=jnp.float32
    ).astype(jnp.bfloat16)
    query_flat = query_key_value_mix[:, :model_width]
    queries = query_flat.reshape(head_shape)
    key_local = query_key_value_mix[:, model_width : 2 * model_width]
    value_local = query_key_value_mix[:, 2 * model_width :]

    def forward_step(carried, blocks, key_first):
        running_top, running_sum, running_out = carried
        key_rows = blocks[0].reshape(blocks[0].shape[0], HEADS, HEAD_DIM)
        value_rows = blocks[1].reshape(blocks[1].shape[0], HEADS, HEAD_DIM)
        scores, allowed = masked_scores(queries, key_rows, query_first, key_first, score_scale)
        top_new = jnp.maximum(running_top, jnp.max(jnp.where(allowed, scores, MASKED), axis=2))
        weights = jnp.where(allowed, jnp.exp(scores - top_new[:, :, None]), 0.0)
        factor = jnp.exp(running_top - top_new)
        running_sum = running_sum * factor + jnp.sum(weights, axis=2)
        running_out = running_out * factor.T[:, :, None] + jnp.einsum(
            "hqk,khd->qhd",
            weights.astype(jnp.bfloat16),
            value_rows,
            preferred_element_type=jnp.float32,
        )
        return (top_new, running_sum, running_out)

    initial = (
        jnp.full((HEADS, tok_rows), MASKED, jnp.float32),
        jnp.zeros((HEADS, tok_rows), jnp.float32),
        jnp.zeros(head_shape, jnp.float32),
    )
    running_top, running_sum, running_out = over_blocks(
        forward_step,
        initial,
        (
            lax.all_gather(key_local, "blk", axis=0, tiled=True),
            lax.all_gather(value_local, "blk", axis=0, tiled=True),
        ),
        tok_rows,
    )
    attention_result = running_out / running_sum.T[:, :, None]
    log_total = running_top + jnp.log(running_sum)
    attended_low = attention_result.reshape(tok_rows, model_width).astype(jnp.bfloat16)
    residual_stream = block_input + jnp.dot(
        attended_low, proj_weight, preferred_element_type=jnp.float32
    )
    normed_moe, moe_norm_back = jax.vjp(layer_norm, residual_stream, moe_gain)

    def gate_of(normalized_rows, route_matrix, anchors):
        return router_gate(normalized_rows, route_matrix, anchors, route_onehot)

    gate_value, gate_back = jax.vjp(gate_of, normed_moe, route_weight, anchor_table)
    order_rows = priority[0, 0]
    same_route = route_ids[:, None] == route_ids[None, :]
    earlier = order_rows[None, :] < order_rows[:, None]
    slot_ids = jnp.sum((same_route & earlier).astype(jnp.int32), axis=1)
    target = jnp.where(slot_ids < capacity, route_ids * capacity + slot_ids, -1)
    selector = lax.broadcasted_iota(jnp.int32, (tok_rows, tok_rows), 0) == target[None, :]
    selector_low = selector.astype(jnp.bfloat16)
    outgoing = jnp.dot(
        selector_low, normed_moe.astype(jnp.bfloat16), preferred_element_type=jnp.float32
    )
    outgoing = outgoing.astype(jnp.bfloat16).reshape(experts_all, capacity, model_width)
    arrived = lax.all_to_all(outgoing, "expert", split_axis=0, concat_axis=0, tiled=True)
    sources = arrived.shape[0] // local_experts
    grouped = arrived.reshape(sources, local_experts, arrived.shape[1], arrived.shape[2])
    hidden = jnp.einsum("secd,edf->secf", grouped, first_weight, preferred_element_type=jnp.float32)
    act_low = jax.nn.gelu(hidden).astype(jnp.bfloat16)
    result = jnp.einsum(
        "secf,efd->secd", act_low, second_weight, preferred_element_type=jnp.float32
    )
    result = result.astype(jnp.bfloat16).reshape(arrived.shape)
    returned = lax.all_to_all(result, "expert", split_axis=0, concat_axis=0, tiled=True)
    returned, arrived = (returned, arrived)
    fetched = jnp.einsum(
        "st,sd->td",
        selector_low,
        returned.reshape(tok_rows, model_width),
        preferred_element_type=jnp.float32,
    )
    block_out = (residual_stream + gate_value[:, None] * fetched).astype(jnp.bfloat16)[None]
    grad_out = cotangent[0].astype(jnp.float32) * loss_mask[0].astype(jnp.float32)[:, None]
    grad_fetched = grad_out * gate_value[:, None]
    grad_gate = jnp.sum(grad_out * fetched, axis=1)
    grad_slots = jnp.dot(selector.astype(jnp.float32), grad_fetched, precision=TOP_PRECISION)
    grad_slots = grad_slots.astype(jnp.bfloat16).reshape(experts_all, capacity, model_width)
    grad_arrived = lax.all_to_all(grad_slots, "expert", split_axis=0, concat_axis=0, tiled=True)
    sources = grad_arrived.shape[0] // local_experts
    slot_shape = (sources, local_experts, capacity, model_width)
    grouped_in = arrived.reshape(slot_shape)
    grouped_grad = grad_arrived.reshape(slot_shape)
    hidden = jnp.einsum(
        "secd,edf->secf", grouped_in, first_weight, preferred_element_type=jnp.float32
    )
    act_low = jax.nn.gelu(hidden).astype(jnp.bfloat16)
    grad_second = jnp.einsum(
        "secf,secd->efd", act_low, grouped_grad, preferred_element_type=jnp.float32
    )
    grad_act = jnp.einsum(
        "secd,efd->secf", grouped_grad, second_weight, preferred_element_type=jnp.float32
    )
    unused, gelu_back = jax.vjp(jax.nn.gelu, hidden)
    grad_hidden = gelu_back(grad_act)[0].astype(jnp.bfloat16)
    grad_first = jnp.einsum(
        "secd,secf->edf", grouped_in, grad_hidden, preferred_element_type=jnp.float32
    )
    grad_sent = jnp.einsum(
        "secf,edf->secd", grad_hidden, first_weight, preferred_element_type=jnp.float32
    )
    grad_sent = grad_sent.astype(jnp.bfloat16).reshape(grad_arrived.shape)
    grad_returned = lax.all_to_all(grad_sent, "expert", split_axis=0, concat_axis=0, tiled=True)
    grad_first, grad_second = (
        lax.psum_scatter(
            grad_first.astype(jnp.bfloat16), "blk", scatter_dimension=2, tiled=True
        ).astype(jnp.float32),
        lax.psum_scatter(
            grad_second.astype(jnp.bfloat16), "blk", scatter_dimension=1, tiled=True
        ).astype(jnp.float32),
    )
    grad_moe_rows = jnp.einsum(
        "st,sd->td",
        selector_low,
        grad_returned.reshape(tok_rows, model_width),
        preferred_element_type=jnp.float32,
    )
    grad_router_rows, grad_route, grad_anchor = gate_back(grad_gate)
    grad_residual_norm, grad_moe_gain = moe_norm_back(grad_moe_rows + grad_router_rows)
    grad_residual = grad_out + grad_residual_norm
    grad_attn_low = grad_residual.astype(jnp.bfloat16)
    grad_proj = jnp.dot(attended_low.T, grad_attn_low, preferred_element_type=jnp.float32)
    grad_attended_flat = jnp.dot(
        grad_attn_low, proj_weight.T, preferred_element_type=jnp.float32
    ).astype(jnp.bfloat16)
    grad_attended = grad_attended_flat.reshape(head_shape)
    delta_rows = jnp.sum(grad_attended.astype(jnp.float32) * attention_result, axis=2).T
    key_all, value_all = (
        lax.all_gather(key_local, "blk", axis=0, tiled=True),
        lax.all_gather(value_local, "blk", axis=0, tiled=True),
    )
    block_count = seq_rows // tok_rows
    key_blocks = key_all.reshape(block_count, tok_rows, model_width)
    value_blocks = value_all.reshape(block_count, tok_rows, model_width)

    def key_block_step(running_grad, packed):
        position, key_block, value_block = packed
        key_rows = key_block.reshape(head_shape)
        value_rows = value_block.reshape(head_shape)
        scores, allowed = masked_scores(
            queries, key_rows, query_first, position * tok_rows, score_scale
        )
        soft_rows = jnp.where(allowed, jnp.exp(scores - log_total[:, :, None]), 0.0)
        grad_values = jnp.einsum(
            "hqk,qhd->khd",
            soft_rows.astype(jnp.bfloat16),
            grad_attended,
            preferred_element_type=jnp.float32,
        )
        grad_soft = jnp.einsum(
            "qhd,khd->hqk", grad_attended, value_rows, preferred_element_type=jnp.float32
        )
        grad_scores = (soft_rows * (grad_soft - delta_rows[:, :, None])).astype(jnp.bfloat16)
        grad_keys = score_scale * jnp.einsum(
            "hqk,qhd->khd", grad_scores, queries, preferred_element_type=jnp.float32
        )
        running_grad = running_grad + score_scale * jnp.einsum(
            "hqk,khd->qhd", grad_scores, key_rows, preferred_element_type=jnp.float32
        )
        term = jnp.concatenate(
            [grad_keys.reshape(tok_rows, model_width), grad_values.reshape(tok_rows, model_width)],
            axis=1,
        )
        return (running_grad, term)

    grad_queries, stacked_terms = lax.scan(
        key_block_step,
        jnp.zeros(head_shape, jnp.float32),
        (jnp.arange(block_count, dtype=jnp.int32), key_blocks, value_blocks),
    )
    all_terms = stacked_terms.reshape(seq_rows, 2 * model_width)
    key_value_grads = lax.psum_scatter(
        all_terms.astype(jnp.bfloat16), "blk", scatter_dimension=0, tiled=True
    ).astype(jnp.float32)
    grad_query_rows = grad_queries.reshape(tok_rows, model_width)
    grad_qkv_rows = jnp.concatenate([grad_query_rows, key_value_grads], axis=1).astype(jnp.bfloat16)
    grad_qkv = jnp.dot(normed_low.T, grad_qkv_rows, preferred_element_type=jnp.float32)
    grad_normed = jnp.dot(grad_qkv_rows, qkv_weight.T, preferred_element_type=jnp.float32)
    grad_source_norm, grad_attn_gain = attn_norm_back(grad_normed)
    grad_tokens = (grad_residual + grad_source_norm)[None]
    grad_qkv, grad_proj, grad_attn_gain, grad_moe_gain, grad_route, grad_anchor = lax.psum(
        (grad_qkv, grad_proj, grad_attn_gain, grad_moe_gain, grad_route, grad_anchor),
        ("blk", "expert"),
    )
    histogram_out = histogram + total_counts
    return (
        block_out,
        grad_tokens,
        grad_qkv,
        grad_proj,
        grad_attn_gain,
        grad_moe_gain,
        grad_route,
        grad_anchor,
        grad_first,
        grad_second,
        histogram_out,
    )


MESH = pl.DeviceIdType.MESH
F32 = jnp.float32
BF16 = jnp.bfloat16
VMEM_BYTES = 58 * 1024 * 1024


def dot(left, right, precision=None):
    return lax.dot_general(
        left, right, (((1,), (0,)), ((), ())), precision=precision, preferred_element_type=F32
    )


def dot_nt(left, right, precision=None):
    return lax.dot_general(
        left, right, (((1,), (1,)), ((), ())), precision=precision, preferred_element_type=F32
    )


def dot_tn(left, right, precision=None):
    return lax.dot_general(
        left, right, (((0,), (0,)), ((), ())), precision=precision, preferred_element_type=F32
    )


def rows_at(index, size):
    return pl.ds(pl.multiple_of(index * size, size), size)


def places():
    blk = lax.axis_index("blk")
    expert = lax.axis_index("expert")
    return blk, expert, blk + 1 - 2 * lax.rem(blk, 2), lax.rem(blk + 2, 4), 3 - blk


def greet(peers):
    barrier = pltpu.get_barrier_semaphore()
    for peer in peers:
        pl.semaphore_signal(barrier, inc=1, device_id=peer, device_id_type=MESH)
    return lambda: pl.semaphore_wait(barrier, len(peers))


def push(src, dst, sems, index, peer):
    copy = pltpu.make_async_remote_copy(
        src_ref=src,
        dst_ref=dst,
        send_sem=sems.at[0, index],
        recv_sem=sems.at[1, index],
        device_id=peer,
        device_id_type=MESH,
    )
    copy.start()
    return copy


def standardise(values):
    average = jnp.mean(values, axis=-1, keepdims=True)
    centered = values - average
    scale = lax.rsqrt(jnp.mean(centered * centered, axis=-1, keepdims=True) + EPSILON)
    return centered * scale, scale


def lower_triangle(keys, queries):
    return lax.broadcasted_iota(jnp.int32, (keys, queries), 0) <= lax.broadcasted_iota(
        jnp.int32, (keys, queries), 1
    )


class BlockGather:
    def __init__(self, part, sems, base):
        self.part, self.sems, self.base = part, sems, base

    def send(self, blk, half, index, peer):
        ref = self.part(blk, half)
        return push(ref, ref, self.sems, self.base + index, peer)

    def start(self):
        blk, expert, bx, by, bd = places()
        self.copies = [
            self.send(blk, 0, 0, (bx, expert)),
            self.send(blk, 1, 1, (by, expert)),
            self.send(blk, 1, 2, (bx, expert)),
            self.send(blk, 0, 3, (by, expert)),
        ]

    def forward(self):
        blk, expert, bx, by, bd = places()
        self.copies[0].wait_recv()
        self.copies.append(self.send(bx, 0, 4, (by, expert)))
        self.copies[1].wait_recv()
        self.copies.append(self.send(by, 1, 5, (bx, expert)))

    def wait_neighbours(self):
        self.copies[2].wait_recv()
        self.copies[3].wait_recv()

    def wait_diagonal(self):
        self.copies[4].wait_recv()
        self.copies[5].wait_recv()

    def wait_sends(self):
        for copy in self.copies:
            copy.wait_send()


def row_halves(buf, rows):
    size = rows // 2
    return lambda blk, half: buf.at[pl.ds(pl.multiple_of(blk * rows + half * size, size), size)]


class ExpertExchange:
    def __init__(self, src, dst, sems, rows, dst_base=0):
        self.src, self.dst, self.sems, self.rows = src, dst, sems, rows
        blk, expert = lax.axis_index("blk"), lax.axis_index("expert")
        self.place = pl.ds(pl.multiple_of(dst_base + expert * rows, rows), rows)
        side, step = expert // 4, lax.rem(expert, 4)
        self.near = [side * 4 + lax.rem(step + shift, 4) for shift in range(1, 4)]
        self.far = [(1 - side) * 4 + lax.rem(step + shift, 4) for shift in range(4)]
        self.copies = [[], []]

    def start(self, far):
        blk, expert = lax.axis_index("blk"), lax.axis_index("expert")
        for n, peer in enumerate(self.far if far else self.near):
            self.copies[far].append(
                push(self.src.at[rows_at(peer, self.rows)], self.dst.at[self.place], self.sems,
                     n + 3 * far, (blk, peer))
            )
        if not far:
            self.dst[self.place] = self.src[rows_at(expert, self.rows)]

    def wait_recv(self, far):
        for copy in self.copies[far]:
            copy.wait_recv()

    def wait_sends(self):
        for copy in self.copies[0] + self.copies[1]:
            copy.wait_send()

    def start_all(self):
        self.start(1)
        self.start(0)

    def wait_all(self):
        self.wait_recv(0)
        self.wait_recv(1)
        self.wait_sends()


def blk_peers():
    blk, expert, bx, by, bd = places()
    return [(bx, expert), (by, expert), (bd, expert)]


def expert_peers():
    blk, expert = lax.axis_index("blk"), lax.axis_index("expert")
    n = lax.axis_size("expert")
    return [(blk, lax.rem(expert + shift, n)) for shift in range(1, n)]


def attend_kernel(
    tok_ref, gain_ref, wqkv_ref, cot_ref, rows_ref, cols_ref,
    nall_ref, qkv_ref, out_ref, lse_ref, att_ref, target_row_ref, target_col_ref, cot_in_ref,
    w_s, wt_s, k_s, att_s, cot_s, w_sem, gather_sems, cot_sems, att_sems,
):
    blk, expert, bx, by, bd = places()
    tok = tok_ref.shape[0]
    width = tok_ref.shape[1]
    heads = HEADS // 4
    group = heads * HEAD_DIM
    arrived = greet(blk_peers() + expert_peers())
    odd = lax.rem(blk, 2)
    loads = []
    for part in range(3):
        first = pl.multiple_of(part * width + blk * group - odd * 64, 128)
        loads.append(
            pltpu.make_async_copy(wqkv_ref.at[:, pl.ds(first, 256)], w_s.at[part], w_sem.at[part])
        )
        loads[-1].start()
    xhat, _ = standardise(tok_ref[...].astype(F32))
    nall_ref[rows_at(blk, tok), :] = (xhat * gain_ref[...]).astype(BF16)
    arrived()
    gather = BlockGather(row_halves(nall_ref, tok), gather_sems, 0)
    gather.start()

    capacity = tok // 8
    route_row, prio_row, mask_row = rows_ref[0:1, :], rows_ref[1:2, :], rows_ref[2:3, :]
    route_col, prio_col = cols_ref[:, 0:1], cols_ref[:, 1:2]
    same = route_col == route_row
    slot_row = jnp.sum(jnp.where(same & (prio_col < prio_row), 1.0, 0.0), axis=0, keepdims=True)
    slot_col = jnp.sum(jnp.where(same & (prio_row < prio_col), 1.0, 0.0), axis=1, keepdims=True)
    target_row = jnp.where(slot_row < capacity, route_row * capacity + slot_row, -1.0)
    target_col = jnp.where(slot_col < capacity, route_col * capacity + slot_col, -1.0)
    target_row_ref[...] = jnp.broadcast_to(target_row, target_row_ref.shape)
    target_col_ref[...] = jnp.broadcast_to(target_col, target_col_ref.shape)
    slots = lax.broadcasted_iota(jnp.int32, (tok, tok), 0).astype(F32)
    chosen = jnp.where((slots == target_row) & (mask_row > 0.0), 1.0, 0.0).astype(BF16)
    cot_s[...] = dot(chosen, cot_ref[...]).astype(BF16)
    cot_move = ExpertExchange(cot_s, cot_in_ref, cot_sems, capacity)
    cot_move.start_all()

    for part in range(3):
        loads[part].wait()
        wide = w_s[part]
        narrow = jnp.where(odd == 1, wide[:, 64:256], wide[:, 0:192])
        wt_s[part * group : (part + 1) * group, :] = narrow.T

    def project(where):
        cols = rows_at(where, tok)
        mixed = dot_nt(wt_s[...], nall_ref[cols, :]).astype(BF16)
        qkv_ref[0:group, cols] = mixed[0:group] * BF16(HEAD_DIM**-0.5)
        qkv_ref[group:, cols] = mixed[group:]
        for head in range(heads):
            k_s[head, cols, :] = mixed[group + head * 64 : group + (head + 1) * 64].T

    project(blk)
    gather.forward()
    gather.wait_neighbours()
    project(bx)
    project(by)
    gather.wait_diagonal()
    project(bd)

    half = tok // 2

    def scores(i, head):
        q = qkv_ref[head * 64 : (head + 1) * 64, i * tok : (i + 1) * tok]
        upper = dot(k_s[head, i * tok : i * tok + half, :], q)
        upper = jnp.where(lower_triangle(half, tok), upper, MASKED)
        lower = dot(k_s[head, i * tok + half : (i + 1) * tok, :], q[:, half:])
        lower = jnp.where(lower_triangle(half, half), lower, MASKED)
        top = jnp.max(upper, axis=0, keepdims=True)
        low_top = jnp.max(lower, axis=0, keepdims=True)
        top = jnp.concatenate([top[:, :half], jnp.maximum(top[:, half:], low_top)], axis=1)
        if i == 0:
            return top, upper, lower, None
        past = dot(k_s[head, 0 : i * tok, :], q)
        return jnp.maximum(top, jnp.max(past, axis=0, keepdims=True)), upper, lower, past

    sends = []

    def finish(i, head, found):
        top, upper, lower, past = found
        v = qkv_ref[2 * group + head * 64 : 2 * group + (head + 1) * 64, :]
        upper = jnp.exp(upper - top)
        lower = jnp.exp(lower - top[:, half:])
        total = jnp.sum(upper, axis=0, keepdims=True)
        low_total = jnp.sum(lower, axis=0, keepdims=True)
        total = jnp.concatenate([total[:, :half], total[:, half:] + low_total], axis=1)
        result = dot(v[:, i * tok : i * tok + half], upper.astype(BF16))
        low_result = dot(v[:, i * tok + half : (i + 1) * tok], lower.astype(BF16))
        result = jnp.concatenate([result[:, :half], result[:, half:] + low_result], axis=1)
        if i:
            past = jnp.exp(past - top)
            total = total + jnp.sum(past, axis=0, keepdims=True)
            result = result + dot(v[:, 0 : i * tok], past.astype(BF16))
        result = result / total
        place = slice(head * 64, (head + 1) * 64)
        out_ref[place, i * tok : (i + 1) * tok] = result
        lse_ref[head : head + 1, i * tok : (i + 1) * tok] = top + jnp.log(total)
        att_s[place, i * tok : (i + 1) * tok] = result.astype(BF16)
        there = pl.ds(pl.multiple_of(blk * group + head * 64, 64), 64)

        def copy():
            return pltpu.make_async_remote_copy(
                src_ref=att_s.at[place, i * tok : (i + 1) * tok],
                dst_ref=att_ref.at[there],
                send_sem=att_sems.at[0, i * heads + head],
                recv_sem=att_sems.at[1, blk * heads + head],
                device_id=(i, expert),
                device_id_type=MESH,
            )

        @pl.when(blk != i)
        def _():
            copy().start()

        @pl.when(blk == i)
        def _():
            att_ref[there, :] = result.astype(BF16)

        sends.append((i, copy))

    before = None
    for i in range(4):
        for head in range(heads):
            found = scores(i, head)
            if before is not None:
                finish(*before)
            before = (i, head, found)
    finish(*before)

    for i, copy in sends:
        @pl.when(blk != i)
        def _():
            copy().wait_send()

    for source in range(4):
        @pl.when(blk != source)
        def _():
            for head in range(heads):
                there = pl.ds(source * group + head * 64, 64)
                pltpu.make_async_remote_copy(
                    src_ref=att_s.at[0:64, 0:tok],
                    dst_ref=att_ref.at[there],
                    send_sem=att_sems.at[0, source * heads + head],
                    recv_sem=att_sems.at[1, source * heads + head],
                    device_id=(source, expert),
                    device_id_type=MESH,
                ).wait_recv()

    cot_move.wait_all()
    gather.wait_sends()


def gelu_pair(hidden):
    squared = hidden * hidden
    curve = jnp.tanh(0.7978845608028654 * hidden * (1.0 + 0.044715 * squared))
    half = 0.5 * (1.0 + curve)
    slope = half + 0.5 * hidden * (1.0 - curve * curve) * (
        0.7978845608028654 * (1.0 + 0.134145 * squared)
    )
    return hidden * half, slope


def spread(row, size):
    shape = (size, row.shape[1])
    eye = lax.broadcasted_iota(jnp.int32, shape, 0) == lax.broadcasted_iota(jnp.int32, shape, 1)
    return jnp.sum(jnp.where(eye, row, 0.0), axis=1, keepdims=True)


def flatten(column, width):
    shape = (column.shape[0], width)
    eye = lax.broadcasted_iota(jnp.int32, shape, 0) == lax.broadcasted_iota(jnp.int32, shape, 1)
    return jnp.sum(jnp.where(eye, column, 0.0), axis=0, keepdims=True)


def expert_kernel(
    att_ref, tok_ref, proj_ref, gain_ref, route_ref, anchor_ref, cols_ref, target_row_ref,
    target_col_ref, cot_ref, cot_in_ref, first_ref, second_ref,
    result_ref, residual_ref, gate_ref, grad_residual_ref, grad_att_ref, grad_proj_ref, small_ref,
    buf_ref, cots_ref, gates_ref,
    first_s, second_s, go_s, gate_s, grad_s, back_s, score_s, score_in_s, res_acc, sent_acc, grad_in_s,
    w_sem, go_sems, gate_sems, back_sems, score_sems, cots_sems, buf_sems, gates_sems,
):
    blk, expert, bx, by, bd = places()
    tok, width = tok_ref.shape
    experts = 8
    capacity = tok // experts
    here = rows_at(blk, tok)
    arrived = greet(blk_peers() + expert_peers())
    loads = [
        pltpu.make_async_copy(first_ref, first_s, w_sem.at[0]),
        pltpu.make_async_copy(second_ref, second_s, w_sem.at[1]),
    ]
    for load in loads:
        load.start()
    cots_ref[here, :] = cot_in_ref[...]

    residual = tok_ref[...].astype(F32) + dot_tn(att_ref[...], proj_ref[...])
    residual_ref[...] = residual
    xhat, scale = standardise(residual)
    normed = xhat * gain_ref[...]
    normed_low = normed.astype(BF16)
    target_row, target_col = target_row_ref[0:1, :], target_col_ref[:, 0:1]
    slots = lax.broadcasted_iota(jnp.int32, (tok, tok), 0).astype(F32)
    go_s[...] = dot(jnp.where(slots == target_row, 1.0, 0.0).astype(BF16), normed_low).astype(BF16)
    arrived()
    go = ExpertExchange(go_s, buf_ref, go_sems, capacity, blk * tok)
    go.start(0)
    go.start(1)
    cots = BlockGather(row_halves(cots_ref, tok), cots_sems, 0)
    cots.start()

    route_col = cols_ref[:, 0:1]
    projected = dot(normed, route_ref[...], TOP_PRECISION)
    unit_scale = lax.rsqrt(1.0 + jnp.sum(projected * projected, axis=1, keepdims=True))
    unit = projected * unit_scale
    anchor = anchor_ref[...]
    anchor_scale = lax.rsqrt(1.0 + jnp.sum(anchor * anchor, axis=1, keepdims=True))
    anchor_unit = anchor * anchor_scale
    logits = dot_nt(unit, anchor_unit, TOP_PRECISION) / ROUTER_SOFTNESS
    soft = jnp.exp(logits - jnp.max(logits, axis=1, keepdims=True))
    soft = soft / jnp.sum(soft, axis=1, keepdims=True)
    onehot = jnp.where(
        lax.broadcasted_iota(jnp.int32, (tok, experts), 1).astype(F32) == route_col, 1.0, 0.0
    )
    gate = jnp.sum(soft * onehot, axis=1, keepdims=True)
    gate_ref[...] = jnp.broadcast_to(gate, gate_ref.shape)
    lane = lax.broadcasted_iota(jnp.int32, (tok, 128), 1).astype(F32)
    lane = jnp.where(lane < capacity, lane, 1e6)
    for peer in range(experts):
        row = jnp.sum(
            jnp.where(target_col == peer * capacity + lane, gate, 0.0), axis=0, keepdims=True
        )
        gate_s[peer * 8 : (peer + 1) * 8, :] = jnp.broadcast_to(row, (8, 128))
    gates = ExpertExchange(gate_s, gates_ref, gate_sems, 8, blk * 64)
    gates.start(0)
    gates.start(1)

    back = ExpertExchange(grad_s, back_s, back_sems, capacity)
    scores = ExpertExchange(score_s, score_in_s, score_sems, 8)
    side = expert // 4
    count = 4 * capacity
    tile = 768
    tiles = first_s.shape[1] // tile
    bufs = []
    for far in range(2):
        first_source = 4 * (side + far - 2 * side * far)
        rows = pl.ds(pl.multiple_of(first_source * capacity, count), count)
        rows_in_buf = pl.ds(pl.multiple_of(blk * tok + first_source * capacity, count), count)
        go.wait_recv(far)

        def halves(block, half, first=first_source * capacity):
            row = pl.multiple_of(block * tok + first + half * (count // 2), count // 2)
            return buf_ref.at[pl.ds(row, count // 2)]

        bufs.append(BlockGather(halves, buf_sems, 6 * far))
        bufs[far].start()
        if not far:
            cots.forward()
            for load in loads:
                load.wait()
        gates.wait_recv(far)
        for n in range(4):
            row = gates_ref[pl.ds(pl.multiple_of(blk * 64 + (first_source + n) * 8, 8), 8), :][0:1, :]
            chunk = pl.ds(pl.multiple_of((first_source + n) * capacity, capacity), capacity)
            grad_in_s[n * capacity : (n + 1) * capacity, :] = (
                cot_in_ref[chunk, :].astype(F32) * spread(row, capacity)
            ).astype(BF16)
        x = buf_ref[rows_in_buf, :]
        grad_in = grad_in_s[0:count, :]
        for t in range(tiles):
            cut = slice(t * tile, (t + 1) * tile)
            hidden = dot(x, first_s[:, cut])
            act, slope = gelu_pair(hidden)
            part = dot(act.astype(BF16), second_s[cut, :])
            grad_hidden = (dot_nt(grad_in, second_s[cut, :]) * slope).astype(BF16)
            sent = dot_nt(grad_hidden, first_s[:, cut])
            if t == 0:
                res_acc[...] = part
                sent_acc[...] = sent
            else:
                res_acc[...] += part
                sent_acc[...] += sent
            if far and t == 1:
                bufs[0].forward()
        result = res_acc[...].astype(BF16)
        score = jnp.sum(
            result.astype(F32) * cot_in_ref[rows, :].astype(F32), axis=1, keepdims=True)
        for n in range(4):
            row = flatten(score[n * capacity : (n + 1) * capacity], 128)
            there = pl.ds(pl.multiple_of((first_source + n) * 8, 8), 8)
            score_s[there, :] = jnp.broadcast_to(row, (8, 128))
        scores.start(far)
        grad_s[rows, :] = sent_acc[...].astype(BF16)
        back.start(far)
        result_ref[rows, :] = result
    gates_here = gates_ref.at[rows_at(blk, 64)]
    gates_out = [
        push(gates_here, gates_here, gates_sems, n, peer) for n, peer in enumerate(blk_peers())
    ]
    grad_out = cot_ref[...].astype(F32) * cols_ref[:, 2:3]

    scores.wait_recv(0)
    scores.wait_recv(1)
    grad_gate = jnp.zeros((tok, 1), F32)
    for peer in range(experts):
        row = score_in_s[peer * 8 : peer * 8 + 1, :]
        grad_gate += jnp.sum(
            jnp.where(target_col == peer * capacity + lane, row, 0.0), axis=1, keepdims=True
        )
    grad_logits = grad_gate * gate * (onehot - soft) / ROUTER_SOFTNESS
    grad_unit = dot(grad_logits, anchor_unit, TOP_PRECISION)
    grad_projected = unit_scale * (
        grad_unit - unit * jnp.sum(unit * grad_unit, axis=1, keepdims=True)
    )
    grad_anchor_unit = dot_tn(grad_logits, unit, TOP_PRECISION)
    grad_anchor = anchor_scale * (
        grad_anchor_unit
        - anchor_unit * jnp.sum(anchor_unit * grad_anchor_unit, axis=1, keepdims=True)
    )
    rdim = route_ref.shape[1]
    small_ref[...] = jnp.zeros_like(small_ref)
    small_ref[0:rdim, :] = dot_tn(grad_projected, normed, TOP_PRECISION)
    small_ref[rdim : rdim + experts, 0:rdim] = grad_anchor
    counts = jnp.sum(onehot, axis=0, keepdims=True)
    small_ref[rdim + experts + 2 : rdim + experts + 3, 0:experts] = counts
    router_rows = dot_nt(grad_projected, route_ref[...], TOP_PRECISION)

    bufs[1].forward()
    back.wait_recv(0)
    back.wait_recv(1)
    lanes = lax.broadcasted_iota(jnp.int32, (tok, tok), 1).astype(F32)
    moe_rows = dot(jnp.where(lanes == target_col, 1.0, 0.0).astype(BF16), back_s[...])
    grad_normed = moe_rows + router_rows
    small_ref[rdim + experts : rdim + experts + 1, :] = jnp.sum(
        grad_normed * xhat, axis=0, keepdims=True
    )
    grad_xhat = grad_normed * gain_ref[...]
    grad_residual = grad_out + scale * (
        grad_xhat
        - jnp.mean(grad_xhat, axis=1, keepdims=True)
        - xhat * jnp.mean(grad_xhat * xhat, axis=1, keepdims=True)
    )
    grad_residual_ref[...] = grad_residual
    grad_low = grad_residual.astype(BF16)
    grad_att_ref[...] = dot_nt(proj_ref[...], grad_low).astype(BF16)
    grad_proj_ref[...] = dot(att_ref[...], grad_low).astype(BF16)

    for gather in (cots, bufs[0], bufs[1]):
        gather.wait_neighbours()
        gather.wait_diagonal()
        gather.wait_sends()
    for exchange in (go, gates, back, scores):
        exchange.wait_sends()
    for copy in gates_out:
        copy.wait()


def attend_back_kernel(
    grad_att_ref, qkv_ref, out_ref, lse_ref, nall_ref, result_ref, residual_ref, gate_ref,
    target_col_ref, gain_ref, wqkv_ref, tok_ref, grad_residual_ref, grad_proj_ref, small_ref,
    buf_ref, cots_ref, gates_ref, first_ref, second_ref,
    block_out_ref, grad_tokens_ref, shared_ref, small_out_ref, grad_first_ref, grad_second_ref,
    do_t, dq_s, dqkv_s, home_s, q_s, k_s, v_s, do_s, back_s, wt_s, proj_in, part_s, sum_s,
    core_out, core_in, line_out, line_in, small_a, small_in, small_b, row_out, row_in,
    first_s, second_s, slot_s, rows_s,
    att_sems, back_sems, home_sems, proj_sems, core_sems, line_sems, join_sems, small_sems,
    row_sems, ring_sems, pair_sems, load_sems,
):
    blk, expert, bx, by, bd = places()
    tok = grad_att_ref.shape[1]
    width = grad_att_ref.shape[0]
    heads = HEADS // 4
    group = heads * HEAD_DIM
    here = rows_at(blk, tok)
    length = qkv_ref.shape[1]
    core = lax.rem(expert, 2)
    line = expert // 2
    lines = 4
    half = width // 2
    other = (blk, expert + 1 - 2 * core)
    mine_lanes = pl.ds(pl.multiple_of(core * half, 128), half)
    other_lanes = pl.ds(pl.multiple_of((1 - core) * half, 128), half)
    line_peers = [(blk, lax.rem(line + shift, lines) * 2 + core) for shift in range(1, lines)]
    arrived = greet(blk_peers() + expert_peers())
    odd = lax.rem(blk, 2)
    quarter = first_s.shape[1]

    def load(src, dst, index):
        copy = pltpu.make_async_copy(src, dst, load_sems.at[index])
        copy.start()
        return copy

    weights = [
        load(first_ref.at[:, rows_at(blk, quarter)], first_s, 0),
        load(second_ref.at[rows_at(blk, quarter)], second_s, 1),
    ]
    slot_loads = []

    def load_slots(t):
        cut = slice(t * tok, (t + 1) * tok)
        slot_loads.append((
            load(buf_ref.at[cut], slot_s.at[t % 2, 0], 2 + t % 2),
            load(cots_ref.at[cut], slot_s.at[t % 2, 1], 4 + t % 2),
        ))

    load_slots(0)
    rows_load = [load(residual_ref, rows_s, 6)]
    arrived()
    mine = rows_at(blk, group)
    att_copies = [
        push(grad_att_ref.at[rows_at(peer[0], group)], do_t.at[:, here], att_sems, n, peer)
        for n, peer in enumerate(blk_peers())
    ]
    back = ExpertExchange(result_ref, back_s, back_sems, tok // 8)
    back.start_all()
    small_core = push(small_ref.at[:, other_lanes], small_in.at[0], small_sems, 0, other)
    do_t[:, here] = grad_att_ref[mine, :]
    for part in range(3):
        first = pl.multiple_of(part * width + blk * group - odd * 64, 128)
        wide = wqkv_ref[:, pl.ds(first, 256)]
        narrow = jnp.where(odd == 1, wide[:, 64:256], wide[:, 0:192]).T
        for head in range(heads):
            place = head * 192 + part * 64
            wt_s[place : place + 64, :] = narrow[head * 64 : (head + 1) * 64]

    def expert_weights(t):
        if t == 0:
            for copy in weights:
                copy.wait()
        if t < 3:
            load_slots(t + 1)
        for copy in slot_loads[t]:
            copy.wait()
        x = slot_s[t % 2, 0]
        rates = [spread(gates_ref[t * 64 + n * 8 : t * 64 + n * 8 + 1, :], 64) for n in range(8)]
        rate = jnp.concatenate(rates, axis=0)
        grad_in = (slot_s[t % 2, 1].astype(F32) * rate).astype(BF16)
        act, slope = gelu_pair(dot(x, first_s[...]))
        grad_hidden = (dot_nt(grad_in, second_s[...]) * slope).astype(BF16)
        grad_second = dot_tn(act.astype(BF16), grad_in)
        grad_first = dot_tn(x, grad_hidden)
        if t == 0:
            grad_second_ref[...] = grad_second
            grad_first_ref[...] = grad_first
        else:
            grad_second_ref[...] += grad_second
            grad_first_ref[...] += grad_first

    expert_weights(0)
    small_core.wait()
    small_a[...] = small_ref[:, mine_lanes] + small_in[0]
    small_in[1 + line] = small_a[...]
    small_line = [
        push(small_a, small_in.at[1 + line], small_sems, 1 + n, peer)
        for n, peer in enumerate(line_peers)
    ]
    expert_weights(1)
    for copy in att_copies:
        copy.wait_recv()
    proj_copies = [
        push(grad_proj_ref.at[rows_at(peer[0], group)], proj_in.at[n], proj_sems, n, peer)
        for n, peer in enumerate(blk_peers())
    ]

    chunk_rows = group
    piece = chunk_rows // lines
    core_copies, line_copies, joins, gathers, pairs = {}, {}, {}, {}, []
    small_blk = []

    def chunk_at(c):
        return slice(c * chunk_rows, (c + 1) * chunk_rows)

    def shared_at(block, c, first, size):
        row = pl.multiple_of(block * width + c * chunk_rows + first, 16)
        return shared_ref.at[pl.ds(row, size), mine_lanes]

    def send_core(c):
        core_out[chunk_at(c), :] = part_s[chunk_at(c), other_lanes].astype(BF16)
        core_copies[c] = push(
            core_out.at[chunk_at(c)], core_in.at[chunk_at(c)], core_sems, c, other)

    def send_line(c):
        core_copies[c].wait()
        summed = part_s[chunk_at(c), mine_lanes] + core_in[chunk_at(c), :].astype(F32)
        sum_s[chunk_at(c), :] = summed
        line_out[chunk_at(c), :] = summed.astype(BF16)
        line_copies[c] = [
            push(
                line_out.at[pl.ds(
                    pl.multiple_of(c * chunk_rows + (peer[1] // 2) * piece, piece), piece)],
                line_in.at[c * 3 + n], line_sems, c * 3 + n, peer)
            for n, peer in enumerate(line_peers)
        ]

    def send_join(c):
        for copy in line_copies[c]:
            copy.wait()
        first = pl.multiple_of(c * chunk_rows + line * piece, piece)
        total = sum_s[pl.ds(first, piece), :]
        for n in range(3):
            total = total + line_in[c * 3 + n].astype(F32)
        row = pl.multiple_of(blk * width + c * chunk_rows + line * piece, 16)
        shared_ref[pl.ds(row, piece), mine_lanes] = total.astype(BF16)
        ref = shared_at(blk, c, line * piece, piece)
        joins[c] = [
            push(ref, ref, join_sems, c * 3 + n, peer) for n, peer in enumerate(line_peers)]

    def pair(block, c):
        ref = shared_at(block, c, 0, chunk_rows)
        pairs.append(push(ref, ref, pair_sems, len(pairs), other))

    def send_ring(c):
        for copy in joins[c]:
            copy.wait()
        size = chunk_rows // 2
        gathers[c] = BlockGather(
            lambda block, part: shared_at(block, c, part * size, size), ring_sems, c * 6)
        gathers[c].start()
        pair(blk, c)

    def forward(c):
        gathers[c].forward()

    def pair_neighbours(c):
        gathers[c].wait_neighbours()
        pair(bx, c)
        pair(by, c)

    def pair_diagonal(c):
        gathers[c].wait_diagonal()
        pair(bd, c)

    def sum_proj():
        for copy in proj_copies:
            copy.wait()
        part_s[chunk_at(3), :] = (
            (grad_proj_ref[mine, :].astype(F32) + proj_in[0].astype(F32))
            + (proj_in[1].astype(F32) + proj_in[2].astype(F32))
        )
        send_core(3)

    def sum_small():
        for copy in small_line:
            copy.wait()
        small_b[...] = (small_in[1] + small_in[2]) + (small_in[3] + small_in[4])
        small_in[5 + blk] = small_b[...]
        small_blk.extend(
            push(small_b, small_in.at[5 + blk], small_sems, 4 + n, peer)
            for n, peer in enumerate(blk_peers())
        )

    sent = []

    def send_home(head, part, block):
        src = slice(head * 192 + part * 64, head * 192 + (part + 1) * 64)
        there = pl.ds(pl.multiple_of(part * width + blk * group + head * 64, 64), 64)

        def copy():
            return pltpu.make_async_remote_copy(
                src_ref=dqkv_s.at[src, block * tok : (block + 1) * tok],
                dst_ref=home_s.at[there],
                send_sem=home_sems.at[0, (block * heads + head) * 3 + part],
                recv_sem=home_sems.at[1, (blk * heads + head) * 3 + part],
                device_id=(block, expert),
                device_id_type=MESH,
            )

        @pl.when(blk != block)
        def _():
            copy().start()

        @pl.when(blk == block)
        def _():
            home_s[there, :] = dqkv_s[src, block * tok : (block + 1) * tok]

        sent.append((block, copy))

    after = {
        (0, 0): [sum_small], (0, 1): [sum_proj], (0, 2): [lambda: send_line(3)],
        (1, 0): [lambda: send_line(0), lambda: send_join(3)],
        (1, 2): [lambda: send_join(0), lambda: send_ring(3)],
        (2, 0): [lambda: send_line(1), lambda: send_ring(0), lambda: forward(3)],
        (2, 2): [lambda: send_join(1), lambda: forward(0), lambda: pair_neighbours(3)],
    }
    gain_total = None
    for head in range(heads):
        cut = slice(head * 64, (head + 1) * 64)
        kt_cut = slice(group + head * 64, group + (head + 1) * 64)
        vt_cut = slice(2 * group + head * 64, 2 * group + (head + 1) * 64)
        q_s[...] = qkv_ref[cut, :].T
        k_s[...] = qkv_ref[kt_cut, :].T
        v_s[...] = qkv_ref[vt_cut, :].T
        do_s[...] = do_t[cut, :].T
        delta = jnp.sum(out_ref[cut, :] * do_t[cut, :].astype(F32), axis=0, keepdims=True)
        base = head * 192
        for j in range(4):
            keys = slice(j * tok, (j + 1) * tok)
            queries = slice(j * tok, length)
            s = dot(k_s[keys, :], qkv_ref[cut, queries])
            p = jnp.exp(s - lse_ref[head : head + 1, queries])
            allowed = lower_triangle(tok, length - j * tok)
            p = jnp.where(allowed, p, 0.0)
            dp = dot(v_s[keys, :], do_t[cut, queries])
            ds = (p * (dp - delta[:, queries])).astype(BF16)
            dv = dot(p.astype(BF16), do_s[queries, :])
            dk = dot(ds, q_s[queries, :])
            dqkv_s[base + 64 : base + 128, keys] = dk.T.astype(BF16)
            dqkv_s[base + 128 : base + 192, keys] = dv.T.astype(BF16)
            send_home(head, 1, j)
            send_home(head, 2, j)
            dq = dot(qkv_ref[kt_cut, keys], ds)
            if j == 0:
                dq_s[...] = dq
            else:
                dq_s[:, queries] += dq
            for action in after.get((head, j), ()):
                action()
        dqkv_s[base : base + 64, :] = (dq_s[...] * HEAD_DIM**-0.5).astype(BF16)
        for block in range(4):
            send_home(head, 0, block)
        grad_group = dot(dqkv_s[base : base + 192, :], nall_ref[...])
        part_s[chunk_at(head), :] = grad_group
        send_core(head)
        share = jnp.sum(
            grad_group * wt_s[base : base + 192, :].astype(F32), axis=0, keepdims=True)
        gain_total = share if gain_total is None else gain_total + share

    attn_gain = gain_total / gain_ref[...]
    row_out[0] = jnp.concatenate(
        [attn_gain[:, n * 128 : (n + 1) * 128] for n in range(width // 128)]
        + [jnp.zeros((8 - width // 128, 128), F32)], axis=0)
    row_core = push(row_out.at[0], row_in.at[0], row_sems, 0, other)
    send_ring(1)
    for copy in small_blk:
        copy.wait()
    small_out_ref[:, mine_lanes] = (small_in[5] + small_in[6]) + (small_in[7] + small_in[8])
    small_pair = push(
        small_out_ref.at[:, mine_lanes], small_out_ref.at[:, mine_lanes], small_sems, 7, other)
    send_line(2)
    row_core.wait()
    row_out[1] = row_out[0] + row_in[0]
    row_in[1 + line] = row_out[1]
    row_line = [
        push(row_out.at[1], row_in.at[1 + line], row_sems, 1 + n, peer)
        for n, peer in enumerate(line_peers)
    ]
    pair_neighbours(0)
    pair_diagonal(3)
    back.wait_all()
    lanes = lax.broadcasted_iota(jnp.int32, (tok, tok), 1).astype(F32)
    chosen = jnp.where(lanes == target_col_ref[:, 0:1], 1.0, 0.0).astype(BF16)
    fetched = dot(chosen, back_s[...])
    rows_load[0].wait()
    block_out_ref[...] = (rows_s[...] + gate_ref[:, 0:1] * fetched).astype(BF16)
    rows_load.append(load(grad_residual_ref, rows_s, 6))
    send_join(2)
    forward(1)
    for copy in row_line:
        copy.wait()
    row_out[2] = (row_in[1] + row_in[2]) + (row_in[3] + row_in[4])
    row_in[5 + blk] = row_out[2]
    row_blk = [
        push(row_out.at[2], row_in.at[5 + blk], row_sems, 4 + n, peer)
        for n, peer in enumerate(blk_peers())
    ]
    expert_weights(2)
    send_ring(2)
    pair_neighbours(1)
    pair_diagonal(0)

    for source in range(4):
        @pl.when(blk != source)
        def _():
            for item in range(9):
                index = source * 9 + item
                pltpu.make_async_remote_copy(
                    src_ref=dqkv_s.at[0:64, 0:tok],
                    dst_ref=home_s.at[0:64],
                    send_sem=home_sems.at[0, index],
                    recv_sem=home_sems.at[1, index],
                    device_id=(source, expert),
                    device_id_type=MESH,
                ).wait_recv()
    rows_load[1].wait()
    xhat, scale = standardise(tok_ref[...].astype(F32))

    def tokens_part(n):
        cut = slice(n * 256, (n + 1) * 256)
        grad_normed = dot(wqkv_ref[...], home_s[:, cut]).T
        grad_xhat = grad_normed * gain_ref[...]
        x = xhat[cut]
        grad_tokens_ref[cut, :] = rows_s[cut, :] + scale[cut] * (
            grad_xhat
            - jnp.mean(grad_xhat, axis=1, keepdims=True)
            - x * jnp.mean(grad_xhat * x, axis=1, keepdims=True)
        )

    tokens_part(0)
    forward(2)
    tokens_part(1)
    pair_diagonal(1)
    expert_weights(3)
    pair_neighbours(2)
    pair_diagonal(2)
    for copy in row_blk:
        copy.wait()
    small_pair.wait()
    total = (row_in[5] + row_in[6]) + (row_in[7] + row_in[8])
    small_out_ref[25:26, :] = jnp.concatenate(
        [total[n : n + 1, :] for n in range(width // 128)], axis=1)
    for copy in pairs:
        copy.wait_recv()
    for copy in pairs:
        copy.wait_send()
    for gather in gathers.values():
        gather.wait_sends()
    for copy in att_copies:
        copy.wait_send()
    for block, copy in sent:
        @pl.when(blk != block)
        def _():
            copy().wait_send()


def unfold_kernel(shared_ref, grad_qkv_ref, grad_proj_ref):
    blocks, group = shared_ref.shape[0], HEADS // shared_ref.shape[0] * HEAD_DIM
    part = pl.program_id(0)
    for block in range(blocks):
        for head in range(group // HEAD_DIM):
            rows = pl.ds(pl.multiple_of(head * 192 + part * 64, 64), 64)
            cut = slice(block * group + head * 64, block * group + (head + 1) * 64)
            grad_qkv_ref[:, cut] = shared_ref[block, rows, :].astype(F32).T

    @pl.when(part == 0)
    def _():
        for block in range(blocks):
            grad_proj_ref[block * group : (block + 1) * group, :] = (
                shared_ref[block, 3 * group :, :].astype(F32))


def unfold(shared, blocks, group, width):
    shared = shared.reshape(blocks, width, width)
    return pl.pallas_call(
        unfold_kernel,
        grid=(3,),
        out_shape=(
            jax.ShapeDtypeStruct((width, 3 * width), F32),
            jax.ShapeDtypeStruct((width, width), F32),
        ),
        in_specs=[pl.BlockSpec((blocks, width, width), lambda n: (0, 0, 0))],
        out_specs=(
            pl.BlockSpec((width, width), lambda n: (0, n)),
            pl.BlockSpec((width, width), lambda n: (0, 0)),
        ),
        name="unfold",
        compiler_params=pltpu.CompilerParams(vmem_limit_bytes=VMEM_BYTES),
    )(shared)


def call(kernel, name, args, outs, scratch, in_any=(), collective=None):
    specs = [
        pl.BlockSpec(memory_space=pl.ANY if n in in_any else pltpu.VMEM) for n in range(len(args))
    ]
    shapes = tuple(jax.ShapeDtypeStruct(shape, dtype) for shape, dtype in outs)
    return pl.pallas_call(
        kernel,
        out_shape=shapes,
        in_specs=specs,
        out_specs=tuple(pl.BlockSpec(memory_space=pltpu.VMEM) for _ in outs),
        scratch_shapes=scratch,
        name=name,
        compiler_params=pltpu.CompilerParams(
            vmem_limit_bytes=VMEM_BYTES,
            collective_id=collective,
            has_side_effects=collective is not None,
        ),
    )(*args)


def fast_body(
    tokens, cotangent, loss_mask, routes, priority, histogram, qkv_weight, proj_weight, attn_gain,
    moe_gain, route_weight, anchor_table, first_weight, second_weight,
):
    tok, width = tokens.shape[1:]
    blocks, experts = lax.axis_size("blk"), lax.axis_size("expert")
    length = tok * blocks
    heads = HEADS // blocks
    group = heads * HEAD_DIM
    hidden = first_weight.shape[2]
    x, cot = tokens[0], cotangent[0]
    rows = jnp.stack([routes[0, :, 0], priority[0, 0], loss_mask[0]]).astype(F32)
    rows = jnp.pad(rows, ((0, 5), (0, 0)))
    cols = rows.T
    gain1, gain2 = attn_gain[None], moe_gain[None]
    dma = pltpu.SemaphoreType.DMA
    nall, qkv, out, lse, att, target_row, target_col, cot_in = call(
        attend_kernel, "attend", (x, gain1, qkv_weight, cot, rows, cols),
        [((length, width), BF16), ((3 * group, length), BF16), ((group, length), F32),
         ((8, length), F32), ((width, tok), BF16), ((8, tok), F32), ((tok, 128), F32),
         ((tok, width), BF16)],
        [pltpu.VMEM((3, width, 256), BF16), pltpu.VMEM((3 * group, width), BF16),
         pltpu.VMEM((heads, length, HEAD_DIM), BF16), pltpu.VMEM((group, length), BF16),
         pltpu.VMEM((tok, width), BF16), dma((3,)), dma((2, 6)), dma((2, experts)),
         dma((2, blocks * heads))],
        in_any=(2,), collective=1,
    )
    (result, residual, gate, grad_residual, grad_att, grad_proj, small, buf, cots, gates) = call(
        expert_kernel, "expert",
        (att, x, proj_weight, gain2, route_weight, anchor_table, cols, target_row, target_col, cot,
         cot_in, first_weight[0], second_weight[0]),
        [((tok, width), BF16), ((tok, width), F32), ((tok, 128), F32), ((tok, width), F32),
         ((width, tok), BF16), ((width, width), BF16), ((32, width), F32),
         ((length, width), BF16), ((length, width), BF16), ((blocks * 64, 128), F32)],
        [pltpu.VMEM((width, hidden), BF16), pltpu.VMEM((hidden, width), BF16),
         pltpu.VMEM((tok, width), BF16), pltpu.VMEM((64, 128), F32), pltpu.VMEM((tok, width), BF16),
         pltpu.VMEM((tok, width), BF16), pltpu.VMEM((64, 128), F32), pltpu.VMEM((64, 128), F32),
         pltpu.VMEM((tok // 2, width), F32), pltpu.VMEM((tok // 2, width), F32),
         pltpu.VMEM((tok // 2, width), BF16),
         dma((2,)), dma((2, experts)), dma((2, experts)), dma((2, experts)), dma((2, experts)),
         dma((2, 6)), dma((2, 12)), dma((2, 3))],
        in_any=(11, 12), collective=2,
    )
    half, piece, quarter = width // 2, group // 4, hidden // blocks
    block_out, grad_tokens, shared, small, grad_first, grad_second = call(
        attend_back_kernel, "attend_back",
        (grad_att, qkv, out, lse, nall, result, residual, gate, target_col, gain1, qkv_weight, x,
         grad_residual, grad_proj, small, buf, cots, gates, first_weight[0], second_weight[0]),
        [((tok, width), BF16), ((tok, width), F32), ((blocks * width, width), BF16),
         ((32, width), F32), ((width, quarter), F32), ((quarter, width), F32)],
        [pltpu.VMEM((group, length), BF16), pltpu.VMEM((HEAD_DIM, length), F32),
         pltpu.VMEM((3 * group, length), BF16), pltpu.VMEM((3 * width, tok), BF16)]
        + [pltpu.VMEM((length, HEAD_DIM), BF16)] * 4
        + [pltpu.VMEM((tok, width), BF16), pltpu.VMEM((3 * group, width), BF16),
           pltpu.VMEM((3, group, width), BF16),
           pltpu.VMEM((width, width), F32), pltpu.VMEM((width, half), F32),
           pltpu.VMEM((width, half), BF16), pltpu.VMEM((width, half), BF16),
           pltpu.VMEM((width, half), BF16), pltpu.VMEM((12, piece, half), BF16),
           pltpu.VMEM((32, half), F32), pltpu.VMEM((9, 32, half), F32), pltpu.VMEM((32, half), F32),
           pltpu.VMEM((3, 8, 128), F32), pltpu.VMEM((9, 8, 128), F32),
           pltpu.VMEM((width, quarter), BF16), pltpu.VMEM((quarter, width), BF16),
           pltpu.VMEM((2, 2, tok, width), BF16), pltpu.VMEM((tok, width), F32),
           dma((2, 3)), dma((2, experts)), dma((2, 36)), dma((2, 3)), dma((2, 4)), dma((2, 12)),
           dma((2, 12)), dma((2, 8)), dma((2, 7)), dma((2, 24)), dma((2, 16)), dma((7,))],
        in_any=(6, 12, 15, 16, 18, 19), collective=3,
    )
    grad_qkv, grad_proj = unfold(shared, blocks, group, width)
    rdim = route_weight.shape[1]
    return (
        block_out[None],
        grad_tokens[None],
        grad_qkv,
        grad_proj,
        small[rdim + experts + 1],
        small[rdim + experts],
        small[:rdim].T,
        small[rdim : rdim + experts, :rdim],
        grad_first[None],
        grad_second[None],
        histogram + small[rdim + experts + 2, :experts].astype(jnp.int32),
    )


def solution(mesh):
    in_specs = (
        P("expert", "blk", None),
        P("expert", "blk", None),
        P("expert", "blk"),
        P("expert", "blk", None),
        P("expert", "blk", None),
        P(),
        P(),
        P(),
        P(),
        P(),
        P(),
        P(),
        P("expert", None, None),
        P("expert", None, None),
    )
    out_specs = (
        P("expert", "blk", None),
        P("expert", "blk", None),
        P(),
        P(),
        P(),
        P(),
        P(),
        P(),
        P("expert", None, "blk"),
        P("expert", "blk", None),
        P(),
    )
    blocks, experts = mesh.shape["blk"], mesh.shape["expert"]
    body = fast_body if (blocks, experts) == (4, 8) else general_body
    return jax.shard_map(body, mesh=mesh, in_specs=in_specs, out_specs=out_specs, check_vma=False)
```

```python
import functools

import jax
import jax.numpy as jnp
from jax import lax
from jax.experimental import pallas as pl
from jax.experimental.pallas import tpu as pltpu
from jax.sharding import PartitionSpec as P

HEADS = 12
HEAD_DIM = 64


TOP_PRECISION = lax.Precision.HIGHEST
EPSILON = 1e-05
ROUTER_SOFTNESS = 0.4
MASKED = -1e30


def layer_norm(values, norm_gain):
    average = jnp.mean(values, axis=-1, keepdims=True)
    centered = values - average
    variance = jnp.mean(centered * centered, axis=-1, keepdims=True)
    return centered * lax.rsqrt(variance + EPSILON) * norm_gain


def unit_rows(matrix):
    return matrix * lax.rsqrt(1.0 + jnp.sum(matrix * matrix, axis=-1, keepdims=True))


def router_gate(normalized_rows, route_matrix, anchors, route_onehot):
    projection_output = unit_rows(jnp.dot(normalized_rows, route_matrix, precision=TOP_PRECISION))
    expert_anchor_rows = unit_rows(anchors)
    route_logit_scores = (
        jnp.dot(projection_output, expert_anchor_rows.T, precision=TOP_PRECISION) / ROUTER_SOFTNESS
    )
    return jnp.sum(jax.nn.softmax(route_logit_scores, axis=-1) * route_onehot, axis=-1)


def masked_scores(queries, key_rows, query_first, key_first, score_scale):
    scores = (
        jnp.einsum("qhd,khd->hqk", queries, key_rows, preferred_element_type=jnp.float32)
        * score_scale
    )
    grid_shape = (queries.shape[0], key_rows.shape[0])
    query_place = query_first + lax.broadcasted_iota(jnp.int32, grid_shape, 0)
    key_place = key_first + lax.broadcasted_iota(jnp.int32, grid_shape, 1)
    return (scores, (key_place <= query_place)[None])


def over_blocks(step_fn, carried, arrays, block_rows):
    row_total = arrays[0].shape[0]
    block_count = row_total // block_rows
    stacked = tuple(
        (member.reshape((block_count, block_rows) + member.shape[1:]) for member in arrays)
    )

    def scan_step(running, packed):
        position, blocks = packed
        return (step_fn(running, blocks, position * block_rows), None)

    result, unused = lax.scan(
        scan_step, carried, (jnp.arange(block_count, dtype=jnp.int32), stacked)
    )
    return result


def general_body(
    tokens,
    cotangent,
    loss_mask,
    routes,
    priority,
    histogram,
    qkv_weight,
    proj_weight,
    attn_gain,
    moe_gain,
    route_weight,
    anchor_table,
    first_weight,
    second_weight,
):
    tok_rows = tokens.shape[1]
    model_width = tokens.shape[2]
    score_scale = HEAD_DIM ** (-0.5)
    query_first = lax.axis_index("blk") * tok_rows
    local_experts = first_weight.shape[0]
    experts_all = local_experts * lax.axis_size("expert")
    capacity = tok_rows // experts_all
    head_shape = (tok_rows, HEADS, HEAD_DIM)
    seq_rows = tok_rows * lax.axis_size("blk")
    route_ids = routes[0, :, 0]
    route_onehot = (
        route_ids[:, None] == lax.broadcasted_iota(jnp.int32, (tok_rows, experts_all), 1)
    ).astype(jnp.float32)
    count_rows = jnp.sum(route_onehot, axis=0)
    total_counts = lax.psum(count_rows.astype(jnp.int32), ("blk", "expert"))
    block_input = tokens[0].astype(jnp.float32)
    normed_attn, attn_norm_back = jax.vjp(layer_norm, block_input, attn_gain)
    normed_low = normed_attn.astype(jnp.bfloat16)
    query_key_value_mix = jnp.dot(
        normed_low, qkv_weight, preferred_element_type=jnp.float32
    ).astype(jnp.bfloat16)
    query_flat = query_key_value_mix[:, :model_width]
    queries = query_flat.reshape(head_shape)
    key_local = query_key_value_mix[:, model_width : 2 * model_width]
    value_local = query_key_value_mix[:, 2 * model_width :]

    def forward_step(carried, blocks, key_first):
        running_top, running_sum, running_out = carried
        key_rows = blocks[0].reshape(blocks[0].shape[0], HEADS, HEAD_DIM)
        value_rows = blocks[1].reshape(blocks[1].shape[0], HEADS, HEAD_DIM)
        scores, allowed = masked_scores(queries, key_rows, query_first, key_first, score_scale)
        top_new = jnp.maximum(running_top, jnp.max(jnp.where(allowed, scores, MASKED), axis=2))
        weights = jnp.where(allowed, jnp.exp(scores - top_new[:, :, None]), 0.0)
        factor = jnp.exp(running_top - top_new)
        running_sum = running_sum * factor + jnp.sum(weights, axis=2)
        running_out = running_out * factor.T[:, :, None] + jnp.einsum(
            "hqk,khd->qhd",
            weights.astype(jnp.bfloat16),
            value_rows,
            preferred_element_type=jnp.float32,
        )
        return (top_new, running_sum, running_out)

    initial = (
        jnp.full((HEADS, tok_rows), MASKED, jnp.float32),
        jnp.zeros((HEADS, tok_rows), jnp.float32),
        jnp.zeros(head_shape, jnp.float32),
    )
    running_top, running_sum, running_out = over_blocks(
        forward_step,
        initial,
        (
            lax.all_gather(key_local, "blk", axis=0, tiled=True),
            lax.all_gather(value_local, "blk", axis=0, tiled=True),
        ),
        tok_rows,
    )
    attention_result = running_out / running_sum.T[:, :, None]
    log_total = running_top + jnp.log(running_sum)
    attended_low = attention_result.reshape(tok_rows, model_width).astype(jnp.bfloat16)
    residual_stream = block_input + jnp.dot(
        attended_low, proj_weight, preferred_element_type=jnp.float32
    )
    normed_moe, moe_norm_back = jax.vjp(layer_norm, residual_stream, moe_gain)

    def gate_of(normalized_rows, route_matrix, anchors):
        return router_gate(normalized_rows, route_matrix, anchors, route_onehot)

    gate_value, gate_back = jax.vjp(gate_of, normed_moe, route_weight, anchor_table)
    order_rows = priority[0, 0]
    same_route = route_ids[:, None] == route_ids[None, :]
    earlier = order_rows[None, :] < order_rows[:, None]
    slot_ids = jnp.sum((same_route & earlier).astype(jnp.int32), axis=1)
    target = jnp.where(slot_ids < capacity, route_ids * capacity + slot_ids, -1)
    selector = lax.broadcasted_iota(jnp.int32, (tok_rows, tok_rows), 0) == target[None, :]
    selector_low = selector.astype(jnp.bfloat16)
    outgoing = jnp.dot(
        selector_low, normed_moe.astype(jnp.bfloat16), preferred_element_type=jnp.float32
    )
    outgoing = outgoing.astype(jnp.bfloat16).reshape(experts_all, capacity, model_width)
    arrived = lax.all_to_all(outgoing, "expert", split_axis=0, concat_axis=0, tiled=True)
    sources = arrived.shape[0] // local_experts
    grouped = arrived.reshape(sources, local_experts, arrived.shape[1], arrived.shape[2])
    hidden = jnp.einsum("secd,edf->secf", grouped, first_weight, preferred_element_type=jnp.float32)
    act_low = jax.nn.gelu(hidden).astype(jnp.bfloat16)
    result = jnp.einsum(
        "secf,efd->secd", act_low, second_weight, preferred_element_type=jnp.float32
    )
    result = result.astype(jnp.bfloat16).reshape(arrived.shape)
    returned = lax.all_to_all(result, "expert", split_axis=0, concat_axis=0, tiled=True)
    returned, arrived = (returned, arrived)
    fetched = jnp.einsum(
        "st,sd->td",
        selector_low,
        returned.reshape(tok_rows, model_width),
        preferred_element_type=jnp.float32,
    )
    block_out = (residual_stream + gate_value[:, None] * fetched).astype(jnp.bfloat16)[None]
    grad_out = cotangent[0].astype(jnp.float32) * loss_mask[0].astype(jnp.float32)[:, None]
    grad_fetched = grad_out * gate_value[:, None]
    grad_gate = jnp.sum(grad_out * fetched, axis=1)
    grad_slots = jnp.dot(selector.astype(jnp.float32), grad_fetched, precision=TOP_PRECISION)
    grad_slots = grad_slots.astype(jnp.bfloat16).reshape(experts_all, capacity, model_width)
    grad_arrived = lax.all_to_all(grad_slots, "expert", split_axis=0, concat_axis=0, tiled=True)
    sources = grad_arrived.shape[0] // local_experts
    slot_shape = (sources, local_experts, capacity, model_width)
    grouped_in = arrived.reshape(slot_shape)
    grouped_grad = grad_arrived.reshape(slot_shape)
    hidden = jnp.einsum(
        "secd,edf->secf", grouped_in, first_weight, preferred_element_type=jnp.float32
    )
    act_low = jax.nn.gelu(hidden).astype(jnp.bfloat16)
    grad_second = jnp.einsum(
        "secf,secd->efd", act_low, grouped_grad, preferred_element_type=jnp.float32
    )
    grad_act = jnp.einsum(
        "secd,efd->secf", grouped_grad, second_weight, preferred_element_type=jnp.float32
    )
    unused, gelu_back = jax.vjp(jax.nn.gelu, hidden)
    grad_hidden = gelu_back(grad_act)[0].astype(jnp.bfloat16)
    grad_first = jnp.einsum(
        "secd,secf->edf", grouped_in, grad_hidden, preferred_element_type=jnp.float32
    )
    grad_sent = jnp.einsum(
        "secf,edf->secd", grad_hidden, first_weight, preferred_element_type=jnp.float32
    )
    grad_sent = grad_sent.astype(jnp.bfloat16).reshape(grad_arrived.shape)
    grad_returned = lax.all_to_all(grad_sent, "expert", split_axis=0, concat_axis=0, tiled=True)
    grad_first, grad_second = (
        lax.psum_scatter(
            grad_first.astype(jnp.bfloat16), "blk", scatter_dimension=2, tiled=True
        ).astype(jnp.float32),
        lax.psum_scatter(
            grad_second.astype(jnp.bfloat16), "blk", scatter_dimension=1, tiled=True
        ).astype(jnp.float32),
    )
    grad_moe_rows = jnp.einsum(
        "st,sd->td",
        selector_low,
        grad_returned.reshape(tok_rows, model_width),
        preferred_element_type=jnp.float32,
    )
    grad_router_rows, grad_route, grad_anchor = gate_back(grad_gate)
    grad_residual_norm, grad_moe_gain = moe_norm_back(grad_moe_rows + grad_router_rows)
    grad_residual = grad_out + grad_residual_norm
    grad_attn_low = grad_residual.astype(jnp.bfloat16)
    grad_proj = jnp.dot(attended_low.T, grad_attn_low, preferred_element_type=jnp.float32)
    grad_attended_flat = jnp.dot(
        grad_attn_low, proj_weight.T, preferred_element_type=jnp.float32
    ).astype(jnp.bfloat16)
    grad_attended = grad_attended_flat.reshape(head_shape)
    delta_rows = jnp.sum(grad_attended.astype(jnp.float32) * attention_result, axis=2).T
    key_all, value_all = (
        lax.all_gather(key_local, "blk", axis=0, tiled=True),
        lax.all_gather(value_local, "blk", axis=0, tiled=True),
    )
    block_count = seq_rows // tok_rows
    key_blocks = key_all.reshape(block_count, tok_rows, model_width)
    value_blocks = value_all.reshape(block_count, tok_rows, model_width)

    def key_block_step(running_grad, packed):
        position, key_block, value_block = packed
        key_rows = key_block.reshape(head_shape)
        value_rows = value_block.reshape(head_shape)
        scores, allowed = masked_scores(
            queries, key_rows, query_first, position * tok_rows, score_scale
        )
        soft_rows = jnp.where(allowed, jnp.exp(scores - log_total[:, :, None]), 0.0)
        grad_values = jnp.einsum(
            "hqk,qhd->khd",
            soft_rows.astype(jnp.bfloat16),
            grad_attended,
            preferred_element_type=jnp.float32,
        )
        grad_soft = jnp.einsum(
            "qhd,khd->hqk", grad_attended, value_rows, preferred_element_type=jnp.float32
        )
        grad_scores = (soft_rows * (grad_soft - delta_rows[:, :, None])).astype(jnp.bfloat16)
        grad_keys = score_scale * jnp.einsum(
            "hqk,qhd->khd", grad_scores, queries, preferred_element_type=jnp.float32
        )
        running_grad = running_grad + score_scale * jnp.einsum(
            "hqk,khd->qhd", grad_scores, key_rows, preferred_element_type=jnp.float32
        )
        term = jnp.concatenate(
            [grad_keys.reshape(tok_rows, model_width), grad_values.reshape(tok_rows, model_width)],
            axis=1,
        )
        return (running_grad, term)

    grad_queries, stacked_terms = lax.scan(
        key_block_step,
        jnp.zeros(head_shape, jnp.float32),
        (jnp.arange(block_count, dtype=jnp.int32), key_blocks, value_blocks),
    )
    all_terms = stacked_terms.reshape(seq_rows, 2 * model_width)
    key_value_grads = lax.psum_scatter(
        all_terms.astype(jnp.bfloat16), "blk", scatter_dimension=0, tiled=True
    ).astype(jnp.float32)
    grad_query_rows = grad_queries.reshape(tok_rows, model_width)
    grad_qkv_rows = jnp.concatenate([grad_query_rows, key_value_grads], axis=1).astype(jnp.bfloat16)
    grad_qkv = jnp.dot(normed_low.T, grad_qkv_rows, preferred_element_type=jnp.float32)
    grad_normed = jnp.dot(grad_qkv_rows, qkv_weight.T, preferred_element_type=jnp.float32)
    grad_source_norm, grad_attn_gain = attn_norm_back(grad_normed)
    grad_tokens = (grad_residual + grad_source_norm)[None]
    grad_qkv, grad_proj, grad_attn_gain, grad_moe_gain, grad_route, grad_anchor = lax.psum(
        (grad_qkv, grad_proj, grad_attn_gain, grad_moe_gain, grad_route, grad_anchor),
        ("blk", "expert"),
    )
    histogram_out = histogram + total_counts
    return (
        block_out,
        grad_tokens,
        grad_qkv,
        grad_proj,
        grad_attn_gain,
        grad_moe_gain,
        grad_route,
        grad_anchor,
        grad_first,
        grad_second,
        histogram_out,
    )


MESH = pl.DeviceIdType.MESH
F32 = jnp.float32
BF16 = jnp.bfloat16
VMEM_BYTES = 58 * 1024 * 1024


def dot(left, right, precision=None):
    return lax.dot_general(
        left, right, (((1,), (0,)), ((), ())), precision=precision, preferred_element_type=F32
    )


def dot_nt(left, right, precision=None):
    return lax.dot_general(
        left, right, (((1,), (1,)), ((), ())), precision=precision, preferred_element_type=F32
    )


def dot_tn(left, right, precision=None):
    return lax.dot_general(
        left, right, (((0,), (0,)), ((), ())), precision=precision, preferred_element_type=F32
    )


def split(values):
    high = values.astype(BF16)
    return high, (values - high.astype(F32)).astype(BF16)


def fine(product, left, right):
    left_high, left_low = split(left)
    right_high, right_low = split(right)
    return product(left_high, right_high) + (
        product(left_high, right_low) + product(left_low, right_high)
    )


def rows_at(index, size):
    return pl.ds(pl.multiple_of(index * size, size), size)


def places():
    blk = lax.axis_index("blk")
    expert = lax.axis_index("expert")
    return blk, expert, blk + 1 - 2 * lax.rem(blk, 2), lax.rem(blk + 2, 4), 3 - blk


def greet(peers):
    barrier = pltpu.get_barrier_semaphore()
    for peer in peers:
        pl.semaphore_signal(barrier, inc=1, device_id=peer, device_id_type=MESH)
    return lambda: pl.semaphore_wait(barrier, len(peers))


def push(src, dst, sems, index, peer):
    copy = pltpu.make_async_remote_copy(
        src_ref=src,
        dst_ref=dst,
        send_sem=sems.at[0, index],
        recv_sem=sems.at[1, index],
        device_id=peer,
        device_id_type=MESH,
    )
    copy.start()
    return copy


def standardise(values):
    average = jnp.mean(values, axis=-1, keepdims=True)
    centered = values - average
    scale = lax.rsqrt(jnp.mean(centered * centered, axis=-1, keepdims=True) + EPSILON)
    return centered * scale, scale


def lower_triangle(keys, queries):
    return lax.broadcasted_iota(jnp.int32, (keys, queries), 0) <= lax.broadcasted_iota(
        jnp.int32, (keys, queries), 1
    )


class BlockGather:
    def __init__(self, part, sems, base, own=None):
        self.part, self.sems, self.base, self.own = part, sems, base, own

    def send(self, blk, half, index, peer):
        ref = self.part(blk, half)
        src = ref if self.own is None or index > 3 else self.own(half)
        return push(src, ref, self.sems, self.base + index, peer)

    def start(self):
        self.start_first()
        self.start_second()

    def start_first(self):
        blk, expert, bx, by, bd = places()
        self.copies = [self.send(blk, 0, 0, (bx, expert)), self.send(blk, 1, 1, (by, expert))]

    def start_second(self):
        blk, expert, bx, by, bd = places()
        self.copies += [self.send(blk, 1, 2, (bx, expert)), self.send(blk, 0, 3, (by, expert))]

    def forward(self):
        blk, expert, bx, by, bd = places()
        self.copies[0].wait_recv()
        self.copies.append(self.send(bx, 0, 4, (by, expert)))
        self.copies[1].wait_recv()
        self.copies.append(self.send(by, 1, 5, (bx, expert)))

    def wait_neighbours(self):
        self.copies[2].wait_recv()
        self.copies[3].wait_recv()

    def wait_diagonal(self):
        self.copies[4].wait_recv()
        self.copies[5].wait_recv()

    def wait_sends(self):
        for copy in self.copies:
            copy.wait_send()


def row_halves(buf, rows):
    size = rows // 2
    return lambda blk, half: buf.at[pl.ds(pl.multiple_of(blk * rows + half * size, size), size)]


def expert_groups():
    expert = lax.axis_index("expert")
    line, core = expert // 2, lax.rem(expert, 2)
    side, place = line // 2, lax.rem(line, 2)
    beside = (side * 2 + 1 - place) * 2
    first = ((1 - side) * 2 + place) * 2
    second = ((1 - side) * 2 + 1 - place) * 2
    return [
        (side * 4, 4, [expert + 1 - 2 * core, beside + core, beside + 1 - core]),
        (first, 2, [first + core, first + 1 - core]),
        (second, 2, [second + core, second + 1 - core]),
    ]


class ExpertExchange:
    def __init__(self, src, dst, sems, rows):
        self.src, self.dst, self.sems, self.rows = src, dst, sems, rows
        self.groups = expert_groups()
        self.copies = [[], [], []]

    def start(self, group, keep=True):
        blk, expert = lax.axis_index("blk"), lax.axis_index("expert")
        place = rows_at(expert, self.rows)
        base = (0, 3, 5)[group]
        for n, peer in enumerate(self.groups[group][2]):
            self.copies[group].append(
                push(self.src.at[rows_at(peer, self.rows)], self.dst.at[place], self.sems,
                     base + n, (blk, peer))
            )
        if group == 0 and keep:
            self.dst[place] = self.src[place]

    def wait_recv(self, group):
        for copy in self.copies[group]:
            copy.wait_recv()

    def wait_sends(self):
        for copy in sum(self.copies, []):
            copy.wait_send()

    def start_all(self, keep=True):
        self.start(1)
        self.start(2)
        self.start(0, keep)

    def wait_all(self):
        for group in range(3):
            self.wait_recv(group)
        self.wait_sends()


class Lazy:
    def __init__(self, src, dst, sem):
        self.dst, self.shape, self.fresh = dst, dst.shape, True
        self.copy = pltpu.make_async_copy(src, dst, sem)
        self.copy.start()

    def ref(self):
        if self.fresh:
            self.copy.wait()
            self.fresh = False
        return self.dst

    def __getitem__(self, where):
        return self.ref()[where]

    @property
    def at(self):
        return self.ref().at


class LazyOut:
    def __init__(self, src, dst, sem):
        self.src, self.dst, self.sem, self.shape, self.copy = src, dst, sem, src.shape, None

    def flush(self):
        if self.copy is None:
            self.copy = pltpu.make_async_copy(self.src, self.dst, self.sem)
            self.copy.start()

    def __getitem__(self, where):
        return self.src[where]

    def __setitem__(self, where, value):
        self.src[where] = value

    @property
    def at(self):
        return self.src.at


def blk_peers():
    blk, expert, bx, by, bd = places()
    return [(bx, expert), (by, expert), (bd, expert)]


def expert_peers():
    blk, expert = lax.axis_index("blk"), lax.axis_index("expert")
    n = lax.axis_size("expert")
    return [(blk, lax.rem(expert + shift, n)) for shift in range(1, n)]


def forward_kernel(
    tok_ref, rows_ref, wqkv_ref, cot_ref, proj_ref, route_ref, anchor_ref, first_ref, second_ref,
    nall_ref, qkv_ref, out_ref, lse_ref, cols_ref, result_ref, residual_ref, gate_ref,
    grad_residual_ref, grad_att_ref, grad_proj_ref, small_ref, buf_ref, cots_ref, gates_ref,
    w_s, wt_s, k_s, att_s, cot_s, att_ref, cot_in_ref,
    first_s, second_s, slope_s, buf_s, gates_s, go_s, gate_s, grad_s, back_s, score_s, score_in_s,
    res_acc, sent_acc, grad_in_s,
    w_sem, gather_sems, cot_sems, att_sems, go_sems, gate_sems, back_sems, score_sems, cots_sems,
    buf_sems, gates_sems,
):
    blk, expert, bx, by, bd = places()
    tok = tok_ref.shape[0]
    width = tok_ref.shape[1]
    heads = HEADS // 4
    group = heads * HEAD_DIM
    arrived = greet(blk_peers() + expert_peers())
    odd = lax.rem(blk, 2)
    loads = []
    for part in range(3):
        first = pl.multiple_of(part * width + blk * group - odd * 64, 128)
        loads.append(
            pltpu.make_async_copy(wqkv_ref.at[:, pl.ds(first, 256)], w_s.at[part], w_sem.at[part])
        )
        loads[-1].start()
    weights = [
        pltpu.make_async_copy(first_ref, first_s, w_sem.at[3]),
        pltpu.make_async_copy(second_ref, second_s, w_sem.at[4]),
    ]
    for load in weights:
        load.start()
    xhat, _ = standardise(tok_ref[...].astype(F32))
    nall_ref[rows_at(blk, tok), :] = (xhat * rows_ref[0:1, :]).astype(BF16)
    arrived()
    gather = BlockGather(row_halves(nall_ref, tok), gather_sems, 0)
    gather.start()

    capacity = tok // 8
    rows = rows_ref[:, 0:tok]
    cols = jnp.concatenate([rows, jnp.zeros((120, tok), F32)], axis=0).T
    route_row, prio_row, mask_row = rows[2:3, :], rows[3:4, :], rows[4:5, :]
    route_col, prio_col = cols[:, 2:3], cols[:, 3:4]
    same = route_col == route_row
    slot_row = jnp.sum(jnp.where(same & (prio_col < prio_row), 1.0, 0.0), axis=0, keepdims=True)
    slot_col = jnp.sum(jnp.where(same & (prio_row < prio_col), 1.0, 0.0), axis=1, keepdims=True)
    target_row = jnp.where(slot_row < capacity, route_row * capacity + slot_row, -1.0)
    target_col = jnp.where(slot_col < capacity, route_col * capacity + slot_col, -1.0)
    lane = lax.broadcasted_iota(jnp.int32, cols.shape, 1)
    cols_ref[...] = jnp.where(lane == 0, target_col, cols)
    cols_ref.flush()
    slots = lax.broadcasted_iota(jnp.int32, (tok, tok), 0).astype(F32)
    chosen = jnp.where((slots == target_row) & (mask_row > 0.0), 1.0, 0.0).astype(BF16)
    cot_s[...] = dot(chosen, cot_ref[...]).astype(BF16)
    cot_move = ExpertExchange(cot_s, cot_in_ref, cot_sems, capacity)
    cot_move.start_all()

    for part in range(3):
        loads[part].wait()
        wide = w_s[part]
        narrow = jnp.where(odd == 1, wide[:, 64:256], wide[:, 0:192])
        wt_s[part * group : (part + 1) * group, :] = narrow.T

    def project(where):
        cols = rows_at(where, tok)
        mixed = dot_nt(wt_s[...], nall_ref[cols, :]).astype(BF16)
        qkv_ref[0:group, cols] = mixed[0:group] * BF16(HEAD_DIM**-0.5)
        qkv_ref[group:, cols] = mixed[group:]
        for head in range(heads):
            k_s[head, cols, :] = mixed[group + head * 64 : group + (head + 1) * 64].T

    project(blk)
    gather.forward()
    gather.wait_neighbours()
    project(bx)
    project(by)
    gather.wait_diagonal()
    nall_ref.flush()
    cot_move.wait_all()
    here = rows_at(blk, tok)
    cots_own = pltpu.make_async_copy(cot_in_ref, cots_ref.at[here], w_sem.at[5])
    cots_own.start()
    quarter = tok // 4
    cots = []
    for part in range(2):

        def own(half, part=part):
            return cot_in_ref.at[pl.ds((2 * part + half) * quarter, quarter)]

        def halves(block, half, part=part):
            row = pl.multiple_of(block * tok + (2 * part + half) * quarter, quarter)
            return cots_ref.at[pl.ds(row, quarter)]

        cots.append(BlockGather(halves, cots_sems, 6 * part, own))
    cots[0].start_first()
    project(bd)
    qkv_ref.flush()

    half = tok // 2

    def scores(i, head):
        q = qkv_ref[head * 64 : (head + 1) * 64, i * tok : (i + 1) * tok]
        upper = dot(k_s[head, i * tok : i * tok + half, :], q)
        upper = jnp.where(lower_triangle(half, tok), upper, MASKED)
        lower = dot(k_s[head, i * tok + half : (i + 1) * tok, :], q[:, half:])
        lower = jnp.where(lower_triangle(half, half), lower, MASKED)
        top = jnp.max(upper, axis=0, keepdims=True)
        low_top = jnp.max(lower, axis=0, keepdims=True)
        top = jnp.concatenate([top[:, :half], jnp.maximum(top[:, half:], low_top)], axis=1)
        if i == 0:
            return top, upper, lower, None
        past = dot(k_s[head, 0 : i * tok, :], q)
        return jnp.maximum(top, jnp.max(past, axis=0, keepdims=True)), upper, lower, past

    sends = []

    def finish(i, head, found):
        top, upper, lower, past = found
        v = qkv_ref[2 * group + head * 64 : 2 * group + (head + 1) * 64, :]
        upper = jnp.exp(upper - top)
        lower = jnp.exp(lower - top[:, half:])
        total = jnp.sum(upper, axis=0, keepdims=True)
        low_total = jnp.sum(lower, axis=0, keepdims=True)
        total = jnp.concatenate([total[:, :half], total[:, half:] + low_total], axis=1)
        result = dot(v[:, i * tok : i * tok + half], upper.astype(BF16))
        low_result = dot(v[:, i * tok + half : (i + 1) * tok], lower.astype(BF16))
        result = jnp.concatenate([result[:, :half], result[:, half:] + low_result], axis=1)
        if i:
            past = jnp.exp(past - top)
            total = total + jnp.sum(past, axis=0, keepdims=True)
            result = result + dot(v[:, 0 : i * tok], past.astype(BF16))
        result = result / total
        place = slice(head * 64, (head + 1) * 64)
        out_ref[place, i * tok : (i + 1) * tok] = result
        lse_ref[head : head + 1, i * tok : (i + 1) * tok] = top + jnp.log(total)
        att_s[place, i * tok : (i + 1) * tok] = result.astype(BF16)
        there = pl.ds(pl.multiple_of(blk * group + head * 64, 64), 64)

        def copy():
            return pltpu.make_async_remote_copy(
                src_ref=att_s.at[place, i * tok : (i + 1) * tok],
                dst_ref=att_ref.at[there],
                send_sem=att_sems.at[0, i * heads + head],
                recv_sem=att_sems.at[1, blk * heads + head],
                device_id=(i, expert),
                device_id_type=MESH,
            )

        @pl.when(blk != i)
        def _():
            copy().start()

        @pl.when(blk == i)
        def _():
            att_ref[there, :] = result.astype(BF16)

        sends.append((i, copy))

    before = None
    for i in range(4):
        for head in range(heads):
            found = scores(i, head)
            if before is not None:
                finish(*before)
            before = (i, head, found)
    finish(*before)

    for i, copy in sends:
        @pl.when(blk != i)
        def _():
            copy().wait_send()

    for source in range(4):
        @pl.when(blk != source)
        def _():
            for head in range(heads):
                there = pl.ds(source * group + head * 64, 64)
                pltpu.make_async_remote_copy(
                    src_ref=att_s.at[0:64, 0:tok],
                    dst_ref=att_ref.at[there],
                    send_sem=att_sems.at[0, source * heads + head],
                    recv_sem=att_sems.at[1, source * heads + head],
                    device_id=(source, expert),
                    device_id_type=MESH,
                ).wait_recv()

    cots[0].start_second()
    cots[1].start()
    out_ref.flush()
    gather.wait_sends()

    gain = rows_ref[1:2, :]
    experts = 8
    residual = tok_ref[...].astype(F32) + dot_tn(att_ref[...], proj_ref[...])
    residual_ref[...] = residual
    residual_ref.flush()
    xhat, scale = standardise(residual)
    normed = xhat * gain
    normed_low = normed.astype(BF16)
    go_s[...] = dot(jnp.where(slots == target_row, 1.0, 0.0).astype(BF16), normed_low).astype(BF16)
    go = ExpertExchange(go_s, buf_s, go_sems, capacity)
    go.start(0)
    go.start(1)

    projected = fine(dot_nt, normed, route_ref[...])
    unit_scale = lax.rsqrt(1.0 + jnp.sum(projected * projected, axis=1, keepdims=True))
    unit = projected * unit_scale
    anchor = anchor_ref[...]
    anchor_scale = lax.rsqrt(1.0 + jnp.sum(anchor * anchor, axis=1, keepdims=True))
    anchor_unit = anchor * anchor_scale
    logits = fine(dot_nt, unit, anchor_unit) / ROUTER_SOFTNESS
    soft = jnp.exp(logits - jnp.max(logits, axis=1, keepdims=True))
    soft = soft / jnp.sum(soft, axis=1, keepdims=True)
    onehot = jnp.where(
        lax.broadcasted_iota(jnp.int32, (tok, experts), 1).astype(F32) == route_col, 1.0, 0.0
    )
    gate = jnp.sum(soft * onehot, axis=1, keepdims=True)
    gate_ref[...] = jnp.broadcast_to(gate, gate_ref.shape)
    gate_ref.flush()
    lane = lax.broadcasted_iota(jnp.int32, (tok, 128), 1).astype(F32)
    lane = jnp.where(lane < capacity, lane, 1e6)
    for peer in range(experts):
        row = jnp.sum(
            jnp.where(target_col == peer * capacity + lane, gate, 0.0), axis=0, keepdims=True
        )
        gate_s[peer * 8 : (peer + 1) * 8, :] = jnp.broadcast_to(row, (8, 128))
    gates = ExpertExchange(gate_s, gates_s, gate_sems, 8)
    for group in range(3):
        gates.start(group)

    back = ExpertExchange(grad_s, back_s, back_sems, capacity)
    scores = ExpertExchange(score_s, score_in_s, score_sems, 8)
    tile = 768
    tiles = first_s.shape[1] // tile
    bufs, kept = [], []
    for group, (first_source, sources, _) in enumerate(go.groups):
        count = sources * capacity
        rows = pl.ds(pl.multiple_of(first_source * capacity, count), count)
        go.wait_recv(group)
        if group == 0:
            go.start(2)

        def halves(block, half, first=first_source * capacity, size=count // 2):
            return buf_ref.at[pl.ds(pl.multiple_of(block * tok + first + half * size, size), size)]

        def own(half, first=first_source * capacity, size=count // 2):
            return buf_s.at[pl.ds(pl.multiple_of(first + half * size, size), size)]

        bufs.append(BlockGather(halves, buf_sems, 6 * group, own))
        bufs[group].start()
        there = pl.ds(pl.multiple_of(blk * tok + first_source * capacity, count), count)
        kept.append(pltpu.make_async_copy(buf_s.at[rows], buf_ref.at[there], w_sem.at[6 + group]))
        kept[group].start()
        if group == 0:
            for load in weights:
                load.wait()
        x = buf_s[rows, :]
        for t in range(tiles):
            cut = slice(t * tile, (t + 1) * tile)
            act, slope = gelu_pair(dot(x, first_s[:, cut]))
            slope_s[0:count, cut] = slope
            part = dot(act.astype(BF16), second_s[cut, :])
            if t == 0:
                res_acc[0:count, :] = part
            else:
                res_acc[0:count, :] += part
        result = res_acc[0:count, :].astype(BF16)
        score = jnp.sum(
            result.astype(F32) * cot_in_ref[rows, :].astype(F32), axis=1, keepdims=True)
        for n in range(sources):
            row = flatten(score[n * capacity : (n + 1) * capacity], 128)
            score_s[rows_at(first_source + n, 8), :] = jnp.broadcast_to(row, (8, 128))
        scores.start(group)
        result_ref[rows, :] = result
        if group == 0:
            cots[0].forward()
        if group == 1:
            cots[1].forward()
        gates.wait_recv(group)
        for n in range(sources):
            row = gates_s[rows_at(first_source + n, 8), :][0:1, :]
            chunk = rows_at(first_source + n, capacity)
            grad_in_s[n * capacity : (n + 1) * capacity, :] = (
                cot_in_ref[chunk, :].astype(F32) * spread(row, capacity)
            ).astype(BF16)
        grad_in = grad_in_s[0:count, :]
        for t in range(tiles):
            cut = slice(t * tile, (t + 1) * tile)
            grad_hidden = (dot_nt(grad_in, second_s[cut, :]) * slope_s[0:count, cut]).astype(BF16)
            sent = dot_nt(grad_hidden, first_s[:, cut])
            if t == 0:
                sent_acc[0:count, :] = sent
            else:
                sent_acc[0:count, :] += sent
        grad_s[rows, :] = sent_acc[0:count, :].astype(BF16)
        back.start(group)
    bufs[0].forward()
    result_ref.flush()
    gates_ref[rows_at(blk, 64), :] = gates_s[...]
    gates_here = gates_ref.at[rows_at(blk, 64)]
    gates_out = [
        push(gates_here, gates_here, gates_sems, n, peer) for n, peer in enumerate(blk_peers())
    ]
    grad_out = cot_ref[...].astype(F32) * cols_ref[:, 4:5]

    for group in range(3):
        scores.wait_recv(group)
    grad_gate = jnp.zeros((tok, 1), F32)
    for peer in range(experts):
        row = score_in_s[peer * 8 : peer * 8 + 1, :]
        grad_gate += jnp.sum(
            jnp.where(target_col == peer * capacity + lane, row, 0.0), axis=1, keepdims=True
        )
    grad_logits = grad_gate * gate * (onehot - soft) / ROUTER_SOFTNESS
    grad_unit = fine(dot, grad_logits, anchor_unit)
    grad_projected = unit_scale * (
        grad_unit - unit * jnp.sum(unit * grad_unit, axis=1, keepdims=True)
    )
    grad_anchor_unit = fine(dot_tn, grad_logits, unit)
    grad_anchor = anchor_scale * (
        grad_anchor_unit
        - anchor_unit * jnp.sum(anchor_unit * grad_anchor_unit, axis=1, keepdims=True)
    )
    rdim = route_ref.shape[0]
    small_ref[...] = jnp.zeros_like(small_ref)
    small_ref[0:rdim, :] = fine(dot_tn, grad_projected, normed)
    small_ref[rdim : rdim + experts, 0:rdim] = grad_anchor
    counts = jnp.sum(onehot, axis=0, keepdims=True)
    small_ref[rdim + experts + 2 : rdim + experts + 3, 0:experts] = counts
    router_rows = fine(dot, grad_projected, route_ref[...])

    bufs[1].forward()
    for group in range(3):
        back.wait_recv(group)
    lanes = lax.broadcasted_iota(jnp.int32, (tok, tok), 1).astype(F32)
    moe_rows = dot(jnp.where(lanes == target_col, 1.0, 0.0).astype(BF16), back_s[...])
    grad_normed = moe_rows + router_rows
    small_ref[rdim + experts : rdim + experts + 1, :] = jnp.sum(
        grad_normed * xhat, axis=0, keepdims=True
    )
    grad_xhat = grad_normed * gain
    grad_residual = grad_out + scale * (
        grad_xhat
        - jnp.mean(grad_xhat, axis=1, keepdims=True)
        - xhat * jnp.mean(grad_xhat * xhat, axis=1, keepdims=True)
    )
    grad_residual_ref[...] = grad_residual
    grad_low = grad_residual.astype(BF16)
    grad_residual_ref.flush()
    bufs[2].forward()
    grad_att_ref[...] = dot_nt(proj_ref[...], grad_low).astype(BF16)
    grad_att_ref.flush()
    grad_proj_ref[...] = dot(att_ref[...], grad_low).astype(BF16)

    grad_proj_ref.flush()
    for copy in kept + [cots_own]:
        copy.wait()
    for gather in cots + bufs:
        gather.wait_neighbours()
        gather.wait_diagonal()
        gather.wait_sends()
    for exchange in (go, gates, back, scores):
        exchange.wait_sends()
    for copy in gates_out:
        copy.wait()


def gelu_pair(hidden):
    squared = hidden * hidden
    curve = jnp.tanh(0.7978845608028654 * hidden * (1.0 + 0.044715 * squared))
    half = 0.5 * (1.0 + curve)
    slope = half + 0.5 * hidden * (1.0 - curve * curve) * (
        0.7978845608028654 * (1.0 + 0.134145 * squared)
    )
    return hidden * half, slope


def spread(row, size):
    shape = (size, row.shape[1])
    eye = lax.broadcasted_iota(jnp.int32, shape, 0) == lax.broadcasted_iota(jnp.int32, shape, 1)
    return jnp.sum(jnp.where(eye, row, 0.0), axis=1, keepdims=True)


def flatten(column, width):
    shape = (column.shape[0], width)
    eye = lax.broadcasted_iota(jnp.int32, shape, 0) == lax.broadcasted_iota(jnp.int32, shape, 1)
    return jnp.sum(jnp.where(eye, column, 0.0), axis=0, keepdims=True)


def attend_back_kernel(
    grad_att_ref, qkv_ref, out_ref, lse_ref, nall_ref, result_ref, residual_ref, gate_ref,
    cols_ref, rows_ref, wqkv_ref, tok_ref, grad_residual_ref, grad_proj_ref, small_ref,
    buf_ref, cots_ref, gates_ref, first_ref, second_ref,
    block_out_ref, grad_tokens_ref, shared_ref, small_out_ref, grad_first_ref, grad_second_ref,
    do_t, dq_s, dqkv_s, home_s, q_s, k_s, v_s, do_s, back_s, wt_s, proj_in, part_s, sum_s,
    core_out, core_in, line_out, line_in, small_a, small_in, small_b, row_out, row_in,
    first_s, second_s, slot_s, rows_s, shared_s,
    att_sems, back_sems, home_sems, proj_sems, core_sems, line_sems, join_sems, small_sems,
    row_sems, ring_sems, pair_sems, load_sems,
):
    blk, expert, bx, by, bd = places()
    tok = grad_att_ref.shape[1]
    width = grad_att_ref.shape[0]
    heads = HEADS // 4
    group = heads * HEAD_DIM
    here = rows_at(blk, tok)
    length = qkv_ref.shape[1]
    core = lax.rem(expert, 2)
    line = expert // 2
    lines = 4
    half = width // 2
    other = (blk, expert + 1 - 2 * core)
    mine_lanes = pl.ds(pl.multiple_of(core * half, 128), half)
    other_lanes = pl.ds(pl.multiple_of((1 - core) * half, 128), half)
    line_peers = [(blk, lax.rem(line + shift, lines) * 2 + core) for shift in range(1, lines)]
    gain = rows_ref[0:1, :]
    arrived = greet(blk_peers() + expert_peers())
    odd = lax.rem(blk, 2)
    quarter = first_s.shape[1]

    def load(src, dst, index):
        copy = pltpu.make_async_copy(src, dst, load_sems.at[index])
        copy.start()
        return copy

    weights = [
        load(first_ref.at[:, rows_at(blk, quarter)], first_s, 0),
        load(second_ref.at[rows_at(blk, quarter)], second_s, 1),
    ]
    slot_loads = []

    def load_slots(t):
        cut = slice(t * tok, (t + 1) * tok)
        slot_loads.append((
            load(buf_ref.at[cut], slot_s.at[t % 2, 0], 2 + t % 2),
            load(cots_ref.at[cut], slot_s.at[t % 2, 1], 4 + t % 2),
        ))

    load_slots(0)
    rows_load = [load(residual_ref, rows_s, 6)]
    mine = rows_at(blk, group)
    mine_load = load(grad_att_ref.at[mine], do_t.at[:, here], 7)
    own_slots = rows_at(expert, tok // 8)
    result_load = load(result_ref.at[own_slots], back_s.at[own_slots], 8)
    arrived()
    att_copies = [
        push(grad_att_ref.at[rows_at(peer[0], group)], do_t.at[:, here], att_sems, n, peer)
        for n, peer in enumerate(blk_peers())
    ]
    back = ExpertExchange(result_ref, back_s, back_sems, tok // 8)
    small_core = push(small_ref.at[:, other_lanes], small_in.at[0], small_sems, 0, other)
    for part in range(3):
        first = pl.multiple_of(part * width + blk * group - odd * 64, 128)
        wide = wqkv_ref[:, pl.ds(first, 256)]
        narrow = jnp.where(odd == 1, wide[:, 64:256], wide[:, 0:192]).T
        for head in range(heads):
            place = head * 192 + part * 64
            wt_s[place : place + 64, :] = narrow[head * 64 : (head + 1) * 64]

    def expert_weights(t):
        if t == 0:
            for copy in weights:
                copy.wait()
        if t < 3:
            load_slots(t + 1)
        for copy in slot_loads[t]:
            copy.wait()
        x = slot_s[t % 2, 0]
        rates = [spread(gates_ref[t * 64 + n * 8 : t * 64 + n * 8 + 1, :], 64) for n in range(8)]
        rate = jnp.concatenate(rates, axis=0)
        grad_in = (slot_s[t % 2, 1].astype(F32) * rate).astype(BF16)
        act, slope = gelu_pair(dot(x, first_s[...]))
        grad_hidden = (dot_nt(grad_in, second_s[...]) * slope).astype(BF16)
        grad_second = dot_tn(act.astype(BF16), grad_in)
        grad_first = dot_tn(x, grad_hidden)
        if t == 0:
            grad_second_ref[...] = grad_second
            grad_first_ref[...] = grad_first
        else:
            grad_second_ref[...] += grad_second
            grad_first_ref[...] += grad_first

    expert_weights(0)
    small_core.wait()
    small_a[...] = small_ref[:, mine_lanes] + small_in[0]
    small_in[1 + line] = small_a[...]
    small_line = [
        push(small_a, small_in.at[1 + line], small_sems, 1 + n, peer)
        for n, peer in enumerate(line_peers)
    ]
    back.start_all(False)
    expert_weights(1)
    mine_load.wait()
    for copy in att_copies:
        copy.wait_recv()
    proj_copies = [
        push(grad_proj_ref.at[rows_at(peer[0], group)], proj_in.at[n], proj_sems, n, peer)
        for n, peer in enumerate(blk_peers())
    ]

    chunk_rows = group
    piece = chunk_rows // lines
    core_copies, line_copies, joins, gathers, pairs = {}, {}, {}, {}, []
    small_blk = []

    def chunk_at(c):
        return slice(c * chunk_rows, (c + 1) * chunk_rows)

    def shared_at(block, c, first, size):
        row = pl.multiple_of(block * width + c * chunk_rows + first, 16)
        return shared_ref.at[pl.ds(row, size), mine_lanes]

    def send_core(c):
        core_out[chunk_at(c), :] = part_s[chunk_at(c), other_lanes].astype(BF16)
        core_copies[c] = push(
            core_out.at[chunk_at(c)], core_in.at[chunk_at(c)], core_sems, c, other)

    def send_line(c):
        core_copies[c].wait()
        summed = part_s[chunk_at(c), mine_lanes] + core_in[chunk_at(c), :].astype(F32)
        sum_s[chunk_at(c), :] = summed
        line_out[chunk_at(c), :] = summed.astype(BF16)
        line_copies[c] = [
            push(
                line_out.at[pl.ds(
                    pl.multiple_of(c * chunk_rows + (peer[1] // 2) * piece, piece), piece)],
                line_in.at[c * 3 + n], line_sems, c * 3 + n, peer)
            for n, peer in enumerate(line_peers)
        ]

    def send_join(c):
        for copy in line_copies[c]:
            copy.wait()
        first = pl.multiple_of(c * chunk_rows + line * piece, piece)
        total = sum_s[pl.ds(first, piece), :]
        for n in range(3):
            total = total + line_in[c * 3 + n].astype(F32)
        shared_s[c] = total.astype(BF16)
        ref = shared_at(blk, c, line * piece, piece)
        joins[c] = [
            push(shared_s.at[c], ref, join_sems, c * 3 + n, peer)
            for n, peer in enumerate(line_peers)]
        joins[c].append(load(shared_s.at[c], ref, 9 + c))

    def pair(block, c):
        ref = shared_at(block, c, 0, chunk_rows)
        pairs.append(push(ref, ref, pair_sems, len(pairs), other))

    def send_ring(c):
        for copy in joins[c]:
            copy.wait()
        size = chunk_rows // 2
        gathers[c] = BlockGather(
            lambda block, part: shared_at(block, c, part * size, size), ring_sems, c * 6)
        gathers[c].start()
        pair(blk, c)

    def forward(c):
        gathers[c].forward()

    def pair_neighbours(c):
        gathers[c].wait_neighbours()
        pair(bx, c)
        pair(by, c)

    def pair_diagonal(c):
        gathers[c].wait_diagonal()
        pair(bd, c)

    def sum_proj():
        for copy in proj_copies:
            copy.wait()
        part_s[chunk_at(3), :] = (
            (grad_proj_ref[mine, :].astype(F32) + proj_in[0].astype(F32))
            + (proj_in[1].astype(F32) + proj_in[2].astype(F32))
        )
        send_core(3)

    def sum_small():
        for copy in small_line:
            copy.wait()
        small_b[...] = (small_in[1] + small_in[2]) + (small_in[3] + small_in[4])
        small_in[5 + blk] = small_b[...]
        small_blk.extend(
            push(small_b, small_in.at[5 + blk], small_sems, 4 + n, peer)
            for n, peer in enumerate(blk_peers())
        )

    sent = []

    def send_home(head, part, block):
        src = slice(head * 192 + part * 64, head * 192 + (part + 1) * 64)
        there = pl.ds(pl.multiple_of(part * width + blk * group + head * 64, 64), 64)

        def copy():
            return pltpu.make_async_remote_copy(
                src_ref=dqkv_s.at[src, block * tok : (block + 1) * tok],
                dst_ref=home_s.at[there],
                send_sem=home_sems.at[0, (block * heads + head) * 3 + part],
                recv_sem=home_sems.at[1, (blk * heads + head) * 3 + part],
                device_id=(block, expert),
                device_id_type=MESH,
            )

        @pl.when(blk != block)
        def _():
            copy().start()

        @pl.when(blk == block)
        def _():
            home_s[there, :] = dqkv_s[src, block * tok : (block + 1) * tok]

        sent.append((block, copy))

    after = {
        (0, 3): [sum_small],
        (1, 1): [lambda: send_line(0)],
        (1, 2): [sum_proj],
        (1, 3): [lambda: send_join(0)],
        (2, 0): [lambda: send_line(3)],
        (2, 1): [lambda: send_ring(0), lambda: send_line(1)],
        (2, 2): [lambda: send_join(3)],
        (2, 3): [lambda: send_join(1)],
    }
    gain_total = None
    for head in range(heads):
        cut = slice(head * 64, (head + 1) * 64)
        kt_cut = slice(group + head * 64, group + (head + 1) * 64)
        vt_cut = slice(2 * group + head * 64, 2 * group + (head + 1) * 64)
        q_s[...] = qkv_ref[cut, :].T
        k_s[...] = qkv_ref[kt_cut, :].T
        v_s[...] = qkv_ref[vt_cut, :].T
        do_s[...] = do_t[cut, :].T
        delta = jnp.sum(out_ref[cut, :] * do_t[cut, :].astype(F32), axis=0, keepdims=True)
        base = head * 192
        for j in range(4):
            keys = slice(j * tok, (j + 1) * tok)
            queries = slice(j * tok, length)
            s = dot(k_s[keys, :], qkv_ref[cut, queries])
            p = jnp.exp(s - lse_ref[head : head + 1, queries])
            allowed = lower_triangle(tok, length - j * tok)
            p = jnp.where(allowed, p, 0.0)
            dp = dot(v_s[keys, :], do_t[cut, queries])
            ds = (p * (dp - delta[:, queries])).astype(BF16)
            dv = dot(p.astype(BF16), do_s[queries, :])
            dk = dot(ds, q_s[queries, :])
            dqkv_s[base + 64 : base + 128, keys] = dk.T.astype(BF16)
            dqkv_s[base + 128 : base + 192, keys] = dv.T.astype(BF16)
            send_home(head, 1, j)
            send_home(head, 2, j)
            dq = dot(qkv_ref[kt_cut, keys], ds)
            if j == 0:
                dq_s[...] = dq
            else:
                dq_s[:, queries] += dq
            for action in after.get((head, j), ()):
                action()
        dqkv_s[base : base + 64, :] = (dq_s[...] * HEAD_DIM**-0.5).astype(BF16)
        for block in range(4):
            send_home(head, 0, block)
        grad_group = dot(dqkv_s[base : base + 192, :], nall_ref[...])
        part_s[chunk_at(head), :] = grad_group
        send_core(head)
        share = jnp.sum(
            grad_group * wt_s[base : base + 192, :].astype(F32), axis=0, keepdims=True)
        gain_total = share if gain_total is None else gain_total + share

    attn_gain = gain_total / gain
    row_out[0] = jnp.concatenate(
        [attn_gain[:, n * 128 : (n + 1) * 128] for n in range(width // 128)]
        + [jnp.zeros((8 - width // 128, 128), F32)], axis=0)
    row_core = push(row_out.at[0], row_in.at[0], row_sems, 0, other)
    expert_weights(2)
    send_line(2)
    send_ring(3)
    for copy in small_blk:
        copy.wait()
    small_out_ref[:, mine_lanes] = (small_in[5] + small_in[6]) + (small_in[7] + small_in[8])
    small_pair = push(
        small_out_ref.at[:, mine_lanes], small_out_ref.at[:, mine_lanes], small_sems, 7, other)
    row_core.wait()
    row_out[1] = row_out[0] + row_in[0]
    row_in[1 + line] = row_out[1]
    row_line = [
        push(row_out.at[1], row_in.at[1 + line], row_sems, 1 + n, peer)
        for n, peer in enumerate(line_peers)
    ]
    send_ring(1)
    forward(0)
    back.wait_all()
    result_load.wait()
    lanes = lax.broadcasted_iota(jnp.int32, (tok, tok), 1).astype(F32)
    chosen = jnp.where(lanes == cols_ref[:, 0:1], 1.0, 0.0).astype(BF16)
    fetched = dot(chosen, back_s[...])
    rows_load[0].wait()
    block_out_ref[...] = (rows_s[...] + gate_ref[:, 0:1] * fetched).astype(BF16)
    block_out_ref.flush()
    rows_load.append(load(grad_residual_ref, rows_s, 6))
    send_join(2)
    forward(3)
    pair_neighbours(0)
    for copy in row_line:
        copy.wait()
    row_out[2] = (row_in[1] + row_in[2]) + (row_in[3] + row_in[4])
    row_in[5 + blk] = row_out[2]
    row_blk = [
        push(row_out.at[2], row_in.at[5 + blk], row_sems, 4 + n, peer)
        for n, peer in enumerate(blk_peers())
    ]
    forward(1)
    send_ring(2)
    pair_diagonal(0)
    pair_neighbours(3)

    for source in range(4):
        @pl.when(blk != source)
        def _():
            for item in range(9):
                index = source * 9 + item
                pltpu.make_async_remote_copy(
                    src_ref=dqkv_s.at[0:64, 0:tok],
                    dst_ref=home_s.at[0:64],
                    send_sem=home_sems.at[0, index],
                    recv_sem=home_sems.at[1, index],
                    device_id=(source, expert),
                    device_id_type=MESH,
                ).wait_recv()
    rows_load[1].wait()
    xhat, scale = standardise(tok_ref[...].astype(F32))

    def tokens_part(n):
        cut = slice(n * 256, (n + 1) * 256)
        grad_normed = dot(wqkv_ref[...], home_s[:, cut]).T
        grad_xhat = grad_normed * gain
        x = xhat[cut]
        grad_tokens_ref[cut, :] = rows_s[cut, :] + scale[cut] * (
            grad_xhat
            - jnp.mean(grad_xhat, axis=1, keepdims=True)
            - x * jnp.mean(grad_xhat * x, axis=1, keepdims=True)
        )

    tokens_part(0)
    pair_diagonal(3)
    pair_neighbours(1)
    forward(2)
    tokens_part(1)
    grad_tokens_ref.flush()
    pair_diagonal(1)
    expert_weights(3)
    grad_first_ref.flush()
    grad_second_ref.flush()
    pair_neighbours(2)
    pair_diagonal(2)
    for copy in row_blk:
        copy.wait()
    small_pair.wait()
    total = (row_in[5] + row_in[6]) + (row_in[7] + row_in[8])
    small_out_ref[25:26, :] = jnp.concatenate(
        [total[n : n + 1, :] for n in range(width // 128)], axis=1)
    for copy in pairs:
        copy.wait_recv()
    for copy in pairs:
        copy.wait_send()
    for gather in gathers.values():
        gather.wait_sends()
    for copy in att_copies:
        copy.wait_send()
    for block, copy in sent:
        @pl.when(blk != block)
        def _():
            copy().wait_send()


def unfold_kernel(shared_ref, grad_qkv_ref, grad_proj_ref):
    blocks, group = shared_ref.shape[0], grad_qkv_ref.shape[1] // shared_ref.shape[0]
    part = pl.program_id(1)
    for block in range(blocks):
        for head in range(group // HEAD_DIM):
            rows = pl.ds(pl.multiple_of(head * 192 + part * 64, 64), 64)
            cut = slice(block * group + head * 64, block * group + (head + 1) * 64)
            grad_qkv_ref[:, cut] = shared_ref[block, rows, :].astype(F32).T

    @pl.when(part == 0)
    def _():
        for block in range(blocks):
            grad_proj_ref[block * group : (block + 1) * group, :] = (
                shared_ref[block, 3 * group :, :].astype(F32))


def unfold(shared, blocks, group, width):
    shared = shared.reshape(blocks, width, width)
    pairs = blocks // 2
    return pl.pallas_call(
        unfold_kernel,
        grid=(pairs, 3),
        out_shape=(
            jax.ShapeDtypeStruct((width, 3 * width), F32),
            jax.ShapeDtypeStruct((width, width), F32),
        ),
        in_specs=[pl.BlockSpec((2, width, width), lambda n, part: (n, 0, 0))],
        out_specs=(
            pl.BlockSpec((width, 2 * group), lambda n, part: (0, part * pairs + n)),
            pl.BlockSpec((2 * group, width), lambda n, part: (n, 0)),
        ),
        name="unfold",
        compiler_params=pltpu.CompilerParams(vmem_limit_bytes=VMEM_BYTES),
    )(shared)


def call(kernel, name, args, outs, scratch, lazy=(), lazy_out=(), in_any=(), out_any=(),
         collective=None):
    n_in, n_out = len(args), len(outs)
    shapes = tuple(jax.ShapeDtypeStruct(shape, dtype) for shape, dtype in outs)
    staged = [pltpu.VMEM(args[n].shape, args[n].dtype) for n in lazy]
    staged += [pltpu.VMEM(shapes[n].shape, shapes[n].dtype) for n in lazy_out]
    sems = [pltpu.SemaphoreType.DMA((len(staged),))] if staged else []

    def wrapped(*refs):
        ins, results = list(refs[:n_in]), list(refs[n_in : n_in + n_out])
        rest = refs[n_in + n_out : n_in + n_out + len(scratch)]
        extra = refs[n_in + n_out + len(scratch) :]
        for k, n in enumerate(lazy):
            ins[n] = Lazy(ins[n], extra[k], extra[-1].at[k])
        for k, n in enumerate(lazy_out):
            k += len(lazy)
            results[n] = LazyOut(extra[k], results[n], extra[-1].at[k])
        kernel(*ins, *results, *rest)
        for n in lazy_out:
            results[n].flush()
        for n in lazy:
            ins[n].ref()
        for n in lazy_out:
            results[n].copy.wait()

    def spec(n, outside):
        return pl.BlockSpec(memory_space=pl.ANY if n in outside else pltpu.VMEM)

    return pl.pallas_call(
        wrapped,
        out_shape=shapes,
        in_specs=[spec(n, tuple(lazy) + tuple(in_any)) for n in range(n_in)],
        out_specs=tuple(spec(n, tuple(lazy_out) + tuple(out_any)) for n in range(n_out)),
        scratch_shapes=list(scratch) + staged + sems,
        name=name,
        compiler_params=pltpu.CompilerParams(
            vmem_limit_bytes=VMEM_BYTES,
            collective_id=collective,
            has_side_effects=collective is not None,
        ),
    )(*args)


def fast_body(
    tokens, cotangent, loss_mask, routes, priority, histogram, qkv_weight, proj_weight, attn_gain,
    moe_gain, route_weight, anchor_table, first_weight, second_weight,
):
    tok, width = tokens.shape[1:]
    blocks, experts = lax.axis_size("blk"), lax.axis_size("expert")
    length = tok * blocks
    heads = HEADS // blocks
    group = heads * HEAD_DIM
    hidden = first_weight.shape[2]
    x, cot = tokens[0], cotangent[0]
    pad = ((0, width - tok),)
    rows = jnp.stack(
        [attn_gain, moe_gain]
        + [jnp.pad(row.astype(F32), pad) for row in (routes[0, :, 0], priority[0, 0], loss_mask[0])]
        + [jnp.zeros((width,), F32)] * 3
    )
    dma = pltpu.SemaphoreType.DMA
    (nall, qkv, out, lse, cols, result, residual, gate, grad_residual, grad_att, grad_proj, small,
     buf, cots, gates) = call(
        forward_kernel, "forward",
        (x, rows, qkv_weight, cot, proj_weight, route_weight.T, anchor_table, first_weight[0],
         second_weight[0]),
        [((length, width), BF16), ((3 * group, length), BF16), ((group, length), F32),
         ((8, length), F32), ((tok, 128), F32),
         ((tok, width), BF16), ((tok, width), F32), ((tok, 128), F32), ((tok, width), F32),
         ((width, tok), BF16), ((width, width), BF16), ((32, width), F32),
         ((length, width), BF16), ((length, width), BF16), ((blocks * 64, 128), F32)],
        [pltpu.VMEM((3, width, 256), BF16), pltpu.VMEM((3 * group, width), BF16),
         pltpu.VMEM((heads, length, HEAD_DIM), BF16), pltpu.VMEM((group, length), BF16),
         pltpu.VMEM((tok, width), BF16), pltpu.VMEM((width, tok), BF16),
         pltpu.VMEM((tok, width), BF16),
         pltpu.VMEM((width, hidden), BF16), pltpu.VMEM((hidden, width), BF16),
         pltpu.VMEM((tok // 2, hidden), F32),
         pltpu.VMEM((tok, width), BF16), pltpu.VMEM((64, 128), F32),
         pltpu.VMEM((tok, width), BF16), pltpu.VMEM((64, 128), F32), pltpu.VMEM((tok, width), BF16),
         pltpu.VMEM((tok, width), BF16), pltpu.VMEM((64, 128), F32), pltpu.VMEM((64, 128), F32),
         pltpu.VMEM((tok // 2, width), F32), pltpu.VMEM((tok // 2, width), F32),
         pltpu.VMEM((tok // 2, width), BF16),
         dma((9,)), dma((2, 6)), dma((2, experts)), dma((2, blocks * heads)), dma((2, experts)),
         dma((2, experts)), dma((2, experts)), dma((2, experts)), dma((2, 12)), dma((2, 18)),
         dma((2, 3))],
        lazy=(3, 4), lazy_out=(0, 1, 2, 4, 5, 6, 7, 8, 9, 10), in_any=(2, 7, 8), out_any=(12, 13),
        collective=1,
    )
    half, piece, quarter = width // 2, group // 4, hidden // blocks
    block_out, grad_tokens, shared, small, grad_first, grad_second = call(
        attend_back_kernel, "attend_back",
        (grad_att, qkv, out, lse, nall, result, residual, gate, cols, rows, qkv_weight, x,
         grad_residual, grad_proj, small, buf, cots, gates, first_weight[0], second_weight[0]),
        [((tok, width), BF16), ((tok, width), F32), ((blocks * width, width), BF16),
         ((32, width), F32), ((width, quarter), F32), ((quarter, width), F32)],
        [pltpu.VMEM((group, length), BF16), pltpu.VMEM((HEAD_DIM, length), F32),
         pltpu.VMEM((3 * group, length), BF16), pltpu.VMEM((3 * width, tok), BF16)]
        + [pltpu.VMEM((length, HEAD_DIM), BF16)] * 4
        + [pltpu.VMEM((tok, width), BF16), pltpu.VMEM((3 * group, width), BF16),
           pltpu.VMEM((3, group, width), BF16),
           pltpu.VMEM((width, width), F32), pltpu.VMEM((width, half), F32),
           pltpu.VMEM((width, half), BF16), pltpu.VMEM((width, half), BF16),
           pltpu.VMEM((width, half), BF16), pltpu.VMEM((12, piece, half), BF16),
           pltpu.VMEM((32, half), F32), pltpu.VMEM((9, 32, half), F32), pltpu.VMEM((32, half), F32),
           pltpu.VMEM((3, 8, 128), F32), pltpu.VMEM((9, 8, 128), F32),
           pltpu.VMEM((width, quarter), BF16), pltpu.VMEM((quarter, width), BF16),
           pltpu.VMEM((2, 2, tok, width), BF16), pltpu.VMEM((tok, width), F32),
           pltpu.VMEM((4, piece, half), BF16),
           dma((2, 3)), dma((2, experts)), dma((2, 36)), dma((2, 3)), dma((2, 4)), dma((2, 12)),
           dma((2, 12)), dma((2, 8)), dma((2, 7)), dma((2, 24)), dma((2, 16)), dma((13,))],
        lazy=(1, 2, 4, 7, 8, 10, 11, 13), lazy_out=(0, 1, 4, 5),
        in_any=(0, 5, 6, 12, 15, 16, 18, 19), out_any=(2,), collective=3,
    )
    grad_qkv, grad_proj = unfold(shared, blocks, group, width)
    rdim = route_weight.shape[1]
    return (
        block_out[None],
        grad_tokens[None],
        grad_qkv,
        grad_proj,
        small[rdim + experts + 1],
        small[rdim + experts],
        small[:rdim].T,
        small[rdim : rdim + experts, :rdim],
        grad_first[None],
        grad_second[None],
        histogram + small[rdim + experts + 2, :experts].astype(jnp.int32),
    )


def solution(mesh):
    in_specs = (
        P("expert", "blk", None),
        P("expert", "blk", None),
        P("expert", "blk"),
        P("expert", "blk", None),
        P("expert", "blk", None),
        P(),
        P(),
        P(),
        P(),
        P(),
        P(),
        P(),
        P("expert", None, None),
        P("expert", None, None),
    )
    out_specs = (
        P("expert", "blk", None),
        P("expert", "blk", None),
        P(),
        P(),
        P(),
        P(),
        P(),
        P(),
        P("expert", None, "blk"),
        P("expert", "blk", None),
        P(),
    )
    blocks, experts = mesh.shape["blk"], mesh.shape["expert"]
    body = fast_body if (blocks, experts) == (4, 8) else general_body
    return jax.shard_map(body, mesh=mesh, in_specs=in_specs, out_specs=out_specs, check_vma=False)
```

```python
import functools

import jax
import jax.numpy as jnp
from jax import lax
from jax.experimental import pallas as pl
from jax.experimental.pallas import tpu as pltpu
from jax.sharding import PartitionSpec as P

HEADS = 12
HEAD_DIM = 64


TOP_PRECISION = lax.Precision.HIGHEST
EPSILON = 1e-05
ROUTER_SOFTNESS = 0.4
MASKED = -1e30


def layer_norm(values, norm_gain):
    average = jnp.mean(values, axis=-1, keepdims=True)
    centered = values - average
    variance = jnp.mean(centered * centered, axis=-1, keepdims=True)
    return centered * lax.rsqrt(variance + EPSILON) * norm_gain


def unit_rows(matrix):
    return matrix * lax.rsqrt(1.0 + jnp.sum(matrix * matrix, axis=-1, keepdims=True))


def router_gate(normalized_rows, route_matrix, anchors, route_onehot):
    projection_output = unit_rows(jnp.dot(normalized_rows, route_matrix, precision=TOP_PRECISION))
    expert_anchor_rows = unit_rows(anchors)
    route_logit_scores = (
        jnp.dot(projection_output, expert_anchor_rows.T, precision=TOP_PRECISION) / ROUTER_SOFTNESS
    )
    return jnp.sum(jax.nn.softmax(route_logit_scores, axis=-1) * route_onehot, axis=-1)


def masked_scores(queries, key_rows, query_first, key_first, score_scale):
    scores = (
        jnp.einsum("qhd,khd->hqk", queries, key_rows, preferred_element_type=jnp.float32)
        * score_scale
    )
    grid_shape = (queries.shape[0], key_rows.shape[0])
    query_place = query_first + lax.broadcasted_iota(jnp.int32, grid_shape, 0)
    key_place = key_first + lax.broadcasted_iota(jnp.int32, grid_shape, 1)
    return (scores, (key_place <= query_place)[None])


def over_blocks(step_fn, carried, arrays, block_rows):
    row_total = arrays[0].shape[0]
    block_count = row_total // block_rows
    stacked = tuple(
        (member.reshape((block_count, block_rows) + member.shape[1:]) for member in arrays)
    )

    def scan_step(running, packed):
        position, blocks = packed
        return (step_fn(running, blocks, position * block_rows), None)

    result, unused = lax.scan(
        scan_step, carried, (jnp.arange(block_count, dtype=jnp.int32), stacked)
    )
    return result


def general_body(
    tokens,
    cotangent,
    loss_mask,
    routes,
    priority,
    histogram,
    qkv_weight,
    proj_weight,
    attn_gain,
    moe_gain,
    route_weight,
    anchor_table,
    first_weight,
    second_weight,
):
    tok_rows = tokens.shape[1]
    model_width = tokens.shape[2]
    score_scale = HEAD_DIM ** (-0.5)
    query_first = lax.axis_index("blk") * tok_rows
    local_experts = first_weight.shape[0]
    experts_all = local_experts * lax.axis_size("expert")
    capacity = tok_rows // experts_all
    head_shape = (tok_rows, HEADS, HEAD_DIM)
    seq_rows = tok_rows * lax.axis_size("blk")
    route_ids = routes[0, :, 0]
    route_onehot = (
        route_ids[:, None] == lax.broadcasted_iota(jnp.int32, (tok_rows, experts_all), 1)
    ).astype(jnp.float32)
    count_rows = jnp.sum(route_onehot, axis=0)
    total_counts = lax.psum(count_rows.astype(jnp.int32), ("blk", "expert"))
    block_input = tokens[0].astype(jnp.float32)
    normed_attn, attn_norm_back = jax.vjp(layer_norm, block_input, attn_gain)
    normed_low = normed_attn.astype(jnp.bfloat16)
    query_key_value_mix = jnp.dot(
        normed_low, qkv_weight, preferred_element_type=jnp.float32
    ).astype(jnp.bfloat16)
    query_flat = query_key_value_mix[:, :model_width]
    queries = query_flat.reshape(head_shape)
    key_local = query_key_value_mix[:, model_width : 2 * model_width]
    value_local = query_key_value_mix[:, 2 * model_width :]

    def forward_step(carried, blocks, key_first):
        running_top, running_sum, running_out = carried
        key_rows = blocks[0].reshape(blocks[0].shape[0], HEADS, HEAD_DIM)
        value_rows = blocks[1].reshape(blocks[1].shape[0], HEADS, HEAD_DIM)
        scores, allowed = masked_scores(queries, key_rows, query_first, key_first, score_scale)
        top_new = jnp.maximum(running_top, jnp.max(jnp.where(allowed, scores, MASKED), axis=2))
        weights = jnp.where(allowed, jnp.exp(scores - top_new[:, :, None]), 0.0)
        factor = jnp.exp(running_top - top_new)
        running_sum = running_sum * factor + jnp.sum(weights, axis=2)
        running_out = running_out * factor.T[:, :, None] + jnp.einsum(
            "hqk,khd->qhd",
            weights.astype(jnp.bfloat16),
            value_rows,
            preferred_element_type=jnp.float32,
        )
        return (top_new, running_sum, running_out)

    initial = (
        jnp.full((HEADS, tok_rows), MASKED, jnp.float32),
        jnp.zeros((HEADS, tok_rows), jnp.float32),
        jnp.zeros(head_shape, jnp.float32),
    )
    running_top, running_sum, running_out = over_blocks(
        forward_step,
        initial,
        (
            lax.all_gather(key_local, "blk", axis=0, tiled=True),
            lax.all_gather(value_local, "blk", axis=0, tiled=True),
        ),
        tok_rows,
    )
    attention_result = running_out / running_sum.T[:, :, None]
    log_total = running_top + jnp.log(running_sum)
    attended_low = attention_result.reshape(tok_rows, model_width).astype(jnp.bfloat16)
    residual_stream = block_input + jnp.dot(
        attended_low, proj_weight, preferred_element_type=jnp.float32
    )
    normed_moe, moe_norm_back = jax.vjp(layer_norm, residual_stream, moe_gain)

    def gate_of(normalized_rows, route_matrix, anchors):
        return router_gate(normalized_rows, route_matrix, anchors, route_onehot)

    gate_value, gate_back = jax.vjp(gate_of, normed_moe, route_weight, anchor_table)
    order_rows = priority[0, 0]
    same_route = route_ids[:, None] == route_ids[None, :]
    earlier = order_rows[None, :] < order_rows[:, None]
    slot_ids = jnp.sum((same_route & earlier).astype(jnp.int32), axis=1)
    target = jnp.where(slot_ids < capacity, route_ids * capacity + slot_ids, -1)
    selector = lax.broadcasted_iota(jnp.int32, (tok_rows, tok_rows), 0) == target[None, :]
    selector_low = selector.astype(jnp.bfloat16)
    outgoing = jnp.dot(
        selector_low, normed_moe.astype(jnp.bfloat16), preferred_element_type=jnp.float32
    )
    outgoing = outgoing.astype(jnp.bfloat16).reshape(experts_all, capacity, model_width)
    arrived = lax.all_to_all(outgoing, "expert", split_axis=0, concat_axis=0, tiled=True)
    sources = arrived.shape[0] // local_experts
    grouped = arrived.reshape(sources, local_experts, arrived.shape[1], arrived.shape[2])
    hidden = jnp.einsum("secd,edf->secf", grouped, first_weight, preferred_element_type=jnp.float32)
    act_low = jax.nn.gelu(hidden).astype(jnp.bfloat16)
    result = jnp.einsum(
        "secf,efd->secd", act_low, second_weight, preferred_element_type=jnp.float32
    )
    result = result.astype(jnp.bfloat16).reshape(arrived.shape)
    returned = lax.all_to_all(result, "expert", split_axis=0, concat_axis=0, tiled=True)
    returned, arrived = (returned, arrived)
    fetched = jnp.einsum(
        "st,sd->td",
        selector_low,
        returned.reshape(tok_rows, model_width),
        preferred_element_type=jnp.float32,
    )
    block_out = (residual_stream + gate_value[:, None] * fetched).astype(jnp.bfloat16)[None]
    grad_out = cotangent[0].astype(jnp.float32) * loss_mask[0].astype(jnp.float32)[:, None]
    grad_fetched = grad_out * gate_value[:, None]
    grad_gate = jnp.sum(grad_out * fetched, axis=1)
    grad_slots = jnp.dot(selector.astype(jnp.float32), grad_fetched, precision=TOP_PRECISION)
    grad_slots = grad_slots.astype(jnp.bfloat16).reshape(experts_all, capacity, model_width)
    grad_arrived = lax.all_to_all(grad_slots, "expert", split_axis=0, concat_axis=0, tiled=True)
    sources = grad_arrived.shape[0] // local_experts
    slot_shape = (sources, local_experts, capacity, model_width)
    grouped_in = arrived.reshape(slot_shape)
    grouped_grad = grad_arrived.reshape(slot_shape)
    hidden = jnp.einsum(
        "secd,edf->secf", grouped_in, first_weight, preferred_element_type=jnp.float32
    )
    act_low = jax.nn.gelu(hidden).astype(jnp.bfloat16)
    grad_second = jnp.einsum(
        "secf,secd->efd", act_low, grouped_grad, preferred_element_type=jnp.float32
    )
    grad_act = jnp.einsum(
        "secd,efd->secf", grouped_grad, second_weight, preferred_element_type=jnp.float32
    )
    unused, gelu_back = jax.vjp(jax.nn.gelu, hidden)
    grad_hidden = gelu_back(grad_act)[0].astype(jnp.bfloat16)
    grad_first = jnp.einsum(
        "secd,secf->edf", grouped_in, grad_hidden, preferred_element_type=jnp.float32
    )
    grad_sent = jnp.einsum(
        "secf,edf->secd", grad_hidden, first_weight, preferred_element_type=jnp.float32
    )
    grad_sent = grad_sent.astype(jnp.bfloat16).reshape(grad_arrived.shape)
    grad_returned = lax.all_to_all(grad_sent, "expert", split_axis=0, concat_axis=0, tiled=True)
    grad_first, grad_second = (
        lax.psum_scatter(
            grad_first.astype(jnp.bfloat16), "blk", scatter_dimension=2, tiled=True
        ).astype(jnp.float32),
        lax.psum_scatter(
            grad_second.astype(jnp.bfloat16), "blk", scatter_dimension=1, tiled=True
        ).astype(jnp.float32),
    )
    grad_moe_rows = jnp.einsum(
        "st,sd->td",
        selector_low,
        grad_returned.reshape(tok_rows, model_width),
        preferred_element_type=jnp.float32,
    )
    grad_router_rows, grad_route, grad_anchor = gate_back(grad_gate)
    grad_residual_norm, grad_moe_gain = moe_norm_back(grad_moe_rows + grad_router_rows)
    grad_residual = grad_out + grad_residual_norm
    grad_attn_low = grad_residual.astype(jnp.bfloat16)
    grad_proj = jnp.dot(attended_low.T, grad_attn_low, preferred_element_type=jnp.float32)
    grad_attended_flat = jnp.dot(
        grad_attn_low, proj_weight.T, preferred_element_type=jnp.float32
    ).astype(jnp.bfloat16)
    grad_attended = grad_attended_flat.reshape(head_shape)
    delta_rows = jnp.sum(grad_attended.astype(jnp.float32) * attention_result, axis=2).T
    key_all, value_all = (
        lax.all_gather(key_local, "blk", axis=0, tiled=True),
        lax.all_gather(value_local, "blk", axis=0, tiled=True),
    )
    block_count = seq_rows // tok_rows
    key_blocks = key_all.reshape(block_count, tok_rows, model_width)
    value_blocks = value_all.reshape(block_count, tok_rows, model_width)

    def key_block_step(running_grad, packed):
        position, key_block, value_block = packed
        key_rows = key_block.reshape(head_shape)
        value_rows = value_block.reshape(head_shape)
        scores, allowed = masked_scores(
            queries, key_rows, query_first, position * tok_rows, score_scale
        )
        soft_rows = jnp.where(allowed, jnp.exp(scores - log_total[:, :, None]), 0.0)
        grad_values = jnp.einsum(
            "hqk,qhd->khd",
            soft_rows.astype(jnp.bfloat16),
            grad_attended,
            preferred_element_type=jnp.float32,
        )
        grad_soft = jnp.einsum(
            "qhd,khd->hqk", grad_attended, value_rows, preferred_element_type=jnp.float32
        )
        grad_scores = (soft_rows * (grad_soft - delta_rows[:, :, None])).astype(jnp.bfloat16)
        grad_keys = score_scale * jnp.einsum(
            "hqk,qhd->khd", grad_scores, queries, preferred_element_type=jnp.float32
        )
        running_grad = running_grad + score_scale * jnp.einsum(
            "hqk,khd->qhd", grad_scores, key_rows, preferred_element_type=jnp.float32
        )
        term = jnp.concatenate(
            [grad_keys.reshape(tok_rows, model_width), grad_values.reshape(tok_rows, model_width)],
            axis=1,
        )
        return (running_grad, term)

    grad_queries, stacked_terms = lax.scan(
        key_block_step,
        jnp.zeros(head_shape, jnp.float32),
        (jnp.arange(block_count, dtype=jnp.int32), key_blocks, value_blocks),
    )
    all_terms = stacked_terms.reshape(seq_rows, 2 * model_width)
    key_value_grads = lax.psum_scatter(
        all_terms.astype(jnp.bfloat16), "blk", scatter_dimension=0, tiled=True
    ).astype(jnp.float32)
    grad_query_rows = grad_queries.reshape(tok_rows, model_width)
    grad_qkv_rows = jnp.concatenate([grad_query_rows, key_value_grads], axis=1).astype(jnp.bfloat16)
    grad_qkv = jnp.dot(normed_low.T, grad_qkv_rows, preferred_element_type=jnp.float32)
    grad_normed = jnp.dot(grad_qkv_rows, qkv_weight.T, preferred_element_type=jnp.float32)
    grad_source_norm, grad_attn_gain = attn_norm_back(grad_normed)
    grad_tokens = (grad_residual + grad_source_norm)[None]
    grad_qkv, grad_proj, grad_attn_gain, grad_moe_gain, grad_route, grad_anchor = lax.psum(
        (grad_qkv, grad_proj, grad_attn_gain, grad_moe_gain, grad_route, grad_anchor),
        ("blk", "expert"),
    )
    histogram_out = histogram + total_counts
    return (
        block_out,
        grad_tokens,
        grad_qkv,
        grad_proj,
        grad_attn_gain,
        grad_moe_gain,
        grad_route,
        grad_anchor,
        grad_first,
        grad_second,
        histogram_out,
    )


MESH = pl.DeviceIdType.MESH
F32 = jnp.float32
BF16 = jnp.bfloat16
VMEM_BYTES = 58 * 1024 * 1024


def dot(left, right, precision=None):
    return lax.dot_general(
        left, right, (((1,), (0,)), ((), ())), precision=precision, preferred_element_type=F32
    )


def dot_nt(left, right, precision=None):
    return lax.dot_general(
        left, right, (((1,), (1,)), ((), ())), precision=precision, preferred_element_type=F32
    )


def dot_tn(left, right, precision=None):
    return lax.dot_general(
        left, right, (((0,), (0,)), ((), ())), precision=precision, preferred_element_type=F32
    )


def split(values):
    high = values.astype(BF16)
    return high, (values - high.astype(F32)).astype(BF16)


def fine(product, left, right):
    left_high, left_low = split(left)
    right_high, right_low = split(right)
    return product(left_high, right_high) + (
        product(left_high, right_low) + product(left_low, right_high)
    )


def rows_at(index, size):
    return pl.ds(pl.multiple_of(index * size, size), size)


def places():
    blk = lax.axis_index("blk")
    expert = lax.axis_index("expert")
    return blk, expert, blk + 1 - 2 * lax.rem(blk, 2), lax.rem(blk + 2, 4), 3 - blk


def greet(peers):
    barrier = pltpu.get_barrier_semaphore()
    for peer in peers:
        pl.semaphore_signal(barrier, inc=1, device_id=peer, device_id_type=MESH)
    return lambda: pl.semaphore_wait(barrier, len(peers))


def push(src, dst, sems, index, peer):
    copy = pltpu.make_async_remote_copy(
        src_ref=src,
        dst_ref=dst,
        send_sem=sems.at[0, index],
        recv_sem=sems.at[1, index],
        device_id=peer,
        device_id_type=MESH,
    )
    copy.start()
    return copy


def standardise(values):
    average = jnp.mean(values, axis=-1, keepdims=True)
    centered = values - average
    scale = lax.rsqrt(jnp.mean(centered * centered, axis=-1, keepdims=True) + EPSILON)
    return centered * scale, scale


def lower_triangle(keys, queries):
    return lax.broadcasted_iota(jnp.int32, (keys, queries), 0) <= lax.broadcasted_iota(
        jnp.int32, (keys, queries), 1
    )


class BlockGather:
    def __init__(self, part, sems, base, own=None):
        self.part, self.sems, self.base, self.own = part, sems, base, own

    def send(self, blk, half, index, peer):
        ref = self.part(blk, half)
        src = ref if self.own is None or index > 3 else self.own(half)
        return push(src, ref, self.sems, self.base + index, peer)

    def start(self):
        self.start_first()
        self.start_second()

    def start_first(self):
        blk, expert, bx, by, bd = places()
        self.copies = [self.send(blk, 0, 0, (bx, expert)), self.send(blk, 1, 1, (by, expert))]

    def start_second(self):
        blk, expert, bx, by, bd = places()
        self.copies += [self.send(blk, 1, 2, (bx, expert)), self.send(blk, 0, 3, (by, expert))]

    def forward(self):
        blk, expert, bx, by, bd = places()
        self.copies[0].wait_recv()
        self.copies.append(self.send(bx, 0, 4, (by, expert)))
        self.copies[1].wait_recv()
        self.copies.append(self.send(by, 1, 5, (bx, expert)))

    def wait_neighbours(self):
        self.copies[2].wait_recv()
        self.copies[3].wait_recv()

    def wait_diagonal(self):
        self.copies[4].wait_recv()
        self.copies[5].wait_recv()

    def wait_sends(self):
        for copy in self.copies:
            copy.wait_send()


def row_halves(buf, rows):
    size = rows // 2
    return lambda blk, half: buf.at[pl.ds(pl.multiple_of(blk * rows + half * size, size), size)]


def expert_groups():
    expert = lax.axis_index("expert")
    line, core = expert // 2, lax.rem(expert, 2)
    side, place = line // 2, lax.rem(line, 2)
    beside = (side * 2 + 1 - place) * 2
    first = ((1 - side) * 2 + place) * 2
    second = ((1 - side) * 2 + 1 - place) * 2
    return [
        (side * 4, 4, [expert + 1 - 2 * core, beside + core, beside + 1 - core]),
        (first, 2, [first + core, first + 1 - core]),
        (second, 2, [second + core, second + 1 - core]),
    ]


class ExpertExchange:
    def __init__(self, src, dst, sems, rows):
        self.src, self.dst, self.sems, self.rows = src, dst, sems, rows
        self.groups = expert_groups()
        self.copies = [[], [], []]

    def start(self, group, keep=True):
        blk, expert = lax.axis_index("blk"), lax.axis_index("expert")
        place = rows_at(expert, self.rows)
        base = (0, 3, 5)[group]
        for n, peer in enumerate(self.groups[group][2]):
            self.copies[group].append(
                push(self.src.at[rows_at(peer, self.rows)], self.dst.at[place], self.sems,
                     base + n, (blk, peer))
            )
        if group == 0 and keep:
            self.dst[place] = self.src[place]

    def wait_recv(self, group):
        for copy in self.copies[group]:
            copy.wait_recv()

    def wait_sends(self):
        for copy in sum(self.copies, []):
            copy.wait_send()

    def start_all(self, keep=True):
        self.start(1)
        self.start(2)
        self.start(0, keep)

    def wait_all(self):
        for group in range(3):
            self.wait_recv(group)
        self.wait_sends()


class Lazy:
    def __init__(self, src, dst, sem):
        self.dst, self.shape, self.fresh = dst, dst.shape, True
        self.copy = pltpu.make_async_copy(src, dst, sem)
        self.copy.start()

    def ref(self):
        if self.fresh:
            self.copy.wait()
            self.fresh = False
        return self.dst

    def __getitem__(self, where):
        return self.ref()[where]

    @property
    def at(self):
        return self.ref().at


class LazyOut:
    def __init__(self, src, dst, sem):
        self.src, self.dst, self.sem, self.shape, self.copy = src, dst, sem, src.shape, None

    def flush(self):
        if self.copy is None:
            self.copy = pltpu.make_async_copy(self.src, self.dst, self.sem)
            self.copy.start()

    def __getitem__(self, where):
        return self.src[where]

    def __setitem__(self, where, value):
        self.src[where] = value

    @property
    def at(self):
        return self.src.at


def blk_peers():
    blk, expert, bx, by, bd = places()
    return [(bx, expert), (by, expert), (bd, expert)]


def expert_peers():
    blk, expert = lax.axis_index("blk"), lax.axis_index("expert")
    n = lax.axis_size("expert")
    return [(blk, lax.rem(expert + shift, n)) for shift in range(1, n)]


def forward_kernel(
    tok_ref, attn_gain_ref, moe_gain_ref, routes_ref, priority_ref, mask_ref, wqkv_ref, cot_ref, proj_ref, route_ref, anchor_ref, first_ref, second_ref,
    nall_ref, qkv_ref, out_ref, lse_ref, cols_ref, result_ref, residual_ref, gate_ref,
    grad_residual_ref, grad_att_ref, grad_proj_ref, small_ref, buf_ref, cots_ref, gates_ref,
    w_s, wt_s, k_s, att_s, cot_s, att_ref, cot_in_ref,
    first_s, second_s, slope_s, buf_s, gates_s, go_s, gate_s, grad_s, back_s, score_s, score_in_s,
    res_acc, sent_acc, grad_in_s,
    w_sem, gather_sems, cot_sems, att_sems, go_sems, gate_sems, back_sems, score_sems, cots_sems,
    buf_sems, gates_sems,
):
    blk, expert, bx, by, bd = places()
    tok = tok_ref.shape[0]
    width = tok_ref.shape[1]
    heads = HEADS // 4
    group = heads * HEAD_DIM
    arrived = greet(blk_peers() + expert_peers())
    odd = lax.rem(blk, 2)
    loads = []
    for part in range(3):
        first = pl.multiple_of(part * width + blk * group - odd * 64, 128)
        loads.append(
            pltpu.make_async_copy(wqkv_ref.at[:, pl.ds(first, 256)], w_s.at[part], w_sem.at[part])
        )
        loads[-1].start()
    weights = [
        pltpu.make_async_copy(first_ref, first_s, w_sem.at[3]),
        pltpu.make_async_copy(second_ref, second_s, w_sem.at[4]),
    ]
    for load in weights:
        load.start()
    xhat, _ = standardise(tok_ref[...].astype(F32))
    nall_ref[rows_at(blk, tok), :] = (xhat * attn_gain_ref[...].reshape(1, width)).astype(BF16)
    arrived()
    gather = BlockGather(row_halves(nall_ref, tok), gather_sems, 0)
    gather.start()

    capacity = tok // 8
    route_row, prio_row, mask_row = (
        ref[...].astype(F32) for ref in (routes_ref, priority_ref, mask_ref))
    cols = jnp.concatenate(
        [jnp.zeros((1, tok), F32), route_row, prio_row, mask_row, jnp.zeros((124, tok), F32)],
        axis=0).T
    route_col, prio_col = cols[:, 1:2], cols[:, 2:3]
    same = route_col == route_row
    slot_row = jnp.sum(jnp.where(same & (prio_col < prio_row), 1.0, 0.0), axis=0, keepdims=True)
    slot_col = jnp.sum(jnp.where(same & (prio_row < prio_col), 1.0, 0.0), axis=1, keepdims=True)
    target_row = jnp.where(slot_row < capacity, route_row * capacity + slot_row, -1.0)
    target_col = jnp.where(slot_col < capacity, route_col * capacity + slot_col, -1.0)
    lane = lax.broadcasted_iota(jnp.int32, cols.shape, 1)
    cols_ref[...] = jnp.where(lane == 0, target_col, cols)
    cols_ref.flush()
    slots = lax.broadcasted_iota(jnp.int32, (tok, tok), 0).astype(F32)
    chosen = jnp.where((slots == target_row) & (mask_row > 0.0), 1.0, 0.0).astype(BF16)
    cot_s[...] = dot(chosen, cot_ref[...]).astype(BF16)
    cot_move = ExpertExchange(cot_s, cot_in_ref, cot_sems, capacity)
    cot_move.start_all()

    for part in range(3):
        loads[part].wait()
        wide = w_s[part]
        narrow = jnp.where(odd == 1, wide[:, 64:256], wide[:, 0:192])
        wt_s[part * group : (part + 1) * group, :] = narrow.T

    def project(where):
        cols = rows_at(where, tok)
        mixed = dot_nt(wt_s[...], nall_ref[cols, :]).astype(BF16)
        qkv_ref[0:group, cols] = mixed[0:group] * BF16(HEAD_DIM**-0.5)
        qkv_ref[group:, cols] = mixed[group:]
        for head in range(heads):
            k_s[head, cols, :] = mixed[group + head * 64 : group + (head + 1) * 64].T

    project(blk)
    gather.forward()
    gather.wait_neighbours()
    project(bx)
    project(by)
    gather.wait_diagonal()
    nall_ref.flush()
    cot_move.wait_all()
    here = rows_at(blk, tok)
    cots_own = pltpu.make_async_copy(cot_in_ref, cots_ref.at[here], w_sem.at[5])
    cots_own.start()
    quarter = tok // 4
    cots = []
    for part in range(2):

        def own(half, part=part):
            return cot_in_ref.at[pl.ds((2 * part + half) * quarter, quarter)]

        def halves(block, half, part=part):
            row = pl.multiple_of(block * tok + (2 * part + half) * quarter, quarter)
            return cots_ref.at[pl.ds(row, quarter)]

        cots.append(BlockGather(halves, cots_sems, 6 * part, own))
    cots[0].start_first()
    project(bd)
    qkv_ref.flush()

    half = tok // 2

    def scores(i, head):
        q = qkv_ref[head * 64 : (head + 1) * 64, i * tok : (i + 1) * tok]
        upper = dot(k_s[head, i * tok : i * tok + half, :], q)
        upper = jnp.where(lower_triangle(half, tok), upper, MASKED)
        lower = dot(k_s[head, i * tok + half : (i + 1) * tok, :], q[:, half:])
        lower = jnp.where(lower_triangle(half, half), lower, MASKED)
        top = jnp.max(upper, axis=0, keepdims=True)
        low_top = jnp.max(lower, axis=0, keepdims=True)
        top = jnp.concatenate([top[:, :half], jnp.maximum(top[:, half:], low_top)], axis=1)
        if i == 0:
            return top, upper, lower, None
        past = dot(k_s[head, 0 : i * tok, :], q)
        return jnp.maximum(top, jnp.max(past, axis=0, keepdims=True)), upper, lower, past

    sends = []

    def finish(i, head, found):
        top, upper, lower, past = found
        v = qkv_ref[2 * group + head * 64 : 2 * group + (head + 1) * 64, :]
        upper = jnp.exp(upper - top)
        lower = jnp.exp(lower - top[:, half:])
        total = jnp.sum(upper, axis=0, keepdims=True)
        low_total = jnp.sum(lower, axis=0, keepdims=True)
        total = jnp.concatenate([total[:, :half], total[:, half:] + low_total], axis=1)
        result = dot(v[:, i * tok : i * tok + half], upper.astype(BF16))
        low_result = dot(v[:, i * tok + half : (i + 1) * tok], lower.astype(BF16))
        result = jnp.concatenate([result[:, :half], result[:, half:] + low_result], axis=1)
        if i:
            past = jnp.exp(past - top)
            total = total + jnp.sum(past, axis=0, keepdims=True)
            result = result + dot(v[:, 0 : i * tok], past.astype(BF16))
        result = result / total
        place = slice(head * 64, (head + 1) * 64)
        out_ref[place, i * tok : (i + 1) * tok] = result
        lse_ref[head : head + 1, i * tok : (i + 1) * tok] = top + jnp.log(total)
        att_s[place, i * tok : (i + 1) * tok] = result.astype(BF16)
        there = pl.ds(pl.multiple_of(blk * group + head * 64, 64), 64)

        def copy():
            return pltpu.make_async_remote_copy(
                src_ref=att_s.at[place, i * tok : (i + 1) * tok],
                dst_ref=att_ref.at[there],
                send_sem=att_sems.at[0, i * heads + head],
                recv_sem=att_sems.at[1, blk * heads + head],
                device_id=(i, expert),
                device_id_type=MESH,
            )

        @pl.when(blk != i)
        def _():
            copy().start()

        @pl.when(blk == i)
        def _():
            att_ref[there, :] = result.astype(BF16)

        sends.append((i, copy))

    before = None
    for i in range(4):
        for head in range(heads):
            found = scores(i, head)
            if before is not None:
                finish(*before)
            before = (i, head, found)
    finish(*before)

    for i, copy in sends:
        @pl.when(blk != i)
        def _():
            copy().wait_send()

    for source in range(4):
        @pl.when(blk != source)
        def _():
            for head in range(heads):
                there = pl.ds(source * group + head * 64, 64)
                pltpu.make_async_remote_copy(
                    src_ref=att_s.at[0:64, 0:tok],
                    dst_ref=att_ref.at[there],
                    send_sem=att_sems.at[0, source * heads + head],
                    recv_sem=att_sems.at[1, source * heads + head],
                    device_id=(source, expert),
                    device_id_type=MESH,
                ).wait_recv()

    cots[0].forward()
    cots[0].start_second()
    cots[1].start()
    out_ref.flush()
    gather.wait_sends()

    gain = moe_gain_ref[...].reshape(1, width)
    experts = 8
    residual = tok_ref[...].astype(F32) + dot_tn(att_ref[...], proj_ref[...])
    residual_ref[...] = residual
    residual_ref.flush()
    xhat, scale = standardise(residual)
    normed = xhat * gain
    normed_low = normed.astype(BF16)
    go_s[...] = dot(jnp.where(slots == target_row, 1.0, 0.0).astype(BF16), normed_low).astype(BF16)
    go = ExpertExchange(go_s, buf_s, go_sems, capacity)
    go.start(0)
    go.start(1)

    projected = fine(dot_nt, normed, route_ref[...])
    unit_scale = lax.rsqrt(1.0 + jnp.sum(projected * projected, axis=1, keepdims=True))
    unit = projected * unit_scale
    anchor = anchor_ref[...]
    anchor_scale = lax.rsqrt(1.0 + jnp.sum(anchor * anchor, axis=1, keepdims=True))
    anchor_unit = anchor * anchor_scale
    logits = fine(dot_nt, unit, anchor_unit) / ROUTER_SOFTNESS
    soft = jnp.exp(logits - jnp.max(logits, axis=1, keepdims=True))
    soft = soft / jnp.sum(soft, axis=1, keepdims=True)
    onehot = jnp.where(
        lax.broadcasted_iota(jnp.int32, (tok, experts), 1).astype(F32) == route_col, 1.0, 0.0
    )
    gate = jnp.sum(soft * onehot, axis=1, keepdims=True)
    gate_ref[...] = jnp.broadcast_to(gate, gate_ref.shape)
    gate_ref.flush()
    lane = lax.broadcasted_iota(jnp.int32, (tok, 128), 1).astype(F32)
    lane = jnp.where(lane < capacity, lane, 1e6)
    for peer in range(experts):
        row = jnp.sum(
            jnp.where(target_col == peer * capacity + lane, gate, 0.0), axis=0, keepdims=True
        )
        gate_s[peer * 8 : (peer + 1) * 8, :] = jnp.broadcast_to(row, (8, 128))
    gates = ExpertExchange(gate_s, gates_s, gate_sems, 8)
    for group in range(3):
        gates.start(group)

    back = ExpertExchange(grad_s, back_s, back_sems, capacity)
    scores = ExpertExchange(score_s, score_in_s, score_sems, 8)
    tile = 768
    tiles = first_s.shape[1] // tile
    bufs, kept = [], []
    for group, (first_source, sources, _) in enumerate(go.groups):
        count = sources * capacity
        rows = pl.ds(pl.multiple_of(first_source * capacity, count), count)
        go.wait_recv(group)
        if group == 0:
            go.start(2)

        def halves(block, half, first=first_source * capacity, size=count // 2):
            return buf_ref.at[pl.ds(pl.multiple_of(block * tok + first + half * size, size), size)]

        def own(half, first=first_source * capacity, size=count // 2):
            return buf_s.at[pl.ds(pl.multiple_of(first + half * size, size), size)]

        bufs.append(BlockGather(halves, buf_sems, 6 * group, own))
        bufs[group].start()
        there = pl.ds(pl.multiple_of(blk * tok + first_source * capacity, count), count)
        kept.append(pltpu.make_async_copy(buf_s.at[rows], buf_ref.at[there], w_sem.at[6 + group]))
        kept[group].start()
        if group == 0:
            for load in weights:
                load.wait()
        x = buf_s[rows, :]
        for t in range(tiles):
            cut = slice(t * tile, (t + 1) * tile)
            act, slope = gelu_pair(dot(x, first_s[:, cut]))
            slope_s[0:count, cut] = slope
            part = dot(act.astype(BF16), second_s[cut, :])
            if t == 0:
                res_acc[0:count, :] = part
            else:
                res_acc[0:count, :] += part
        result = res_acc[0:count, :].astype(BF16)
        score = jnp.sum(
            result.astype(F32) * cot_in_ref[rows, :].astype(F32), axis=1, keepdims=True)
        for n in range(sources):
            row = flatten(score[n * capacity : (n + 1) * capacity], 128)
            score_s[rows_at(first_source + n, 8), :] = jnp.broadcast_to(row, (8, 128))
        scores.start(group)
        result_ref[rows, :] = result
        if group == 0:
            cots[1].forward()
        gates.wait_recv(group)
        for n in range(sources):
            row = gates_s[rows_at(first_source + n, 8), :][0:1, :]
            chunk = rows_at(first_source + n, capacity)
            grad_in_s[n * capacity : (n + 1) * capacity, :] = (
                cot_in_ref[chunk, :].astype(F32) * spread(row, capacity)
            ).astype(BF16)
        grad_in = grad_in_s[0:count, :]
        for t in range(tiles):
            cut = slice(t * tile, (t + 1) * tile)
            grad_hidden = (dot_nt(grad_in, second_s[cut, :]) * slope_s[0:count, cut]).astype(BF16)
            sent = dot_nt(grad_hidden, first_s[:, cut])
            if t == 0:
                sent_acc[0:count, :] = sent
            else:
                sent_acc[0:count, :] += sent
        grad_s[rows, :] = sent_acc[0:count, :].astype(BF16)
        back.start(group)
    bufs[0].forward()
    result_ref.flush()
    gates_ref[rows_at(blk, 64), :] = gates_s[...]
    gates_here = gates_ref.at[rows_at(blk, 64)]
    gates_out = [
        push(gates_here, gates_here, gates_sems, n, peer) for n, peer in enumerate(blk_peers())
    ]
    grad_out = cot_ref[...].astype(F32) * cols_ref[:, 3:4]

    for group in range(3):
        scores.wait_recv(group)
    grad_gate = jnp.zeros((tok, 1), F32)
    for peer in range(experts):
        row = score_in_s[peer * 8 : peer * 8 + 1, :]
        grad_gate += jnp.sum(
            jnp.where(target_col == peer * capacity + lane, row, 0.0), axis=1, keepdims=True
        )
    grad_logits = grad_gate * gate * (onehot - soft) / ROUTER_SOFTNESS
    grad_unit = fine(dot, grad_logits, anchor_unit)
    grad_projected = unit_scale * (
        grad_unit - unit * jnp.sum(unit * grad_unit, axis=1, keepdims=True)
    )
    grad_anchor_unit = fine(dot_tn, grad_logits, unit)
    grad_anchor = anchor_scale * (
        grad_anchor_unit
        - anchor_unit * jnp.sum(anchor_unit * grad_anchor_unit, axis=1, keepdims=True)
    )
    rdim = route_ref.shape[0]
    small_ref[...] = jnp.zeros_like(small_ref)
    small_ref[0:rdim, :] = fine(dot_tn, grad_projected, normed)
    small_ref[rdim : rdim + experts, 0:rdim] = grad_anchor
    counts = jnp.sum(onehot, axis=0, keepdims=True)
    small_ref[rdim + experts + 2 : rdim + experts + 3, 0:experts] = counts
    router_rows = fine(dot, grad_projected, route_ref[...])

    bufs[1].forward()
    for group in range(3):
        back.wait_recv(group)
    lanes = lax.broadcasted_iota(jnp.int32, (tok, tok), 1).astype(F32)
    moe_rows = dot(jnp.where(lanes == target_col, 1.0, 0.0).astype(BF16), back_s[...])
    grad_normed = moe_rows + router_rows
    small_ref[rdim + experts : rdim + experts + 1, :] = jnp.sum(
        grad_normed * xhat, axis=0, keepdims=True
    )
    grad_xhat = grad_normed * gain
    grad_residual = grad_out + scale * (
        grad_xhat
        - jnp.mean(grad_xhat, axis=1, keepdims=True)
        - xhat * jnp.mean(grad_xhat * xhat, axis=1, keepdims=True)
    )
    grad_residual_ref[...] = grad_residual
    grad_low = grad_residual.astype(BF16)
    grad_residual_ref.flush()
    bufs[2].forward()
    grad_att_ref[...] = dot_nt(proj_ref[...], grad_low).astype(BF16)
    grad_att_ref.flush()
    grad_proj_ref[...] = dot(att_ref[...], grad_low).astype(BF16)

    grad_proj_ref.flush()
    for copy in kept + [cots_own]:
        copy.wait()
    for gather in cots + bufs:
        gather.wait_neighbours()
        gather.wait_diagonal()
        gather.wait_sends()
    for exchange in (go, gates, back, scores):
        exchange.wait_sends()
    for copy in gates_out:
        copy.wait()


def gelu_pair(hidden):
    squared = hidden * hidden
    curve = jnp.tanh(0.7978845608028654 * hidden * (1.0 + 0.044715 * squared))
    half = 0.5 * (1.0 + curve)
    slope = half + 0.5 * hidden * (1.0 - curve * curve) * (
        0.7978845608028654 * (1.0 + 0.134145 * squared)
    )
    return hidden * half, slope


def spread(row, size):
    shape = (size, row.shape[1])
    eye = lax.broadcasted_iota(jnp.int32, shape, 0) == lax.broadcasted_iota(jnp.int32, shape, 1)
    return jnp.sum(jnp.where(eye, row, 0.0), axis=1, keepdims=True)


def flatten(column, width):
    shape = (column.shape[0], width)
    eye = lax.broadcasted_iota(jnp.int32, shape, 0) == lax.broadcasted_iota(jnp.int32, shape, 1)
    return jnp.sum(jnp.where(eye, column, 0.0), axis=0, keepdims=True)


def attend_back_kernel(
    grad_att_ref, qkv_ref, out_ref, lse_ref, nall_ref, result_ref, residual_ref, gate_ref,
    cols_ref, gain_ref, wqkv_ref, tok_ref, grad_residual_ref, grad_proj_ref, small_ref,
    buf_ref, cots_ref, gates_ref, first_ref, second_ref,
    block_out_ref, grad_tokens_ref, shared_ref, small_out_ref, grad_first_ref, grad_second_ref,
    do_t, dq_s, dqkv_s, home_s, q_s, k_s, v_s, do_s, back_s, wt_s, proj_in, part_s, sum_s,
    core_out, core_in, line_out, line_in, small_a, small_in, small_b, row_out, row_in,
    first_s, second_s, slot_s, rows_s, shared_s,
    att_sems, back_sems, home_sems, proj_sems, core_sems, line_sems, join_sems, small_sems,
    row_sems, ring_sems, pair_sems, load_sems,
):
    blk, expert, bx, by, bd = places()
    tok = grad_att_ref.shape[1]
    width = grad_att_ref.shape[0]
    heads = HEADS // 4
    group = heads * HEAD_DIM
    here = rows_at(blk, tok)
    length = qkv_ref.shape[1]
    core = lax.rem(expert, 2)
    line = expert // 2
    lines = 4
    half = width // 2
    other = (blk, expert + 1 - 2 * core)
    mine_lanes = pl.ds(pl.multiple_of(core * half, 128), half)
    other_lanes = pl.ds(pl.multiple_of((1 - core) * half, 128), half)
    line_peers = [(blk, lax.rem(line + shift, lines) * 2 + core) for shift in range(1, lines)]
    gain = gain_ref[...].reshape(1, width)
    arrived = greet(blk_peers() + expert_peers())
    odd = lax.rem(blk, 2)
    quarter = first_s.shape[1]

    def load(src, dst, index):
        copy = pltpu.make_async_copy(src, dst, load_sems.at[index])
        copy.start()
        return copy

    weights = [
        load(first_ref.at[:, rows_at(blk, quarter)], first_s, 0),
        load(second_ref.at[rows_at(blk, quarter)], second_s, 1),
    ]
    slot_loads = []

    def load_slots(t):
        cut = slice(t * tok, (t + 1) * tok)
        slot_loads.append((
            load(buf_ref.at[cut], slot_s.at[t % 2, 0], 2 + t % 2),
            load(cots_ref.at[cut], slot_s.at[t % 2, 1], 4 + t % 2),
        ))

    load_slots(0)
    rows_load = [load(residual_ref, rows_s, 6)]
    mine = rows_at(blk, group)
    mine_load = load(grad_att_ref.at[mine], do_t.at[:, here], 7)
    own_slots = rows_at(expert, tok // 8)
    result_load = load(result_ref.at[own_slots], back_s.at[own_slots], 8)
    arrived()
    att_copies = [
        push(grad_att_ref.at[rows_at(peer[0], group)], do_t.at[:, here], att_sems, n, peer)
        for n, peer in enumerate(blk_peers())
    ]
    back = ExpertExchange(result_ref, back_s, back_sems, tok // 8)
    small_core = push(small_ref.at[:, other_lanes], small_in.at[0], small_sems, 0, other)
    for part in range(3):
        first = pl.multiple_of(part * width + blk * group - odd * 64, 128)
        wide = wqkv_ref[:, pl.ds(first, 256)]
        narrow = jnp.where(odd == 1, wide[:, 64:256], wide[:, 0:192]).T
        for head in range(heads):
            place = head * 192 + part * 64
            wt_s[place : place + 64, :] = narrow[head * 64 : (head + 1) * 64]

    def expert_weights(t):
        if t == 0:
            for copy in weights:
                copy.wait()
        if t < 3:
            load_slots(t + 1)
        for copy in slot_loads[t]:
            copy.wait()
        x = slot_s[t % 2, 0]
        rates = [spread(gates_ref[t * 64 + n * 8 : t * 64 + n * 8 + 1, :], 64) for n in range(8)]
        rate = jnp.concatenate(rates, axis=0)
        grad_in = (slot_s[t % 2, 1].astype(F32) * rate).astype(BF16)
        act, slope = gelu_pair(dot(x, first_s[...]))
        grad_hidden = (dot_nt(grad_in, second_s[...]) * slope).astype(BF16)
        grad_second = dot_tn(act.astype(BF16), grad_in)
        grad_first = dot_tn(x, grad_hidden)
        if t == 0:
            grad_second_ref[...] = grad_second
            grad_first_ref[...] = grad_first
        else:
            grad_second_ref[...] += grad_second
            grad_first_ref[...] += grad_first

    expert_weights(0)
    small_core.wait()
    small_a[...] = small_ref[:, mine_lanes] + small_in[0]
    small_in[1 + line] = small_a[...]
    small_line = [
        push(small_a, small_in.at[1 + line], small_sems, 1 + n, peer)
        for n, peer in enumerate(line_peers)
    ]
    back.start_all(False)
    expert_weights(1)
    mine_load.wait()
    for copy in att_copies:
        copy.wait_recv()
    proj_copies = [
        push(grad_proj_ref.at[rows_at(peer[0], group)], proj_in.at[n], proj_sems, n, peer)
        for n, peer in enumerate(blk_peers())
    ]

    chunk_rows = group
    piece = chunk_rows // lines
    core_copies, line_copies, joins, gathers, pairs = {}, {}, {}, {}, []
    small_blk = []

    def chunk_at(c):
        return slice(c * chunk_rows, (c + 1) * chunk_rows)

    def shared_at(block, c, first, size):
        row = pl.multiple_of(block * width + c * chunk_rows + first, 16)
        return shared_ref.at[pl.ds(row, size), mine_lanes]

    def send_core(c):
        core_out[chunk_at(c), :] = part_s[chunk_at(c), other_lanes].astype(BF16)
        core_copies[c] = push(
            core_out.at[chunk_at(c)], core_in.at[chunk_at(c)], core_sems, c, other)

    def send_line(c):
        core_copies[c].wait()
        summed = part_s[chunk_at(c), mine_lanes] + core_in[chunk_at(c), :].astype(F32)
        sum_s[chunk_at(c), :] = summed
        line_out[chunk_at(c), :] = summed.astype(BF16)
        line_copies[c] = [
            push(
                line_out.at[pl.ds(
                    pl.multiple_of(c * chunk_rows + (peer[1] // 2) * piece, piece), piece)],
                line_in.at[c * 3 + n], line_sems, c * 3 + n, peer)
            for n, peer in enumerate(line_peers)
        ]

    def send_join(c):
        for copy in line_copies[c]:
            copy.wait()
        first = pl.multiple_of(c * chunk_rows + line * piece, piece)
        total = sum_s[pl.ds(first, piece), :]
        for n in range(3):
            total = total + line_in[c * 3 + n].astype(F32)
        shared_s[c] = total.astype(BF16)
        ref = shared_at(blk, c, line * piece, piece)
        joins[c] = [
            push(shared_s.at[c], ref, join_sems, c * 3 + n, peer)
            for n, peer in enumerate(line_peers)]
        joins[c].append(load(shared_s.at[c], ref, 9 + c))

    def pair(block, c):
        ref = shared_at(block, c, 0, chunk_rows)
        pairs.append(push(ref, ref, pair_sems, len(pairs), other))

    def send_ring(c):
        for copy in joins[c]:
            copy.wait()
        size = chunk_rows // 2
        gathers[c] = BlockGather(
            lambda block, part: shared_at(block, c, part * size, size), ring_sems, c * 6)
        gathers[c].start()
        pair(blk, c)

    def forward(c):
        gathers[c].forward()

    def pair_neighbours(c):
        gathers[c].wait_neighbours()
        pair(bx, c)
        pair(by, c)

    def pair_diagonal(c):
        gathers[c].wait_diagonal()
        pair(bd, c)

    def sum_proj():
        for copy in proj_copies:
            copy.wait()
        part_s[chunk_at(3), :] = (
            (grad_proj_ref[mine, :].astype(F32) + proj_in[0].astype(F32))
            + (proj_in[1].astype(F32) + proj_in[2].astype(F32))
        )
        send_core(3)

    def sum_small():
        for copy in small_line:
            copy.wait()
        small_b[...] = (small_in[1] + small_in[2]) + (small_in[3] + small_in[4])
        small_in[5 + blk] = small_b[...]
        small_blk.extend(
            push(small_b, small_in.at[5 + blk], small_sems, 4 + n, peer)
            for n, peer in enumerate(blk_peers())
        )

    sent = []

    def send_home(head, part, block):
        src = slice(head * 192 + part * 64, head * 192 + (part + 1) * 64)
        there = pl.ds(pl.multiple_of(part * width + blk * group + head * 64, 64), 64)

        def copy():
            return pltpu.make_async_remote_copy(
                src_ref=dqkv_s.at[src, block * tok : (block + 1) * tok],
                dst_ref=home_s.at[there],
                send_sem=home_sems.at[0, (block * heads + head) * 3 + part],
                recv_sem=home_sems.at[1, (blk * heads + head) * 3 + part],
                device_id=(block, expert),
                device_id_type=MESH,
            )

        @pl.when(blk != block)
        def _():
            copy().start()

        @pl.when(blk == block)
        def _():
            home_s[there, :] = dqkv_s[src, block * tok : (block + 1) * tok]

        sent.append((block, copy))

    after = {
        (0, 3): [sum_small],
        (1, 1): [lambda: send_line(0)],
        (1, 2): [sum_proj],
        (1, 3): [lambda: send_join(0)],
        (2, 0): [lambda: send_line(3)],
        (2, 1): [lambda: send_ring(0), lambda: send_line(1)],
        (2, 2): [lambda: send_join(3)],
        (2, 3): [lambda: send_join(1)],
    }
    gain_total = None
    for head in range(heads):
        cut = slice(head * 64, (head + 1) * 64)
        kt_cut = slice(group + head * 64, group + (head + 1) * 64)
        vt_cut = slice(2 * group + head * 64, 2 * group + (head + 1) * 64)
        q_s[...] = qkv_ref[cut, :].T
        k_s[...] = qkv_ref[kt_cut, :].T
        v_s[...] = qkv_ref[vt_cut, :].T
        do_s[...] = do_t[cut, :].T
        delta = jnp.sum(out_ref[cut, :] * do_t[cut, :].astype(F32), axis=0, keepdims=True)
        base = head * 192
        for j in range(4):
            keys = slice(j * tok, (j + 1) * tok)
            queries = slice(j * tok, length)
            s = dot(k_s[keys, :], qkv_ref[cut, queries])
            p = jnp.exp(s - lse_ref[head : head + 1, queries])
            allowed = lower_triangle(tok, length - j * tok)
            p = jnp.where(allowed, p, 0.0)
            dp = dot(v_s[keys, :], do_t[cut, queries])
            ds = (p * (dp - delta[:, queries])).astype(BF16)
            dv = dot(p.astype(BF16), do_s[queries, :])
            dk = dot(ds, q_s[queries, :])
            dqkv_s[base + 64 : base + 128, keys] = dk.T.astype(BF16)
            dqkv_s[base + 128 : base + 192, keys] = dv.T.astype(BF16)
            send_home(head, 1, j)
            send_home(head, 2, j)
            dq = dot(qkv_ref[kt_cut, keys], ds)
            if j == 0:
                dq_s[...] = dq
            else:
                dq_s[:, queries] += dq
            for action in after.get((head, j), ()):
                action()
        dqkv_s[base : base + 64, :] = (dq_s[...] * HEAD_DIM**-0.5).astype(BF16)
        for block in range(4):
            send_home(head, 0, block)
        grad_group = dot(dqkv_s[base : base + 192, :], nall_ref[...])
        part_s[chunk_at(head), :] = grad_group
        send_core(head)
        share = jnp.sum(
            grad_group * wt_s[base : base + 192, :].astype(F32), axis=0, keepdims=True)
        gain_total = share if gain_total is None else gain_total + share

    attn_gain = gain_total / gain
    row_out[0] = jnp.concatenate(
        [attn_gain[:, n * 128 : (n + 1) * 128] for n in range(width // 128)]
        + [jnp.zeros((8 - width // 128, 128), F32)], axis=0)
    row_core = push(row_out.at[0], row_in.at[0], row_sems, 0, other)
    send_ring(3)
    for copy in small_blk:
        copy.wait()
    small_out_ref[:, mine_lanes] = (small_in[5] + small_in[6]) + (small_in[7] + small_in[8])
    small_pair = push(
        small_out_ref.at[:, mine_lanes], small_out_ref.at[:, mine_lanes], small_sems, 7, other)
    back.wait_all()
    result_load.wait()
    lanes = lax.broadcasted_iota(jnp.int32, (tok, tok), 1).astype(F32)
    chosen = jnp.where(lanes == cols_ref[:, 0:1], 1.0, 0.0).astype(BF16)
    fetched = dot(chosen, back_s[...])
    rows_load[0].wait()
    block_out_ref[...] = (rows_s[...] + gate_ref[:, 0:1] * fetched).astype(BF16)
    block_out_ref.flush()
    send_line(2)
    row_core.wait()
    row_out[1] = row_out[0] + row_in[0]
    row_in[1 + line] = row_out[1]
    row_line = [
        push(row_out.at[1], row_in.at[1 + line], row_sems, 1 + n, peer)
        for n, peer in enumerate(line_peers)
    ]
    forward(0)
    send_ring(1)
    expert_weights(2)
    rows_load.append(load(grad_residual_ref, rows_s, 6))
    send_join(2)
    forward(3)
    pair_neighbours(0)
    for copy in row_line:
        copy.wait()
    row_out[2] = (row_in[1] + row_in[2]) + (row_in[3] + row_in[4])
    row_in[5 + blk] = row_out[2]
    row_blk = [
        push(row_out.at[2], row_in.at[5 + blk], row_sems, 4 + n, peer)
        for n, peer in enumerate(blk_peers())
    ]
    forward(1)
    expert_weights(3)
    grad_first_ref.flush()
    grad_second_ref.flush()
    send_ring(2)
    pair_diagonal(0)
    pair_neighbours(3)

    for source in range(4):
        @pl.when(blk != source)
        def _():
            for item in range(9):
                index = source * 9 + item
                pltpu.make_async_remote_copy(
                    src_ref=dqkv_s.at[0:64, 0:tok],
                    dst_ref=home_s.at[0:64],
                    send_sem=home_sems.at[0, index],
                    recv_sem=home_sems.at[1, index],
                    device_id=(source, expert),
                    device_id_type=MESH,
                ).wait_recv()
    rows_load[1].wait()
    xhat, scale = standardise(tok_ref[...].astype(F32))

    def tokens_part(n):
        cut = slice(n * 256, (n + 1) * 256)
        grad_normed = dot(wqkv_ref[...], home_s[:, cut]).T
        grad_xhat = grad_normed * gain
        x = xhat[cut]
        grad_tokens_ref[cut, :] = rows_s[cut, :] + scale[cut] * (
            grad_xhat
            - jnp.mean(grad_xhat, axis=1, keepdims=True)
            - x * jnp.mean(grad_xhat * x, axis=1, keepdims=True)
        )

    tokens_part(0)
    pair_diagonal(3)
    pair_neighbours(1)
    forward(2)
    tokens_part(1)
    grad_tokens_ref.flush()
    pair_diagonal(1)
    pair_neighbours(2)
    pair_diagonal(2)
    for copy in row_blk:
        copy.wait()
    small_pair.wait()
    total = (row_in[5] + row_in[6]) + (row_in[7] + row_in[8])
    small_out_ref[25:26, :] = jnp.concatenate(
        [total[n : n + 1, :] for n in range(width // 128)], axis=1)
    for copy in pairs:
        copy.wait_recv()
    for copy in pairs:
        copy.wait_send()
    for gather in gathers.values():
        gather.wait_sends()
    for copy in att_copies:
        copy.wait_send()
    for block, copy in sent:
        @pl.when(blk != block)
        def _():
            copy().wait_send()


def unfold_kernel(
    shared_ref, small_ref, histogram_ref, block_out_ref, tokens_ref, first_ref, second_ref,
    grad_qkv_ref, grad_proj_ref, attn_gain_ref, moe_gain_ref, route_ref, anchor_ref, counts_ref,
    block_out_out, tokens_out, first_out, second_out,
    in_s, qkv_s, proj_s, block_out_s, tokens_s, first_s, second_s,
    in_sems, qkv_sems, proj_sem, move_sems,
):
    blocks = in_s.shape[0]
    width = in_s.shape[2]
    group = width // blocks
    rdim, experts = route_ref.shape[0], anchor_ref.shape[0]
    loads = []
    for block in range(blocks):
        loads.append(pltpu.make_async_copy(
            shared_ref.at[block * width : (block + 1) * width], in_s.at[block], in_sems.at[block]))
        loads[-1].start()
    moves = [
        (pltpu.make_async_copy(src, held, move_sems.at[0, n]),
         pltpu.make_async_copy(held, dst, move_sems.at[1, n]))
        for n, (src, held, dst) in enumerate((
            (first_ref, first_s, first_out), (second_ref, second_s, second_out),
            (tokens_ref, tokens_s, tokens_out), (block_out_ref, block_out_s, block_out_out)))
    ]
    for load, _ in moves:
        load.start()
    route_ref[...] = small_ref[0:rdim, :]
    anchor_ref[...] = small_ref[rdim : rdim + experts, 0:rdim]
    moe_gain_ref[...] = small_ref[rdim + experts : rdim + experts + 1, :].reshape(width)
    attn_gain_ref[...] = small_ref[rdim + experts + 1 : rdim + experts + 2, :].reshape(width)
    counts = small_ref[rdim + experts + 2 : rdim + experts + 3, 0:experts].astype(jnp.int32)
    counts_ref[...] = histogram_ref[...] + counts.reshape(experts)
    stores = []
    for load, store in moves:
        load.wait()
        store.start()
    for first in range(0, blocks, 2):
        for block in range(first, first + 2):
            loads[block].wait()
            proj_s[block * group : (block + 1) * group, :] = (
                in_s[block, 3 * group :, :].astype(F32))
        for part in range(3):
            cut = slice(part * width + first * group, part * width + (first + 2) * group)
            qkv_s[:, cut] = jnp.concatenate(
                [
                    in_s[block, head * 192 + part * 64 : head * 192 + part * 64 + 64, :]
                    for block in range(first, first + 2)
                    for head in range(group // HEAD_DIM)
                ],
                axis=0,
            ).T.astype(F32)
            stores.append(pltpu.make_async_copy(
                qkv_s.at[:, cut], grad_qkv_ref.at[:, cut], qkv_sems.at[len(stores)]))
            stores[-1].start()
    stores.append(pltpu.make_async_copy(proj_s, grad_proj_ref, proj_sem.at[0]))
    stores[-1].start()
    for copy in stores + [store for _, store in moves]:
        copy.wait()


def unfold(shared, small, histogram, moved, rdim, experts):
    width = shared.shape[1]
    blocks = shared.shape[0] // width
    whole, outside = pl.BlockSpec(memory_space=pltpu.VMEM), pl.BlockSpec(memory_space=pl.ANY)
    shapes = [
        ((width, 3 * width), F32), ((width, width), F32), ((width,), F32), ((width,), F32),
        ((rdim, width), F32), ((experts, rdim), F32), ((experts,), jnp.int32),
    ]
    dma = pltpu.SemaphoreType.DMA
    return pl.pallas_call(
        unfold_kernel,
        out_shape=tuple(jax.ShapeDtypeStruct(*shape) for shape in shapes)
        + tuple(jax.ShapeDtypeStruct(array.shape, array.dtype) for array in moved),
        in_specs=[outside, whole, whole] + [outside] * len(moved),
        out_specs=tuple([outside] * 2 + [whole] * 5 + [outside] * len(moved)),
        scratch_shapes=[
            pltpu.VMEM((blocks, width, width), BF16), pltpu.VMEM((width, 3 * width), F32),
            pltpu.VMEM((width, width), F32),
        ]
        + [pltpu.VMEM(array.shape, array.dtype) for array in moved]
        + [dma((blocks,)), dma((3 * blocks // 2,)), dma((1,)), dma((2, len(moved)))],
        name="unfold",
        compiler_params=pltpu.CompilerParams(vmem_limit_bytes=VMEM_BYTES),
    )(shared, small, histogram, *moved)


def call(kernel, name, args, outs, scratch, lazy=(), lazy_out=(), in_any=(), out_any=(),
         collective=None):
    n_in, n_out = len(args), len(outs)
    shapes = tuple(jax.ShapeDtypeStruct(shape, dtype) for shape, dtype in outs)
    staged = [pltpu.VMEM(args[n].shape, args[n].dtype) for n in lazy]
    staged += [pltpu.VMEM(shapes[n].shape, shapes[n].dtype) for n in lazy_out]
    sems = [pltpu.SemaphoreType.DMA((len(staged),))] if staged else []

    def wrapped(*refs):
        ins, results = list(refs[:n_in]), list(refs[n_in : n_in + n_out])
        rest = refs[n_in + n_out : n_in + n_out + len(scratch)]
        extra = refs[n_in + n_out + len(scratch) :]
        for k, n in enumerate(lazy):
            ins[n] = Lazy(ins[n], extra[k], extra[-1].at[k])
        for k, n in enumerate(lazy_out):
            k += len(lazy)
            results[n] = LazyOut(extra[k], results[n], extra[-1].at[k])
        kernel(*ins, *results, *rest)
        for n in lazy_out:
            results[n].flush()
        for n in lazy:
            ins[n].ref()
        for n in lazy_out:
            results[n].copy.wait()

    def spec(n, outside):
        return pl.BlockSpec(memory_space=pl.ANY if n in outside else pltpu.VMEM)

    return pl.pallas_call(
        wrapped,
        out_shape=shapes,
        in_specs=[spec(n, tuple(lazy) + tuple(in_any)) for n in range(n_in)],
        out_specs=tuple(spec(n, tuple(lazy_out) + tuple(out_any)) for n in range(n_out)),
        scratch_shapes=list(scratch) + staged + sems,
        name=name,
        compiler_params=pltpu.CompilerParams(
            vmem_limit_bytes=VMEM_BYTES,
            collective_id=collective,
            has_side_effects=collective is not None,
        ),
    )(*args)


def fast_body(
    tokens, cotangent, loss_mask, routes, priority, histogram, qkv_weight, proj_weight, attn_gain,
    moe_gain, route_weight, anchor_table, first_weight, second_weight,
):
    tok, width = tokens.shape[1:]
    blocks, experts = lax.axis_size("blk"), lax.axis_size("expert")
    length = tok * blocks
    heads = HEADS // blocks
    group = heads * HEAD_DIM
    hidden = first_weight.shape[2]
    x, cot = tokens[0], cotangent[0]
    gains = [attn_gain, moe_gain]
    rows = [routes.reshape(1, tok), priority.reshape(1, tok), loss_mask.reshape(1, tok)]
    dma = pltpu.SemaphoreType.DMA
    (nall, qkv, out, lse, cols, result, residual, gate, grad_residual, grad_att, grad_proj, small,
     buf, cots, gates) = call(
        forward_kernel, "forward",
        (x, *gains, *rows, qkv_weight, cot, proj_weight, route_weight.T, anchor_table, first_weight[0],
         second_weight[0]),
        [((length, width), BF16), ((3 * group, length), BF16), ((group, length), F32),
         ((8, length), F32), ((tok, 128), F32),
         ((tok, width), BF16), ((tok, width), F32), ((tok, 128), F32), ((tok, width), F32),
         ((width, tok), BF16), ((width, width), BF16), ((32, width), F32),
         ((length, width), BF16), ((length, width), BF16), ((blocks * 64, 128), F32)],
        [pltpu.VMEM((3, width, 256), BF16), pltpu.VMEM((3 * group, width), BF16),
         pltpu.VMEM((heads, length, HEAD_DIM), BF16), pltpu.VMEM((group, length), BF16),
         pltpu.VMEM((tok, width), BF16), pltpu.VMEM((width, tok), BF16),
         pltpu.VMEM((tok, width), BF16),
         pltpu.VMEM((width, hidden), BF16), pltpu.VMEM((hidden, width), BF16),
         pltpu.VMEM((tok // 2, hidden), F32),
         pltpu.VMEM((tok, width), BF16), pltpu.VMEM((64, 128), F32),
         pltpu.VMEM((tok, width), BF16), pltpu.VMEM((64, 128), F32), pltpu.VMEM((tok, width), BF16),
         pltpu.VMEM((tok, width), BF16), pltpu.VMEM((64, 128), F32), pltpu.VMEM((64, 128), F32),
         pltpu.VMEM((tok // 2, width), F32), pltpu.VMEM((tok // 2, width), F32),
         pltpu.VMEM((tok // 2, width), BF16),
         dma((9,)), dma((2, 6)), dma((2, experts)), dma((2, blocks * heads)), dma((2, experts)),
         dma((2, experts)), dma((2, experts)), dma((2, experts)), dma((2, 12)), dma((2, 18)),
         dma((2, 3))],
        lazy=(7, 8), lazy_out=(0, 1, 2, 4, 5, 6, 7, 8, 9, 10), in_any=(6, 11, 12), out_any=(12, 13),
        collective=1,
    )
    half, piece, quarter = width // 2, group // 4, hidden // blocks
    block_out, grad_tokens, shared, small, grad_first, grad_second = call(
        attend_back_kernel, "attend_back",
        (grad_att, qkv, out, lse, nall, result, residual, gate, cols, attn_gain, qkv_weight, x,
         grad_residual, grad_proj, small, buf, cots, gates, first_weight[0], second_weight[0]),
        [((tok, width), BF16), ((tok, width), F32), ((blocks * width, width), BF16),
         ((32, width), F32), ((width, quarter), F32), ((quarter, width), F32)],
        [pltpu.VMEM((group, length), BF16), pltpu.VMEM((HEAD_DIM, length), F32),
         pltpu.VMEM((3 * group, length), BF16), pltpu.VMEM((3 * width, tok), BF16)]
        + [pltpu.VMEM((length, HEAD_DIM), BF16)] * 4
        + [pltpu.VMEM((tok, width), BF16), pltpu.VMEM((3 * group, width), BF16),
           pltpu.VMEM((3, group, width), BF16),
           pltpu.VMEM((width, width), F32), pltpu.VMEM((width, half), F32),
           pltpu.VMEM((width, half), BF16), pltpu.VMEM((width, half), BF16),
           pltpu.VMEM((width, half), BF16), pltpu.VMEM((12, piece, half), BF16),
           pltpu.VMEM((32, half), F32), pltpu.VMEM((9, 32, half), F32), pltpu.VMEM((32, half), F32),
           pltpu.VMEM((3, 8, 128), F32), pltpu.VMEM((9, 8, 128), F32),
           pltpu.VMEM((width, quarter), BF16), pltpu.VMEM((quarter, width), BF16),
           pltpu.VMEM((2, 2, tok, width), BF16), pltpu.VMEM((tok, width), F32),
           pltpu.VMEM((4, piece, half), BF16),
           dma((2, 3)), dma((2, experts)), dma((2, 36)), dma((2, 3)), dma((2, 4)), dma((2, 12)),
           dma((2, 12)), dma((2, 8)), dma((2, 7)), dma((2, 24)), dma((2, 16)), dma((13,))],
        lazy=(1, 2, 4, 7, 8, 10, 11, 13), lazy_out=(0, 1, 4, 5),
        in_any=(0, 5, 6, 12, 15, 16, 18, 19), out_any=(2,), collective=3,
    )
    (grad_qkv, grad_proj, grad_attn_gain, grad_moe_gain, grad_route, grad_anchor, counts,
     block_out, grad_tokens, grad_first, grad_second) = unfold(
        shared, small, histogram, (block_out, grad_tokens, grad_first, grad_second),
        route_weight.shape[1], experts)
    return (
        block_out[None],
        grad_tokens[None],
        grad_qkv,
        grad_proj,
        grad_attn_gain,
        grad_moe_gain,
        grad_route.T,
        grad_anchor,
        grad_first[None],
        grad_second[None],
        counts,
    )


def solution(mesh):
    in_specs = (
        P("expert", "blk", None),
        P("expert", "blk", None),
        P("expert", "blk"),
        P("expert", "blk", None),
        P("expert", "blk", None),
        P(),
        P(),
        P(),
        P(),
        P(),
        P(),
        P(),
        P("expert", None, None),
        P("expert", None, None),
    )
    out_specs = (
        P("expert", "blk", None),
        P("expert", "blk", None),
        P(),
        P(),
        P(),
        P(),
        P(),
        P(),
        P("expert", None, "blk"),
        P("expert", "blk", None),
        P(),
    )
    blocks, experts = mesh.shape["blk"], mesh.shape["expert"]
    body = fast_body if (blocks, experts) == (4, 8) else general_body
    return jax.shard_map(body, mesh=mesh, in_specs=in_specs, out_specs=out_specs, check_vma=False)
```

```python
import functools

import jax
import jax.numpy as jnp
from jax import lax
from jax.experimental import pallas as pl
from jax.experimental.pallas import tpu as pltpu
from jax.sharding import PartitionSpec as P

HEADS = 12
HEAD_DIM = 64


TOP_PRECISION = lax.Precision.HIGHEST
EPSILON = 1e-05
ROUTER_SOFTNESS = 0.4
MASKED = -1e30


def layer_norm(values, norm_gain):
    average = jnp.mean(values, axis=-1, keepdims=True)
    centered = values - average
    variance = jnp.mean(centered * centered, axis=-1, keepdims=True)
    return centered * lax.rsqrt(variance + EPSILON) * norm_gain


def unit_rows(matrix):
    return matrix * lax.rsqrt(1.0 + jnp.sum(matrix * matrix, axis=-1, keepdims=True))


def router_gate(normalized_rows, route_matrix, anchors, route_onehot):
    projection_output = unit_rows(jnp.dot(normalized_rows, route_matrix, precision=TOP_PRECISION))
    expert_anchor_rows = unit_rows(anchors)
    route_logit_scores = (
        jnp.dot(projection_output, expert_anchor_rows.T, precision=TOP_PRECISION) / ROUTER_SOFTNESS
    )
    return jnp.sum(jax.nn.softmax(route_logit_scores, axis=-1) * route_onehot, axis=-1)


def masked_scores(queries, key_rows, query_first, key_first, score_scale):
    scores = (
        jnp.einsum("qhd,khd->hqk", queries, key_rows, preferred_element_type=jnp.float32)
        * score_scale
    )
    grid_shape = (queries.shape[0], key_rows.shape[0])
    query_place = query_first + lax.broadcasted_iota(jnp.int32, grid_shape, 0)
    key_place = key_first + lax.broadcasted_iota(jnp.int32, grid_shape, 1)
    return (scores, (key_place <= query_place)[None])


def over_blocks(step_fn, carried, arrays, block_rows):
    row_total = arrays[0].shape[0]
    block_count = row_total // block_rows
    stacked = tuple(
        (member.reshape((block_count, block_rows) + member.shape[1:]) for member in arrays)
    )

    def scan_step(running, packed):
        position, blocks = packed
        return (step_fn(running, blocks, position * block_rows), None)

    result, unused = lax.scan(
        scan_step, carried, (jnp.arange(block_count, dtype=jnp.int32), stacked)
    )
    return result


def general_body(
    tokens,
    cotangent,
    loss_mask,
    routes,
    priority,
    histogram,
    qkv_weight,
    proj_weight,
    attn_gain,
    moe_gain,
    route_weight,
    anchor_table,
    first_weight,
    second_weight,
):
    tok_rows = tokens.shape[1]
    model_width = tokens.shape[2]
    score_scale = HEAD_DIM ** (-0.5)
    query_first = lax.axis_index("blk") * tok_rows
    local_experts = first_weight.shape[0]
    experts_all = local_experts * lax.axis_size("expert")
    capacity = tok_rows // experts_all
    head_shape = (tok_rows, HEADS, HEAD_DIM)
    seq_rows = tok_rows * lax.axis_size("blk")
    route_ids = routes[0, :, 0]
    route_onehot = (
        route_ids[:, None] == lax.broadcasted_iota(jnp.int32, (tok_rows, experts_all), 1)
    ).astype(jnp.float32)
    count_rows = jnp.sum(route_onehot, axis=0)
    total_counts = lax.psum(count_rows.astype(jnp.int32), ("blk", "expert"))
    block_input = tokens[0].astype(jnp.float32)
    normed_attn, attn_norm_back = jax.vjp(layer_norm, block_input, attn_gain)
    normed_low = normed_attn.astype(jnp.bfloat16)
    query_key_value_mix = jnp.dot(
        normed_low, qkv_weight, preferred_element_type=jnp.float32
    ).astype(jnp.bfloat16)
    query_flat = query_key_value_mix[:, :model_width]
    queries = query_flat.reshape(head_shape)
    key_local = query_key_value_mix[:, model_width : 2 * model_width]
    value_local = query_key_value_mix[:, 2 * model_width :]

    def forward_step(carried, blocks, key_first):
        running_top, running_sum, running_out = carried
        key_rows = blocks[0].reshape(blocks[0].shape[0], HEADS, HEAD_DIM)
        value_rows = blocks[1].reshape(blocks[1].shape[0], HEADS, HEAD_DIM)
        scores, allowed = masked_scores(queries, key_rows, query_first, key_first, score_scale)
        top_new = jnp.maximum(running_top, jnp.max(jnp.where(allowed, scores, MASKED), axis=2))
        weights = jnp.where(allowed, jnp.exp(scores - top_new[:, :, None]), 0.0)
        factor = jnp.exp(running_top - top_new)
        running_sum = running_sum * factor + jnp.sum(weights, axis=2)
        running_out = running_out * factor.T[:, :, None] + jnp.einsum(
            "hqk,khd->qhd",
            weights.astype(jnp.bfloat16),
            value_rows,
            preferred_element_type=jnp.float32,
        )
        return (top_new, running_sum, running_out)

    initial = (
        jnp.full((HEADS, tok_rows), MASKED, jnp.float32),
        jnp.zeros((HEADS, tok_rows), jnp.float32),
        jnp.zeros(head_shape, jnp.float32),
    )
    running_top, running_sum, running_out = over_blocks(
        forward_step,
        initial,
        (
            lax.all_gather(key_local, "blk", axis=0, tiled=True),
            lax.all_gather(value_local, "blk", axis=0, tiled=True),
        ),
        tok_rows,
    )
    attention_result = running_out / running_sum.T[:, :, None]
    log_total = running_top + jnp.log(running_sum)
    attended_low = attention_result.reshape(tok_rows, model_width).astype(jnp.bfloat16)
    residual_stream = block_input + jnp.dot(
        attended_low, proj_weight, preferred_element_type=jnp.float32
    )
    normed_moe, moe_norm_back = jax.vjp(layer_norm, residual_stream, moe_gain)

    def gate_of(normalized_rows, route_matrix, anchors):
        return router_gate(normalized_rows, route_matrix, anchors, route_onehot)

    gate_value, gate_back = jax.vjp(gate_of, normed_moe, route_weight, anchor_table)
    order_rows = priority[0, 0]
    same_route = route_ids[:, None] == route_ids[None, :]
    earlier = order_rows[None, :] < order_rows[:, None]
    slot_ids = jnp.sum((same_route & earlier).astype(jnp.int32), axis=1)
    target = jnp.where(slot_ids < capacity, route_ids * capacity + slot_ids, -1)
    selector = lax.broadcasted_iota(jnp.int32, (tok_rows, tok_rows), 0) == target[None, :]
    selector_low = selector.astype(jnp.bfloat16)
    outgoing = jnp.dot(
        selector_low, normed_moe.astype(jnp.bfloat16), preferred_element_type=jnp.float32
    )
    outgoing = outgoing.astype(jnp.bfloat16).reshape(experts_all, capacity, model_width)
    arrived = lax.all_to_all(outgoing, "expert", split_axis=0, concat_axis=0, tiled=True)
    sources = arrived.shape[0] // local_experts
    grouped = arrived.reshape(sources, local_experts, arrived.shape[1], arrived.shape[2])
    hidden = jnp.einsum("secd,edf->secf", grouped, first_weight, preferred_element_type=jnp.float32)
    act_low = jax.nn.gelu(hidden).astype(jnp.bfloat16)
    result = jnp.einsum(
        "secf,efd->secd", act_low, second_weight, preferred_element_type=jnp.float32
    )
    result = result.astype(jnp.bfloat16).reshape(arrived.shape)
    returned = lax.all_to_all(result, "expert", split_axis=0, concat_axis=0, tiled=True)
    returned, arrived = (returned, arrived)
    fetched = jnp.einsum(
        "st,sd->td",
        selector_low,
        returned.reshape(tok_rows, model_width),
        preferred_element_type=jnp.float32,
    )
    block_out = (residual_stream + gate_value[:, None] * fetched).astype(jnp.bfloat16)[None]
    grad_out = cotangent[0].astype(jnp.float32) * loss_mask[0].astype(jnp.float32)[:, None]
    grad_fetched = grad_out * gate_value[:, None]
    grad_gate = jnp.sum(grad_out * fetched, axis=1)
    grad_slots = jnp.dot(selector.astype(jnp.float32), grad_fetched, precision=TOP_PRECISION)
    grad_slots = grad_slots.astype(jnp.bfloat16).reshape(experts_all, capacity, model_width)
    grad_arrived = lax.all_to_all(grad_slots, "expert", split_axis=0, concat_axis=0, tiled=True)
    sources = grad_arrived.shape[0] // local_experts
    slot_shape = (sources, local_experts, capacity, model_width)
    grouped_in = arrived.reshape(slot_shape)
    grouped_grad = grad_arrived.reshape(slot_shape)
    hidden = jnp.einsum(
        "secd,edf->secf", grouped_in, first_weight, preferred_element_type=jnp.float32
    )
    act_low = jax.nn.gelu(hidden).astype(jnp.bfloat16)
    grad_second = jnp.einsum(
        "secf,secd->efd", act_low, grouped_grad, preferred_element_type=jnp.float32
    )
    grad_act = jnp.einsum(
        "secd,efd->secf", grouped_grad, second_weight, preferred_element_type=jnp.float32
    )
    unused, gelu_back = jax.vjp(jax.nn.gelu, hidden)
    grad_hidden = gelu_back(grad_act)[0].astype(jnp.bfloat16)
    grad_first = jnp.einsum(
        "secd,secf->edf", grouped_in, grad_hidden, preferred_element_type=jnp.float32
    )
    grad_sent = jnp.einsum(
        "secf,edf->secd", grad_hidden, first_weight, preferred_element_type=jnp.float32
    )
    grad_sent = grad_sent.astype(jnp.bfloat16).reshape(grad_arrived.shape)
    grad_returned = lax.all_to_all(grad_sent, "expert", split_axis=0, concat_axis=0, tiled=True)
    grad_first, grad_second = (
        lax.psum_scatter(
            grad_first.astype(jnp.bfloat16), "blk", scatter_dimension=2, tiled=True
        ).astype(jnp.float32),
        lax.psum_scatter(
            grad_second.astype(jnp.bfloat16), "blk", scatter_dimension=1, tiled=True
        ).astype(jnp.float32),
    )
    grad_moe_rows = jnp.einsum(
        "st,sd->td",
        selector_low,
        grad_returned.reshape(tok_rows, model_width),
        preferred_element_type=jnp.float32,
    )
    grad_router_rows, grad_route, grad_anchor = gate_back(grad_gate)
    grad_residual_norm, grad_moe_gain = moe_norm_back(grad_moe_rows + grad_router_rows)
    grad_residual = grad_out + grad_residual_norm
    grad_attn_low = grad_residual.astype(jnp.bfloat16)
    grad_proj = jnp.dot(attended_low.T, grad_attn_low, preferred_element_type=jnp.float32)
    grad_attended_flat = jnp.dot(
        grad_attn_low, proj_weight.T, preferred_element_type=jnp.float32
    ).astype(jnp.bfloat16)
    grad_attended = grad_attended_flat.reshape(head_shape)
    delta_rows = jnp.sum(grad_attended.astype(jnp.float32) * attention_result, axis=2).T
    key_all, value_all = (
        lax.all_gather(key_local, "blk", axis=0, tiled=True),
        lax.all_gather(value_local, "blk", axis=0, tiled=True),
    )
    block_count = seq_rows // tok_rows
    key_blocks = key_all.reshape(block_count, tok_rows, model_width)
    value_blocks = value_all.reshape(block_count, tok_rows, model_width)

    def key_block_step(running_grad, packed):
        position, key_block, value_block = packed
        key_rows = key_block.reshape(head_shape)
        value_rows = value_block.reshape(head_shape)
        scores, allowed = masked_scores(
            queries, key_rows, query_first, position * tok_rows, score_scale
        )
        soft_rows = jnp.where(allowed, jnp.exp(scores - log_total[:, :, None]), 0.0)
        grad_values = jnp.einsum(
            "hqk,qhd->khd",
            soft_rows.astype(jnp.bfloat16),
            grad_attended,
            preferred_element_type=jnp.float32,
        )
        grad_soft = jnp.einsum(
            "qhd,khd->hqk", grad_attended, value_rows, preferred_element_type=jnp.float32
        )
        grad_scores = (soft_rows * (grad_soft - delta_rows[:, :, None])).astype(jnp.bfloat16)
        grad_keys = score_scale * jnp.einsum(
            "hqk,qhd->khd", grad_scores, queries, preferred_element_type=jnp.float32
        )
        running_grad = running_grad + score_scale * jnp.einsum(
            "hqk,khd->qhd", grad_scores, key_rows, preferred_element_type=jnp.float32
        )
        term = jnp.concatenate(
            [grad_keys.reshape(tok_rows, model_width), grad_values.reshape(tok_rows, model_width)],
            axis=1,
        )
        return (running_grad, term)

    grad_queries, stacked_terms = lax.scan(
        key_block_step,
        jnp.zeros(head_shape, jnp.float32),
        (jnp.arange(block_count, dtype=jnp.int32), key_blocks, value_blocks),
    )
    all_terms = stacked_terms.reshape(seq_rows, 2 * model_width)
    key_value_grads = lax.psum_scatter(
        all_terms.astype(jnp.bfloat16), "blk", scatter_dimension=0, tiled=True
    ).astype(jnp.float32)
    grad_query_rows = grad_queries.reshape(tok_rows, model_width)
    grad_qkv_rows = jnp.concatenate([grad_query_rows, key_value_grads], axis=1).astype(jnp.bfloat16)
    grad_qkv = jnp.dot(normed_low.T, grad_qkv_rows, preferred_element_type=jnp.float32)
    grad_normed = jnp.dot(grad_qkv_rows, qkv_weight.T, preferred_element_type=jnp.float32)
    grad_source_norm, grad_attn_gain = attn_norm_back(grad_normed)
    grad_tokens = (grad_residual + grad_source_norm)[None]
    grad_qkv, grad_proj, grad_attn_gain, grad_moe_gain, grad_route, grad_anchor = lax.psum(
        (grad_qkv, grad_proj, grad_attn_gain, grad_moe_gain, grad_route, grad_anchor),
        ("blk", "expert"),
    )
    histogram_out = histogram + total_counts
    return (
        block_out,
        grad_tokens,
        grad_qkv,
        grad_proj,
        grad_attn_gain,
        grad_moe_gain,
        grad_route,
        grad_anchor,
        grad_first,
        grad_second,
        histogram_out,
    )


MESH = pl.DeviceIdType.MESH
F32 = jnp.float32
BF16 = jnp.bfloat16
VMEM_BYTES = 58 * 1024 * 1024


def dot(left, right, precision=None):
    return lax.dot_general(
        left, right, (((1,), (0,)), ((), ())), precision=precision, preferred_element_type=F32
    )


def dot_nt(left, right, precision=None):
    return lax.dot_general(
        left, right, (((1,), (1,)), ((), ())), precision=precision, preferred_element_type=F32
    )


def dot_tn(left, right, precision=None):
    return lax.dot_general(
        left, right, (((0,), (0,)), ((), ())), precision=precision, preferred_element_type=F32
    )


def split(values):
    high = values.astype(BF16)
    return high, (values - high.astype(F32)).astype(BF16)


def fine(product, left, right):
    left_high, left_low = split(left)
    right_high, right_low = split(right)
    return product(left_high, right_high) + (
        product(left_high, right_low) + product(left_low, right_high)
    )


def rows_at(index, size):
    return pl.ds(pl.multiple_of(index * size, size), size)


def places():
    blk = lax.axis_index("blk")
    expert = lax.axis_index("expert")
    return blk, expert, blk + 1 - 2 * lax.rem(blk, 2), lax.rem(blk + 2, 4), 3 - blk


def greet(peers):
    barrier = pltpu.get_barrier_semaphore()
    for peer in peers:
        pl.semaphore_signal(barrier, inc=1, device_id=peer, device_id_type=MESH)
    return lambda: pl.semaphore_wait(barrier, len(peers))


def push(src, dst, sems, index, peer):
    copy = pltpu.make_async_remote_copy(
        src_ref=src,
        dst_ref=dst,
        send_sem=sems.at[0, index],
        recv_sem=sems.at[1, index],
        device_id=peer,
        device_id_type=MESH,
    )
    copy.start()
    return copy


def standardise(values):
    average = jnp.mean(values, axis=-1, keepdims=True)
    centered = values - average
    scale = lax.rsqrt(jnp.mean(centered * centered, axis=-1, keepdims=True) + EPSILON)
    return centered * scale, scale


def lower_triangle(keys, queries):
    return lax.broadcasted_iota(jnp.int32, (keys, queries), 0) <= lax.broadcasted_iota(
        jnp.int32, (keys, queries), 1
    )


class BlockGather:
    def __init__(self, part, sems, base, own=None):
        self.part, self.sems, self.base, self.own = part, sems, base, own

    def send(self, blk, half, index, peer):
        ref = self.part(blk, half)
        src = ref if self.own is None or index > 3 else self.own(half)
        return push(src, ref, self.sems, self.base + index, peer)

    def start(self):
        self.start_first()
        self.start_second()

    def start_first(self):
        blk, expert, bx, by, bd = places()
        self.copies = [self.send(blk, 0, 0, (bx, expert)), self.send(blk, 1, 1, (by, expert))]

    def start_second(self):
        blk, expert, bx, by, bd = places()
        self.copies += [self.send(blk, 1, 2, (bx, expert)), self.send(blk, 0, 3, (by, expert))]

    def forward(self):
        blk, expert, bx, by, bd = places()
        self.copies[0].wait_recv()
        self.copies.append(self.send(bx, 0, 4, (by, expert)))
        self.copies[1].wait_recv()
        self.copies.append(self.send(by, 1, 5, (bx, expert)))

    def wait_neighbours(self):
        self.copies[2].wait_recv()
        self.copies[3].wait_recv()

    def wait_diagonal(self):
        self.copies[4].wait_recv()
        self.copies[5].wait_recv()

    def wait_sends(self):
        for copy in self.copies:
            copy.wait_send()


def row_halves(buf, rows):
    size = rows // 2
    return lambda blk, half: buf.at[pl.ds(pl.multiple_of(blk * rows + half * size, size), size)]


def expert_groups():
    expert = lax.axis_index("expert")
    line, core = expert // 2, lax.rem(expert, 2)
    side, place = line // 2, lax.rem(line, 2)
    beside = (side * 2 + 1 - place) * 2
    first = ((1 - side) * 2 + place) * 2
    second = ((1 - side) * 2 + 1 - place) * 2
    return [
        (side * 4, 4, [expert + 1 - 2 * core, beside + core, beside + 1 - core]),
        (first, 2, [first + core, first + 1 - core]),
        (second, 2, [second + core, second + 1 - core]),
    ]


class ExpertExchange:
    def __init__(self, src, dst, sems, rows):
        self.src, self.dst, self.sems, self.rows = src, dst, sems, rows
        self.groups = expert_groups()
        self.copies = [[], [], []]

    def start(self, group, keep=True):
        blk, expert = lax.axis_index("blk"), lax.axis_index("expert")
        place = rows_at(expert, self.rows)
        base = (0, 3, 5)[group]
        for n, peer in enumerate(self.groups[group][2]):
            self.copies[group].append(
                push(self.src.at[rows_at(peer, self.rows)], self.dst.at[place], self.sems,
                     base + n, (blk, peer))
            )
        if group == 0 and keep:
            self.dst[place] = self.src[place]

    def wait_recv(self, group):
        for copy in self.copies[group]:
            copy.wait_recv()

    def wait_sends(self):
        for copy in sum(self.copies, []):
            copy.wait_send()

    def start_all(self, keep=True):
        self.start(1)
        self.start(2)
        self.start(0, keep)

    def wait_all(self):
        for group in range(3):
            self.wait_recv(group)
        self.wait_sends()


class Lazy:
    def __init__(self, src, dst, sem):
        self.dst, self.shape, self.fresh = dst, dst.shape, True
        self.copy = pltpu.make_async_copy(src, dst, sem)
        self.copy.start()

    def ref(self):
        if self.fresh:
            self.copy.wait()
            self.fresh = False
        return self.dst

    def __getitem__(self, where):
        return self.ref()[where]

    @property
    def at(self):
        return self.ref().at


class LazyOut:
    def __init__(self, src, dst, sem):
        self.src, self.dst, self.sem, self.shape, self.copy = src, dst, sem, src.shape, None

    def flush(self):
        if self.copy is None:
            self.copy = pltpu.make_async_copy(self.src, self.dst, self.sem)
            self.copy.start()

    def __getitem__(self, where):
        return self.src[where]

    def __setitem__(self, where, value):
        self.src[where] = value

    @property
    def at(self):
        return self.src.at


def blk_peers():
    blk, expert, bx, by, bd = places()
    return [(bx, expert), (by, expert), (bd, expert)]


def expert_peers():
    blk, expert = lax.axis_index("blk"), lax.axis_index("expert")
    n = lax.axis_size("expert")
    return [(blk, lax.rem(expert + shift, n)) for shift in range(1, n)]


def forward_kernel(
    tok_ref, attn_gain_ref, moe_gain_ref, routes_ref, priority_ref, mask_ref, wqkv_ref, cot_ref, proj_ref, route_ref, anchor_ref, first_ref, second_ref,
    nall_ref, qkv_ref, out_ref, lse_ref, cols_ref, result_ref, residual_ref, gate_ref,
    grad_residual_ref, grad_att_ref, grad_proj_ref, small_ref, buf_ref, cots_ref, gates_ref,
    w_s, wt_s, k_s, att_s, cot_s, att_ref, cot_in_ref,
    first_s, second_s, slope_s, buf_s, gates_s, go_s, gate_s, grad_s, back_s, score_s, score_in_s,
    res_acc, sent_acc, grad_in_s,
    w_sem, gather_sems, cot_sems, att_sems, go_sems, gate_sems, back_sems, score_sems, cots_sems,
    buf_sems, gates_sems,
):
    blk, expert, bx, by, bd = places()
    tok = tok_ref.shape[0]
    width = tok_ref.shape[1]
    heads = HEADS // 4
    group = heads * HEAD_DIM
    arrived = greet(blk_peers() + expert_peers())
    odd = lax.rem(blk, 2)
    loads = []
    for part in range(3):
        first = pl.multiple_of(part * width + blk * group - odd * 64, 128)
        loads.append(
            pltpu.make_async_copy(wqkv_ref.at[:, pl.ds(first, 256)], w_s.at[part], w_sem.at[part])
        )
        loads[-1].start()
    weights = [
        pltpu.make_async_copy(first_ref, first_s, w_sem.at[3]),
        pltpu.make_async_copy(second_ref, second_s, w_sem.at[4]),
    ]
    for load in weights:
        load.start()
    xhat, _ = standardise(tok_ref[...].astype(F32))
    nall_ref[rows_at(blk, tok), :] = (xhat * attn_gain_ref[...].reshape(1, width)).astype(BF16)
    arrived()
    gather = BlockGather(row_halves(nall_ref, tok), gather_sems, 0)
    gather.start()

    capacity = tok // 8
    route_row, prio_row, mask_row = (
        ref[...].astype(F32) for ref in (routes_ref, priority_ref, mask_ref))
    cols = jnp.concatenate(
        [jnp.zeros((1, tok), F32), route_row, prio_row, mask_row, jnp.zeros((124, tok), F32)],
        axis=0).T
    route_col, prio_col = cols[:, 1:2], cols[:, 2:3]
    same = route_col == route_row
    slot_row = jnp.sum(jnp.where(same & (prio_col < prio_row), 1.0, 0.0), axis=0, keepdims=True)
    slot_col = jnp.sum(jnp.where(same & (prio_row < prio_col), 1.0, 0.0), axis=1, keepdims=True)
    target_row = jnp.where(slot_row < capacity, route_row * capacity + slot_row, -1.0)
    target_col = jnp.where(slot_col < capacity, route_col * capacity + slot_col, -1.0)
    lane = lax.broadcasted_iota(jnp.int32, cols.shape, 1)
    cols_ref[...] = jnp.where(lane == 0, target_col, cols)
    cols_ref.flush()
    slots = lax.broadcasted_iota(jnp.int32, (tok, tok), 0).astype(F32)
    chosen = jnp.where((slots == target_row) & (mask_row > 0.0), 1.0, 0.0).astype(BF16)
    cot_s[...] = dot(chosen, cot_ref[...]).astype(BF16)
    cot_move = ExpertExchange(cot_s, cot_in_ref, cot_sems, capacity)
    cot_move.start_all()

    for part in range(3):
        loads[part].wait()
        wide = w_s[part]
        narrow = jnp.where(odd == 1, wide[:, 64:256], wide[:, 0:192])
        wt_s[part * group : (part + 1) * group, :] = narrow.T

    def project(where):
        cols = rows_at(where, tok)
        mixed = dot_nt(wt_s[...], nall_ref[cols, :]).astype(BF16)
        qkv_ref[0:group, cols] = mixed[0:group] * BF16(HEAD_DIM**-0.5)
        qkv_ref[group:, cols] = mixed[group:]
        for head in range(heads):
            k_s[head, cols, :] = mixed[group + head * 64 : group + (head + 1) * 64].T

    project(blk)
    gather.forward()
    gather.wait_neighbours()
    project(bx)
    project(by)
    gather.wait_diagonal()
    nall_ref.flush()
    cot_move.wait_all()
    here = rows_at(blk, tok)
    cots_own = pltpu.make_async_copy(cot_in_ref, cots_ref.at[here], w_sem.at[5])
    cots_own.start()
    quarter = tok // 4
    cots = []
    for part in range(2):

        def own(half, part=part):
            return cot_in_ref.at[pl.ds((2 * part + half) * quarter, quarter)]

        def halves(block, half, part=part):
            row = pl.multiple_of(block * tok + (2 * part + half) * quarter, quarter)
            return cots_ref.at[pl.ds(row, quarter)]

        cots.append(BlockGather(halves, cots_sems, 6 * part, own))
    cots[0].start_first()
    project(bd)
    qkv_ref.flush()

    half = tok // 2

    def scores(i, head):
        q = qkv_ref[head * 64 : (head + 1) * 64, i * tok : (i + 1) * tok]
        upper = dot(k_s[head, i * tok : i * tok + half, :], q)
        upper = jnp.where(lower_triangle(half, tok), upper, MASKED)
        lower = dot(k_s[head, i * tok + half : (i + 1) * tok, :], q[:, half:])
        lower = jnp.where(lower_triangle(half, half), lower, MASKED)
        top = jnp.max(upper, axis=0, keepdims=True)
        low_top = jnp.max(lower, axis=0, keepdims=True)
        top = jnp.concatenate([top[:, :half], jnp.maximum(top[:, half:], low_top)], axis=1)
        if i == 0:
            return top, upper, lower, None
        past = dot(k_s[head, 0 : i * tok, :], q)
        return jnp.maximum(top, jnp.max(past, axis=0, keepdims=True)), upper, lower, past

    sends = []

    def finish(i, head, found):
        top, upper, lower, past = found
        v = qkv_ref[2 * group + head * 64 : 2 * group + (head + 1) * 64, :]
        upper = jnp.exp(upper - top)
        lower = jnp.exp(lower - top[:, half:])
        total = jnp.sum(upper, axis=0, keepdims=True)
        low_total = jnp.sum(lower, axis=0, keepdims=True)
        total = jnp.concatenate([total[:, :half], total[:, half:] + low_total], axis=1)
        result = dot(v[:, i * tok : i * tok + half], upper.astype(BF16))
        low_result = dot(v[:, i * tok + half : (i + 1) * tok], lower.astype(BF16))
        result = jnp.concatenate([result[:, :half], result[:, half:] + low_result], axis=1)
        if i:
            past = jnp.exp(past - top)
            total = total + jnp.sum(past, axis=0, keepdims=True)
            result = result + dot(v[:, 0 : i * tok], past.astype(BF16))
        result = result / total
        place = slice(head * 64, (head + 1) * 64)
        out_ref[place, i * tok : (i + 1) * tok] = result
        lse_ref[head : head + 1, i * tok : (i + 1) * tok] = top + jnp.log(total)
        att_s[place, i * tok : (i + 1) * tok] = result.astype(BF16)
        there = pl.ds(pl.multiple_of(blk * group + head * 64, 64), 64)

        def copy():
            return pltpu.make_async_remote_copy(
                src_ref=att_s.at[place, i * tok : (i + 1) * tok],
                dst_ref=att_ref.at[there],
                send_sem=att_sems.at[0, i * heads + head],
                recv_sem=att_sems.at[1, blk * heads + head],
                device_id=(i, expert),
                device_id_type=MESH,
            )

        @pl.when(blk != i)
        def _():
            copy().start()

        @pl.when(blk == i)
        def _():
            att_ref[there, :] = result.astype(BF16)

        sends.append((i, copy))

    before = None
    for i in range(4):
        for head in range(heads):
            found = scores(i, head)
            if before is not None:
                finish(*before)
            before = (i, head, found)
    finish(*before)

    for i, copy in sends:
        @pl.when(blk != i)
        def _():
            copy().wait_send()

    for source in range(4):
        @pl.when(blk != source)
        def _():
            for head in range(heads):
                there = pl.ds(source * group + head * 64, 64)
                pltpu.make_async_remote_copy(
                    src_ref=att_s.at[0:64, 0:tok],
                    dst_ref=att_ref.at[there],
                    send_sem=att_sems.at[0, source * heads + head],
                    recv_sem=att_sems.at[1, source * heads + head],
                    device_id=(source, expert),
                    device_id_type=MESH,
                ).wait_recv()

    cots[0].forward()
    cots[0].start_second()
    cots[1].start()
    out_ref.flush()
    gather.wait_sends()

    gain = moe_gain_ref[...].reshape(1, width)
    experts = 8
    residual = tok_ref[...].astype(F32) + dot_tn(att_ref[...], proj_ref[...])
    residual_ref[...] = residual
    residual_ref.flush()
    xhat, scale = standardise(residual)
    normed = xhat * gain
    normed_low = normed.astype(BF16)
    go_s[...] = dot(jnp.where(slots == target_row, 1.0, 0.0).astype(BF16), normed_low).astype(BF16)
    go = ExpertExchange(go_s, buf_s, go_sems, capacity)
    go.start(0)
    go.start(1)

    projected = fine(dot_nt, normed, route_ref[...])
    unit_scale = lax.rsqrt(1.0 + jnp.sum(projected * projected, axis=1, keepdims=True))
    unit = projected * unit_scale
    anchor = anchor_ref[...]
    anchor_scale = lax.rsqrt(1.0 + jnp.sum(anchor * anchor, axis=1, keepdims=True))
    anchor_unit = anchor * anchor_scale
    logits = fine(dot_nt, unit, anchor_unit) / ROUTER_SOFTNESS
    soft = jnp.exp(logits - jnp.max(logits, axis=1, keepdims=True))
    soft = soft / jnp.sum(soft, axis=1, keepdims=True)
    onehot = jnp.where(
        lax.broadcasted_iota(jnp.int32, (tok, experts), 1).astype(F32) == route_col, 1.0, 0.0
    )
    gate = jnp.sum(soft * onehot, axis=1, keepdims=True)
    gate_ref[...] = jnp.broadcast_to(gate, gate_ref.shape)
    gate_ref.flush()
    lane = lax.broadcasted_iota(jnp.int32, (tok, 128), 1).astype(F32)
    lane = jnp.where(lane < capacity, lane, 1e6)
    for peer in range(experts):
        row = jnp.sum(
            jnp.where(target_col == peer * capacity + lane, gate, 0.0), axis=0, keepdims=True
        )
        gate_s[peer * 8 : (peer + 1) * 8, :] = jnp.broadcast_to(row, (8, 128))
    gates = ExpertExchange(gate_s, gates_s, gate_sems, 8)
    for group in range(3):
        gates.start(group)

    back = ExpertExchange(grad_s, back_s, back_sems, capacity)
    scores = ExpertExchange(score_s, score_in_s, score_sems, 8)
    tile = 768
    tiles = first_s.shape[1] // tile
    bufs, kept = [], []
    for group, (first_source, sources, _) in enumerate(go.groups):
        count = sources * capacity
        rows = pl.ds(pl.multiple_of(first_source * capacity, count), count)
        go.wait_recv(group)
        if group == 0:
            go.start(2)

        def halves(block, half, first=first_source * capacity, size=count // 2):
            return buf_ref.at[pl.ds(pl.multiple_of(block * tok + first + half * size, size), size)]

        def own(half, first=first_source * capacity, size=count // 2):
            return buf_s.at[pl.ds(pl.multiple_of(first + half * size, size), size)]

        bufs.append(BlockGather(halves, buf_sems, 6 * group, own))
        bufs[group].start()
        there = pl.ds(pl.multiple_of(blk * tok + first_source * capacity, count), count)
        kept.append(pltpu.make_async_copy(buf_s.at[rows], buf_ref.at[there], w_sem.at[6 + group]))
        kept[group].start()
        if group == 0:
            for load in weights:
                load.wait()
        x = buf_s[rows, :]
        for t in range(tiles):
            cut = slice(t * tile, (t + 1) * tile)
            act, slope = gelu_pair(dot(x, first_s[:, cut]))
            slope_s[0:count, cut] = slope
            part = dot(act.astype(BF16), second_s[cut, :])
            if t == 0:
                res_acc[0:count, :] = part
            else:
                res_acc[0:count, :] += part
        result = res_acc[0:count, :].astype(BF16)
        score = jnp.sum(
            result.astype(F32) * cot_in_ref[rows, :].astype(F32), axis=1, keepdims=True)
        for n in range(sources):
            row = flatten(score[n * capacity : (n + 1) * capacity], 128)
            score_s[rows_at(first_source + n, 8), :] = jnp.broadcast_to(row, (8, 128))
        scores.start(group)
        result_ref[rows, :] = result
        if group == 0:
            cots[1].forward()
        gates.wait_recv(group)
        for n in range(sources):
            row = gates_s[rows_at(first_source + n, 8), :][0:1, :]
            chunk = rows_at(first_source + n, capacity)
            grad_in_s[n * capacity : (n + 1) * capacity, :] = (
                cot_in_ref[chunk, :].astype(F32) * spread(row, capacity)
            ).astype(BF16)
        grad_in = grad_in_s[0:count, :]
        for t in range(tiles):
            cut = slice(t * tile, (t + 1) * tile)
            grad_hidden = (dot_nt(grad_in, second_s[cut, :]) * slope_s[0:count, cut]).astype(BF16)
            sent = dot_nt(grad_hidden, first_s[:, cut])
            if t == 0:
                sent_acc[0:count, :] = sent
            else:
                sent_acc[0:count, :] += sent
        grad_s[rows, :] = sent_acc[0:count, :].astype(BF16)
        back.start(group)
    bufs[0].forward()
    result_ref.flush()
    gates_ref[rows_at(blk, 64), :] = gates_s[...]
    gates_here = gates_ref.at[rows_at(blk, 64)]
    gates_out = [
        push(gates_here, gates_here, gates_sems, n, peer) for n, peer in enumerate(blk_peers())
    ]
    grad_out = cot_ref[...].astype(F32) * cols_ref[:, 3:4]

    for group in range(3):
        scores.wait_recv(group)
    grad_gate = jnp.zeros((tok, 1), F32)
    for peer in range(experts):
        row = score_in_s[peer * 8 : peer * 8 + 1, :]
        grad_gate += jnp.sum(
            jnp.where(target_col == peer * capacity + lane, row, 0.0), axis=1, keepdims=True
        )
    grad_logits = grad_gate * gate * (onehot - soft) / ROUTER_SOFTNESS
    grad_unit = fine(dot, grad_logits, anchor_unit)
    grad_projected = unit_scale * (
        grad_unit - unit * jnp.sum(unit * grad_unit, axis=1, keepdims=True)
    )
    grad_anchor_unit = fine(dot_tn, grad_logits, unit)
    grad_anchor = anchor_scale * (
        grad_anchor_unit
        - anchor_unit * jnp.sum(anchor_unit * grad_anchor_unit, axis=1, keepdims=True)
    )
    rdim = route_ref.shape[0]
    small_ref[...] = jnp.zeros_like(small_ref)
    small_ref[0:rdim, :] = fine(dot_tn, grad_projected, normed)
    small_ref[rdim : rdim + experts, 0:rdim] = grad_anchor
    counts = jnp.sum(onehot, axis=0, keepdims=True)
    small_ref[rdim + experts + 2 : rdim + experts + 3, 0:experts] = counts
    router_rows = fine(dot, grad_projected, route_ref[...])

    bufs[1].forward()
    for group in range(3):
        back.wait_recv(group)
    lanes = lax.broadcasted_iota(jnp.int32, (tok, tok), 1).astype(F32)
    moe_rows = dot(jnp.where(lanes == target_col, 1.0, 0.0).astype(BF16), back_s[...])
    grad_normed = moe_rows + router_rows
    small_ref[rdim + experts : rdim + experts + 1, :] = jnp.sum(
        grad_normed * xhat, axis=0, keepdims=True
    )
    grad_xhat = grad_normed * gain
    grad_residual = grad_out + scale * (
        grad_xhat
        - jnp.mean(grad_xhat, axis=1, keepdims=True)
        - xhat * jnp.mean(grad_xhat * xhat, axis=1, keepdims=True)
    )
    grad_residual_ref[...] = grad_residual
    grad_low = grad_residual.astype(BF16)
    grad_residual_ref.flush()
    bufs[2].forward()
    grad_att_ref[...] = dot_nt(proj_ref[...], grad_low).astype(BF16)
    grad_att_ref.flush()
    grad_proj_ref[...] = dot(att_ref[...], grad_low).astype(BF16)

    grad_proj_ref.flush()
    for copy in kept + [cots_own]:
        copy.wait()
    for gather in cots + bufs:
        gather.wait_neighbours()
        gather.wait_diagonal()
        gather.wait_sends()
    for exchange in (go, gates, back, scores):
        exchange.wait_sends()
    for copy in gates_out:
        copy.wait()


def gelu_pair(hidden):
    squared = hidden * hidden
    curve = jnp.tanh(0.7978845608028654 * hidden * (1.0 + 0.044715 * squared))
    half = 0.5 * (1.0 + curve)
    slope = half + 0.5 * hidden * (1.0 - curve * curve) * (
        0.7978845608028654 * (1.0 + 0.134145 * squared)
    )
    return hidden * half, slope


def spread(row, size):
    shape = (size, row.shape[1])
    eye = lax.broadcasted_iota(jnp.int32, shape, 0) == lax.broadcasted_iota(jnp.int32, shape, 1)
    return jnp.sum(jnp.where(eye, row, 0.0), axis=1, keepdims=True)


def flatten(column, width):
    shape = (column.shape[0], width)
    eye = lax.broadcasted_iota(jnp.int32, shape, 0) == lax.broadcasted_iota(jnp.int32, shape, 1)
    return jnp.sum(jnp.where(eye, column, 0.0), axis=0, keepdims=True)


def attend_back_kernel(
    grad_att_ref, qkv_ref, out_ref, lse_ref, nall_ref, result_ref, residual_ref, gate_ref,
    cols_ref, gain_ref, wqkv_ref, tok_ref, grad_residual_ref, grad_proj_ref, small_ref,
    buf_ref, cots_ref, gates_ref, first_ref, second_ref,
    block_out_ref, grad_tokens_ref, shared_ref, small_out_ref, grad_first_ref, grad_second_ref,
    do_t, dq_s, dqkv_s, home_s, q_s, k_s, v_s, do_s, back_s, wt_s, proj_in, part_s, sum_s,
    core_out, core_in, line_out, line_in, small_a, small_in, small_b, row_out, row_in,
    first_s, second_s, slot_s, rows_s, shared_s, first_acc, second_acc,
    att_sems, back_sems, home_sems, proj_sems, core_sems, line_sems, join_sems, small_sems,
    row_sems, ring_sems, pair_sems, load_sems,
):
    blk, expert, bx, by, bd = places()
    tok = grad_att_ref.shape[1]
    width = grad_att_ref.shape[0]
    heads = HEADS // 4
    group = heads * HEAD_DIM
    here = rows_at(blk, tok)
    length = qkv_ref.shape[1]
    core = lax.rem(expert, 2)
    line = expert // 2
    lines = 4
    half = width // 2
    other = (blk, expert + 1 - 2 * core)
    mine_lanes = pl.ds(pl.multiple_of(core * half, 128), half)
    other_lanes = pl.ds(pl.multiple_of((1 - core) * half, 128), half)
    line_peers = [(blk, lax.rem(line + shift, lines) * 2 + core) for shift in range(1, lines)]
    gain = gain_ref[...].reshape(1, width)
    arrived = greet(blk_peers() + expert_peers())
    odd = lax.rem(blk, 2)
    quarter = first_s.shape[1]

    def load(src, dst, index):
        copy = pltpu.make_async_copy(src, dst, load_sems.at[index])
        copy.start()
        return copy

    weights = [
        load(first_ref.at[:, rows_at(blk, quarter)], first_s, 0),
        load(second_ref.at[rows_at(blk, quarter)], second_s, 1),
    ]
    slot_loads = []

    def load_slots(t):
        cut = slice(t * tok, (t + 1) * tok)
        slot_loads.append((
            load(buf_ref.at[cut], slot_s.at[t % 2, 0], 2 + t % 2),
            load(cots_ref.at[cut], slot_s.at[t % 2, 1], 4 + t % 2),
        ))

    load_slots(0)
    rows_load = [load(residual_ref, rows_s, 6)]
    mine = rows_at(blk, group)
    mine_load = load(grad_att_ref.at[mine], do_t.at[:, here], 7)
    own_slots = rows_at(expert, tok // 8)
    result_load = load(result_ref.at[own_slots], back_s.at[own_slots], 8)
    arrived()
    att_copies = []

    def send_att(head):
        cut = slice(head * 64, (head + 1) * 64)
        att_copies.append([
            push(
                grad_att_ref.at[pl.ds(pl.multiple_of(peer[0] * group + head * 64, 64), 64)],
                do_t.at[cut, here], att_sems, head * 3 + n, peer)
            for n, peer in enumerate(blk_peers())
        ])

    send_att(0)
    back = ExpertExchange(result_ref, back_s, back_sems, tok // 8)
    small_core = push(small_ref.at[:, other_lanes], small_in.at[0], small_sems, 0, other)
    for part in range(3):
        first = pl.multiple_of(part * width + blk * group - odd * 64, 128)
        wide = wqkv_ref[:, pl.ds(first, 256)]
        narrow = jnp.where(odd == 1, wide[:, 64:256], wide[:, 0:192]).T
        for head in range(heads):
            place = head * 192 + part * 64
            wt_s[place : place + 64, :] = narrow[head * 64 : (head + 1) * 64]

    def expert_weights(t):
        if t == 0:
            for copy in weights:
                copy.wait()
        if t < 3:
            load_slots(t + 1)
        for copy in slot_loads[t]:
            copy.wait()
        x = slot_s[t % 2, 0]
        rates = [spread(gates_ref[t * 64 + n * 8 : t * 64 + n * 8 + 1, :], 64) for n in range(8)]
        rate = jnp.concatenate(rates, axis=0)
        grad_in = (slot_s[t % 2, 1].astype(F32) * rate).astype(BF16)
        act, slope = gelu_pair(dot(x, first_s[...]))
        grad_hidden = (dot_nt(grad_in, second_s[...]) * slope).astype(BF16)
        grad_second = dot_tn(act.astype(BF16), grad_in)
        grad_first = dot_tn(x, grad_hidden)
        if t == 0:
            second_acc[...] = grad_second
            first_acc[...] = grad_first
        elif t < 3:
            second_acc[...] += grad_second
            first_acc[...] += grad_first
        else:
            grad_second_ref[...] = (second_acc[...] + grad_second).astype(BF16)
            grad_first_ref[...] = (first_acc[...] + grad_first).astype(BF16)

    send_att(1)
    expert_weights(0)
    send_att(2)
    small_core.wait()
    small_a[...] = small_ref[:, mine_lanes] + small_in[0]
    small_in[1 + line] = small_a[...]
    small_line = [
        push(small_a, small_in.at[1 + line], small_sems, 1 + n, peer)
        for n, peer in enumerate(line_peers)
    ]
    back.start_all(False)
    mine_load.wait()
    proj_copies = [
        push(grad_proj_ref.at[rows_at(peer[0], group)], proj_in.at[n], proj_sems, n, peer)
        for n, peer in enumerate(blk_peers())
    ]

    chunk_rows = group
    piece = chunk_rows // lines
    core_copies, line_copies, joins, gathers, pairs = {}, {}, {}, {}, []
    small_blk = []

    def chunk_at(c):
        return slice(c * chunk_rows, (c + 1) * chunk_rows)

    def shared_at(block, c, first, size):
        row = pl.multiple_of(block * width + c * chunk_rows + first, 16)
        return shared_ref.at[pl.ds(row, size), mine_lanes]

    def send_core(c):
        core_out[chunk_at(c), :] = part_s[chunk_at(c), other_lanes].astype(BF16)
        core_copies[c] = push(
            core_out.at[chunk_at(c)], core_in.at[chunk_at(c)], core_sems, c, other)

    def send_line(c):
        core_copies[c].wait()
        summed = part_s[chunk_at(c), mine_lanes] + core_in[chunk_at(c), :].astype(F32)
        sum_s[chunk_at(c), :] = summed
        line_out[chunk_at(c), :] = summed.astype(BF16)
        line_copies[c] = [
            push(
                line_out.at[pl.ds(
                    pl.multiple_of(c * chunk_rows + (peer[1] // 2) * piece, piece), piece)],
                line_in.at[c * 3 + n], line_sems, c * 3 + n, peer)
            for n, peer in enumerate(line_peers)
        ]

    def send_join(c):
        for copy in line_copies[c]:
            copy.wait()
        first = pl.multiple_of(c * chunk_rows + line * piece, piece)
        total = sum_s[pl.ds(first, piece), :]
        for n in range(3):
            total = total + line_in[c * 3 + n].astype(F32)
        shared_s[c] = total.astype(BF16)
        ref = shared_at(blk, c, line * piece, piece)
        joins[c] = [
            push(shared_s.at[c], ref, join_sems, c * 3 + n, peer)
            for n, peer in enumerate(line_peers)]
        joins[c].append(load(shared_s.at[c], ref, 9 + c))

    def pair(block, c):
        ref = shared_at(block, c, 0, chunk_rows)
        pairs.append(push(ref, ref, pair_sems, len(pairs), other))

    def send_ring(c):
        for copy in joins[c]:
            copy.wait()
        size = chunk_rows // 2
        gathers[c] = BlockGather(
            lambda block, part: shared_at(block, c, part * size, size), ring_sems, c * 6)
        gathers[c].start()
        pair(blk, c)

    def forward(c):
        gathers[c].forward()

    def pair_neighbours(c):
        gathers[c].wait_neighbours()
        pair(bx, c)
        pair(by, c)

    def pair_diagonal(c):
        gathers[c].wait_diagonal()
        pair(bd, c)

    def sum_proj():
        for copy in proj_copies:
            copy.wait()
        part_s[chunk_at(3), :] = (
            (grad_proj_ref[mine, :].astype(F32) + proj_in[0].astype(F32))
            + (proj_in[1].astype(F32) + proj_in[2].astype(F32))
        )
        send_core(3)

    def sum_small():
        for copy in small_line:
            copy.wait()
        small_b[...] = (small_in[1] + small_in[2]) + (small_in[3] + small_in[4])
        small_in[5 + blk] = small_b[...]
        small_blk.extend(
            push(small_b, small_in.at[5 + blk], small_sems, 4 + n, peer)
            for n, peer in enumerate(blk_peers())
        )

    sent = []

    def send_home(head, part, block):
        src = slice(head * 192 + part * 64, head * 192 + (part + 1) * 64)
        there = pl.ds(pl.multiple_of(part * width + blk * group + head * 64, 64), 64)

        def copy():
            return pltpu.make_async_remote_copy(
                src_ref=dqkv_s.at[src, block * tok : (block + 1) * tok],
                dst_ref=home_s.at[there],
                send_sem=home_sems.at[0, (block * heads + head) * 3 + part],
                recv_sem=home_sems.at[1, (blk * heads + head) * 3 + part],
                device_id=(block, expert),
                device_id_type=MESH,
            )

        @pl.when(blk != block)
        def _():
            copy().start()

        @pl.when(blk == block)
        def _():
            home_s[there, :] = dqkv_s[src, block * tok : (block + 1) * tok]

        sent.append((block, copy))

    after = {
        (1, 1): [sum_small],
        (1, 3): [lambda: send_line(0)],
        (1, 5): [sum_proj],
        (2, 0): [lambda: send_line(3)],
        (2, 1): [lambda: send_join(0)],
        (2, 3): [lambda: send_line(1)],
        (2, 5): [lambda: send_ring(0)],
        (2, 7): [lambda: send_join(3), lambda: send_join(1)],
    }
    gain_total = None
    for head in range(heads):
        cut = slice(head * 64, (head + 1) * 64)
        kt_cut = slice(group + head * 64, group + (head + 1) * 64)
        vt_cut = slice(2 * group + head * 64, 2 * group + (head + 1) * 64)
        for copy in att_copies[head]:
            copy.wait_recv()
        q_s[...] = qkv_ref[cut, :].T
        k_s[...] = qkv_ref[kt_cut, :].T
        v_s[...] = qkv_ref[vt_cut, :].T
        do_s[...] = do_t[cut, :].T
        delta = jnp.sum(out_ref[cut, :] * do_t[cut, :].astype(F32), axis=0, keepdims=True)
        base = head * 192
        step = tok // 2
        for j in range(length // step):
            keys = slice(j * step, (j + 1) * step)
            queries = slice(j * step, length)
            s = dot(k_s[keys, :], qkv_ref[cut, queries])
            p = jnp.exp(s - lse_ref[head : head + 1, queries])
            edge = jnp.where(lower_triangle(step, step), p[:, :step], 0.0)
            p = edge if p.shape[1] == step else jnp.concatenate([edge, p[:, step:]], axis=1)
            dp = dot(v_s[keys, :], do_t[cut, queries])
            ds = (p * (dp - delta[:, queries])).astype(BF16)
            dv = dot(p.astype(BF16), do_s[queries, :])
            dk = dot(ds, q_s[queries, :])
            dqkv_s[base + 64 : base + 128, keys] = dk.T.astype(BF16)
            dqkv_s[base + 128 : base + 192, keys] = dv.T.astype(BF16)
            if j % 2:
                send_home(head, 1, j // 2)
                send_home(head, 2, j // 2)
            dq = dot(qkv_ref[kt_cut, keys], ds)
            if j == 0:
                dq_s[...] = dq
            else:
                dq_s[:, queries] += dq
            for action in after.get((head, j), ()):
                action()
        dqkv_s[base : base + 64, :] = (dq_s[...] * HEAD_DIM**-0.5).astype(BF16)
        for block in range(4):
            send_home(head, 0, block)
        grad_group = dot(dqkv_s[base : base + 192, :], nall_ref[...])
        part_s[chunk_at(head), :] = grad_group
        send_core(head)
        share = jnp.sum(
            grad_group * wt_s[base : base + 192, :].astype(F32), axis=0, keepdims=True)
        gain_total = share if gain_total is None else gain_total + share

    attn_gain = gain_total / gain
    row_out[0] = jnp.concatenate(
        [attn_gain[:, n * 128 : (n + 1) * 128] for n in range(width // 128)]
        + [jnp.zeros((8 - width // 128, 128), F32)], axis=0)
    row_core = push(row_out.at[0], row_in.at[0], row_sems, 0, other)
    send_line(2)
    send_ring(3)
    send_ring(1)
    for copy in small_blk:
        copy.wait()
    small_out_ref[:, mine_lanes] = (small_in[5] + small_in[6]) + (small_in[7] + small_in[8])
    small_pair = push(
        small_out_ref.at[:, mine_lanes], small_out_ref.at[:, mine_lanes], small_sems, 7, other)
    row_core.wait()
    row_out[1] = row_out[0] + row_in[0]
    row_in[1 + line] = row_out[1]
    row_line = [
        push(row_out.at[1], row_in.at[1 + line], row_sems, 1 + n, peer)
        for n, peer in enumerate(line_peers)
    ]
    back.wait_all()
    result_load.wait()
    lanes = lax.broadcasted_iota(jnp.int32, (tok, tok), 1).astype(F32)
    chosen = jnp.where(lanes == cols_ref[:, 0:1], 1.0, 0.0).astype(BF16)
    fetched = dot(chosen, back_s[...])
    rows_load[0].wait()
    block_out_ref[...] = (rows_s[...] + gate_ref[:, 0:1] * fetched).astype(BF16)
    block_out_ref.flush()
    rows_load.append(load(grad_residual_ref, rows_s, 6))
    expert_weights(1)
    send_join(2)
    forward(0)
    for copy in row_line:
        copy.wait()
    row_out[2] = (row_in[1] + row_in[2]) + (row_in[3] + row_in[4])
    row_in[5 + blk] = row_out[2]
    row_blk = [
        push(row_out.at[2], row_in.at[5 + blk], row_sems, 4 + n, peer)
        for n, peer in enumerate(blk_peers())
    ]
    expert_weights(2)
    send_ring(2)
    forward(3)
    expert_weights(3)
    grad_first_ref.flush()
    grad_second_ref.flush()
    forward(1)
    pair_neighbours(0)
    pair_diagonal(0)
    pair_neighbours(3)

    for source in range(4):
        @pl.when(blk != source)
        def _():
            for item in range(9):
                index = source * 9 + item
                pltpu.make_async_remote_copy(
                    src_ref=dqkv_s.at[0:64, 0:tok],
                    dst_ref=home_s.at[0:64],
                    send_sem=home_sems.at[0, index],
                    recv_sem=home_sems.at[1, index],
                    device_id=(source, expert),
                    device_id_type=MESH,
                ).wait_recv()
    rows_load[1].wait()
    xhat, scale = standardise(tok_ref[...].astype(F32))

    def tokens_part(n):
        cut = slice(n * 256, (n + 1) * 256)
        grad_normed = dot(wqkv_ref[...], home_s[:, cut]).T
        grad_xhat = grad_normed * gain
        x = xhat[cut]
        grad_tokens_ref[cut, :] = (rows_s[cut, :] + scale[cut] * (
            grad_xhat
            - jnp.mean(grad_xhat, axis=1, keepdims=True)
            - x * jnp.mean(grad_xhat * x, axis=1, keepdims=True)
        )).astype(BF16)

    forward(2)
    tokens_part(0)
    pair_diagonal(3)
    pair_neighbours(1)
    tokens_part(1)
    grad_tokens_ref.flush()
    pair_diagonal(1)
    pair_neighbours(2)
    pair_diagonal(2)
    for copy in row_blk:
        copy.wait()
    small_pair.wait()
    total = (row_in[5] + row_in[6]) + (row_in[7] + row_in[8])
    small_out_ref[25:26, :] = jnp.concatenate(
        [total[n : n + 1, :] for n in range(width // 128)], axis=1)
    for copy in pairs:
        copy.wait_recv()
    for copy in pairs:
        copy.wait_send()
    for gather in gathers.values():
        gather.wait_sends()
    for copy in sum(att_copies, []):
        copy.wait_send()
    for block, copy in sent:
        @pl.when(blk != block)
        def _():
            copy().wait_send()


def unfold_kernel(
    shared_ref, small_ref, histogram_ref, block_out_ref, tokens_ref, first_ref, second_ref,
    grad_qkv_ref, grad_proj_ref, attn_gain_ref, moe_gain_ref, route_ref, anchor_ref, counts_ref,
    block_out_out, tokens_out, first_out, second_out,
    in_s, qkv_s, proj_s, block_out_s, tokens_s, first_s, second_s, tokens_w, first_w, second_w,
    in_sems, qkv_sems, proj_sem, move_sems,
):
    blocks = in_s.shape[0]
    width = in_s.shape[2]
    group = width // blocks
    rdim, experts = route_ref.shape[0], anchor_ref.shape[0]
    loads = []
    for block in range(blocks):
        loads.append(pltpu.make_async_copy(
            shared_ref.at[block * width : (block + 1) * width], in_s.at[block], in_sems.at[block]))
        loads[-1].start()
    narrow = (first_s, second_s, tokens_s, block_out_s)
    wide = (first_w, second_w, tokens_w, block_out_s)
    sources = (first_ref, second_ref, tokens_ref, block_out_ref)
    results = (first_out, second_out, tokens_out, block_out_out)
    moves = [
        (pltpu.make_async_copy(sources[n], narrow[n], move_sems.at[0, n]),
         pltpu.make_async_copy(wide[n], results[n], move_sems.at[1, n]))
        for n in range(4)
    ]
    for load, _ in moves:
        load.start()
    route_ref[...] = small_ref[0:rdim, :]
    anchor_ref[...] = small_ref[rdim : rdim + experts, 0:rdim]
    moe_gain_ref[...] = small_ref[rdim + experts : rdim + experts + 1, :].reshape(width)
    attn_gain_ref[...] = small_ref[rdim + experts + 1 : rdim + experts + 2, :].reshape(width)
    counts = small_ref[rdim + experts + 2 : rdim + experts + 3, 0:experts].astype(jnp.int32)
    counts_ref[...] = histogram_ref[...] + counts.reshape(experts)
    stores = []
    for n, (load, store) in enumerate(moves):
        load.wait()
        if wide[n] is not narrow[n]:
            wide[n][...] = narrow[n][...].astype(F32)
        store.start()
    for first in range(0, blocks, 2):
        for block in range(first, first + 2):
            loads[block].wait()
            proj_s[block * group : (block + 1) * group, :] = (
                in_s[block, 3 * group :, :].astype(F32))
        for part in range(3):
            cut = slice(part * width + first * group, part * width + (first + 2) * group)
            qkv_s[:, cut] = jnp.concatenate(
                [
                    in_s[block, head * 192 + part * 64 : head * 192 + part * 64 + 64, :]
                    for block in range(first, first + 2)
                    for head in range(group // HEAD_DIM)
                ],
                axis=0,
            ).T.astype(F32)
            stores.append(pltpu.make_async_copy(
                qkv_s.at[:, cut], grad_qkv_ref.at[:, cut], qkv_sems.at[len(stores)]))
            stores[-1].start()
    stores.append(pltpu.make_async_copy(proj_s, grad_proj_ref, proj_sem.at[0]))
    stores[-1].start()
    for copy in stores + [store for _, store in moves]:
        copy.wait()


def unfold(shared, small, histogram, moved, rdim, experts):
    width = shared.shape[1]
    blocks = shared.shape[0] // width
    whole, outside = pl.BlockSpec(memory_space=pltpu.VMEM), pl.BlockSpec(memory_space=pl.ANY)
    shapes = [
        ((width, 3 * width), F32), ((width, width), F32), ((width,), F32), ((width,), F32),
        ((rdim, width), F32), ((experts, rdim), F32), ((experts,), jnp.int32),
    ]
    dma = pltpu.SemaphoreType.DMA
    return pl.pallas_call(
        unfold_kernel,
        out_shape=tuple(jax.ShapeDtypeStruct(*shape) for shape in shapes)
        + tuple(
            jax.ShapeDtypeStruct(array.shape, F32 if n else array.dtype)
            for n, array in enumerate(moved)),
        in_specs=[outside, whole, whole] + [outside] * len(moved),
        out_specs=tuple([outside] * 2 + [whole] * 5 + [outside] * len(moved)),
        scratch_shapes=[
            pltpu.VMEM((blocks, width, width), BF16), pltpu.VMEM((width, 3 * width), F32),
            pltpu.VMEM((width, width), F32),
        ]
        + [pltpu.VMEM(array.shape, array.dtype) for array in moved]
        + [pltpu.VMEM(array.shape, F32) for array in moved[1:]]
        + [dma((blocks,)), dma((3 * blocks // 2,)), dma((1,)), dma((2, len(moved)))],
        name="unfold",
        compiler_params=pltpu.CompilerParams(vmem_limit_bytes=VMEM_BYTES),
    )(shared, small, histogram, *moved)


def call(kernel, name, args, outs, scratch, lazy=(), lazy_out=(), in_any=(), out_any=(),
         collective=None):
    n_in, n_out = len(args), len(outs)
    shapes = tuple(jax.ShapeDtypeStruct(shape, dtype) for shape, dtype in outs)
    staged = [pltpu.VMEM(args[n].shape, args[n].dtype) for n in lazy]
    staged += [pltpu.VMEM(shapes[n].shape, shapes[n].dtype) for n in lazy_out]
    sems = [pltpu.SemaphoreType.DMA((len(staged),))] if staged else []

    def wrapped(*refs):
        ins, results = list(refs[:n_in]), list(refs[n_in : n_in + n_out])
        rest = refs[n_in + n_out : n_in + n_out + len(scratch)]
        extra = refs[n_in + n_out + len(scratch) :]
        for k, n in enumerate(lazy):
            ins[n] = Lazy(ins[n], extra[k], extra[-1].at[k])
        for k, n in enumerate(lazy_out):
            k += len(lazy)
            results[n] = LazyOut(extra[k], results[n], extra[-1].at[k])
        kernel(*ins, *results, *rest)
        for n in lazy_out:
            results[n].flush()
        for n in lazy:
            ins[n].ref()
        for n in lazy_out:
            results[n].copy.wait()

    def spec(n, outside):
        return pl.BlockSpec(memory_space=pl.ANY if n in outside else pltpu.VMEM)

    return pl.pallas_call(
        wrapped,
        out_shape=shapes,
        in_specs=[spec(n, tuple(lazy) + tuple(in_any)) for n in range(n_in)],
        out_specs=tuple(spec(n, tuple(lazy_out) + tuple(out_any)) for n in range(n_out)),
        scratch_shapes=list(scratch) + staged + sems,
        name=name,
        compiler_params=pltpu.CompilerParams(
            vmem_limit_bytes=VMEM_BYTES,
            collective_id=collective,
            has_side_effects=collective is not None,
        ),
    )(*args)


def fast_body(
    tokens, cotangent, loss_mask, routes, priority, histogram, qkv_weight, proj_weight, attn_gain,
    moe_gain, route_weight, anchor_table, first_weight, second_weight,
):
    tok, width = tokens.shape[1:]
    blocks, experts = lax.axis_size("blk"), lax.axis_size("expert")
    length = tok * blocks
    heads = HEADS // blocks
    group = heads * HEAD_DIM
    hidden = first_weight.shape[2]
    x, cot = tokens[0], cotangent[0]
    gains = [attn_gain, moe_gain]
    rows = [routes.reshape(1, tok), priority.reshape(1, tok), loss_mask.reshape(1, tok)]
    dma = pltpu.SemaphoreType.DMA
    (nall, qkv, out, lse, cols, result, residual, gate, grad_residual, grad_att, grad_proj, small,
     buf, cots, gates) = call(
        forward_kernel, "forward",
        (x, *gains, *rows, qkv_weight, cot, proj_weight, route_weight.T, anchor_table, first_weight[0],
         second_weight[0]),
        [((length, width), BF16), ((3 * group, length), BF16), ((group, length), F32),
         ((8, length), F32), ((tok, 128), F32),
         ((tok, width), BF16), ((tok, width), F32), ((tok, 128), F32), ((tok, width), F32),
         ((width, tok), BF16), ((width, width), BF16), ((32, width), F32),
         ((length, width), BF16), ((length, width), BF16), ((blocks * 64, 128), F32)],
        [pltpu.VMEM((3, width, 256), BF16), pltpu.VMEM((3 * group, width), BF16),
         pltpu.VMEM((heads, length, HEAD_DIM), BF16), pltpu.VMEM((group, length), BF16),
         pltpu.VMEM((tok, width), BF16), pltpu.VMEM((width, tok), BF16),
         pltpu.VMEM((tok, width), BF16),
         pltpu.VMEM((width, hidden), BF16), pltpu.VMEM((hidden, width), BF16),
         pltpu.VMEM((tok // 2, hidden), F32),
         pltpu.VMEM((tok, width), BF16), pltpu.VMEM((64, 128), F32),
         pltpu.VMEM((tok, width), BF16), pltpu.VMEM((64, 128), F32), pltpu.VMEM((tok, width), BF16),
         pltpu.VMEM((tok, width), BF16), pltpu.VMEM((64, 128), F32), pltpu.VMEM((64, 128), F32),
         pltpu.VMEM((tok // 2, width), F32), pltpu.VMEM((tok // 2, width), F32),
         pltpu.VMEM((tok // 2, width), BF16),
         dma((9,)), dma((2, 6)), dma((2, experts)), dma((2, blocks * heads)), dma((2, experts)),
         dma((2, experts)), dma((2, experts)), dma((2, experts)), dma((2, 12)), dma((2, 18)),
         dma((2, 3))],
        lazy=(7, 8), lazy_out=(0, 1, 2, 4, 5, 6, 7, 8, 9, 10), in_any=(6, 11, 12), out_any=(12, 13),
        collective=1,
    )
    half, piece, quarter = width // 2, group // 4, hidden // blocks
    block_out, grad_tokens, shared, small, grad_first, grad_second = call(
        attend_back_kernel, "attend_back",
        (grad_att, qkv, out, lse, nall, result, residual, gate, cols, attn_gain, qkv_weight, x,
         grad_residual, grad_proj, small, buf, cots, gates, first_weight[0], second_weight[0]),
        [((tok, width), BF16), ((tok, width), BF16), ((blocks * width, width), BF16),
         ((32, width), F32), ((width, quarter), BF16), ((quarter, width), BF16)],
        [pltpu.VMEM((group, length), BF16), pltpu.VMEM((HEAD_DIM, length), F32),
         pltpu.VMEM((3 * group, length), BF16), pltpu.VMEM((3 * width, tok), BF16)]
        + [pltpu.VMEM((length, HEAD_DIM), BF16)] * 4
        + [pltpu.VMEM((tok, width), BF16), pltpu.VMEM((3 * group, width), BF16),
           pltpu.VMEM((3, group, width), BF16),
           pltpu.VMEM((width, width), F32), pltpu.VMEM((width, half), F32),
           pltpu.VMEM((width, half), BF16), pltpu.VMEM((width, half), BF16),
           pltpu.VMEM((width, half), BF16), pltpu.VMEM((12, piece, half), BF16),
           pltpu.VMEM((32, half), F32), pltpu.VMEM((9, 32, half), F32), pltpu.VMEM((32, half), F32),
           pltpu.VMEM((3, 8, 128), F32), pltpu.VMEM((9, 8, 128), F32),
           pltpu.VMEM((width, quarter), BF16), pltpu.VMEM((quarter, width), BF16),
           pltpu.VMEM((2, 2, tok, width), BF16), pltpu.VMEM((tok, width), F32),
           pltpu.VMEM((4, piece, half), BF16), pltpu.VMEM((width, quarter), F32),
           pltpu.VMEM((quarter, width), F32),
           dma((2, 9)), dma((2, experts)), dma((2, 36)), dma((2, 3)), dma((2, 4)), dma((2, 12)),
           dma((2, 12)), dma((2, 8)), dma((2, 7)), dma((2, 24)), dma((2, 16)), dma((13,))],
        lazy=(1, 2, 4, 7, 8, 10, 11, 13), lazy_out=(0, 1, 4, 5),
        in_any=(0, 5, 6, 12, 15, 16, 18, 19), out_any=(2,), collective=3,
    )
    (grad_qkv, grad_proj, grad_attn_gain, grad_moe_gain, grad_route, grad_anchor, counts,
     block_out, grad_tokens, grad_first, grad_second) = unfold(
        shared, small, histogram, (block_out, grad_tokens, grad_first, grad_second),
        route_weight.shape[1], experts)
    return (
        block_out[None],
        grad_tokens[None],
        grad_qkv,
        grad_proj,
        grad_attn_gain,
        grad_moe_gain,
        grad_route.T,
        grad_anchor,
        grad_first[None],
        grad_second[None],
        counts,
    )


def solution(mesh):
    in_specs = (
        P("expert", "blk", None),
        P("expert", "blk", None),
        P("expert", "blk"),
        P("expert", "blk", None),
        P("expert", "blk", None),
        P(),
        P(),
        P(),
        P(),
        P(),
        P(),
        P(),
        P("expert", None, None),
        P("expert", None, None),
    )
    out_specs = (
        P("expert", "blk", None),
        P("expert", "blk", None),
        P(),
        P(),
        P(),
        P(),
        P(),
        P(),
        P("expert", None, "blk"),
        P("expert", "blk", None),
        P(),
    )
    blocks, experts = mesh.shape["blk"], mesh.shape["expert"]
    body = fast_body if (blocks, experts) == (4, 8) else general_body
    return jax.shard_map(body, mesh=mesh, in_specs=in_specs, out_specs=out_specs, check_vma=False)
```

```python
import functools

import jax
import jax.numpy as jnp
from jax import lax
from jax.experimental import pallas as pl
from jax.experimental.pallas import tpu as pltpu
from jax.sharding import PartitionSpec as P

HEADS = 12
HEAD_DIM = 64


TOP_PRECISION = lax.Precision.HIGHEST
EPSILON = 1e-05
ROUTER_SOFTNESS = 0.4
MASKED = -1e30


def layer_norm(values, norm_gain):
    average = jnp.mean(values, axis=-1, keepdims=True)
    centered = values - average
    variance = jnp.mean(centered * centered, axis=-1, keepdims=True)
    return centered * lax.rsqrt(variance + EPSILON) * norm_gain


def unit_rows(matrix):
    return matrix * lax.rsqrt(1.0 + jnp.sum(matrix * matrix, axis=-1, keepdims=True))


def router_gate(normalized_rows, route_matrix, anchors, route_onehot):
    projection_output = unit_rows(jnp.dot(normalized_rows, route_matrix, precision=TOP_PRECISION))
    expert_anchor_rows = unit_rows(anchors)
    route_logit_scores = (
        jnp.dot(projection_output, expert_anchor_rows.T, precision=TOP_PRECISION) / ROUTER_SOFTNESS
    )
    return jnp.sum(jax.nn.softmax(route_logit_scores, axis=-1) * route_onehot, axis=-1)


def masked_scores(queries, key_rows, query_first, key_first, score_scale):
    scores = (
        jnp.einsum("qhd,khd->hqk", queries, key_rows, preferred_element_type=jnp.float32)
        * score_scale
    )
    grid_shape = (queries.shape[0], key_rows.shape[0])
    query_place = query_first + lax.broadcasted_iota(jnp.int32, grid_shape, 0)
    key_place = key_first + lax.broadcasted_iota(jnp.int32, grid_shape, 1)
    return (scores, (key_place <= query_place)[None])


def over_blocks(step_fn, carried, arrays, block_rows):
    row_total = arrays[0].shape[0]
    block_count = row_total // block_rows
    stacked = tuple(
        (member.reshape((block_count, block_rows) + member.shape[1:]) for member in arrays)
    )

    def scan_step(running, packed):
        position, blocks = packed
        return (step_fn(running, blocks, position * block_rows), None)

    result, unused = lax.scan(
        scan_step, carried, (jnp.arange(block_count, dtype=jnp.int32), stacked)
    )
    return result


def general_body(
    tokens,
    cotangent,
    loss_mask,
    routes,
    priority,
    histogram,
    qkv_weight,
    proj_weight,
    attn_gain,
    moe_gain,
    route_weight,
    anchor_table,
    first_weight,
    second_weight,
):
    tok_rows = tokens.shape[1]
    model_width = tokens.shape[2]
    score_scale = HEAD_DIM ** (-0.5)
    query_first = lax.axis_index("blk") * tok_rows
    local_experts = first_weight.shape[0]
    experts_all = local_experts * lax.axis_size("expert")
    capacity = tok_rows // experts_all
    head_shape = (tok_rows, HEADS, HEAD_DIM)
    seq_rows = tok_rows * lax.axis_size("blk")
    route_ids = routes[0, :, 0]
    route_onehot = (
        route_ids[:, None] == lax.broadcasted_iota(jnp.int32, (tok_rows, experts_all), 1)
    ).astype(jnp.float32)
    count_rows = jnp.sum(route_onehot, axis=0)
    total_counts = lax.psum(count_rows.astype(jnp.int32), ("blk", "expert"))
    block_input = tokens[0].astype(jnp.float32)
    normed_attn, attn_norm_back = jax.vjp(layer_norm, block_input, attn_gain)
    normed_low = normed_attn.astype(jnp.bfloat16)
    query_key_value_mix = jnp.dot(
        normed_low, qkv_weight, preferred_element_type=jnp.float32
    ).astype(jnp.bfloat16)
    query_flat = query_key_value_mix[:, :model_width]
    queries = query_flat.reshape(head_shape)
    key_local = query_key_value_mix[:, model_width : 2 * model_width]
    value_local = query_key_value_mix[:, 2 * model_width :]

    def forward_step(carried, blocks, key_first):
        running_top, running_sum, running_out = carried
        key_rows = blocks[0].reshape(blocks[0].shape[0], HEADS, HEAD_DIM)
        value_rows = blocks[1].reshape(blocks[1].shape[0], HEADS, HEAD_DIM)
        scores, allowed = masked_scores(queries, key_rows, query_first, key_first, score_scale)
        top_new = jnp.maximum(running_top, jnp.max(jnp.where(allowed, scores, MASKED), axis=2))
        weights = jnp.where(allowed, jnp.exp(scores - top_new[:, :, None]), 0.0)
        factor = jnp.exp(running_top - top_new)
        running_sum = running_sum * factor + jnp.sum(weights, axis=2)
        running_out = running_out * factor.T[:, :, None] + jnp.einsum(
            "hqk,khd->qhd",
            weights.astype(jnp.bfloat16),
            value_rows,
            preferred_element_type=jnp.float32,
        )
        return (top_new, running_sum, running_out)

    initial = (
        jnp.full((HEADS, tok_rows), MASKED, jnp.float32),
        jnp.zeros((HEADS, tok_rows), jnp.float32),
        jnp.zeros(head_shape, jnp.float32),
    )
    running_top, running_sum, running_out = over_blocks(
        forward_step,
        initial,
        (
            lax.all_gather(key_local, "blk", axis=0, tiled=True),
            lax.all_gather(value_local, "blk", axis=0, tiled=True),
        ),
        tok_rows,
    )
    attention_result = running_out / running_sum.T[:, :, None]
    log_total = running_top + jnp.log(running_sum)
    attended_low = attention_result.reshape(tok_rows, model_width).astype(jnp.bfloat16)
    residual_stream = block_input + jnp.dot(
        attended_low, proj_weight, preferred_element_type=jnp.float32
    )
    normed_moe, moe_norm_back = jax.vjp(layer_norm, residual_stream, moe_gain)

    def gate_of(normalized_rows, route_matrix, anchors):
        return router_gate(normalized_rows, route_matrix, anchors, route_onehot)

    gate_value, gate_back = jax.vjp(gate_of, normed_moe, route_weight, anchor_table)
    order_rows = priority[0, 0]
    same_route = route_ids[:, None] == route_ids[None, :]
    earlier = order_rows[None, :] < order_rows[:, None]
    slot_ids = jnp.sum((same_route & earlier).astype(jnp.int32), axis=1)
    target = jnp.where(slot_ids < capacity, route_ids * capacity + slot_ids, -1)
    selector = lax.broadcasted_iota(jnp.int32, (tok_rows, tok_rows), 0) == target[None, :]
    selector_low = selector.astype(jnp.bfloat16)
    outgoing = jnp.dot(
        selector_low, normed_moe.astype(jnp.bfloat16), preferred_element_type=jnp.float32
    )
    outgoing = outgoing.astype(jnp.bfloat16).reshape(experts_all, capacity, model_width)
    arrived = lax.all_to_all(outgoing, "expert", split_axis=0, concat_axis=0, tiled=True)
    sources = arrived.shape[0] // local_experts
    grouped = arrived.reshape(sources, local_experts, arrived.shape[1], arrived.shape[2])
    hidden = jnp.einsum("secd,edf->secf", grouped, first_weight, preferred_element_type=jnp.float32)
    act_low = jax.nn.gelu(hidden).astype(jnp.bfloat16)
    result = jnp.einsum(
        "secf,efd->secd", act_low, second_weight, preferred_element_type=jnp.float32
    )
    result = result.astype(jnp.bfloat16).reshape(arrived.shape)
    returned = lax.all_to_all(result, "expert", split_axis=0, concat_axis=0, tiled=True)
    returned, arrived = (returned, arrived)
    fetched = jnp.einsum(
        "st,sd->td",
        selector_low,
        returned.reshape(tok_rows, model_width),
        preferred_element_type=jnp.float32,
    )
    block_out = (residual_stream + gate_value[:, None] * fetched).astype(jnp.bfloat16)[None]
    grad_out = cotangent[0].astype(jnp.float32) * loss_mask[0].astype(jnp.float32)[:, None]
    grad_fetched = grad_out * gate_value[:, None]
    grad_gate = jnp.sum(grad_out * fetched, axis=1)
    grad_slots = jnp.dot(selector.astype(jnp.float32), grad_fetched, precision=TOP_PRECISION)
    grad_slots = grad_slots.astype(jnp.bfloat16).reshape(experts_all, capacity, model_width)
    grad_arrived = lax.all_to_all(grad_slots, "expert", split_axis=0, concat_axis=0, tiled=True)
    sources = grad_arrived.shape[0] // local_experts
    slot_shape = (sources, local_experts, capacity, model_width)
    grouped_in = arrived.reshape(slot_shape)
    grouped_grad = grad_arrived.reshape(slot_shape)
    hidden = jnp.einsum(
        "secd,edf->secf", grouped_in, first_weight, preferred_element_type=jnp.float32
    )
    act_low = jax.nn.gelu(hidden).astype(jnp.bfloat16)
    grad_second = jnp.einsum(
        "secf,secd->efd", act_low, grouped_grad, preferred_element_type=jnp.float32
    )
    grad_act = jnp.einsum(
        "secd,efd->secf", grouped_grad, second_weight, preferred_element_type=jnp.float32
    )
    unused, gelu_back = jax.vjp(jax.nn.gelu, hidden)
    grad_hidden = gelu_back(grad_act)[0].astype(jnp.bfloat16)
    grad_first = jnp.einsum(
        "secd,secf->edf", grouped_in, grad_hidden, preferred_element_type=jnp.float32
    )
    grad_sent = jnp.einsum(
        "secf,edf->secd", grad_hidden, first_weight, preferred_element_type=jnp.float32
    )
    grad_sent = grad_sent.astype(jnp.bfloat16).reshape(grad_arrived.shape)
    grad_returned = lax.all_to_all(grad_sent, "expert", split_axis=0, concat_axis=0, tiled=True)
    grad_first, grad_second = (
        lax.psum_scatter(
            grad_first.astype(jnp.bfloat16), "blk", scatter_dimension=2, tiled=True
        ).astype(jnp.float32),
        lax.psum_scatter(
            grad_second.astype(jnp.bfloat16), "blk", scatter_dimension=1, tiled=True
        ).astype(jnp.float32),
    )
    grad_moe_rows = jnp.einsum(
        "st,sd->td",
        selector_low,
        grad_returned.reshape(tok_rows, model_width),
        preferred_element_type=jnp.float32,
    )
    grad_router_rows, grad_route, grad_anchor = gate_back(grad_gate)
    grad_residual_norm, grad_moe_gain = moe_norm_back(grad_moe_rows + grad_router_rows)
    grad_residual = grad_out + grad_residual_norm
    grad_attn_low = grad_residual.astype(jnp.bfloat16)
    grad_proj = jnp.dot(attended_low.T, grad_attn_low, preferred_element_type=jnp.float32)
    grad_attended_flat = jnp.dot(
        grad_attn_low, proj_weight.T, preferred_element_type=jnp.float32
    ).astype(jnp.bfloat16)
    grad_attended = grad_attended_flat.reshape(head_shape)
    delta_rows = jnp.sum(grad_attended.astype(jnp.float32) * attention_result, axis=2).T
    key_all, value_all = (
        lax.all_gather(key_local, "blk", axis=0, tiled=True),
        lax.all_gather(value_local, "blk", axis=0, tiled=True),
    )
    block_count = seq_rows // tok_rows
    key_blocks = key_all.reshape(block_count, tok_rows, model_width)
    value_blocks = value_all.reshape(block_count, tok_rows, model_width)

    def key_block_step(running_grad, packed):
        position, key_block, value_block = packed
        key_rows = key_block.reshape(head_shape)
        value_rows = value_block.reshape(head_shape)
        scores, allowed = masked_scores(
            queries, key_rows, query_first, position * tok_rows, score_scale
        )
        soft_rows = jnp.where(allowed, jnp.exp(scores - log_total[:, :, None]), 0.0)
        grad_values = jnp.einsum(
            "hqk,qhd->khd",
            soft_rows.astype(jnp.bfloat16),
            grad_attended,
            preferred_element_type=jnp.float32,
        )
        grad_soft = jnp.einsum(
            "qhd,khd->hqk", grad_attended, value_rows, preferred_element_type=jnp.float32
        )
        grad_scores = (soft_rows * (grad_soft - delta_rows[:, :, None])).astype(jnp.bfloat16)
        grad_keys = score_scale * jnp.einsum(
            "hqk,qhd->khd", grad_scores, queries, preferred_element_type=jnp.float32
        )
        running_grad = running_grad + score_scale * jnp.einsum(
            "hqk,khd->qhd", grad_scores, key_rows, preferred_element_type=jnp.float32
        )
        term = jnp.concatenate(
            [grad_keys.reshape(tok_rows, model_width), grad_values.reshape(tok_rows, model_width)],
            axis=1,
        )
        return (running_grad, term)

    grad_queries, stacked_terms = lax.scan(
        key_block_step,
        jnp.zeros(head_shape, jnp.float32),
        (jnp.arange(block_count, dtype=jnp.int32), key_blocks, value_blocks),
    )
    all_terms = stacked_terms.reshape(seq_rows, 2 * model_width)
    key_value_grads = lax.psum_scatter(
        all_terms.astype(jnp.bfloat16), "blk", scatter_dimension=0, tiled=True
    ).astype(jnp.float32)
    grad_query_rows = grad_queries.reshape(tok_rows, model_width)
    grad_qkv_rows = jnp.concatenate([grad_query_rows, key_value_grads], axis=1).astype(jnp.bfloat16)
    grad_qkv = jnp.dot(normed_low.T, grad_qkv_rows, preferred_element_type=jnp.float32)
    grad_normed = jnp.dot(grad_qkv_rows, qkv_weight.T, preferred_element_type=jnp.float32)
    grad_source_norm, grad_attn_gain = attn_norm_back(grad_normed)
    grad_tokens = (grad_residual + grad_source_norm)[None]
    grad_qkv, grad_proj, grad_attn_gain, grad_moe_gain, grad_route, grad_anchor = lax.psum(
        (grad_qkv, grad_proj, grad_attn_gain, grad_moe_gain, grad_route, grad_anchor),
        ("blk", "expert"),
    )
    histogram_out = histogram + total_counts
    return (
        block_out,
        grad_tokens,
        grad_qkv,
        grad_proj,
        grad_attn_gain,
        grad_moe_gain,
        grad_route,
        grad_anchor,
        grad_first,
        grad_second,
        histogram_out,
    )


MESH = pl.DeviceIdType.MESH
F32 = jnp.float32
BF16 = jnp.bfloat16
VMEM_BYTES = 58 * 1024 * 1024


def dot(left, right, precision=None):
    return lax.dot_general(
        left, right, (((1,), (0,)), ((), ())), precision=precision, preferred_element_type=F32
    )


def dot_nt(left, right, precision=None):
    return lax.dot_general(
        left, right, (((1,), (1,)), ((), ())), precision=precision, preferred_element_type=F32
    )


def dot_tn(left, right, precision=None):
    return lax.dot_general(
        left, right, (((0,), (0,)), ((), ())), precision=precision, preferred_element_type=F32
    )


def split(values):
    high = values.astype(BF16)
    return high, (values - high.astype(F32)).astype(BF16)


def fine(product, left, right):
    left_high, left_low = split(left)
    right_high, right_low = split(right)
    return product(left_high, right_high) + (
        product(left_high, right_low) + product(left_low, right_high)
    )


def rows_at(index, size):
    return pl.ds(pl.multiple_of(index * size, size), size)


def places():
    blk = lax.axis_index("blk")
    expert = lax.axis_index("expert")
    return blk, expert, blk + 1 - 2 * lax.rem(blk, 2), lax.rem(blk + 2, 4), 3 - blk


def greet(peers):
    barrier = pltpu.get_barrier_semaphore()
    for peer in peers:
        pl.semaphore_signal(barrier, inc=1, device_id=peer, device_id_type=MESH)
    return lambda: pl.semaphore_wait(barrier, len(peers))


def push(src, dst, sems, index, peer):
    copy = pltpu.make_async_remote_copy(
        src_ref=src,
        dst_ref=dst,
        send_sem=sems.at[0, index],
        recv_sem=sems.at[1, index],
        device_id=peer,
        device_id_type=MESH,
    )
    copy.start()
    return copy


def standardise(values):
    average = jnp.mean(values, axis=-1, keepdims=True)
    centered = values - average
    scale = lax.rsqrt(jnp.mean(centered * centered, axis=-1, keepdims=True) + EPSILON)
    return centered * scale, scale


def lower_triangle(keys, queries):
    return lax.broadcasted_iota(jnp.int32, (keys, queries), 0) <= lax.broadcasted_iota(
        jnp.int32, (keys, queries), 1
    )


class BlockGather:
    def __init__(self, part, sems, base, own=None):
        self.part, self.sems, self.base, self.own = part, sems, base, own

    def send(self, blk, half, index, peer):
        ref = self.part(blk, half)
        src = ref if self.own is None or index > 3 else self.own(half)
        return push(src, ref, self.sems, self.base + index, peer)

    def start(self):
        self.start_first()
        self.start_second()

    def start_first(self):
        blk, expert, bx, by, bd = places()
        self.copies = [self.send(blk, 0, 0, (bx, expert)), self.send(blk, 1, 1, (by, expert))]

    def start_second(self):
        blk, expert, bx, by, bd = places()
        self.copies += [self.send(blk, 1, 2, (bx, expert)), self.send(blk, 0, 3, (by, expert))]

    def forward(self):
        blk, expert, bx, by, bd = places()
        self.copies[0].wait_recv()
        self.copies.append(self.send(bx, 0, 4, (by, expert)))
        self.copies[1].wait_recv()
        self.copies.append(self.send(by, 1, 5, (bx, expert)))

    def wait_neighbours(self):
        self.copies[2].wait_recv()
        self.copies[3].wait_recv()

    def wait_diagonal(self):
        self.copies[4].wait_recv()
        self.copies[5].wait_recv()

    def wait_sends(self):
        for copy in self.copies:
            copy.wait_send()


def row_halves(buf, rows):
    size = rows // 2
    return lambda blk, half: buf.at[pl.ds(pl.multiple_of(blk * rows + half * size, size), size)]


def expert_groups():
    expert = lax.axis_index("expert")
    line, core = expert // 2, lax.rem(expert, 2)
    side, place = line // 2, lax.rem(line, 2)
    beside = (side * 2 + 1 - place) * 2
    first = ((1 - side) * 2 + place) * 2
    second = ((1 - side) * 2 + 1 - place) * 2
    return [
        (side * 4, 4, [expert + 1 - 2 * core, beside + core, beside + 1 - core]),
        (first, 2, [first + core, first + 1 - core]),
        (second, 2, [second + core, second + 1 - core]),
    ]


class ExpertExchange:
    def __init__(self, src, dst, sems, rows):
        self.src, self.dst, self.sems, self.rows = src, dst, sems, rows
        self.groups = expert_groups()
        self.copies = [[], [], []]

    def start(self, group, keep=True):
        blk, expert = lax.axis_index("blk"), lax.axis_index("expert")
        place = rows_at(expert, self.rows)
        base = (0, 3, 5)[group]
        for n, peer in enumerate(self.groups[group][2]):
            self.copies[group].append(
                push(self.src.at[rows_at(peer, self.rows)], self.dst.at[place], self.sems,
                     base + n, (blk, peer))
            )
        if group == 0 and keep:
            self.dst[place] = self.src[place]

    def wait_recv(self, group):
        for copy in self.copies[group]:
            copy.wait_recv()

    def wait_sends(self):
        for copy in sum(self.copies, []):
            copy.wait_send()

    def start_all(self, keep=True):
        self.start(1)
        self.start(2)
        self.start(0, keep)

    def wait_all(self):
        for group in range(3):
            self.wait_recv(group)
        self.wait_sends()


class Lazy:
    def __init__(self, src, dst, sem):
        self.dst, self.shape, self.fresh = dst, dst.shape, True
        self.copy = pltpu.make_async_copy(src, dst, sem)
        self.copy.start()

    def ref(self):
        if self.fresh:
            self.copy.wait()
            self.fresh = False
        return self.dst

    def __getitem__(self, where):
        return self.ref()[where]

    @property
    def at(self):
        return self.ref().at


class LazyOut:
    def __init__(self, src, dst, sem):
        self.src, self.dst, self.sem, self.shape, self.copy = src, dst, sem, src.shape, None

    def flush(self):
        if self.copy is None:
            self.copy = pltpu.make_async_copy(self.src, self.dst, self.sem)
            self.copy.start()

    def __getitem__(self, where):
        return self.src[where]

    def __setitem__(self, where, value):
        self.src[where] = value

    @property
    def at(self):
        return self.src.at


def blk_peers():
    blk, expert, bx, by, bd = places()
    return [(bx, expert), (by, expert), (bd, expert)]


def expert_peers():
    blk, expert = lax.axis_index("blk"), lax.axis_index("expert")
    n = lax.axis_size("expert")
    return [(blk, lax.rem(expert + shift, n)) for shift in range(1, n)]


def forward_kernel(
    tok_ref, attn_gain_ref, moe_gain_ref, routes_ref, priority_ref, mask_ref, wqkv_ref, cot_ref, proj_ref, route_ref, anchor_ref, first_ref, second_ref,
    nall_ref, qkv_ref, out_ref, lse_ref, cols_ref, result_ref, residual_ref, gate_ref,
    grad_residual_ref, grad_att_ref, grad_proj_ref, small_ref, buf_ref, cots_ref, gates_ref,
    w_s, wt_s, k_s, att_s, cot_s, att_ref, cot_in_ref,
    first_s, second_s, slope_s, buf_s, gates_s, go_s, gate_s, grad_s, back_s, score_s, score_in_s,
    res_acc, sent_acc, grad_in_s,
    w_sem, gather_sems, cot_sems, att_sems, go_sems, gate_sems, back_sems, score_sems, cots_sems,
    buf_sems, gates_sems,
):
    blk, expert, bx, by, bd = places()
    tok = tok_ref.shape[0]
    width = tok_ref.shape[1]
    heads = HEADS // 4
    group = heads * HEAD_DIM
    arrived = greet(blk_peers() + expert_peers())
    odd = lax.rem(blk, 2)
    loads = []
    for part in range(3):
        first = pl.multiple_of(part * width + blk * group - odd * 64, 128)
        loads.append(
            pltpu.make_async_copy(wqkv_ref.at[:, pl.ds(first, 256)], w_s.at[part], w_sem.at[part])
        )
        loads[-1].start()
    weights = [
        pltpu.make_async_copy(first_ref, first_s, w_sem.at[3]),
        pltpu.make_async_copy(second_ref, second_s, w_sem.at[4]),
    ]
    for load in weights:
        load.start()
    xhat, _ = standardise(tok_ref[...].astype(F32))
    nall_ref[rows_at(blk, tok), :] = (xhat * attn_gain_ref[...].reshape(1, width)).astype(BF16)
    arrived()
    gather = BlockGather(row_halves(nall_ref, tok), gather_sems, 0)
    gather.start()

    capacity = tok // 8
    route_row, prio_row, mask_row = (
        ref[...].astype(F32) for ref in (routes_ref, priority_ref, mask_ref))
    cols = jnp.concatenate(
        [jnp.zeros((1, tok), F32), route_row, prio_row, mask_row, jnp.zeros((124, tok), F32)],
        axis=0).T
    route_col, prio_col = cols[:, 1:2], cols[:, 2:3]
    same = route_col == route_row
    slot_row = jnp.sum(jnp.where(same & (prio_col < prio_row), 1.0, 0.0), axis=0, keepdims=True)
    slot_col = jnp.sum(jnp.where(same & (prio_row < prio_col), 1.0, 0.0), axis=1, keepdims=True)
    target_row = jnp.where(slot_row < capacity, route_row * capacity + slot_row, -1.0)
    target_col = jnp.where(slot_col < capacity, route_col * capacity + slot_col, -1.0)
    lane = lax.broadcasted_iota(jnp.int32, cols.shape, 1)
    cols_ref[...] = jnp.where(lane == 0, target_col, cols)
    cols_ref.flush()
    slots = lax.broadcasted_iota(jnp.int32, (tok, tok), 0).astype(F32)
    chosen = jnp.where((slots == target_row) & (mask_row > 0.0), 1.0, 0.0).astype(BF16)
    cot_s[...] = dot(chosen, cot_ref[...]).astype(BF16)
    cot_move = ExpertExchange(cot_s, cot_in_ref, cot_sems, capacity)
    cot_move.start_all()

    for part in range(3):
        loads[part].wait()
        wide = w_s[part]
        narrow = jnp.where(odd == 1, wide[:, 64:256], wide[:, 0:192])
        wt_s[part * group : (part + 1) * group, :] = narrow.T

    def project(where):
        cols = rows_at(where, tok)
        mixed = dot_nt(wt_s[...], nall_ref[cols, :]).astype(BF16)
        qkv_ref[0:group, cols] = mixed[0:group] * BF16(HEAD_DIM**-0.5)
        qkv_ref[group:, cols] = mixed[group:]
        for head in range(heads):
            k_s[head, cols, :] = mixed[group + head * 64 : group + (head + 1) * 64].T

    project(blk)
    gather.forward()
    gather.wait_neighbours()
    project(bx)
    project(by)
    gather.wait_diagonal()
    nall_ref.flush()
    cot_move.wait_all()
    here = rows_at(blk, tok)
    cots_own = pltpu.make_async_copy(cot_in_ref, cots_ref.at[here], w_sem.at[5])
    cots_own.start()
    quarter = tok // 4
    cots = []
    for part in range(2):

        def own(half, part=part):
            return cot_in_ref.at[pl.ds((2 * part + half) * quarter, quarter)]

        def halves(block, half, part=part):
            row = pl.multiple_of(block * tok + (2 * part + half) * quarter, quarter)
            return cots_ref.at[pl.ds(row, quarter)]

        cots.append(BlockGather(halves, cots_sems, 6 * part, own))
    cots[0].start_first()
    cots[1].start_first()
    project(bd)
    qkv_ref.flush()

    half = tok // 2

    def scores(i, head):
        q = qkv_ref[head * 64 : (head + 1) * 64, i * tok : (i + 1) * tok]
        upper = dot(k_s[head, i * tok : i * tok + half, :], q)
        upper = jnp.where(lower_triangle(half, tok), upper, MASKED)
        lower = dot(k_s[head, i * tok + half : (i + 1) * tok, :], q[:, half:])
        lower = jnp.where(lower_triangle(half, half), lower, MASKED)
        top = jnp.max(upper, axis=0, keepdims=True)
        low_top = jnp.max(lower, axis=0, keepdims=True)
        top = jnp.concatenate([top[:, :half], jnp.maximum(top[:, half:], low_top)], axis=1)
        if i == 0:
            return top, upper, lower, None
        past = dot(k_s[head, 0 : i * tok, :], q)
        return jnp.maximum(top, jnp.max(past, axis=0, keepdims=True)), upper, lower, past

    sends = []

    def finish(i, head, found):
        top, upper, lower, past = found
        v = qkv_ref[2 * group + head * 64 : 2 * group + (head + 1) * 64, :]
        upper = jnp.exp(upper - top)
        lower = jnp.exp(lower - top[:, half:])
        total = jnp.sum(upper, axis=0, keepdims=True)
        low_total = jnp.sum(lower, axis=0, keepdims=True)
        total = jnp.concatenate([total[:, :half], total[:, half:] + low_total], axis=1)
        result = dot(v[:, i * tok : i * tok + half], upper.astype(BF16))
        low_result = dot(v[:, i * tok + half : (i + 1) * tok], lower.astype(BF16))
        result = jnp.concatenate([result[:, :half], result[:, half:] + low_result], axis=1)
        if i:
            past = jnp.exp(past - top)
            total = total + jnp.sum(past, axis=0, keepdims=True)
            result = result + dot(v[:, 0 : i * tok], past.astype(BF16))
        result = result / total
        place = slice(head * 64, (head + 1) * 64)
        out_ref[place, i * tok : (i + 1) * tok] = result
        lse_ref[head : head + 1, i * tok : (i + 1) * tok] = top + jnp.log(total)
        att_s[place, i * tok : (i + 1) * tok] = result.astype(BF16)
        there = pl.ds(pl.multiple_of(blk * group + head * 64, 64), 64)

        def copy():
            return pltpu.make_async_remote_copy(
                src_ref=att_s.at[place, i * tok : (i + 1) * tok],
                dst_ref=att_ref.at[there],
                send_sem=att_sems.at[0, i * heads + head],
                recv_sem=att_sems.at[1, blk * heads + head],
                device_id=(i, expert),
                device_id_type=MESH,
            )

        @pl.when(blk != i)
        def _():
            copy().start()

        @pl.when(blk == i)
        def _():
            att_ref[there, :] = result.astype(BF16)

        sends.append((i, copy))

    before = None
    for i in range(4):
        for head in range(heads):
            found = scores(i, head)
            if before is not None:
                finish(*before)
            before = (i, head, found)
    finish(*before)

    for i, copy in sends:
        @pl.when(blk != i)
        def _():
            copy().wait_send()

    for source in range(4):
        @pl.when(blk != source)
        def _():
            for head in range(heads):
                there = pl.ds(source * group + head * 64, 64)
                pltpu.make_async_remote_copy(
                    src_ref=att_s.at[0:64, 0:tok],
                    dst_ref=att_ref.at[there],
                    send_sem=att_sems.at[0, source * heads + head],
                    recv_sem=att_sems.at[1, source * heads + head],
                    device_id=(source, expert),
                    device_id_type=MESH,
                ).wait_recv()

    cots[0].forward()
    cots[1].forward()
    cots[0].start_second()
    cots[1].start_second()
    out_ref.flush()
    gather.wait_sends()

    gain = moe_gain_ref[...].reshape(1, width)
    experts = 8
    residual = tok_ref[...].astype(F32) + dot_tn(att_ref[...], proj_ref[...])
    residual_ref[...] = residual
    residual_ref.flush()
    xhat, scale = standardise(residual)
    normed = xhat * gain
    normed_low = normed.astype(BF16)
    go_s[...] = dot(jnp.where(slots == target_row, 1.0, 0.0).astype(BF16), normed_low).astype(BF16)
    go = ExpertExchange(go_s, buf_s, go_sems, capacity)
    go.start(0)

    projected = fine(dot_nt, normed, route_ref[...])
    unit_scale = lax.rsqrt(1.0 + jnp.sum(projected * projected, axis=1, keepdims=True))
    unit = projected * unit_scale
    anchor = anchor_ref[...]
    anchor_scale = lax.rsqrt(1.0 + jnp.sum(anchor * anchor, axis=1, keepdims=True))
    anchor_unit = anchor * anchor_scale
    logits = fine(dot_nt, unit, anchor_unit) / ROUTER_SOFTNESS
    soft = jnp.exp(logits - jnp.max(logits, axis=1, keepdims=True))
    soft = soft / jnp.sum(soft, axis=1, keepdims=True)
    onehot = jnp.where(
        lax.broadcasted_iota(jnp.int32, (tok, experts), 1).astype(F32) == route_col, 1.0, 0.0
    )
    gate = jnp.sum(soft * onehot, axis=1, keepdims=True)
    gate_ref[...] = jnp.broadcast_to(gate, gate_ref.shape)
    gate_ref.flush()
    lane = lax.broadcasted_iota(jnp.int32, (tok, 128), 1).astype(F32)
    lane = jnp.where(lane < capacity, lane, 1e6)
    for peer in range(experts):
        row = jnp.sum(
            jnp.where(target_col == peer * capacity + lane, gate, 0.0), axis=0, keepdims=True
        )
        gate_s[peer * 8 : (peer + 1) * 8, :] = jnp.broadcast_to(row, (8, 128))
    gates = ExpertExchange(gate_s, gates_s, gate_sems, 8)
    go.start(1)
    for group in range(3):
        gates.start(group)

    back = ExpertExchange(grad_s, back_s, back_sems, capacity)
    scores = ExpertExchange(score_s, score_in_s, score_sems, 8)
    tile = 768
    tiles = first_s.shape[1] // tile
    bufs, kept = [], []
    for group, (first_source, sources, _) in enumerate(go.groups):
        count = sources * capacity
        rows = pl.ds(pl.multiple_of(first_source * capacity, count), count)
        go.wait_recv(group)
        if group == 0:
            go.start(2)

        def halves(block, half, first=first_source * capacity, size=count // 2):
            return buf_ref.at[pl.ds(pl.multiple_of(block * tok + first + half * size, size), size)]

        def own(half, first=first_source * capacity, size=count // 2):
            return buf_s.at[pl.ds(pl.multiple_of(first + half * size, size), size)]

        bufs.append(BlockGather(halves, buf_sems, 6 * group, own))
        bufs[group].start()
        there = pl.ds(pl.multiple_of(blk * tok + first_source * capacity, count), count)
        kept.append(pltpu.make_async_copy(buf_s.at[rows], buf_ref.at[there], w_sem.at[6 + group]))
        kept[group].start()
        if group == 0:
            for load in weights:
                load.wait()
        x = buf_s[rows, :]
        for t in range(tiles):
            cut = slice(t * tile, (t + 1) * tile)
            act, slope = gelu_pair(dot(x, first_s[:, cut]))
            slope_s[0:count, cut] = slope
            part = dot(act.astype(BF16), second_s[cut, :])
            if t == 0:
                res_acc[0:count, :] = part
            else:
                res_acc[0:count, :] += part
        result = res_acc[0:count, :].astype(BF16)
        score = jnp.sum(
            result.astype(F32) * cot_in_ref[rows, :].astype(F32), axis=1, keepdims=True)
        for n in range(sources):
            row = flatten(score[n * capacity : (n + 1) * capacity], 128)
            score_s[rows_at(first_source + n, 8), :] = jnp.broadcast_to(row, (8, 128))
        scores.start(group)
        result_ref[rows, :] = result
        gates.wait_recv(group)
        for n in range(sources):
            row = gates_s[rows_at(first_source + n, 8), :][0:1, :]
            chunk = rows_at(first_source + n, capacity)
            grad_in_s[n * capacity : (n + 1) * capacity, :] = (
                cot_in_ref[chunk, :].astype(F32) * spread(row, capacity)
            ).astype(BF16)
        grad_in = grad_in_s[0:count, :]
        for t in range(tiles):
            cut = slice(t * tile, (t + 1) * tile)
            grad_hidden = (dot_nt(grad_in, second_s[cut, :]) * slope_s[0:count, cut]).astype(BF16)
            sent = dot_nt(grad_hidden, first_s[:, cut])
            if t == 0:
                sent_acc[0:count, :] = sent
            else:
                sent_acc[0:count, :] += sent
        grad_s[rows, :] = sent_acc[0:count, :].astype(BF16)
        back.start(group)
    bufs[0].forward()
    result_ref.flush()
    gates_ref[rows_at(blk, 64), :] = gates_s[...]
    gates_here = gates_ref.at[rows_at(blk, 64)]
    gates_out = [
        push(gates_here, gates_here, gates_sems, n, peer) for n, peer in enumerate(blk_peers())
    ]
    grad_out = cot_ref[...].astype(F32) * cols_ref[:, 3:4]

    for group in range(3):
        scores.wait_recv(group)
    grad_gate = jnp.zeros((tok, 1), F32)
    for peer in range(experts):
        row = score_in_s[peer * 8 : peer * 8 + 1, :]
        grad_gate += jnp.sum(
            jnp.where(target_col == peer * capacity + lane, row, 0.0), axis=1, keepdims=True
        )
    grad_logits = grad_gate * gate * (onehot - soft) / ROUTER_SOFTNESS
    grad_unit = fine(dot, grad_logits, anchor_unit)
    grad_projected = unit_scale * (
        grad_unit - unit * jnp.sum(unit * grad_unit, axis=1, keepdims=True)
    )
    grad_anchor_unit = fine(dot_tn, grad_logits, unit)
    grad_anchor = anchor_scale * (
        grad_anchor_unit
        - anchor_unit * jnp.sum(anchor_unit * grad_anchor_unit, axis=1, keepdims=True)
    )
    rdim = route_ref.shape[0]
    small_ref[...] = jnp.zeros_like(small_ref)
    small_ref[0:rdim, :] = fine(dot_tn, grad_projected, normed)
    small_ref[rdim : rdim + experts, 0:rdim] = grad_anchor
    counts = jnp.sum(onehot, axis=0, keepdims=True)
    small_ref[rdim + experts + 2 : rdim + experts + 3, 0:experts] = counts
    router_rows = fine(dot, grad_projected, route_ref[...])

    bufs[1].forward()
    for group in range(3):
        back.wait_recv(group)
    lanes = lax.broadcasted_iota(jnp.int32, (tok, tok), 1).astype(F32)
    moe_rows = dot(jnp.where(lanes == target_col, 1.0, 0.0).astype(BF16), back_s[...])
    grad_normed = moe_rows + router_rows
    small_ref[rdim + experts : rdim + experts + 1, :] = jnp.sum(
        grad_normed * xhat, axis=0, keepdims=True
    )
    grad_xhat = grad_normed * gain
    grad_residual = grad_out + scale * (
        grad_xhat
        - jnp.mean(grad_xhat, axis=1, keepdims=True)
        - xhat * jnp.mean(grad_xhat * xhat, axis=1, keepdims=True)
    )
    grad_residual_ref[...] = grad_residual
    grad_low = grad_residual.astype(BF16)
    grad_residual_ref.flush()
    bufs[2].forward()
    grad_att_ref[...] = dot_nt(proj_ref[...], grad_low).astype(BF16)
    grad_att_ref.flush()
    grad_proj_ref[...] = dot(att_ref[...], grad_low).astype(BF16)

    grad_proj_ref.flush()
    for copy in kept + [cots_own]:
        copy.wait()
    for gather in cots + bufs:
        gather.wait_neighbours()
        gather.wait_diagonal()
        gather.wait_sends()
    for exchange in (go, gates, back, scores):
        exchange.wait_sends()
    for copy in gates_out:
        copy.wait()


def gelu_pair(hidden):
    squared = hidden * hidden
    curve = jnp.tanh(0.7978845608028654 * hidden * (1.0 + 0.044715 * squared))
    half = 0.5 * (1.0 + curve)
    slope = half + 0.5 * hidden * (1.0 - curve * curve) * (
        0.7978845608028654 * (1.0 + 0.134145 * squared)
    )
    return hidden * half, slope


def spread(row, size):
    shape = (size, row.shape[1])
    eye = lax.broadcasted_iota(jnp.int32, shape, 0) == lax.broadcasted_iota(jnp.int32, shape, 1)
    return jnp.sum(jnp.where(eye, row, 0.0), axis=1, keepdims=True)


def flatten(column, width):
    shape = (column.shape[0], width)
    eye = lax.broadcasted_iota(jnp.int32, shape, 0) == lax.broadcasted_iota(jnp.int32, shape, 1)
    return jnp.sum(jnp.where(eye, column, 0.0), axis=0, keepdims=True)


def attend_back_kernel(
    grad_att_ref, qkv_ref, out_ref, lse_ref, nall_ref, result_ref, residual_ref, gate_ref,
    cols_ref, gain_ref, wqkv_ref, tok_ref, grad_residual_ref, grad_proj_ref, small_ref,
    buf_ref, cots_ref, gates_ref, first_ref, second_ref,
    block_out_ref, grad_tokens_ref, shared_ref, small_out_ref, grad_first_ref, grad_second_ref,
    do_t, dq_s, dqkv_s, home_s, back_s, wt_s, proj_in, part_s, sum_s,
    core_out, core_in, line_out, line_in, small_a, small_in, small_b, row_out, row_in,
    first_s, second_s, slot_s, rows_s, shared_s, first_acc, second_acc,
    att_sems, back_sems, home_sems, proj_sems, core_sems, line_sems, join_sems, small_sems,
    row_sems, ring_sems, pair_sems, load_sems,
):
    blk, expert, bx, by, bd = places()
    tok = grad_att_ref.shape[1]
    width = grad_att_ref.shape[0]
    heads = HEADS // 4
    group = heads * HEAD_DIM
    here = rows_at(blk, tok)
    length = qkv_ref.shape[1]
    core = lax.rem(expert, 2)
    line = expert // 2
    lines = 4
    half = width // 2
    other = (blk, expert + 1 - 2 * core)
    mine_lanes = pl.ds(pl.multiple_of(core * half, 128), half)
    other_lanes = pl.ds(pl.multiple_of((1 - core) * half, 128), half)
    line_peers = [(blk, lax.rem(line + shift, lines) * 2 + core) for shift in range(1, lines)]
    gain = gain_ref[...].reshape(1, width)
    arrived = greet(blk_peers() + expert_peers())
    odd = lax.rem(blk, 2)
    quarter = first_s.shape[1]

    def load(src, dst, index):
        copy = pltpu.make_async_copy(src, dst, load_sems.at[index])
        copy.start()
        return copy

    weights = [
        load(first_ref.at[:, rows_at(blk, quarter)], first_s, 0),
        load(second_ref.at[rows_at(blk, quarter)], second_s, 1),
    ]
    slot_loads = []

    def load_slots(t):
        cut = slice(t * tok, (t + 1) * tok)
        slot_loads.append((
            load(buf_ref.at[cut], slot_s.at[t % 2, 0], 2 + t % 2),
            load(cots_ref.at[cut], slot_s.at[t % 2, 1], 4 + t % 2),
        ))

    load_slots(0)
    rows_load = [load(residual_ref, rows_s, 6)]
    mine = rows_at(blk, group)
    mine_load = load(grad_att_ref.at[mine], do_t.at[:, here], 7)
    own_slots = rows_at(expert, tok // 8)
    result_load = load(result_ref.at[own_slots], back_s.at[own_slots], 8)
    arrived()
    att_copies = []

    def send_att(head):
        cut = slice(head * 64, (head + 1) * 64)
        att_copies.append([
            push(
                grad_att_ref.at[pl.ds(pl.multiple_of(peer[0] * group + head * 64, 64), 64)],
                do_t.at[cut, here], att_sems, head * 3 + n, peer)
            for n, peer in enumerate(blk_peers())
        ])

    send_att(0)
    back = ExpertExchange(result_ref, back_s, back_sems, tok // 8)
    small_core = push(small_ref.at[:, other_lanes], small_in.at[0], small_sems, 0, other)
    for part in range(3):
        first = pl.multiple_of(part * width + blk * group - odd * 64, 128)
        wide = wqkv_ref[:, pl.ds(first, 256)]
        narrow = jnp.where(odd == 1, wide[:, 64:256], wide[:, 0:192]).T
        for head in range(heads):
            place = head * 192 + part * 64
            wt_s[place : place + 64, :] = narrow[head * 64 : (head + 1) * 64]

    def expert_weights(t):
        if t == 0:
            for copy in weights:
                copy.wait()
        if t < 3:
            load_slots(t + 1)
        for copy in slot_loads[t]:
            copy.wait()
        x = slot_s[t % 2, 0]
        rates = [spread(gates_ref[t * 64 + n * 8 : t * 64 + n * 8 + 1, :], 64) for n in range(8)]
        rate = jnp.concatenate(rates, axis=0)
        grad_in = (slot_s[t % 2, 1].astype(F32) * rate).astype(BF16)
        act, slope = gelu_pair(dot(x, first_s[...]))
        grad_hidden = (dot_nt(grad_in, second_s[...]) * slope).astype(BF16)
        grad_second = dot_tn(act.astype(BF16), grad_in)
        grad_first = dot_tn(x, grad_hidden)
        if t == 0:
            second_acc[...] = grad_second
            first_acc[...] = grad_first
        elif t < 3:
            second_acc[...] += grad_second
            first_acc[...] += grad_first
        else:
            grad_second_ref[...] = (second_acc[...] + grad_second).astype(BF16)
            grad_first_ref[...] = (first_acc[...] + grad_first).astype(BF16)

    send_att(1)
    expert_weights(0)
    send_att(2)
    small_core.wait()
    small_a[...] = small_ref[:, mine_lanes] + small_in[0]
    small_in[1 + line] = small_a[...]
    small_line = [
        push(small_a, small_in.at[1 + line], small_sems, 1 + n, peer)
        for n, peer in enumerate(line_peers)
    ]
    back.start_all(False)
    mine_load.wait()
    proj_copies = [
        push(grad_proj_ref.at[rows_at(peer[0], group)], proj_in.at[n], proj_sems, n, peer)
        for n, peer in enumerate(blk_peers())
    ]

    chunk_rows = group
    piece = chunk_rows // lines
    core_copies, line_copies, joins, gathers, pairs = {}, {}, {}, {}, []
    small_blk = []

    def chunk_at(c):
        return slice(c * chunk_rows, (c + 1) * chunk_rows)

    def shared_at(block, c, first, size):
        row = pl.multiple_of(block * width + c * chunk_rows + first, 16)
        return shared_ref.at[pl.ds(row, size), mine_lanes]

    def send_core(c):
        core_out[chunk_at(c), :] = part_s[chunk_at(c), other_lanes].astype(BF16)
        core_copies[c] = push(
            core_out.at[chunk_at(c)], core_in.at[chunk_at(c)], core_sems, c, other)

    def send_line(c):
        core_copies[c].wait()
        summed = part_s[chunk_at(c), mine_lanes] + core_in[chunk_at(c), :].astype(F32)
        sum_s[chunk_at(c), :] = summed
        line_out[chunk_at(c), :] = summed.astype(BF16)
        line_copies[c] = [
            push(
                line_out.at[pl.ds(
                    pl.multiple_of(c * chunk_rows + (peer[1] // 2) * piece, piece), piece)],
                line_in.at[c * 3 + n], line_sems, c * 3 + n, peer)
            for n, peer in enumerate(line_peers)
        ]

    def send_join(c):
        for copy in line_copies[c]:
            copy.wait()
        first = pl.multiple_of(c * chunk_rows + line * piece, piece)
        total = sum_s[pl.ds(first, piece), :]
        for n in range(3):
            total = total + line_in[c * 3 + n].astype(F32)
        shared_s[c] = total.astype(BF16)
        ref = shared_at(blk, c, line * piece, piece)
        joins[c] = [
            push(shared_s.at[c], ref, join_sems, c * 3 + n, peer)
            for n, peer in enumerate(line_peers)]
        joins[c].append(load(shared_s.at[c], ref, 9 + c))

    def pair(block, c):
        ref = shared_at(block, c, 0, chunk_rows)
        pairs.append(push(ref, ref, pair_sems, len(pairs), other))

    def send_ring(c):
        for copy in joins[c]:
            copy.wait()
        size = chunk_rows // 2
        gathers[c] = BlockGather(
            lambda block, part: shared_at(block, c, part * size, size), ring_sems, c * 6)
        gathers[c].start()
        pair(blk, c)

    def forward(c):
        gathers[c].forward()

    def pair_neighbours(c):
        gathers[c].wait_neighbours()
        pair(bx, c)
        pair(by, c)

    def pair_diagonal(c):
        gathers[c].wait_diagonal()
        pair(bd, c)

    def sum_proj():
        for copy in proj_copies:
            copy.wait()
        part_s[chunk_at(3), :] = (
            (grad_proj_ref[mine, :].astype(F32) + proj_in[0].astype(F32))
            + (proj_in[1].astype(F32) + proj_in[2].astype(F32))
        )
        send_core(3)

    def sum_small():
        for copy in small_line:
            copy.wait()
        small_b[...] = (small_in[1] + small_in[2]) + (small_in[3] + small_in[4])
        small_in[5 + blk] = small_b[...]
        small_blk.extend(
            push(small_b, small_in.at[5 + blk], small_sems, 4 + n, peer)
            for n, peer in enumerate(blk_peers())
        )

    sent = []

    def send_home(head, part, block):
        src = slice(head * 192 + part * 64, head * 192 + (part + 1) * 64)
        there = pl.ds(pl.multiple_of(part * width + blk * group + head * 64, 64), 64)

        def copy():
            return pltpu.make_async_remote_copy(
                src_ref=dqkv_s.at[src, block * tok : (block + 1) * tok],
                dst_ref=home_s.at[there],
                send_sem=home_sems.at[0, (block * heads + head) * 3 + part],
                recv_sem=home_sems.at[1, (blk * heads + head) * 3 + part],
                device_id=(block, expert),
                device_id_type=MESH,
            )

        @pl.when(blk != block)
        def _():
            copy().start()

        @pl.when(blk == block)
        def _():
            home_s[there, :] = dqkv_s[src, block * tok : (block + 1) * tok]

        sent.append((block, copy))

    after = {
        (1, 1): [sum_small],
        (1, 3): [lambda: send_line(0)],
        (1, 5): [sum_proj],
        (2, 0): [lambda: send_line(3)],
        (2, 1): [lambda: send_join(0)],
        (2, 3): [lambda: send_line(1)],
        (2, 5): [lambda: send_ring(0)],
        (2, 7): [lambda: send_join(3), lambda: send_join(1)],
    }
    gain_total = None
    for head in range(heads):
        cut = slice(head * 64, (head + 1) * 64)
        kt_cut = slice(group + head * 64, group + (head + 1) * 64)
        vt_cut = slice(2 * group + head * 64, 2 * group + (head + 1) * 64)
        for copy in att_copies[head]:
            copy.wait_recv()
        delta = jnp.sum(out_ref[cut, :] * do_t[cut, :].astype(F32), axis=0, keepdims=True)
        base = head * 192
        step = tok // 2
        for j in range(length // step):
            keys = slice(j * step, (j + 1) * step)
            queries = slice(j * step, length)
            s = dot_tn(qkv_ref[kt_cut, keys], qkv_ref[cut, queries])
            p = jnp.exp(s - lse_ref[head : head + 1, queries])
            edge = jnp.where(lower_triangle(step, step), p[:, :step], 0.0)
            p = edge if p.shape[1] == step else jnp.concatenate([edge, p[:, step:]], axis=1)
            dp = dot_tn(qkv_ref[vt_cut, keys], do_t[cut, queries])
            ds = (p * (dp - delta[:, queries])).astype(BF16)
            dv = dot_nt(do_t[cut, queries], p.astype(BF16))
            dk = dot_nt(qkv_ref[cut, queries], ds)
            dqkv_s[base + 64 : base + 128, keys] = dk.astype(BF16)
            dqkv_s[base + 128 : base + 192, keys] = dv.astype(BF16)
            if j % 2:
                send_home(head, 1, j // 2)
                send_home(head, 2, j // 2)
            dq = dot(qkv_ref[kt_cut, keys], ds)
            if j == 0:
                dq_s[...] = dq
            else:
                dq_s[:, queries] += dq
            for action in after.get((head, j), ()):
                action()
        dqkv_s[base : base + 64, :] = (dq_s[...] * HEAD_DIM**-0.5).astype(BF16)
        for block in range(4):
            send_home(head, 0, block)
        grad_group = dot(dqkv_s[base : base + 192, :], nall_ref[...])
        part_s[chunk_at(head), :] = grad_group
        send_core(head)
        share = jnp.sum(
            grad_group * wt_s[base : base + 192, :].astype(F32), axis=0, keepdims=True)
        gain_total = share if gain_total is None else gain_total + share

    attn_gain = gain_total / gain
    row_out[0] = jnp.concatenate(
        [attn_gain[:, n * 128 : (n + 1) * 128] for n in range(width // 128)]
        + [jnp.zeros((8 - width // 128, 128), F32)], axis=0)
    row_core = push(row_out.at[0], row_in.at[0], row_sems, 0, other)
    send_line(2)
    send_ring(3)
    send_ring(1)
    for copy in small_blk:
        copy.wait()
    small_out_ref[:, mine_lanes] = (small_in[5] + small_in[6]) + (small_in[7] + small_in[8])
    small_pair = push(
        small_out_ref.at[:, mine_lanes], small_out_ref.at[:, mine_lanes], small_sems, 7, other)
    row_core.wait()
    row_out[1] = row_out[0] + row_in[0]
    row_in[1 + line] = row_out[1]
    row_line = [
        push(row_out.at[1], row_in.at[1 + line], row_sems, 1 + n, peer)
        for n, peer in enumerate(line_peers)
    ]
    back.wait_all()
    result_load.wait()
    lanes = lax.broadcasted_iota(jnp.int32, (tok, tok), 1).astype(F32)
    chosen = jnp.where(lanes == cols_ref[:, 0:1], 1.0, 0.0).astype(BF16)
    fetched = dot(chosen, back_s[...])
    rows_load[0].wait()
    block_out_ref[...] = (rows_s[...] + gate_ref[:, 0:1] * fetched).astype(BF16)
    block_out_ref.flush()
    rows_load.append(load(grad_residual_ref, rows_s, 6))
    expert_weights(1)
    send_join(2)
    forward(0)
    for copy in row_line:
        copy.wait()
    row_out[2] = (row_in[1] + row_in[2]) + (row_in[3] + row_in[4])
    row_in[5 + blk] = row_out[2]
    row_blk = [
        push(row_out.at[2], row_in.at[5 + blk], row_sems, 4 + n, peer)
        for n, peer in enumerate(blk_peers())
    ]
    expert_weights(2)
    send_ring(2)
    forward(3)
    expert_weights(3)
    grad_first_ref.flush()
    grad_second_ref.flush()
    forward(1)
    pair_neighbours(0)
    pair_diagonal(0)
    pair_neighbours(3)

    for source in range(4):
        @pl.when(blk != source)
        def _():
            for item in range(9):
                index = source * 9 + item
                pltpu.make_async_remote_copy(
                    src_ref=dqkv_s.at[0:64, 0:tok],
                    dst_ref=home_s.at[0:64],
                    send_sem=home_sems.at[0, index],
                    recv_sem=home_sems.at[1, index],
                    device_id=(source, expert),
                    device_id_type=MESH,
                ).wait_recv()
    rows_load[1].wait()
    xhat, scale = standardise(tok_ref[...].astype(F32))

    def tokens_part(n):
        cut = slice(n * 256, (n + 1) * 256)
        grad_normed = dot(wqkv_ref[...], home_s[:, cut]).T
        grad_xhat = grad_normed * gain
        x = xhat[cut]
        grad_tokens_ref[cut, :] = (rows_s[cut, :] + scale[cut] * (
            grad_xhat
            - jnp.mean(grad_xhat, axis=1, keepdims=True)
            - x * jnp.mean(grad_xhat * x, axis=1, keepdims=True)
        )).astype(BF16)

    forward(2)
    tokens_part(0)
    pair_diagonal(3)
    pair_neighbours(1)
    tokens_part(1)
    grad_tokens_ref.flush()
    pair_diagonal(1)
    pair_neighbours(2)
    pair_diagonal(2)
    for copy in row_blk:
        copy.wait()
    small_pair.wait()
    total = (row_in[5] + row_in[6]) + (row_in[7] + row_in[8])
    small_out_ref[25:26, :] = jnp.concatenate(
        [total[n : n + 1, :] for n in range(width // 128)], axis=1)
    for copy in pairs:
        copy.wait_recv()
    for copy in pairs:
        copy.wait_send()
    for gather in gathers.values():
        gather.wait_sends()
    for copy in sum(att_copies, []):
        copy.wait_send()
    for block, copy in sent:
        @pl.when(blk != block)
        def _():
            copy().wait_send()


def unfold_kernel(
    shared_ref, small_ref, histogram_ref, block_out_ref, tokens_ref, first_ref, second_ref,
    grad_qkv_ref, grad_proj_ref, attn_gain_ref, moe_gain_ref, route_ref, anchor_ref, counts_ref,
    block_out_out, tokens_out, first_out, second_out,
    in_s, qkv_s, proj_s, block_out_s, tokens_s, first_s, second_s, tokens_w, first_w, second_w,
    in_sems, qkv_sems, proj_sem, move_sems,
):
    blocks = in_s.shape[0]
    width = in_s.shape[2]
    group = width // blocks
    rdim, experts = route_ref.shape[0], anchor_ref.shape[0]
    loads = []
    for block in range(blocks):
        loads.append(pltpu.make_async_copy(
            shared_ref.at[block * width : (block + 1) * width], in_s.at[block], in_sems.at[block]))
        loads[-1].start()
    narrow = (first_s, second_s, tokens_s, block_out_s)
    wide = (first_w, second_w, tokens_w, block_out_s)
    sources = (first_ref, second_ref, tokens_ref, block_out_ref)
    results = (first_out, second_out, tokens_out, block_out_out)
    moves = [
        (pltpu.make_async_copy(sources[n], narrow[n], move_sems.at[0, n]),
         pltpu.make_async_copy(wide[n], results[n], move_sems.at[1, n]))
        for n in range(4)
    ]
    for load, _ in moves:
        load.start()
    route_ref[...] = small_ref[0:rdim, :]
    anchor_ref[...] = small_ref[rdim : rdim + experts, 0:rdim]
    moe_gain_ref[...] = small_ref[rdim + experts : rdim + experts + 1, :].reshape(width)
    attn_gain_ref[...] = small_ref[rdim + experts + 1 : rdim + experts + 2, :].reshape(width)
    counts = small_ref[rdim + experts + 2 : rdim + experts + 3, 0:experts].astype(jnp.int32)
    counts_ref[...] = histogram_ref[...] + counts.reshape(experts)
    stores = []
    for n, (load, store) in enumerate(moves):
        load.wait()
        if wide[n] is not narrow[n]:
            wide[n][...] = narrow[n][...].astype(F32)
        store.start()
    for first in range(0, blocks, 2):
        for block in range(first, first + 2):
            loads[block].wait()
            proj_s[block * group : (block + 1) * group, :] = (
                in_s[block, 3 * group :, :].astype(F32))
        for part in range(3):
            cut = slice(part * width + first * group, part * width + (first + 2) * group)
            qkv_s[:, cut] = jnp.concatenate(
                [
                    in_s[block, head * 192 + part * 64 : head * 192 + part * 64 + 64, :]
                    for block in range(first, first + 2)
                    for head in range(group // HEAD_DIM)
                ],
                axis=0,
            ).T.astype(F32)
            stores.append(pltpu.make_async_copy(
                qkv_s.at[:, cut], grad_qkv_ref.at[:, cut], qkv_sems.at[len(stores)]))
            stores[-1].start()
    stores.append(pltpu.make_async_copy(proj_s, grad_proj_ref, proj_sem.at[0]))
    stores[-1].start()
    for copy in stores + [store for _, store in moves]:
        copy.wait()


def unfold(shared, small, histogram, moved, rdim, experts):
    width = shared.shape[1]
    blocks = shared.shape[0] // width
    whole, outside = pl.BlockSpec(memory_space=pltpu.VMEM), pl.BlockSpec(memory_space=pl.ANY)
    shapes = [
        ((width, 3 * width), F32), ((width, width), F32), ((width,), F32), ((width,), F32),
        ((rdim, width), F32), ((experts, rdim), F32), ((experts,), jnp.int32),
    ]
    dma = pltpu.SemaphoreType.DMA
    return pl.pallas_call(
        unfold_kernel,
        out_shape=tuple(jax.ShapeDtypeStruct(*shape) for shape in shapes)
        + tuple(
            jax.ShapeDtypeStruct(array.shape, F32 if n else array.dtype)
            for n, array in enumerate(moved)),
        in_specs=[outside, whole, whole] + [outside] * len(moved),
        out_specs=tuple([outside] * 2 + [whole] * 5 + [outside] * len(moved)),
        scratch_shapes=[
            pltpu.VMEM((blocks, width, width), BF16), pltpu.VMEM((width, 3 * width), F32),
            pltpu.VMEM((width, width), F32),
        ]
        + [pltpu.VMEM(array.shape, array.dtype) for array in moved]
        + [pltpu.VMEM(array.shape, F32) for array in moved[1:]]
        + [dma((blocks,)), dma((3 * blocks // 2,)), dma((1,)), dma((2, len(moved)))],
        name="unfold",
        compiler_params=pltpu.CompilerParams(vmem_limit_bytes=VMEM_BYTES),
    )(shared, small, histogram, *moved)


def call(kernel, name, args, outs, scratch, lazy=(), lazy_out=(), in_any=(), out_any=(),
         collective=None):
    n_in, n_out = len(args), len(outs)
    shapes = tuple(jax.ShapeDtypeStruct(shape, dtype) for shape, dtype in outs)
    staged = [pltpu.VMEM(args[n].shape, args[n].dtype) for n in lazy]
    staged += [pltpu.VMEM(shapes[n].shape, shapes[n].dtype) for n in lazy_out]
    sems = [pltpu.SemaphoreType.DMA((len(staged),))] if staged else []

    def wrapped(*refs):
        ins, results = list(refs[:n_in]), list(refs[n_in : n_in + n_out])
        rest = refs[n_in + n_out : n_in + n_out + len(scratch)]
        extra = refs[n_in + n_out + len(scratch) :]
        for k, n in enumerate(lazy):
            ins[n] = Lazy(ins[n], extra[k], extra[-1].at[k])
        for k, n in enumerate(lazy_out):
            k += len(lazy)
            results[n] = LazyOut(extra[k], results[n], extra[-1].at[k])
        kernel(*ins, *results, *rest)
        for n in lazy_out:
            results[n].flush()
        for n in lazy:
            ins[n].ref()
        for n in lazy_out:
            results[n].copy.wait()

    def spec(n, outside):
        return pl.BlockSpec(memory_space=pl.ANY if n in outside else pltpu.VMEM)

    return pl.pallas_call(
        wrapped,
        out_shape=shapes,
        in_specs=[spec(n, tuple(lazy) + tuple(in_any)) for n in range(n_in)],
        out_specs=tuple(spec(n, tuple(lazy_out) + tuple(out_any)) for n in range(n_out)),
        scratch_shapes=list(scratch) + staged + sems,
        name=name,
        compiler_params=pltpu.CompilerParams(
            vmem_limit_bytes=VMEM_BYTES,
            collective_id=collective,
            has_side_effects=collective is not None,
        ),
    )(*args)


def fast_body(
    tokens, cotangent, loss_mask, routes, priority, histogram, qkv_weight, proj_weight, attn_gain,
    moe_gain, route_weight, anchor_table, first_weight, second_weight,
):
    tok, width = tokens.shape[1:]
    blocks, experts = lax.axis_size("blk"), lax.axis_size("expert")
    length = tok * blocks
    heads = HEADS // blocks
    group = heads * HEAD_DIM
    hidden = first_weight.shape[2]
    x, cot = tokens[0], cotangent[0]
    gains = [attn_gain, moe_gain]
    rows = [routes.reshape(1, tok), priority.reshape(1, tok), loss_mask.reshape(1, tok)]
    dma = pltpu.SemaphoreType.DMA
    (nall, qkv, out, lse, cols, result, residual, gate, grad_residual, grad_att, grad_proj, small,
     buf, cots, gates) = call(
        forward_kernel, "forward",
        (x, *gains, *rows, qkv_weight, cot, proj_weight, route_weight.T, anchor_table, first_weight[0],
         second_weight[0]),
        [((length, width), BF16), ((3 * group, length), BF16), ((group, length), F32),
         ((8, length), F32), ((tok, 128), F32),
         ((tok, width), BF16), ((tok, width), F32), ((tok, 128), F32), ((tok, width), F32),
         ((width, tok), BF16), ((width, width), BF16), ((32, width), F32),
         ((length, width), BF16), ((length, width), BF16), ((blocks * 64, 128), F32)],
        [pltpu.VMEM((3, width, 256), BF16), pltpu.VMEM((3 * group, width), BF16),
         pltpu.VMEM((heads, length, HEAD_DIM), BF16), pltpu.VMEM((group, length), BF16),
         pltpu.VMEM((tok, width), BF16), pltpu.VMEM((width, tok), BF16),
         pltpu.VMEM((tok, width), BF16),
         pltpu.VMEM((width, hidden), BF16), pltpu.VMEM((hidden, width), BF16),
         pltpu.VMEM((tok // 2, hidden), F32),
         pltpu.VMEM((tok, width), BF16), pltpu.VMEM((64, 128), F32),
         pltpu.VMEM((tok, width), BF16), pltpu.VMEM((64, 128), F32), pltpu.VMEM((tok, width), BF16),
         pltpu.VMEM((tok, width), BF16), pltpu.VMEM((64, 128), F32), pltpu.VMEM((64, 128), F32),
         pltpu.VMEM((tok // 2, width), F32), pltpu.VMEM((tok // 2, width), F32),
         pltpu.VMEM((tok // 2, width), BF16),
         dma((9,)), dma((2, 6)), dma((2, experts)), dma((2, blocks * heads)), dma((2, experts)),
         dma((2, experts)), dma((2, experts)), dma((2, experts)), dma((2, 12)), dma((2, 18)),
         dma((2, 3))],
        lazy=(7, 8), lazy_out=(0, 1, 2, 4, 5, 6, 7, 8, 9, 10), in_any=(6, 11, 12), out_any=(12, 13),
        collective=1,
    )
    half, piece, quarter = width // 2, group // 4, hidden // blocks
    block_out, grad_tokens, shared, small, grad_first, grad_second = call(
        attend_back_kernel, "attend_back",
        (grad_att, qkv, out, lse, nall, result, residual, gate, cols, attn_gain, qkv_weight, x,
         grad_residual, grad_proj, small, buf, cots, gates, first_weight[0], second_weight[0]),
        [((tok, width), BF16), ((tok, width), BF16), ((blocks * width, width), BF16),
         ((32, width), F32), ((width, quarter), BF16), ((quarter, width), BF16)],
        [pltpu.VMEM((group, length), BF16), pltpu.VMEM((HEAD_DIM, length), F32),
         pltpu.VMEM((3 * group, length), BF16), pltpu.VMEM((3 * width, tok), BF16)]
        + [pltpu.VMEM((tok, width), BF16), pltpu.VMEM((3 * group, width), BF16),
           pltpu.VMEM((3, group, width), BF16),
           pltpu.VMEM((width, width), F32), pltpu.VMEM((width, half), F32),
           pltpu.VMEM((width, half), BF16), pltpu.VMEM((width, half), BF16),
           pltpu.VMEM((width, half), BF16), pltpu.VMEM((12, piece, half), BF16),
           pltpu.VMEM((32, half), F32), pltpu.VMEM((9, 32, half), F32), pltpu.VMEM((32, half), F32),
           pltpu.VMEM((3, 8, 128), F32), pltpu.VMEM((9, 8, 128), F32),
           pltpu.VMEM((width, quarter), BF16), pltpu.VMEM((quarter, width), BF16),
           pltpu.VMEM((2, 2, tok, width), BF16), pltpu.VMEM((tok, width), F32),
           pltpu.VMEM((4, piece, half), BF16), pltpu.VMEM((width, quarter), F32),
           pltpu.VMEM((quarter, width), F32),
           dma((2, 9)), dma((2, experts)), dma((2, 36)), dma((2, 3)), dma((2, 4)), dma((2, 12)),
           dma((2, 12)), dma((2, 8)), dma((2, 7)), dma((2, 24)), dma((2, 16)), dma((13,))],
        lazy=(1, 2, 4, 7, 8, 10, 11, 13), lazy_out=(0, 1, 4, 5),
        in_any=(0, 5, 6, 12, 15, 16, 18, 19), out_any=(2,), collective=3,
    )
    (grad_qkv, grad_proj, grad_attn_gain, grad_moe_gain, grad_route, grad_anchor, counts,
     block_out, grad_tokens, grad_first, grad_second) = unfold(
        shared, small, histogram, (block_out, grad_tokens, grad_first, grad_second),
        route_weight.shape[1], experts)
    return (
        block_out[None],
        grad_tokens[None],
        grad_qkv,
        grad_proj,
        grad_attn_gain,
        grad_moe_gain,
        grad_route.T,
        grad_anchor,
        grad_first[None],
        grad_second[None],
        counts,
    )


def solution(mesh):
    in_specs = (
        P("expert", "blk", None),
        P("expert", "blk", None),
        P("expert", "blk"),
        P("expert", "blk", None),
        P("expert", "blk", None),
        P(),
        P(),
        P(),
        P(),
        P(),
        P(),
        P(),
        P("expert", None, None),
        P("expert", None, None),
    )
    out_specs = (
        P("expert", "blk", None),
        P("expert", "blk", None),
        P(),
        P(),
        P(),
        P(),
        P(),
        P(),
        P("expert", None, "blk"),
        P("expert", "blk", None),
        P(),
    )
    blocks, experts = mesh.shape["blk"], mesh.shape["expert"]
    body = fast_body if (blocks, experts) == (4, 8) else general_body
    return jax.shard_map(body, mesh=mesh, in_specs=in_specs, out_specs=out_specs, check_vma=False)
```

```python
import functools

import jax
import jax.numpy as jnp
from jax import lax
from jax.experimental import pallas as pl
from jax.experimental.pallas import tpu as pltpu
from jax.sharding import PartitionSpec as P

HEADS = 12
HEAD_DIM = 64


TOP_PRECISION = lax.Precision.HIGHEST
EPSILON = 1e-05
ROUTER_SOFTNESS = 0.4
MASKED = -1e30


def layer_norm(values, norm_gain):
    average = jnp.mean(values, axis=-1, keepdims=True)
    centered = values - average
    variance = jnp.mean(centered * centered, axis=-1, keepdims=True)
    return centered * lax.rsqrt(variance + EPSILON) * norm_gain


def unit_rows(matrix):
    return matrix * lax.rsqrt(1.0 + jnp.sum(matrix * matrix, axis=-1, keepdims=True))


def router_gate(normalized_rows, route_matrix, anchors, route_onehot):
    projection_output = unit_rows(jnp.dot(normalized_rows, route_matrix, precision=TOP_PRECISION))
    expert_anchor_rows = unit_rows(anchors)
    route_logit_scores = (
        jnp.dot(projection_output, expert_anchor_rows.T, precision=TOP_PRECISION) / ROUTER_SOFTNESS
    )
    return jnp.sum(jax.nn.softmax(route_logit_scores, axis=-1) * route_onehot, axis=-1)


def masked_scores(queries, key_rows, query_first, key_first, score_scale):
    scores = (
        jnp.einsum("qhd,khd->hqk", queries, key_rows, preferred_element_type=jnp.float32)
        * score_scale
    )
    grid_shape = (queries.shape[0], key_rows.shape[0])
    query_place = query_first + lax.broadcasted_iota(jnp.int32, grid_shape, 0)
    key_place = key_first + lax.broadcasted_iota(jnp.int32, grid_shape, 1)
    return (scores, (key_place <= query_place)[None])


def over_blocks(step_fn, carried, arrays, block_rows):
    row_total = arrays[0].shape[0]
    block_count = row_total // block_rows
    stacked = tuple(
        (member.reshape((block_count, block_rows) + member.shape[1:]) for member in arrays)
    )

    def scan_step(running, packed):
        position, blocks = packed
        return (step_fn(running, blocks, position * block_rows), None)

    result, unused = lax.scan(
        scan_step, carried, (jnp.arange(block_count, dtype=jnp.int32), stacked)
    )
    return result


def general_body(
    tokens,
    cotangent,
    loss_mask,
    routes,
    priority,
    histogram,
    qkv_weight,
    proj_weight,
    attn_gain,
    moe_gain,
    route_weight,
    anchor_table,
    first_weight,
    second_weight,
):
    tok_rows = tokens.shape[1]
    model_width = tokens.shape[2]
    score_scale = HEAD_DIM ** (-0.5)
    query_first = lax.axis_index("blk") * tok_rows
    local_experts = first_weight.shape[0]
    experts_all = local_experts * lax.axis_size("expert")
    capacity = tok_rows // experts_all
    head_shape = (tok_rows, HEADS, HEAD_DIM)
    seq_rows = tok_rows * lax.axis_size("blk")
    route_ids = routes[0, :, 0]
    route_onehot = (
        route_ids[:, None] == lax.broadcasted_iota(jnp.int32, (tok_rows, experts_all), 1)
    ).astype(jnp.float32)
    count_rows = jnp.sum(route_onehot, axis=0)
    total_counts = lax.psum(count_rows.astype(jnp.int32), ("blk", "expert"))
    block_input = tokens[0].astype(jnp.float32)
    normed_attn, attn_norm_back = jax.vjp(layer_norm, block_input, attn_gain)
    normed_low = normed_attn.astype(jnp.bfloat16)
    query_key_value_mix = jnp.dot(
        normed_low, qkv_weight, preferred_element_type=jnp.float32
    ).astype(jnp.bfloat16)
    query_flat = query_key_value_mix[:, :model_width]
    queries = query_flat.reshape(head_shape)
    key_local = query_key_value_mix[:, model_width : 2 * model_width]
    value_local = query_key_value_mix[:, 2 * model_width :]

    def forward_step(carried, blocks, key_first):
        running_top, running_sum, running_out = carried
        key_rows = blocks[0].reshape(blocks[0].shape[0], HEADS, HEAD_DIM)
        value_rows = blocks[1].reshape(blocks[1].shape[0], HEADS, HEAD_DIM)
        scores, allowed = masked_scores(queries, key_rows, query_first, key_first, score_scale)
        top_new = jnp.maximum(running_top, jnp.max(jnp.where(allowed, scores, MASKED), axis=2))
        weights = jnp.where(allowed, jnp.exp(scores - top_new[:, :, None]), 0.0)
        factor = jnp.exp(running_top - top_new)
        running_sum = running_sum * factor + jnp.sum(weights, axis=2)
        running_out = running_out * factor.T[:, :, None] + jnp.einsum(
            "hqk,khd->qhd",
            weights.astype(jnp.bfloat16),
            value_rows,
            preferred_element_type=jnp.float32,
        )
        return (top_new, running_sum, running_out)

    initial = (
        jnp.full((HEADS, tok_rows), MASKED, jnp.float32),
        jnp.zeros((HEADS, tok_rows), jnp.float32),
        jnp.zeros(head_shape, jnp.float32),
    )
    running_top, running_sum, running_out = over_blocks(
        forward_step,
        initial,
        (
            lax.all_gather(key_local, "blk", axis=0, tiled=True),
            lax.all_gather(value_local, "blk", axis=0, tiled=True),
        ),
        tok_rows,
    )
    attention_result = running_out / running_sum.T[:, :, None]
    log_total = running_top + jnp.log(running_sum)
    attended_low = attention_result.reshape(tok_rows, model_width).astype(jnp.bfloat16)
    residual_stream = block_input + jnp.dot(
        attended_low, proj_weight, preferred_element_type=jnp.float32
    )
    normed_moe, moe_norm_back = jax.vjp(layer_norm, residual_stream, moe_gain)

    def gate_of(normalized_rows, route_matrix, anchors):
        return router_gate(normalized_rows, route_matrix, anchors, route_onehot)

    gate_value, gate_back = jax.vjp(gate_of, normed_moe, route_weight, anchor_table)
    order_rows = priority[0, 0]
    same_route = route_ids[:, None] == route_ids[None, :]
    earlier = order_rows[None, :] < order_rows[:, None]
    slot_ids = jnp.sum((same_route & earlier).astype(jnp.int32), axis=1)
    target = jnp.where(slot_ids < capacity, route_ids * capacity + slot_ids, -1)
    selector = lax.broadcasted_iota(jnp.int32, (tok_rows, tok_rows), 0) == target[None, :]
    selector_low = selector.astype(jnp.bfloat16)
    outgoing = jnp.dot(
        selector_low, normed_moe.astype(jnp.bfloat16), preferred_element_type=jnp.float32
    )
    outgoing = outgoing.astype(jnp.bfloat16).reshape(experts_all, capacity, model_width)
    arrived = lax.all_to_all(outgoing, "expert", split_axis=0, concat_axis=0, tiled=True)
    sources = arrived.shape[0] // local_experts
    grouped = arrived.reshape(sources, local_experts, arrived.shape[1], arrived.shape[2])
    hidden = jnp.einsum("secd,edf->secf", grouped, first_weight, preferred_element_type=jnp.float32)
    act_low = jax.nn.gelu(hidden).astype(jnp.bfloat16)
    result = jnp.einsum(
        "secf,efd->secd", act_low, second_weight, preferred_element_type=jnp.float32
    )
    result = result.astype(jnp.bfloat16).reshape(arrived.shape)
    returned = lax.all_to_all(result, "expert", split_axis=0, concat_axis=0, tiled=True)
    returned, arrived = (returned, arrived)
    fetched = jnp.einsum(
        "st,sd->td",
        selector_low,
        returned.reshape(tok_rows, model_width),
        preferred_element_type=jnp.float32,
    )
    block_out = (residual_stream + gate_value[:, None] * fetched).astype(jnp.bfloat16)[None]
    grad_out = cotangent[0].astype(jnp.float32) * loss_mask[0].astype(jnp.float32)[:, None]
    grad_fetched = grad_out * gate_value[:, None]
    grad_gate = jnp.sum(grad_out * fetched, axis=1)
    grad_slots = jnp.dot(selector.astype(jnp.float32), grad_fetched, precision=TOP_PRECISION)
    grad_slots = grad_slots.astype(jnp.bfloat16).reshape(experts_all, capacity, model_width)
    grad_arrived = lax.all_to_all(grad_slots, "expert", split_axis=0, concat_axis=0, tiled=True)
    sources = grad_arrived.shape[0] // local_experts
    slot_shape = (sources, local_experts, capacity, model_width)
    grouped_in = arrived.reshape(slot_shape)
    grouped_grad = grad_arrived.reshape(slot_shape)
    hidden = jnp.einsum(
        "secd,edf->secf", grouped_in, first_weight, preferred_element_type=jnp.float32
    )
    act_low = jax.nn.gelu(hidden).astype(jnp.bfloat16)
    grad_second = jnp.einsum(
        "secf,secd->efd", act_low, grouped_grad, preferred_element_type=jnp.float32
    )
    grad_act = jnp.einsum(
        "secd,efd->secf", grouped_grad, second_weight, preferred_element_type=jnp.float32
    )
    unused, gelu_back = jax.vjp(jax.nn.gelu, hidden)
    grad_hidden = gelu_back(grad_act)[0].astype(jnp.bfloat16)
    grad_first = jnp.einsum(
        "secd,secf->edf", grouped_in, grad_hidden, preferred_element_type=jnp.float32
    )
    grad_sent = jnp.einsum(
        "secf,edf->secd", grad_hidden, first_weight, preferred_element_type=jnp.float32
    )
    grad_sent = grad_sent.astype(jnp.bfloat16).reshape(grad_arrived.shape)
    grad_returned = lax.all_to_all(grad_sent, "expert", split_axis=0, concat_axis=0, tiled=True)
    grad_first, grad_second = (
        lax.psum_scatter(
            grad_first.astype(jnp.bfloat16), "blk", scatter_dimension=2, tiled=True
        ).astype(jnp.float32),
        lax.psum_scatter(
            grad_second.astype(jnp.bfloat16), "blk", scatter_dimension=1, tiled=True
        ).astype(jnp.float32),
    )
    grad_moe_rows = jnp.einsum(
        "st,sd->td",
        selector_low,
        grad_returned.reshape(tok_rows, model_width),
        preferred_element_type=jnp.float32,
    )
    grad_router_rows, grad_route, grad_anchor = gate_back(grad_gate)
    grad_residual_norm, grad_moe_gain = moe_norm_back(grad_moe_rows + grad_router_rows)
    grad_residual = grad_out + grad_residual_norm
    grad_attn_low = grad_residual.astype(jnp.bfloat16)
    grad_proj = jnp.dot(attended_low.T, grad_attn_low, preferred_element_type=jnp.float32)
    grad_attended_flat = jnp.dot(
        grad_attn_low, proj_weight.T, preferred_element_type=jnp.float32
    ).astype(jnp.bfloat16)
    grad_attended = grad_attended_flat.reshape(head_shape)
    delta_rows = jnp.sum(grad_attended.astype(jnp.float32) * attention_result, axis=2).T
    key_all, value_all = (
        lax.all_gather(key_local, "blk", axis=0, tiled=True),
        lax.all_gather(value_local, "blk", axis=0, tiled=True),
    )
    block_count = seq_rows // tok_rows
    key_blocks = key_all.reshape(block_count, tok_rows, model_width)
    value_blocks = value_all.reshape(block_count, tok_rows, model_width)

    def key_block_step(running_grad, packed):
        position, key_block, value_block = packed
        key_rows = key_block.reshape(head_shape)
        value_rows = value_block.reshape(head_shape)
        scores, allowed = masked_scores(
            queries, key_rows, query_first, position * tok_rows, score_scale
        )
        soft_rows = jnp.where(allowed, jnp.exp(scores - log_total[:, :, None]), 0.0)
        grad_values = jnp.einsum(
            "hqk,qhd->khd",
            soft_rows.astype(jnp.bfloat16),
            grad_attended,
            preferred_element_type=jnp.float32,
        )
        grad_soft = jnp.einsum(
            "qhd,khd->hqk", grad_attended, value_rows, preferred_element_type=jnp.float32
        )
        grad_scores = (soft_rows * (grad_soft - delta_rows[:, :, None])).astype(jnp.bfloat16)
        grad_keys = score_scale * jnp.einsum(
            "hqk,qhd->khd", grad_scores, queries, preferred_element_type=jnp.float32
        )
        running_grad = running_grad + score_scale * jnp.einsum(
            "hqk,khd->qhd", grad_scores, key_rows, preferred_element_type=jnp.float32
        )
        term = jnp.concatenate(
            [grad_keys.reshape(tok_rows, model_width), grad_values.reshape(tok_rows, model_width)],
            axis=1,
        )
        return (running_grad, term)

    grad_queries, stacked_terms = lax.scan(
        key_block_step,
        jnp.zeros(head_shape, jnp.float32),
        (jnp.arange(block_count, dtype=jnp.int32), key_blocks, value_blocks),
    )
    all_terms = stacked_terms.reshape(seq_rows, 2 * model_width)
    key_value_grads = lax.psum_scatter(
        all_terms.astype(jnp.bfloat16), "blk", scatter_dimension=0, tiled=True
    ).astype(jnp.float32)
    grad_query_rows = grad_queries.reshape(tok_rows, model_width)
    grad_qkv_rows = jnp.concatenate([grad_query_rows, key_value_grads], axis=1).astype(jnp.bfloat16)
    grad_qkv = jnp.dot(normed_low.T, grad_qkv_rows, preferred_element_type=jnp.float32)
    grad_normed = jnp.dot(grad_qkv_rows, qkv_weight.T, preferred_element_type=jnp.float32)
    grad_source_norm, grad_attn_gain = attn_norm_back(grad_normed)
    grad_tokens = (grad_residual + grad_source_norm)[None]
    grad_qkv, grad_proj, grad_attn_gain, grad_moe_gain, grad_route, grad_anchor = lax.psum(
        (grad_qkv, grad_proj, grad_attn_gain, grad_moe_gain, grad_route, grad_anchor),
        ("blk", "expert"),
    )
    histogram_out = histogram + total_counts
    return (
        block_out,
        grad_tokens,
        grad_qkv,
        grad_proj,
        grad_attn_gain,
        grad_moe_gain,
        grad_route,
        grad_anchor,
        grad_first,
        grad_second,
        histogram_out,
    )


MESH = pl.DeviceIdType.MESH
F32 = jnp.float32
BF16 = jnp.bfloat16
VMEM_BYTES = 58 * 1024 * 1024


def dot(left, right, precision=None):
    return lax.dot_general(
        left, right, (((1,), (0,)), ((), ())), precision=precision, preferred_element_type=F32
    )


def dot_nt(left, right, precision=None):
    return lax.dot_general(
        left, right, (((1,), (1,)), ((), ())), precision=precision, preferred_element_type=F32
    )


def dot_tn(left, right, precision=None):
    return lax.dot_general(
        left, right, (((0,), (0,)), ((), ())), precision=precision, preferred_element_type=F32
    )


def split(values):
    high = values.astype(BF16)
    return high, (values - high.astype(F32)).astype(BF16)


def fine(product, left, right):
    left_high, left_low = split(left)
    right_high, right_low = split(right)
    return product(left_high, right_high) + (
        product(left_high, right_low) + product(left_low, right_high)
    )


def rows_at(index, size):
    return pl.ds(pl.multiple_of(index * size, size), size)


def places():
    blk = lax.axis_index("blk")
    expert = lax.axis_index("expert")
    return blk, expert, blk + 1 - 2 * lax.rem(blk, 2), lax.rem(blk + 2, 4), 3 - blk


def greet(peers):
    barrier = pltpu.get_barrier_semaphore()
    for peer in peers:
        pl.semaphore_signal(barrier, inc=1, device_id=peer, device_id_type=MESH)
    return lambda: pl.semaphore_wait(barrier, len(peers))


def push(src, dst, sems, index, peer):
    copy = pltpu.make_async_remote_copy(
        src_ref=src,
        dst_ref=dst,
        send_sem=sems.at[0, index],
        recv_sem=sems.at[1, index],
        device_id=peer,
        device_id_type=MESH,
    )
    copy.start()
    return copy


def standardise(values):
    average = jnp.mean(values, axis=-1, keepdims=True)
    centered = values - average
    scale = lax.rsqrt(jnp.mean(centered * centered, axis=-1, keepdims=True) + EPSILON)
    return centered * scale, scale


def lower_triangle(keys, queries):
    return lax.broadcasted_iota(jnp.int32, (keys, queries), 0) <= lax.broadcasted_iota(
        jnp.int32, (keys, queries), 1
    )


class BlockGather:
    def __init__(self, part, sems, base, own=None):
        self.part, self.sems, self.base, self.own = part, sems, base, own

    def send(self, blk, half, index, peer):
        ref = self.part(blk, half)
        src = ref if self.own is None or index > 3 else self.own(half)
        return push(src, ref, self.sems, self.base + index, peer)

    def start(self):
        self.start_first()
        self.start_second()

    def start_first(self):
        blk, expert, bx, by, bd = places()
        self.copies = [self.send(blk, 0, 0, (bx, expert)), self.send(blk, 1, 1, (by, expert))]

    def start_second(self):
        blk, expert, bx, by, bd = places()
        self.copies += [self.send(blk, 1, 2, (bx, expert)), self.send(blk, 0, 3, (by, expert))]

    def forward(self):
        blk, expert, bx, by, bd = places()
        self.copies[0].wait_recv()
        self.copies.append(self.send(bx, 0, 4, (by, expert)))
        self.copies[1].wait_recv()
        self.copies.append(self.send(by, 1, 5, (bx, expert)))

    def wait_neighbours(self):
        self.copies[2].wait_recv()
        self.copies[3].wait_recv()

    def wait_diagonal(self):
        self.copies[4].wait_recv()
        self.copies[5].wait_recv()

    def wait_sends(self):
        for copy in self.copies:
            copy.wait_send()


def row_halves(buf, rows):
    size = rows // 2
    return lambda blk, half: buf.at[pl.ds(pl.multiple_of(blk * rows + half * size, size), size)]


def expert_groups():
    expert = lax.axis_index("expert")
    line, core = expert // 2, lax.rem(expert, 2)
    side, place = line // 2, lax.rem(line, 2)
    beside = (side * 2 + 1 - place) * 2
    first = ((1 - side) * 2 + place) * 2
    second = ((1 - side) * 2 + 1 - place) * 2
    return [
        (side * 4, 4, [expert + 1 - 2 * core, beside + core, beside + 1 - core]),
        (first, 2, [first + core, first + 1 - core]),
        (second, 2, [second + core, second + 1 - core]),
    ]


class ExpertExchange:
    def __init__(self, src, dst, sems, rows):
        self.src, self.dst, self.sems, self.rows = src, dst, sems, rows
        self.groups = expert_groups()
        self.copies = [[], [], []]

    def start(self, group, keep=True):
        blk, expert = lax.axis_index("blk"), lax.axis_index("expert")
        place = rows_at(expert, self.rows)
        base = (0, 3, 5)[group]
        for n, peer in enumerate(self.groups[group][2]):
            self.copies[group].append(
                push(self.src.at[rows_at(peer, self.rows)], self.dst.at[place], self.sems,
                     base + n, (blk, peer))
            )
        if group == 0 and keep:
            self.dst[place] = self.src[place]

    def wait_recv(self, group):
        for copy in self.copies[group]:
            copy.wait_recv()

    def wait_sends(self):
        for copy in sum(self.copies, []):
            copy.wait_send()

    def start_all(self, keep=True):
        self.start(1)
        self.start(2)
        self.start(0, keep)

    def wait_all(self):
        for group in range(3):
            self.wait_recv(group)
        self.wait_sends()


class Lazy:
    def __init__(self, src, dst, sem):
        self.dst, self.shape, self.fresh = dst, dst.shape, True
        self.copy = pltpu.make_async_copy(src, dst, sem)
        self.copy.start()

    def ref(self):
        if self.fresh:
            self.copy.wait()
            self.fresh = False
        return self.dst

    def __getitem__(self, where):
        return self.ref()[where]

    @property
    def at(self):
        return self.ref().at


class LazyOut:
    def __init__(self, src, dst, sem):
        self.src, self.dst, self.sem, self.shape, self.copy = src, dst, sem, src.shape, None

    def flush(self):
        if self.copy is None:
            self.copy = pltpu.make_async_copy(self.src, self.dst, self.sem)
            self.copy.start()

    def __getitem__(self, where):
        return self.src[where]

    def __setitem__(self, where, value):
        self.src[where] = value

    @property
    def at(self):
        return self.src.at


def blk_peers():
    blk, expert, bx, by, bd = places()
    return [(bx, expert), (by, expert), (bd, expert)]


def expert_peers():
    blk, expert = lax.axis_index("blk"), lax.axis_index("expert")
    n = lax.axis_size("expert")
    return [(blk, lax.rem(expert + shift, n)) for shift in range(1, n)]


def forward_kernel(
    tok_ref, attn_gain_ref, moe_gain_ref, routes_ref, priority_ref, mask_ref, wqkv_ref, cot_ref, proj_ref, route_ref, anchor_ref, first_ref, second_ref,
    nall_ref, qkv_ref, out_ref, lse_ref, cols_ref, result_ref, residual_ref, gate_ref,
    grad_residual_ref, grad_att_ref, grad_proj_ref, small_ref, buf_ref, cots_ref, gates_ref,
    w_s, wt_s, k_s, att_s, cot_s, att_ref, cot_in_ref,
    first_s, second_s, slope_s, buf_s, gates_s, go_s, gate_s, grad_s, back_s, score_s, score_in_s,
    res_acc, sent_acc, grad_in_s,
    w_sem, gather_sems, cot_sems, att_sems, go_sems, gate_sems, back_sems, score_sems, cots_sems,
    buf_sems, gates_sems,
):
    blk, expert, bx, by, bd = places()
    tok = tok_ref.shape[0]
    width = tok_ref.shape[1]
    heads = HEADS // 4
    group = heads * HEAD_DIM
    arrived = greet(blk_peers() + expert_peers())
    odd = lax.rem(blk, 2)
    loads = []
    for part in range(3):
        first = pl.multiple_of(part * width + blk * group - odd * 64, 128)
        loads.append(
            pltpu.make_async_copy(wqkv_ref.at[:, pl.ds(first, 256)], w_s.at[part], w_sem.at[part])
        )
        loads[-1].start()
    weights = [
        pltpu.make_async_copy(first_ref, first_s, w_sem.at[3]),
        pltpu.make_async_copy(second_ref, second_s, w_sem.at[4]),
    ]
    for load in weights:
        load.start()
    xhat, _ = standardise(tok_ref[...].astype(F32))
    nall_ref[rows_at(blk, tok), :] = (xhat * attn_gain_ref[...].reshape(1, width)).astype(BF16)
    arrived()
    gather = BlockGather(row_halves(nall_ref, tok), gather_sems, 0)
    gather.start()

    capacity = tok // 8
    route_row, prio_row, mask_row = (
        ref[...].astype(F32) for ref in (routes_ref, priority_ref, mask_ref))
    cols = jnp.concatenate(
        [jnp.zeros((1, tok), F32), route_row, prio_row, mask_row, jnp.zeros((124, tok), F32)],
        axis=0).T
    route_col, prio_col = cols[:, 1:2], cols[:, 2:3]
    same = route_col == route_row
    slot_row = jnp.sum(jnp.where(same & (prio_col < prio_row), 1.0, 0.0), axis=0, keepdims=True)
    slot_col = jnp.sum(jnp.where(same & (prio_row < prio_col), 1.0, 0.0), axis=1, keepdims=True)
    target_row = jnp.where(slot_row < capacity, route_row * capacity + slot_row, -1.0)
    target_col = jnp.where(slot_col < capacity, route_col * capacity + slot_col, -1.0)
    lane = lax.broadcasted_iota(jnp.int32, cols.shape, 1)
    cols_ref[...] = jnp.where(lane == 0, target_col, cols)
    cols_ref.flush()
    slots = lax.broadcasted_iota(jnp.int32, (tok, tok), 0).astype(F32)
    chosen = jnp.where((slots == target_row) & (mask_row > 0.0), 1.0, 0.0).astype(BF16)
    cot_s[...] = dot(chosen, cot_ref[...]).astype(BF16)
    cot_move = ExpertExchange(cot_s, cot_in_ref, cot_sems, capacity)
    cot_move.start_all()

    for part in range(3):
        loads[part].wait()
        wide = w_s[part]
        narrow = jnp.where(odd == 1, wide[:, 64:256], wide[:, 0:192])
        wt_s[part * group : (part + 1) * group, :] = narrow.T

    def project(where):
        cols = rows_at(where, tok)
        mixed = dot_nt(wt_s[...], nall_ref[cols, :]).astype(BF16)
        qkv_ref[0:group, cols] = mixed[0:group] * BF16(HEAD_DIM**-0.5)
        qkv_ref[group:, cols] = mixed[group:]
        for head in range(heads):
            k_s[head, cols, :] = mixed[group + head * 64 : group + (head + 1) * 64].T

    project(blk)
    gather.forward()
    gather.wait_neighbours()
    project(bx)
    project(by)
    gather.wait_diagonal()
    nall_ref.flush()
    cot_move.wait_all()
    here = rows_at(blk, tok)
    cots_own = pltpu.make_async_copy(cot_in_ref, cots_ref.at[here], w_sem.at[5])
    cots_own.start()
    quarter = tok // 4
    cots = []
    for part in range(2):

        def own(half, part=part):
            return cot_in_ref.at[pl.ds((2 * part + half) * quarter, quarter)]

        def halves(block, half, part=part):
            row = pl.multiple_of(block * tok + (2 * part + half) * quarter, quarter)
            return cots_ref.at[pl.ds(row, quarter)]

        cots.append(BlockGather(halves, cots_sems, 6 * part, own))
    project(bd)
    cots[0].start_first()
    cots[1].start_first()
    qkv_ref.flush()

    half = tok // 2

    def scores(i, head):
        q = qkv_ref[head * 64 : (head + 1) * 64, i * tok : (i + 1) * tok]
        upper = dot(k_s[head, i * tok : i * tok + half, :], q)
        upper = jnp.where(lower_triangle(half, tok), upper, MASKED)
        lower = dot(k_s[head, i * tok + half : (i + 1) * tok, :], q[:, half:])
        lower = jnp.where(lower_triangle(half, half), lower, MASKED)
        top = jnp.max(upper, axis=0, keepdims=True)
        low_top = jnp.max(lower, axis=0, keepdims=True)
        top = jnp.concatenate([top[:, :half], jnp.maximum(top[:, half:], low_top)], axis=1)
        if i == 0:
            return top, upper, lower, None
        past = dot(k_s[head, 0 : i * tok, :], q)
        return jnp.maximum(top, jnp.max(past, axis=0, keepdims=True)), upper, lower, past

    sends = []

    def finish(i, head, found):
        top, upper, lower, past = found
        v = qkv_ref[2 * group + head * 64 : 2 * group + (head + 1) * 64, :]
        upper = jnp.exp(upper - top)
        lower = jnp.exp(lower - top[:, half:])
        total = jnp.sum(upper, axis=0, keepdims=True)
        low_total = jnp.sum(lower, axis=0, keepdims=True)
        total = jnp.concatenate([total[:, :half], total[:, half:] + low_total], axis=1)
        result = dot(v[:, i * tok : i * tok + half], upper.astype(BF16))
        low_result = dot(v[:, i * tok + half : (i + 1) * tok], lower.astype(BF16))
        result = jnp.concatenate([result[:, :half], result[:, half:] + low_result], axis=1)
        if i:
            past = jnp.exp(past - top)
            total = total + jnp.sum(past, axis=0, keepdims=True)
            result = result + dot(v[:, 0 : i * tok], past.astype(BF16))
        result = result / total
        place = slice(head * 64, (head + 1) * 64)
        out_ref[place, i * tok : (i + 1) * tok] = result
        lse_ref[head : head + 1, i * tok : (i + 1) * tok] = top + jnp.log(total)
        att_s[place, i * tok : (i + 1) * tok] = result.astype(BF16)
        there = pl.ds(pl.multiple_of(blk * group + head * 64, 64), 64)

        def copy():
            return pltpu.make_async_remote_copy(
                src_ref=att_s.at[place, i * tok : (i + 1) * tok],
                dst_ref=att_ref.at[there],
                send_sem=att_sems.at[0, i * heads + head],
                recv_sem=att_sems.at[1, blk * heads + head],
                device_id=(i, expert),
                device_id_type=MESH,
            )

        @pl.when(blk != i)
        def _():
            copy().start()

        @pl.when(blk == i)
        def _():
            att_ref[there, :] = result.astype(BF16)

        sends.append((i, copy))

    before = None
    for i in range(4):
        for head in range(heads):
            found = scores(i, head)
            if before is not None:
                finish(*before)
            before = (i, head, found)
    finish(*before)

    for i, copy in sends:
        @pl.when(blk != i)
        def _():
            copy().wait_send()

    for source in range(4):
        @pl.when(blk != source)
        def _():
            for head in range(heads):
                there = pl.ds(source * group + head * 64, 64)
                pltpu.make_async_remote_copy(
                    src_ref=att_s.at[0:64, 0:tok],
                    dst_ref=att_ref.at[there],
                    send_sem=att_sems.at[0, source * heads + head],
                    recv_sem=att_sems.at[1, source * heads + head],
                    device_id=(source, expert),
                    device_id_type=MESH,
                ).wait_recv()

    cots[0].forward()
    cots[1].forward()
    cots[0].start_second()
    out_ref.flush()
    gather.wait_sends()

    gain = moe_gain_ref[...].reshape(1, width)
    experts = 8
    residual = tok_ref[...].astype(F32) + dot_tn(att_ref[...], proj_ref[...])
    residual_ref[...] = residual
    residual_ref.flush()
    xhat, scale = standardise(residual)
    normed = xhat * gain
    normed_low = normed.astype(BF16)
    go_s[...] = dot(jnp.where(slots == target_row, 1.0, 0.0).astype(BF16), normed_low).astype(BF16)
    go = ExpertExchange(go_s, buf_s, go_sems, capacity)
    go.start(0)
    cots[1].start_second()

    projected = fine(dot_nt, normed, route_ref[...])
    unit_scale = lax.rsqrt(1.0 + jnp.sum(projected * projected, axis=1, keepdims=True))
    unit = projected * unit_scale
    anchor = anchor_ref[...]
    anchor_scale = lax.rsqrt(1.0 + jnp.sum(anchor * anchor, axis=1, keepdims=True))
    anchor_unit = anchor * anchor_scale
    logits = fine(dot_nt, unit, anchor_unit) / ROUTER_SOFTNESS
    soft = jnp.exp(logits - jnp.max(logits, axis=1, keepdims=True))
    soft = soft / jnp.sum(soft, axis=1, keepdims=True)
    onehot = jnp.where(
        lax.broadcasted_iota(jnp.int32, (tok, experts), 1).astype(F32) == route_col, 1.0, 0.0
    )
    gate = jnp.sum(soft * onehot, axis=1, keepdims=True)
    gate_ref[...] = jnp.broadcast_to(gate, gate_ref.shape)
    gate_ref.flush()
    lane = lax.broadcasted_iota(jnp.int32, (tok, 128), 1).astype(F32)
    lane = jnp.where(lane < capacity, lane, 1e6)
    for peer in range(experts):
        row = jnp.sum(
            jnp.where(target_col == peer * capacity + lane, gate, 0.0), axis=0, keepdims=True
        )
        gate_s[peer * 8 : (peer + 1) * 8, :] = jnp.broadcast_to(row, (8, 128))
    gates = ExpertExchange(gate_s, gates_s, gate_sems, 8)
    go.start(1)
    for group in range(3):
        gates.start(group)

    back = ExpertExchange(grad_s, back_s, back_sems, capacity)
    scores = ExpertExchange(score_s, score_in_s, score_sems, 8)
    tile = 768
    tiles = first_s.shape[1] // tile
    bufs, kept = [], []
    for group, (first_source, sources, _) in enumerate(go.groups):
        count = sources * capacity
        rows = pl.ds(pl.multiple_of(first_source * capacity, count), count)
        go.wait_recv(group)
        if group == 0:
            go.start(2)

        def halves(block, half, first=first_source * capacity, size=count // 2):
            return buf_ref.at[pl.ds(pl.multiple_of(block * tok + first + half * size, size), size)]

        def own(half, first=first_source * capacity, size=count // 2):
            return buf_s.at[pl.ds(pl.multiple_of(first + half * size, size), size)]

        bufs.append(BlockGather(halves, buf_sems, 6 * group, own))
        bufs[group].start()
        there = pl.ds(pl.multiple_of(blk * tok + first_source * capacity, count), count)
        kept.append(pltpu.make_async_copy(buf_s.at[rows], buf_ref.at[there], w_sem.at[6 + group]))
        kept[group].start()
        if group == 0:
            for load in weights:
                load.wait()
        x = buf_s[rows, :]
        for t in range(tiles):
            cut = slice(t * tile, (t + 1) * tile)
            act, slope = gelu_pair(dot(x, first_s[:, cut]))
            slope_s[0:count, cut] = slope
            part = dot(act.astype(BF16), second_s[cut, :])
            if t == 0:
                res_acc[0:count, :] = part
            else:
                res_acc[0:count, :] += part
        result = res_acc[0:count, :].astype(BF16)
        score = jnp.sum(
            result.astype(F32) * cot_in_ref[rows, :].astype(F32), axis=1, keepdims=True)
        for n in range(sources):
            row = flatten(score[n * capacity : (n + 1) * capacity], 128)
            score_s[rows_at(first_source + n, 8), :] = jnp.broadcast_to(row, (8, 128))
        scores.start(group)
        result_ref[rows, :] = result
        gates.wait_recv(group)
        for n in range(sources):
            row = gates_s[rows_at(first_source + n, 8), :][0:1, :]
            chunk = rows_at(first_source + n, capacity)
            grad_in_s[n * capacity : (n + 1) * capacity, :] = (
                cot_in_ref[chunk, :].astype(F32) * spread(row, capacity)
            ).astype(BF16)
        grad_in = grad_in_s[0:count, :]
        for t in range(tiles):
            cut = slice(t * tile, (t + 1) * tile)
            grad_hidden = (dot_nt(grad_in, second_s[cut, :]) * slope_s[0:count, cut]).astype(BF16)
            sent = dot_nt(grad_hidden, first_s[:, cut])
            if t == 0:
                sent_acc[0:count, :] = sent
            else:
                sent_acc[0:count, :] += sent
        grad_s[rows, :] = sent_acc[0:count, :].astype(BF16)
        back.start(group)
    bufs[0].forward()
    result_ref.flush()
    gates_ref[rows_at(blk, 64), :] = gates_s[...]
    gates_here = gates_ref.at[rows_at(blk, 64)]
    gates_out = [
        push(gates_here, gates_here, gates_sems, n, peer) for n, peer in enumerate(blk_peers())
    ]
    grad_out = cot_ref[...].astype(F32) * cols_ref[:, 3:4]

    for group in range(3):
        scores.wait_recv(group)
    grad_gate = jnp.zeros((tok, 1), F32)
    for peer in range(experts):
        row = score_in_s[peer * 8 : peer * 8 + 1, :]
        grad_gate += jnp.sum(
            jnp.where(target_col == peer * capacity + lane, row, 0.0), axis=1, keepdims=True
        )
    grad_logits = grad_gate * gate * (onehot - soft) / ROUTER_SOFTNESS
    grad_unit = fine(dot, grad_logits, anchor_unit)
    grad_projected = unit_scale * (
        grad_unit - unit * jnp.sum(unit * grad_unit, axis=1, keepdims=True)
    )
    grad_anchor_unit = fine(dot_tn, grad_logits, unit)
    grad_anchor = anchor_scale * (
        grad_anchor_unit
        - anchor_unit * jnp.sum(anchor_unit * grad_anchor_unit, axis=1, keepdims=True)
    )
    rdim = route_ref.shape[0]
    small_ref[...] = jnp.zeros_like(small_ref)
    small_ref[0:rdim, :] = fine(dot_tn, grad_projected, normed)
    small_ref[rdim : rdim + experts, 0:rdim] = grad_anchor
    counts = jnp.sum(onehot, axis=0, keepdims=True)
    small_ref[rdim + experts + 2 : rdim + experts + 3, 0:experts] = counts
    router_rows = fine(dot, grad_projected, route_ref[...])

    bufs[1].forward()
    for group in range(3):
        back.wait_recv(group)
    lanes = lax.broadcasted_iota(jnp.int32, (tok, tok), 1).astype(F32)
    moe_rows = dot(jnp.where(lanes == target_col, 1.0, 0.0).astype(BF16), back_s[...])
    grad_normed = moe_rows + router_rows
    small_ref[rdim + experts : rdim + experts + 1, :] = jnp.sum(
        grad_normed * xhat, axis=0, keepdims=True
    )
    grad_xhat = grad_normed * gain
    grad_residual = grad_out + scale * (
        grad_xhat
        - jnp.mean(grad_xhat, axis=1, keepdims=True)
        - xhat * jnp.mean(grad_xhat * xhat, axis=1, keepdims=True)
    )
    grad_residual_ref[...] = grad_residual
    grad_low = grad_residual.astype(BF16)
    grad_residual_ref.flush()
    bufs[2].forward()
    grad_att_ref[...] = dot_nt(proj_ref[...], grad_low).astype(BF16)
    grad_att_ref.flush()
    grad_proj_ref[...] = dot(att_ref[...], grad_low).astype(BF16)

    grad_proj_ref.flush()
    for copy in kept + [cots_own]:
        copy.wait()
    for gather in cots + bufs:
        gather.wait_neighbours()
        gather.wait_diagonal()
        gather.wait_sends()
    for exchange in (go, gates, back, scores):
        exchange.wait_sends()
    for copy in gates_out:
        copy.wait()


def gelu_pair(hidden):
    squared = hidden * hidden
    curve = jnp.tanh(0.7978845608028654 * hidden * (1.0 + 0.044715 * squared))
    half = 0.5 * (1.0 + curve)
    slope = half + 0.5 * hidden * (1.0 - curve * curve) * (
        0.7978845608028654 * (1.0 + 0.134145 * squared)
    )
    return hidden * half, slope


def spread(row, size):
    shape = (size, row.shape[1])
    eye = lax.broadcasted_iota(jnp.int32, shape, 0) == lax.broadcasted_iota(jnp.int32, shape, 1)
    return jnp.sum(jnp.where(eye, row, 0.0), axis=1, keepdims=True)


def flatten(column, width):
    shape = (column.shape[0], width)
    eye = lax.broadcasted_iota(jnp.int32, shape, 0) == lax.broadcasted_iota(jnp.int32, shape, 1)
    return jnp.sum(jnp.where(eye, column, 0.0), axis=0, keepdims=True)


def attend_back_kernel(
    grad_att_ref, qkv_ref, out_ref, lse_ref, nall_ref, result_ref, residual_ref, gate_ref,
    cols_ref, gain_ref, wqkv_ref, tok_ref, grad_residual_ref, grad_proj_ref, small_ref,
    buf_ref, cots_ref, gates_ref, first_ref, second_ref,
    block_out_ref, grad_tokens_ref, shared_ref, small_out_ref, grad_first_ref, grad_second_ref,
    do_t, dq_s, dqkv_s, home_s, back_s, wt_s, proj_in, part_s, sum_s,
    core_out, core_in, line_out, line_in, small_a, small_in, small_b, row_out, row_in,
    first_s, second_s, slot_s, rows_s, shared_s, first_acc, second_acc,
    att_sems, back_sems, home_sems, proj_sems, core_sems, line_sems, join_sems, small_sems,
    row_sems, ring_sems, pair_sems, load_sems,
):
    blk, expert, bx, by, bd = places()
    tok = grad_att_ref.shape[1]
    width = grad_att_ref.shape[0]
    heads = HEADS // 4
    group = heads * HEAD_DIM
    here = rows_at(blk, tok)
    length = qkv_ref.shape[1]
    core = lax.rem(expert, 2)
    line = expert // 2
    lines = 4
    half = width // 2
    other = (blk, expert + 1 - 2 * core)
    mine_lanes = pl.ds(pl.multiple_of(core * half, 128), half)
    other_lanes = pl.ds(pl.multiple_of((1 - core) * half, 128), half)
    line_peers = [(blk, lax.rem(line + shift, lines) * 2 + core) for shift in range(1, lines)]
    gain = gain_ref[...].reshape(1, width)
    arrived = greet(blk_peers() + expert_peers())
    odd = lax.rem(blk, 2)
    quarter = first_s.shape[1]

    def load(src, dst, index):
        copy = pltpu.make_async_copy(src, dst, load_sems.at[index])
        copy.start()
        return copy

    weights = [
        load(first_ref.at[:, rows_at(blk, quarter)], first_s, 0),
        load(second_ref.at[rows_at(blk, quarter)], second_s, 1),
    ]
    slot_loads = []

    def load_slots(t):
        cut = slice(t * tok, (t + 1) * tok)
        slot_loads.append((
            load(buf_ref.at[cut], slot_s.at[t % 2, 0], 2 + t % 2),
            load(cots_ref.at[cut], slot_s.at[t % 2, 1], 4 + t % 2),
        ))

    load_slots(0)
    rows_load = [load(residual_ref, rows_s, 6)]
    mine = rows_at(blk, group)
    mine_load = load(grad_att_ref.at[mine], do_t.at[:, here], 7)
    own_slots = rows_at(expert, tok // 8)
    result_load = load(result_ref.at[own_slots], back_s.at[own_slots], 8)
    arrived()
    att_copies = []

    def send_att(head):
        cut = slice(head * 64, (head + 1) * 64)
        att_copies.append([
            push(
                grad_att_ref.at[pl.ds(pl.multiple_of(peer[0] * group + head * 64, 64), 64)],
                do_t.at[cut, here], att_sems, head * 3 + n, peer)
            for n, peer in enumerate(blk_peers())
        ])

    send_att(0)
    back = ExpertExchange(result_ref, back_s, back_sems, tok // 8)
    small_core = push(small_ref.at[:, other_lanes], small_in.at[0], small_sems, 0, other)
    for part in range(3):
        first = pl.multiple_of(part * width + blk * group - odd * 64, 128)
        wide = wqkv_ref[:, pl.ds(first, 256)]
        narrow = jnp.where(odd == 1, wide[:, 64:256], wide[:, 0:192]).T
        for head in range(heads):
            place = head * 192 + part * 64
            wt_s[place : place + 64, :] = narrow[head * 64 : (head + 1) * 64]

    def expert_weights(t):
        if t == 0:
            for copy in weights:
                copy.wait()
        if t < 3:
            load_slots(t + 1)
        for copy in slot_loads[t]:
            copy.wait()
        x = slot_s[t % 2, 0]
        rates = [spread(gates_ref[t * 64 + n * 8 : t * 64 + n * 8 + 1, :], 64) for n in range(8)]
        rate = jnp.concatenate(rates, axis=0)
        grad_in = (slot_s[t % 2, 1].astype(F32) * rate).astype(BF16)
        act, slope = gelu_pair(dot(x, first_s[...]))
        grad_hidden = (dot_nt(grad_in, second_s[...]) * slope).astype(BF16)
        grad_second = dot_tn(act.astype(BF16), grad_in)
        grad_first = dot_tn(x, grad_hidden)
        if t == 0:
            second_acc[...] = grad_second
            first_acc[...] = grad_first
        elif t < 3:
            second_acc[...] += grad_second
            first_acc[...] += grad_first
        else:
            grad_second_ref[...] = (second_acc[...] + grad_second).astype(BF16)
            grad_first_ref[...] = (first_acc[...] + grad_first).astype(BF16)

    send_att(1)
    expert_weights(0)
    send_att(2)
    small_core.wait()
    small_a[...] = small_ref[:, mine_lanes] + small_in[0]
    small_in[1 + line] = small_a[...]
    small_line = [
        push(small_a, small_in.at[1 + line], small_sems, 1 + n, peer)
        for n, peer in enumerate(line_peers)
    ]
    back.start_all(False)
    mine_load.wait()
    proj_copies = [
        push(grad_proj_ref.at[rows_at(peer[0], group)], proj_in.at[n], proj_sems, n, peer)
        for n, peer in enumerate(blk_peers())
    ]

    chunk_rows = group
    piece = chunk_rows // lines
    core_copies, line_copies, joins, gathers, pairs = {}, {}, {}, {}, []
    small_blk = []

    def chunk_at(c):
        return slice(c * chunk_rows, (c + 1) * chunk_rows)

    def shared_at(block, c, first, size):
        row = pl.multiple_of(block * width + c * chunk_rows + first, 16)
        return shared_ref.at[pl.ds(row, size), mine_lanes]

    def send_core(c):
        core_out[chunk_at(c), :] = part_s[chunk_at(c), other_lanes].astype(BF16)
        core_copies[c] = push(
            core_out.at[chunk_at(c)], core_in.at[chunk_at(c)], core_sems, c, other)

    def send_line(c):
        core_copies[c].wait()
        summed = part_s[chunk_at(c), mine_lanes] + core_in[chunk_at(c), :].astype(F32)
        sum_s[chunk_at(c), :] = summed
        line_out[chunk_at(c), :] = summed.astype(BF16)
        line_copies[c] = [
            push(
                line_out.at[pl.ds(
                    pl.multiple_of(c * chunk_rows + (peer[1] // 2) * piece, piece), piece)],
                line_in.at[c * 3 + n], line_sems, c * 3 + n, peer)
            for n, peer in enumerate(line_peers)
        ]

    def send_join(c):
        for copy in line_copies[c]:
            copy.wait()
        first = pl.multiple_of(c * chunk_rows + line * piece, piece)
        total = sum_s[pl.ds(first, piece), :]
        for n in range(3):
            total = total + line_in[c * 3 + n].astype(F32)
        shared_s[c] = total.astype(BF16)
        ref = shared_at(blk, c, line * piece, piece)
        joins[c] = [
            push(shared_s.at[c], ref, join_sems, c * 3 + n, peer)
            for n, peer in enumerate(line_peers)]
        joins[c].append(load(shared_s.at[c], ref, 9 + c))

    def pair(block, c):
        ref = shared_at(block, c, 0, chunk_rows)
        pairs.append(push(ref, ref, pair_sems, len(pairs), other))

    def send_ring(c):
        for copy in joins[c]:
            copy.wait()
        size = chunk_rows // 2
        gathers[c] = BlockGather(
            lambda block, part: shared_at(block, c, part * size, size), ring_sems, c * 6)
        gathers[c].start()
        pair(blk, c)

    def forward(c):
        gathers[c].forward()

    def pair_neighbours(c):
        gathers[c].wait_neighbours()
        pair(bx, c)
        pair(by, c)

    def pair_diagonal(c):
        gathers[c].wait_diagonal()
        pair(bd, c)

    def sum_proj():
        for copy in proj_copies:
            copy.wait()
        part_s[chunk_at(3), :] = (
            (grad_proj_ref[mine, :].astype(F32) + proj_in[0].astype(F32))
            + (proj_in[1].astype(F32) + proj_in[2].astype(F32))
        )
        send_core(3)

    def sum_small():
        for copy in small_line:
            copy.wait()
        small_b[...] = (small_in[1] + small_in[2]) + (small_in[3] + small_in[4])
        small_in[5 + blk] = small_b[...]
        small_blk.extend(
            push(small_b, small_in.at[5 + blk], small_sems, 4 + n, peer)
            for n, peer in enumerate(blk_peers())
        )

    sent = []

    def send_home(head, part, block):
        src = slice(head * 192 + part * 64, head * 192 + (part + 1) * 64)
        there = pl.ds(pl.multiple_of(part * width + blk * group + head * 64, 64), 64)

        def copy():
            return pltpu.make_async_remote_copy(
                src_ref=dqkv_s.at[src, block * tok : (block + 1) * tok],
                dst_ref=home_s.at[there],
                send_sem=home_sems.at[0, (block * heads + head) * 3 + part],
                recv_sem=home_sems.at[1, (blk * heads + head) * 3 + part],
                device_id=(block, expert),
                device_id_type=MESH,
            )

        @pl.when(blk != block)
        def _():
            copy().start()

        @pl.when(blk == block)
        def _():
            home_s[there, :] = dqkv_s[src, block * tok : (block + 1) * tok]

        sent.append((block, copy))

    after = {
        (1, 1): [sum_small],
        (1, 3): [lambda: send_line(0)],
        (1, 5): [sum_proj],
        (2, 0): [lambda: send_line(3)],
        (2, 1): [lambda: send_join(0)],
        (2, 3): [lambda: send_line(1)],
        (2, 5): [lambda: send_ring(0)],
        (2, 7): [lambda: send_join(3), lambda: send_join(1)],
    }
    gain_total = None
    for head in range(heads):
        cut = slice(head * 64, (head + 1) * 64)
        kt_cut = slice(group + head * 64, group + (head + 1) * 64)
        vt_cut = slice(2 * group + head * 64, 2 * group + (head + 1) * 64)
        for copy in att_copies[head]:
            copy.wait_recv()
        delta = jnp.sum(out_ref[cut, :] * do_t[cut, :].astype(F32), axis=0, keepdims=True)
        base = head * 192
        step = tok // 2
        for j in range(length // step):
            keys = slice(j * step, (j + 1) * step)
            queries = slice(j * step, length)
            s = dot_tn(qkv_ref[kt_cut, keys], qkv_ref[cut, queries])
            p = jnp.exp(s - lse_ref[head : head + 1, queries])
            edge = jnp.where(lower_triangle(step, step), p[:, :step], 0.0)
            p = edge if p.shape[1] == step else jnp.concatenate([edge, p[:, step:]], axis=1)
            dp = dot_tn(qkv_ref[vt_cut, keys], do_t[cut, queries])
            ds = (p * (dp - delta[:, queries])).astype(BF16)
            dv = dot_nt(do_t[cut, queries], p.astype(BF16))
            dk = dot_nt(qkv_ref[cut, queries], ds)
            dqkv_s[base + 64 : base + 128, keys] = dk.astype(BF16)
            dqkv_s[base + 128 : base + 192, keys] = dv.astype(BF16)
            if j % 2:
                send_home(head, 1, j // 2)
                send_home(head, 2, j // 2)
            dq = dot(qkv_ref[kt_cut, keys], ds)
            if j == 0:
                dq_s[...] = dq
            else:
                dq_s[:, queries] += dq
            for action in after.get((head, j), ()):
                action()
        dqkv_s[base : base + 64, :] = (dq_s[...] * HEAD_DIM**-0.5).astype(BF16)
        for block in range(4):
            send_home(head, 0, block)
        grad_group = dot(dqkv_s[base : base + 192, :], nall_ref[...])
        part_s[chunk_at(head), :] = grad_group
        send_core(head)
        share = jnp.sum(
            grad_group * wt_s[base : base + 192, :].astype(F32), axis=0, keepdims=True)
        gain_total = share if gain_total is None else gain_total + share

    attn_gain = gain_total / gain
    row_out[0] = jnp.concatenate(
        [attn_gain[:, n * 128 : (n + 1) * 128] for n in range(width // 128)]
        + [jnp.zeros((8 - width // 128, 128), F32)], axis=0)
    row_core = push(row_out.at[0], row_in.at[0], row_sems, 0, other)
    send_line(2)
    send_ring(3)
    send_ring(1)
    for copy in small_blk:
        copy.wait()
    small_out_ref[:, mine_lanes] = (small_in[5] + small_in[6]) + (small_in[7] + small_in[8])
    small_pair = push(
        small_out_ref.at[:, mine_lanes], small_out_ref.at[:, mine_lanes], small_sems, 7, other)
    row_core.wait()
    row_out[1] = row_out[0] + row_in[0]
    row_in[1 + line] = row_out[1]
    row_line = [
        push(row_out.at[1], row_in.at[1 + line], row_sems, 1 + n, peer)
        for n, peer in enumerate(line_peers)
    ]
    back.wait_all()
    result_load.wait()
    lanes = lax.broadcasted_iota(jnp.int32, (tok, tok), 1).astype(F32)
    chosen = jnp.where(lanes == cols_ref[:, 0:1], 1.0, 0.0).astype(BF16)
    fetched = dot(chosen, back_s[...])
    rows_load[0].wait()
    block_out_ref[...] = (rows_s[...] + gate_ref[:, 0:1] * fetched).astype(BF16)
    block_out_ref.flush()
    rows_load.append(load(grad_residual_ref, rows_s, 6))
    expert_weights(1)
    send_join(2)
    forward(0)
    for copy in row_line:
        copy.wait()
    row_out[2] = (row_in[1] + row_in[2]) + (row_in[3] + row_in[4])
    row_in[5 + blk] = row_out[2]
    row_blk = [
        push(row_out.at[2], row_in.at[5 + blk], row_sems, 4 + n, peer)
        for n, peer in enumerate(blk_peers())
    ]
    expert_weights(2)
    send_ring(2)
    forward(3)
    expert_weights(3)
    grad_first_ref.flush()
    grad_second_ref.flush()
    forward(1)
    pair_neighbours(0)
    pair_diagonal(0)
    pair_neighbours(3)

    for source in range(4):
        @pl.when(blk != source)
        def _():
            for item in range(9):
                index = source * 9 + item
                pltpu.make_async_remote_copy(
                    src_ref=dqkv_s.at[0:64, 0:tok],
                    dst_ref=home_s.at[0:64],
                    send_sem=home_sems.at[0, index],
                    recv_sem=home_sems.at[1, index],
                    device_id=(source, expert),
                    device_id_type=MESH,
                ).wait_recv()
    rows_load[1].wait()
    xhat, scale = standardise(tok_ref[...].astype(F32))

    def tokens_part(n):
        cut = slice(n * 256, (n + 1) * 256)
        grad_normed = dot(wqkv_ref[...], home_s[:, cut]).T
        grad_xhat = grad_normed * gain
        x = xhat[cut]
        grad_tokens_ref[cut, :] = (rows_s[cut, :] + scale[cut] * (
            grad_xhat
            - jnp.mean(grad_xhat, axis=1, keepdims=True)
            - x * jnp.mean(grad_xhat * x, axis=1, keepdims=True)
        )).astype(BF16)

    forward(2)
    tokens_part(0)
    pair_diagonal(3)
    pair_neighbours(1)
    tokens_part(1)
    grad_tokens_ref.flush()
    pair_diagonal(1)
    pair_neighbours(2)
    pair_diagonal(2)
    for copy in row_blk:
        copy.wait()
    small_pair.wait()
    total = (row_in[5] + row_in[6]) + (row_in[7] + row_in[8])
    small_out_ref[25:26, :] = jnp.concatenate(
        [total[n : n + 1, :] for n in range(width // 128)], axis=1)
    for copy in pairs:
        copy.wait_recv()
    for copy in pairs:
        copy.wait_send()
    for gather in gathers.values():
        gather.wait_sends()
    for copy in sum(att_copies, []):
        copy.wait_send()
    for block, copy in sent:
        @pl.when(blk != block)
        def _():
            copy().wait_send()


def unfold_kernel(
    shared_ref, small_ref, histogram_ref, block_out_ref, tokens_ref, first_ref, second_ref,
    grad_qkv_ref, grad_proj_ref, attn_gain_ref, moe_gain_ref, route_ref, anchor_ref, counts_ref,
    block_out_out, tokens_out, first_out, second_out,
    in_s, qkv_s, proj_s, block_out_s, tokens_s, first_s, second_s, tokens_w, first_w, second_w,
    in_sems, qkv_sems, proj_sem, move_sems,
):
    blocks = in_s.shape[0]
    width = in_s.shape[2]
    group = width // blocks
    rdim, experts = route_ref.shape[0], anchor_ref.shape[0]
    loads = []
    for block in range(blocks):
        loads.append(pltpu.make_async_copy(
            shared_ref.at[block * width : (block + 1) * width], in_s.at[block], in_sems.at[block]))
        loads[-1].start()
    narrow = (first_s, second_s, tokens_s, block_out_s)
    wide = (first_w, second_w, tokens_w, block_out_s)
    sources = (first_ref, second_ref, tokens_ref, block_out_ref)
    results = (first_out, second_out, tokens_out, block_out_out)
    moves = [
        (pltpu.make_async_copy(sources[n], narrow[n], move_sems.at[0, n]),
         pltpu.make_async_copy(wide[n], results[n], move_sems.at[1, n]))
        for n in range(4)
    ]
    for load, _ in moves:
        load.start()
    route_ref[...] = small_ref[0:rdim, :]
    anchor_ref[...] = small_ref[rdim : rdim + experts, 0:rdim]
    moe_gain_ref[...] = small_ref[rdim + experts : rdim + experts + 1, :].reshape(width)
    attn_gain_ref[...] = small_ref[rdim + experts + 1 : rdim + experts + 2, :].reshape(width)
    counts = small_ref[rdim + experts + 2 : rdim + experts + 3, 0:experts].astype(jnp.int32)
    counts_ref[...] = histogram_ref[...] + counts.reshape(experts)
    stores = []
    for n, (load, store) in enumerate(moves):
        load.wait()
        if wide[n] is not narrow[n]:
            wide[n][...] = narrow[n][...].astype(F32)
        store.start()
    for first in range(0, blocks, 2):
        for block in range(first, first + 2):
            loads[block].wait()
            proj_s[block * group : (block + 1) * group, :] = (
                in_s[block, 3 * group :, :].astype(F32))
        for part in range(3):
            cut = slice(part * width + first * group, part * width + (first + 2) * group)
            qkv_s[:, cut] = jnp.concatenate(
                [
                    in_s[block, head * 192 + part * 64 : head * 192 + part * 64 + 64, :]
                    for block in range(first, first + 2)
                    for head in range(group // HEAD_DIM)
                ],
                axis=0,
            ).T.astype(F32)
            stores.append(pltpu.make_async_copy(
                qkv_s.at[:, cut], grad_qkv_ref.at[:, cut], qkv_sems.at[len(stores)]))
            stores[-1].start()
    stores.append(pltpu.make_async_copy(proj_s, grad_proj_ref, proj_sem.at[0]))
    stores[-1].start()
    for copy in stores + [store for _, store in moves]:
        copy.wait()


def unfold(shared, small, histogram, moved, rdim, experts):
    width = shared.shape[1]
    blocks = shared.shape[0] // width
    whole, outside = pl.BlockSpec(memory_space=pltpu.VMEM), pl.BlockSpec(memory_space=pl.ANY)
    shapes = [
        ((width, 3 * width), F32), ((width, width), F32), ((width,), F32), ((width,), F32),
        ((rdim, width), F32), ((experts, rdim), F32), ((experts,), jnp.int32),
    ]
    dma = pltpu.SemaphoreType.DMA
    return pl.pallas_call(
        unfold_kernel,
        out_shape=tuple(jax.ShapeDtypeStruct(*shape) for shape in shapes)
        + tuple(
            jax.ShapeDtypeStruct(array.shape, F32 if n else array.dtype)
            for n, array in enumerate(moved)),
        in_specs=[outside, whole, whole] + [outside] * len(moved),
        out_specs=tuple([outside] * 2 + [whole] * 5 + [outside] * len(moved)),
        scratch_shapes=[
            pltpu.VMEM((blocks, width, width), BF16), pltpu.VMEM((width, 3 * width), F32),
            pltpu.VMEM((width, width), F32),
        ]
        + [pltpu.VMEM(array.shape, array.dtype) for array in moved]
        + [pltpu.VMEM(array.shape, F32) for array in moved[1:]]
        + [dma((blocks,)), dma((3 * blocks // 2,)), dma((1,)), dma((2, len(moved)))],
        name="unfold",
        compiler_params=pltpu.CompilerParams(vmem_limit_bytes=VMEM_BYTES),
    )(shared, small, histogram, *moved)


def call(kernel, name, args, outs, scratch, lazy=(), lazy_out=(), in_any=(), out_any=(),
         collective=None):
    n_in, n_out = len(args), len(outs)
    shapes = tuple(jax.ShapeDtypeStruct(shape, dtype) for shape, dtype in outs)
    staged = [pltpu.VMEM(args[n].shape, args[n].dtype) for n in lazy]
    staged += [pltpu.VMEM(shapes[n].shape, shapes[n].dtype) for n in lazy_out]
    sems = [pltpu.SemaphoreType.DMA((len(staged),))] if staged else []

    def wrapped(*refs):
        ins, results = list(refs[:n_in]), list(refs[n_in : n_in + n_out])
        rest = refs[n_in + n_out : n_in + n_out + len(scratch)]
        extra = refs[n_in + n_out + len(scratch) :]
        for k, n in enumerate(lazy):
            ins[n] = Lazy(ins[n], extra[k], extra[-1].at[k])
        for k, n in enumerate(lazy_out):
            k += len(lazy)
            results[n] = LazyOut(extra[k], results[n], extra[-1].at[k])
        kernel(*ins, *results, *rest)
        for n in lazy_out:
            results[n].flush()
        for n in lazy:
            ins[n].ref()
        for n in lazy_out:
            results[n].copy.wait()

    def spec(n, outside):
        return pl.BlockSpec(memory_space=pl.ANY if n in outside else pltpu.VMEM)

    return pl.pallas_call(
        wrapped,
        out_shape=shapes,
        in_specs=[spec(n, tuple(lazy) + tuple(in_any)) for n in range(n_in)],
        out_specs=tuple(spec(n, tuple(lazy_out) + tuple(out_any)) for n in range(n_out)),
        scratch_shapes=list(scratch) + staged + sems,
        name=name,
        compiler_params=pltpu.CompilerParams(
            vmem_limit_bytes=VMEM_BYTES,
            collective_id=collective,
            has_side_effects=collective is not None,
        ),
    )(*args)


def fast_body(
    tokens, cotangent, loss_mask, routes, priority, histogram, qkv_weight, proj_weight, attn_gain,
    moe_gain, route_weight, anchor_table, first_weight, second_weight,
):
    tok, width = tokens.shape[1:]
    blocks, experts = lax.axis_size("blk"), lax.axis_size("expert")
    length = tok * blocks
    heads = HEADS // blocks
    group = heads * HEAD_DIM
    hidden = first_weight.shape[2]
    x, cot = tokens[0], cotangent[0]
    gains = [attn_gain, moe_gain]
    rows = [routes.reshape(1, tok), priority.reshape(1, tok), loss_mask.reshape(1, tok)]
    dma = pltpu.SemaphoreType.DMA
    (nall, qkv, out, lse, cols, result, residual, gate, grad_residual, grad_att, grad_proj, small,
     buf, cots, gates) = call(
        forward_kernel, "forward",
        (x, *gains, *rows, qkv_weight, cot, proj_weight, route_weight.T, anchor_table, first_weight[0],
         second_weight[0]),
        [((length, width), BF16), ((3 * group, length), BF16), ((group, length), F32),
         ((8, length), F32), ((tok, 128), F32),
         ((tok, width), BF16), ((tok, width), F32), ((tok, 128), F32), ((tok, width), F32),
         ((width, tok), BF16), ((width, width), BF16), ((32, width), F32),
         ((length, width), BF16), ((length, width), BF16), ((blocks * 64, 128), F32)],
        [pltpu.VMEM((3, width, 256), BF16), pltpu.VMEM((3 * group, width), BF16),
         pltpu.VMEM((heads, length, HEAD_DIM), BF16), pltpu.VMEM((group, length), BF16),
         pltpu.VMEM((tok, width), BF16), pltpu.VMEM((width, tok), BF16),
         pltpu.VMEM((tok, width), BF16),
         pltpu.VMEM((width, hidden), BF16), pltpu.VMEM((hidden, width), BF16),
         pltpu.VMEM((tok // 2, hidden), F32),
         pltpu.VMEM((tok, width), BF16), pltpu.VMEM((64, 128), F32),
         pltpu.VMEM((tok, width), BF16), pltpu.VMEM((64, 128), F32), pltpu.VMEM((tok, width), BF16),
         pltpu.VMEM((tok, width), BF16), pltpu.VMEM((64, 128), F32), pltpu.VMEM((64, 128), F32),
         pltpu.VMEM((tok // 2, width), F32), pltpu.VMEM((tok // 2, width), F32),
         pltpu.VMEM((tok // 2, width), BF16),
         dma((9,)), dma((2, 6)), dma((2, experts)), dma((2, blocks * heads)), dma((2, experts)),
         dma((2, experts)), dma((2, experts)), dma((2, experts)), dma((2, 12)), dma((2, 18)),
         dma((2, 3))],
        lazy=(7, 8), lazy_out=(0, 1, 2, 4, 5, 6, 7, 8, 9, 10), in_any=(6, 11, 12), out_any=(12, 13),
        collective=1,
    )
    half, piece, quarter = width // 2, group // 4, hidden // blocks
    block_out, grad_tokens, shared, small, grad_first, grad_second = call(
        attend_back_kernel, "attend_back",
        (grad_att, qkv, out, lse, nall, result, residual, gate, cols, attn_gain, qkv_weight, x,
         grad_residual, grad_proj, small, buf, cots, gates, first_weight[0], second_weight[0]),
        [((tok, width), BF16), ((tok, width), BF16), ((blocks * width, width), BF16),
         ((32, width), F32), ((width, quarter), BF16), ((quarter, width), BF16)],
        [pltpu.VMEM((group, length), BF16), pltpu.VMEM((HEAD_DIM, length), F32),
         pltpu.VMEM((3 * group, length), BF16), pltpu.VMEM((3 * width, tok), BF16)]
        + [pltpu.VMEM((tok, width), BF16), pltpu.VMEM((3 * group, width), BF16),
           pltpu.VMEM((3, group, width), BF16),
           pltpu.VMEM((width, width), F32), pltpu.VMEM((width, half), F32),
           pltpu.VMEM((width, half), BF16), pltpu.VMEM((width, half), BF16),
           pltpu.VMEM((width, half), BF16), pltpu.VMEM((12, piece, half), BF16),
           pltpu.VMEM((32, half), F32), pltpu.VMEM((9, 32, half), F32), pltpu.VMEM((32, half), F32),
           pltpu.VMEM((3, 8, 128), F32), pltpu.VMEM((9, 8, 128), F32),
           pltpu.VMEM((width, quarter), BF16), pltpu.VMEM((quarter, width), BF16),
           pltpu.VMEM((2, 2, tok, width), BF16), pltpu.VMEM((tok, width), F32),
           pltpu.VMEM((4, piece, half), BF16), pltpu.VMEM((width, quarter), F32),
           pltpu.VMEM((quarter, width), F32),
           dma((2, 9)), dma((2, experts)), dma((2, 36)), dma((2, 3)), dma((2, 4)), dma((2, 12)),
           dma((2, 12)), dma((2, 8)), dma((2, 7)), dma((2, 24)), dma((2, 16)), dma((13,))],
        lazy=(1, 2, 4, 7, 8, 10, 11, 13), lazy_out=(0, 1, 4, 5),
        in_any=(0, 5, 6, 12, 15, 16, 18, 19), out_any=(2,), collective=3,
    )
    (grad_qkv, grad_proj, grad_attn_gain, grad_moe_gain, grad_route, grad_anchor, counts,
     block_out, grad_tokens, grad_first, grad_second) = unfold(
        shared, small, histogram, (block_out, grad_tokens, grad_first, grad_second),
        route_weight.shape[1], experts)
    return (
        block_out[None],
        grad_tokens[None],
        grad_qkv,
        grad_proj,
        grad_attn_gain,
        grad_moe_gain,
        grad_route.T,
        grad_anchor,
        grad_first[None],
        grad_second[None],
        counts,
    )


def solution(mesh):
    in_specs = (
        P("expert", "blk", None),
        P("expert", "blk", None),
        P("expert", "blk"),
        P("expert", "blk", None),
        P("expert", "blk", None),
        P(),
        P(),
        P(),
        P(),
        P(),
        P(),
        P(),
        P("expert", None, None),
        P("expert", None, None),
    )
    out_specs = (
        P("expert", "blk", None),
        P("expert", "blk", None),
        P(),
        P(),
        P(),
        P(),
        P(),
        P(),
        P("expert", None, "blk"),
        P("expert", "blk", None),
        P(),
    )
    blocks, experts = mesh.shape["blk"], mesh.shape["expert"]
    body = fast_body if (blocks, experts) == (4, 8) else general_body
    return jax.shard_map(body, mesh=mesh, in_specs=in_specs, out_specs=out_specs, check_vma=False)
```
